32 devices in a mesh: grp: 2 (over y), row: 4 (over x, core), col: 4 (over z).
Axes of the slice: x: 2, y: 2, z: 4, core: 2. Of those that a mesh axis runs over, the one named last changes fastest.
Arguments:
- homolog_embedding: bfloat16 [256, 32, 64], P(('grp', 'col'), 'row'), parts along dimension 0, may hold values from -6 to 6
- presence_indicator: int32 [256, 32], P(('grp', 'col'), 'row'), parts along dimension 0, may hold values 0 or 1
- coupling_change_derivative: bfloat16 [64, 32, 128], P(('grp', 'row'), 'col'), parts along dimension 0, may hold values from -1.5 to 1.5
- standardizer_scale: float32 [64], replicated, may hold values from 0.5 to 1.5
- standardizer_shift: float32 [64], replicated, may hold values from -3 to 3
- first_projection_matrix: bfloat16 [64, 32], replicated, may hold values from -0.75 to 0.75
- second_projection_matrix: bfloat16 [64, 32], replicated, may hold values from -0.75 to 0.75
- final_projection_matrix: bfloat16 [1024, 128], replicated, may hold values from -0.1875 to 0.1875
Outputs:
- embedding_derivative: float32 [256, 32, 64], P(('grp', 'col'), 'row'), parts along dimension 0
- final_matrix_derivative: float32 [2048, 128], P('grp'), parts along dimension 0
- first_matrix_derivative: float32 [128, 32], P('grp'), parts along dimension 0
- second_matrix_derivative: float32 [128, 32], P('grp'), parts along dimension 0
- scale_factor_derivative: float32 [128], P('grp'), parts along dimension 0
- shift_term_derivative: float32 [128], P('grp'), parts along dimension 0
- shift_derivative: float32 [256], P('grp'), parts along dimension 0
The draws below stay inside these ranges and needn't reach their ends.
There are 2 independent parts, one for each index of `grp`. The reference program is written for one: setup_inputs(seed, part) draws one part's arguments, and reference() takes and returns one part's arrays. A program takes and returns all parts, laid end to end along the dimension named above; an argument that names none is the same for every part. Nothing has to cross between parts.
All inputs are finite; a program needn't handle non-finite values. No bound on the sum of `presence_indicator` on one device may be relied on, other than what follows from the above.
Results may differ from the reference program's by a relative error of at most 0.0066.
Values may be sent and summed in bfloat16 or wider, within the bound.
No kernel may reach another device: no remote copies, remote signals or barrier semaphores. Data moves between devices by JAX's collectives and lax.ppermute only.
A program may use at most 64 MiB of HBM per device.

```python
import jax
import jax.numpy as jnp
from jax import lax

FEATURE_WIDTH = 64
FACTOR_WIDTH = 32
COUPLING_WIDTH = 128
HOMOLOG_NUMBER = 128
RESIDUE_WINDOW = 32
N_COL = 4


def set_ends(array, rng, smallest, high):
    longest = array.shape.index(max(array.shape))
    spots = []
    for shift in (0, 1):
        where = [jax.random.randint(jax.random.fold_in(rng, axis), (), 0, length) for axis, length in enumerate(array.shape)]
        where[longest] = (where[longest] + shift) % array.shape[longest]
        spots.append(tuple(where))
    return array.at[spots[0]].set(smallest).at[spots[1]].set(high)


def level_of(stream_key, shape, shards, smallest, largest):
    def one(dim, parts):
        steps = jax.random.uniform(jax.random.fold_in(jax.random.fold_in(stream_key, 6), dim), (parts,), jnp.float32, smallest / len(shards), largest / len(shards))
        return jnp.repeat(jnp.exp(steps), shape[dim] // parts).reshape((-1,) + (1,) * (len(shape) - dim - 1))

    gain = one(*shards[0])
    for cut in shards[1:]:
        gain = gain * one(*cut)
    return gain


def centred(own_key, shape, scale, reach, cuts=(), held_as=jnp.bfloat16):
    gain = level_of(own_key, shape, cuts, -0.22, 0.18) if cuts else 1.0
    values = jax.random.normal(own_key, shape, jnp.float32) * scale * gain
    return jnp.minimum(jnp.maximum(values, -reach), reach).astype(held_as)


def setup_inputs(seed: int = 0, part: int = 0) -> dict:
    streams_of = jax.random.split(jax.random.key(seed), 9)
    part_splits = jax.random.split(jax.random.fold_in(streams_of[8], part), 9)
    return {
        "homolog_embedding": centred(part_splits[0], (HOMOLOG_NUMBER, RESIDUE_WINDOW, FEATURE_WIDTH), 1.0, 6.0, ((0, 4), (1, 4))),
        "presence_indicator": set_ends((jax.random.randint(part_splits[1], (HOMOLOG_NUMBER, RESIDUE_WINDOW), 0, 5) < 4).astype(jnp.int32), jax.random.fold_in(part_splits[1], 1), 0, 1),
        "coupling_change_derivative": centred(part_splits[2], (RESIDUE_WINDOW, RESIDUE_WINDOW, COUPLING_WIDTH), 0.25, 1.5, ((0, 4), (1, 4))),
        "standardizer_scale": jnp.clip(1.0 + 0.1 * jax.random.normal(streams_of[3], (FEATURE_WIDTH,), jnp.float32), 0.5, 1.5),
        "standardizer_shift": centred(streams_of[4], (FEATURE_WIDTH,), 0.5, 3.0, (), jnp.float32),
        "first_projection_matrix": centred(streams_of[5], (FEATURE_WIDTH, FACTOR_WIDTH), FEATURE_WIDTH ** -0.5, 0.75),
        "second_projection_matrix": centred(streams_of[6], (FEATURE_WIDTH, FACTOR_WIDTH), FEATURE_WIDTH ** -0.5, 0.75),
        "final_projection_matrix": centred(streams_of[7], (FACTOR_WIDTH * FACTOR_WIDTH, COUPLING_WIDTH), (FACTOR_WIDTH * FACTOR_WIDTH) ** -0.5, 0.1875),
    }


def standardizer_parts(homolog_embedding, standardizer_scale, standardizer_shift):
    incoming_entries = homolog_embedding.astype(jnp.float32)
    center = lax.optimization_barrier(jnp.mean(incoming_entries, axis=-1, keepdims=True))
    varied = incoming_entries - center
    variance = lax.optimization_barrier(jnp.mean(varied * varied, axis=-1, keepdims=True))
    reciprocal_spread = lax.rsqrt(variance + 1e-05)
    standardized_entries = varied * reciprocal_spread
    standardized_bfloat = (standardized_entries * standardizer_scale + standardizer_shift).astype(jnp.bfloat16)
    return (standardized_entries, reciprocal_spread, standardized_bfloat)

def reference(homolog_embedding, presence_indicator, coupling_change_derivative, standardizer_scale, standardizer_shift, first_projection_matrix, second_projection_matrix, final_projection_matrix):
    standardized_entries, reciprocal_spread, standardized_bfloat = standardizer_parts(homolog_embedding, standardizer_scale, standardizer_shift)
    mask_single_precision = presence_indicator.astype(jnp.float32)
    normal_f = standardized_bfloat.astype(jnp.float32)
    left = (jnp.einsum('sic,cp->sip', normal_f, first_projection_matrix.astype(jnp.float32)) * mask_single_precision[..., None]).astype(jnp.bfloat16)
    right = (jnp.einsum('sic,cp->sip', normal_f, second_projection_matrix.astype(jnp.float32)) * mask_single_precision[..., None]).astype(jnp.bfloat16)
    counts = jnp.einsum('si,sj->ij', mask_single_precision, mask_single_precision)
    scaled = coupling_change_derivative.astype(jnp.float32) / (counts + 0.001)[..., None]
    shift_derivative = lax.optimization_barrier(jnp.sum(scaled, axis=(0, 1)))
    scaled_bf = scaled.astype(jnp.bfloat16)
    wout_f = final_projection_matrix.astype(jnp.float32)
    left_f = left.astype(jnp.float32)
    right_f = right.astype(jnp.float32)

    def step(carry, index):
        right_acc, wout_acc = carry
        start = (index * N_COL).astype(jnp.int32)
        rows_f = lax.dynamic_slice_in_dim(scaled_bf, start, N_COL, 0).astype(jnp.float32)
        outer_grad = jnp.einsum('ijz,fz->ijf', rows_f, wout_f)
        outer_grad = lax.optimization_barrier(outer_grad.astype(jnp.bfloat16)).astype(jnp.float32)
        outer_grad = outer_grad.reshape(N_COL, RESIDUE_WINDOW, FACTOR_WIDTH, FACTOR_WIDTH)
        left_rows = lax.dynamic_slice_in_dim(left_f, start, N_COL, 1)
        first_factor_derivative = jnp.einsum('ijce,sje->sic', outer_grad, right_f)
        right_acc = right_acc + jnp.einsum('ijce,sic->sje', outer_grad, left_rows)
        outer = jnp.einsum('sic,sje->ijce', left_rows, right_f)
        outer = lax.optimization_barrier(outer.astype(jnp.bfloat16)).astype(jnp.float32)
        outer = outer.reshape(N_COL, RESIDUE_WINDOW, FACTOR_WIDTH * FACTOR_WIDTH)
        wout_acc = wout_acc + jnp.einsum('ijf,ijz->fz', outer, rows_f)
        return ((right_acc, wout_acc), first_factor_derivative)
    initial_accumulator = (jnp.zeros((HOMOLOG_NUMBER, RESIDUE_WINDOW, FACTOR_WIDTH), jnp.float32), jnp.zeros((FACTOR_WIDTH * FACTOR_WIDTH, COUPLING_WIDTH), jnp.float32))
    (right_grad, final_matrix_derivative), fragments = lax.scan(step, initial_accumulator, jnp.arange(RESIDUE_WINDOW // N_COL, dtype=jnp.int32))
    first_factor_derivative = jnp.transpose(fragments, (1, 0, 2, 3)).reshape(HOMOLOG_NUMBER, RESIDUE_WINDOW, FACTOR_WIDTH)
    left_in = (first_factor_derivative * mask_single_precision[..., None]).astype(jnp.bfloat16).astype(jnp.float32)
    right_in = (right_grad * mask_single_precision[..., None]).astype(jnp.bfloat16).astype(jnp.float32)
    first_matrix_derivative = jnp.einsum('sic,sip->cp', normal_f, left_in)
    second_matrix_derivative = jnp.einsum('sic,sip->cp', normal_f, right_in)
    d_normal = jnp.einsum('sip,cp->sic', left_in, first_projection_matrix.astype(jnp.float32)) + jnp.einsum('sip,cp->sic', right_in, second_projection_matrix.astype(jnp.float32))
    scale_factor_derivative = lax.optimization_barrier(jnp.sum(d_normal * standardized_entries, axis=(0, 1)))
    shift_term_derivative = lax.optimization_barrier(jnp.sum(d_normal, axis=(0, 1)))
    standardized_derivative = d_normal * standardizer_scale
    embedding_derivative = reciprocal_spread * (standardized_derivative - lax.optimization_barrier(jnp.mean(standardized_derivative, axis=-1, keepdims=True)) - standardized_entries * lax.optimization_barrier(jnp.mean(standardized_derivative * standardized_entries, axis=-1, keepdims=True)))
    return (embedding_derivative, final_matrix_derivative, first_matrix_derivative, second_matrix_derivative, scale_factor_derivative, shift_term_derivative, shift_derivative)
```

```python
import functools

import jax
import jax.numpy as jnp
from jax import lax
from jax.experimental import pallas as pl
from jax.experimental.pallas import tpu as pltpu
from jax.sharding import PartitionSpec as P

TOKB = 2


def standardizer_parts(homolog_embedding, standardizer_scale, standardizer_shift):
    incoming_entries = homolog_embedding.astype(jnp.float32)
    center = jnp.mean(incoming_entries, axis=-1, keepdims=True)
    varied = incoming_entries - center
    variance = jnp.mean(varied * varied, axis=-1, keepdims=True)
    reciprocal_spread = lax.rsqrt(variance + 1e-05)
    standardized_entries = varied * reciprocal_spread
    standardized_bfloat = (standardized_entries * standardizer_scale + standardizer_shift).astype(
        jnp.bfloat16
    )
    return (standardized_entries, reciprocal_spread, standardized_bfloat)


def sharded_body(
    homolog_embedding,
    presence_indicator,
    coupling_change_derivative,
    standardizer_scale,
    standardizer_shift,
    first_projection_matrix,
    second_projection_matrix,
    final_projection_matrix,
):
    shard_homolog_number, residue_line_number, feature_number = homolog_embedding.shape
    tok_cols = coupling_change_derivative.shape[1]
    width = first_projection_matrix.shape[1]
    standardized_entries, reciprocal_spread, standardized_bfloat = standardizer_parts(
        homolog_embedding, standardizer_scale, standardizer_shift
    )
    mask_single_precision = presence_indicator.astype(jnp.float32)
    mask_half_precision = presence_indicator.astype(jnp.bfloat16)
    left = (
        jnp.einsum(
            "sic,cp->sip",
            standardized_bfloat,
            first_projection_matrix,
            preferred_element_type=jnp.float32,
        )
        * mask_single_precision[..., None]
    ).astype(jnp.bfloat16)
    right = (
        jnp.einsum(
            "sic,cp->sip",
            standardized_bfloat,
            second_projection_matrix,
            preferred_element_type=jnp.float32,
        )
        * mask_single_precision[..., None]
    ).astype(jnp.bfloat16)
    left_flat = left.reshape(shard_homolog_number, residue_line_number * width)
    right_flat = right.reshape(shard_homolog_number, residue_line_number * width)
    left_all, mask_left = (
        lax.all_gather(left_flat, "col", axis=0, tiled=True),
        lax.all_gather(mask_half_precision, "col", axis=0, tiled=True),
    )
    right_wide, mask_wide = (
        lax.all_gather(right_flat, "row", axis=1, tiled=True),
        lax.all_gather(mask_half_precision, "row", axis=1, tiled=True),
    )
    right_all, mask_right = (
        lax.all_to_all(right_wide, "col", split_axis=1, concat_axis=0, tiled=True),
        lax.all_to_all(mask_wide, "col", split_axis=1, concat_axis=0, tiled=True),
    )
    seq_total = left_all.shape[0]
    right_three = right_all.reshape(seq_total, tok_cols, width)
    counts = jnp.einsum("si,sj->ij", mask_left, mask_right, preferred_element_type=jnp.float32)
    scaled = coupling_change_derivative.astype(jnp.float32) / (counts + 0.001)[..., None]
    bias_part = jnp.sum(scaled, axis=(0, 1))
    scaled_bf = scaled.astype(jnp.bfloat16)
    block_rows = residue_line_number // TOKB
    right_acc = jnp.zeros((seq_total, tok_cols, width), jnp.float32)
    wout_acc = jnp.zeros(final_projection_matrix.shape, jnp.float32)
    left_pieces = []
    for block_index in range(TOKB):
        first = block_index * block_rows
        rows_bf = scaled_bf[first : first + block_rows]
        outer_grad = jnp.einsum(
            "ijz,fz->ijf", rows_bf, final_projection_matrix, preferred_element_type=jnp.float32
        ).astype(jnp.bfloat16)
        outer_grad = outer_grad.reshape(block_rows, tok_cols, width, width)
        left_block = left_all[:, first * width : (first + block_rows) * width].reshape(
            seq_total, block_rows, width
        )
        first_factor_derivative = jnp.einsum(
            "ijce,sje->sic", outer_grad, right_three, preferred_element_type=jnp.float32
        )
        right_acc = right_acc + jnp.einsum(
            "ijce,sic->sje", outer_grad, left_block, preferred_element_type=jnp.float32
        )
        outer = jnp.einsum(
            "sic,sje->ijce", left_block, right_three, preferred_element_type=jnp.float32
        ).astype(jnp.bfloat16)
        outer = outer.reshape(block_rows, tok_cols, width * width)
        wout_acc = wout_acc + jnp.einsum(
            "ijf,ijz->fz", outer, rows_bf, preferred_element_type=jnp.float32
        )
        first_factor_derivative = first_factor_derivative.reshape(seq_total, block_rows * width)
        left_pieces.append(first_factor_derivative)
    left_terms = jnp.concatenate(left_pieces, axis=1)
    left_own = lax.psum_scatter(left_terms, "col", scatter_dimension=0, tiled=True)
    right_spread = lax.all_to_all(
        right_acc.reshape(seq_total, tok_cols * width),
        "col",
        split_axis=0,
        concat_axis=1,
        tiled=True,
    )
    right_own = lax.psum_scatter(right_spread, "row", scatter_dimension=1, tiled=True)
    left_in = (
        left_own.reshape(shard_homolog_number, residue_line_number, width)
        * mask_single_precision[..., None]
    ).astype(jnp.bfloat16)
    right_in = (
        right_own.reshape(shard_homolog_number, residue_line_number, width)
        * mask_single_precision[..., None]
    ).astype(jnp.bfloat16)
    left_part = jnp.einsum(
        "sic,sip->cp", standardized_bfloat, left_in, preferred_element_type=jnp.float32
    )
    right_part = jnp.einsum(
        "sic,sip->cp", standardized_bfloat, right_in, preferred_element_type=jnp.float32
    )
    d_normal = jnp.einsum(
        "sip,cp->sic", left_in, first_projection_matrix, preferred_element_type=jnp.float32
    ) + jnp.einsum(
        "sip,cp->sic", right_in, second_projection_matrix, preferred_element_type=jnp.float32
    )
    gain_part = jnp.sum(d_normal * standardized_entries, axis=(0, 1))
    beta_part = jnp.sum(d_normal, axis=(0, 1))
    standardized_derivative = d_normal * standardizer_scale
    embedding_derivative = reciprocal_spread * (
        standardized_derivative
        - jnp.mean(standardized_derivative, axis=-1, keepdims=True)
        - standardized_entries
        * jnp.mean(standardized_derivative * standardized_entries, axis=-1, keepdims=True)
    )
    (
        final_matrix_derivative,
        first_matrix_derivative,
        second_matrix_derivative,
        scale_factor_derivative,
        shift_term_derivative,
        shift_derivative,
    ) = lax.psum((wout_acc, left_part, right_part, gain_part, beta_part, bias_part), ("row", "col"))
    return (
        embedding_derivative,
        final_matrix_derivative,
        first_matrix_derivative,
        second_matrix_derivative,
        scale_factor_derivative,
        shift_term_derivative,
        shift_derivative,
    )


BF = jnp.bfloat16
F32 = jnp.float32


def spread(rows, cols, rule):
    r = lax.broadcasted_iota(jnp.int32, (rows, cols), 0)
    c = lax.broadcasted_iota(jnp.int32, (rows, cols), 1)
    return rule(r, c)


def two_terms(value):
    high = value.astype(BF)
    return high, (value - high.astype(F32)).astype(BF)


def mm(a, b):
    return jnp.dot(a, b, preferred_element_type=F32)


def group_mean(value, averager):
    high, low = two_terms(value)
    return mm(high, averager) + mm(low, averager)


def swap_blocks(block):
    lane = lax.broadcasted_iota(jnp.int32, (32, 128), 1)
    upper = lane >= 64
    odd = (lane // 32) % 2 == 1
    piece = [block[32 * a : 32 * a + 32] for a in range(4)]
    for a in (0, 1):
        x, y = piece[a], piece[a + 2]
        piece[a] = jnp.where(upper, pltpu.roll(y, 64, 1), x)
        piece[a + 2] = jnp.where(upper, y, pltpu.roll(x, 64, 1))
    for a in (0, 2):
        x, y = piece[a], piece[a + 1]
        piece[a] = jnp.where(odd, pltpu.roll(y, 32, 1), x)
        piece[a + 1] = jnp.where(odd, y, pltpu.roll(x, 96, 1))
    return jnp.concatenate(piece, axis=0)


def pack_kernel(msa_ref, mask_ref, pair_ref, out_ref):
    msa = msa_ref[...].astype(F32)
    for g in range(4):
        out_ref[32 * g : 32 * g + 32, :] = jnp.concatenate(
            [msa[:, 2 * g, :], msa[:, 2 * g + 1, :]], axis=1
        ).astype(BF)
    pair = pair_ref[...].astype(F32)
    for j in range(0, 8, 2):
        out_ref[128 + 8 * j : 144 + 8 * j, :] = jnp.concatenate(
            [pair[:, j, :], pair[:, j + 1, :]], axis=0
        ).astype(BF)
    mask = mask_ref[...].astype(F32).astype(BF)
    pick = spread(8, 128, lambda r, c: (c % 8 == r).astype(F32)).astype(BF)
    out_ref[192:224, :] = mm(mask, pick).astype(BF)


def part_kernel(n_row, n_col, place_ref, *refs):
    blocks = [[refs[a * n_col + b] for b in range(n_col)] for a in range(n_row)]
    (
        gain_ref, offset_ref, first_ref, second_ref, final_ref,
        emb_out, final_out, first_out, second_out, gain_out, offset_out, bias_out,
        pair_scr, normed_scr, rhs_scr, left_scr, leftt_scr, left2_scr, right_scr, rightt_scr,
        scaled_scr, grad_scr, outer_scr, lin_scr, linc_scr, rin_scr,
    ) = refs[n_row * n_col :]
    place = place_ref[0]

    for a in range(n_row):
        for b in range(n_col):
            at = lax.bitwise_xor(place, b) * 8
            pair_scr[pl.ds(at, 8), 8 * a : 8 * a + 8, :] = (
                blocks[a][b][128:192, :].astype(F32).reshape(8, 8, 128)
            )

    mask_rows = [
        jnp.concatenate([blocks[a][b][192:224, :] for b in range(n_col)], axis=0)
        for a in range(n_row)
    ]
    token_of = lax.broadcasted_iota(jnp.int32, (128, 128), 1) // 8 % 4
    mask = jnp.zeros((128, 128), F32)
    for a in range(n_row):
        mask = jnp.where(token_of == a, mask_rows[a].astype(F32), mask)
    mask_t = mask.T

    gain = jnp.concatenate([gain_ref[...], gain_ref[...]], axis=1)
    offset = jnp.concatenate([offset_ref[...], offset_ref[...]], axis=1)
    averager = spread(128, 128, lambda r, c: jnp.where(r // 64 == c // 64, 1.0 / 64, 0.0)).astype(BF)
    first = first_ref[...].astype(F32)
    second = second_ref[...].astype(F32)
    wide = jnp.concatenate([first] * 4 + [second] * 4, axis=1)
    wide = jnp.concatenate([wide] * 4, axis=0)
    project = jnp.where(
        spread(256, 256, lambda r, c: r // 64 == c % 128 // 32), wide, 0.0
    ).astype(BF)
    chooser = spread(128, 512, lambda r, c: jnp.where(r == c // 64, 1.0, 0.0)).astype(BF)
    inverse_own = None
    for a in range(n_row):
        x = jnp.concatenate(
            [blocks[a][b][32 * g : 32 * g + 32, :] for g in range(4) for b in range(n_col)], axis=0
        )
        varied = x.astype(F32) - mm(x, averager)
        inverse = lax.rsqrt(group_mean(varied * varied, averager) + 1e-05)
        normed = varied * inverse
        if a == 0:
            inverse_own = inverse
        rows = slice(512 * a, 512 * a + 512)
        normed_scr[rows, :] = normed
        normal = (normed * gain + offset).astype(BF)
        high, low = two_terms(normed)
        rhs_scr[rows, 0:128] = normal
        rhs_scr[rows, 128:256] = high
        rhs_scr[rows, 256:384] = low
        rhs_scr[rows, 384:512] = jnp.ones((512, 128), BF)
        mask_wide = mm(mask_rows[a], chooser).astype(BF)
        for h in range(2):
            masked = jnp.concatenate(
                [
                    normal[128 * g : 128 * g + 128] * mask_wide[:, 128 * g : 128 * g + 128]
                    for g in (2 * h, 2 * h + 1)
                ],
                axis=1,
            )
            both = mm(masked, project).astype(BF)
            k = 2 * a + h
            at = slice(128 * k, 128 * k + 128)
            right_scr[:, at] = both[:, 128:]
            rightt_scr[at, :] = both[:, 128:].astype(F32).T.astype(BF)
            left_scr[at, :] = both[:, :128].astype(F32).T
    for q in range(8):
        at = slice(128 * q, 128 * q + 128)
        block = jnp.concatenate(
            [left_scr[pl.ds(4 * q + c, 32, stride=32), :] for c in range(4)], axis=0
        )
        leftt_scr[at, :] = block.astype(BF)
        left2_scr[:, at] = block.T.astype(BF)

    bias = jnp.zeros((1, 128), F32)
    ones = jnp.ones((128, 128), BF)
    for p in range(8):
        both_on = jnp.concatenate(
            [mask_t[0:32] * mask_t[j : j + 1] for j in range(4 * p, 4 * p + 4)], axis=0
        ).astype(BF)
        counts = mm(both_on, ones)
        scaled = pair_scr[4 * p : 4 * p + 4].reshape(128, 128) / (counts + 0.001)
        bias = bias + jnp.sum(scaled, axis=0, keepdims=True)
        scaled_scr[128 * p : 128 * p + 128, :] = scaled.astype(BF)
    bias_out[...] = bias

    for p in range(8):
        at = slice(128 * p, 128 * p + 128)
        grad = lax.dot_general(
            final_ref[...], scaled_scr[at, :], (((1,), (1,)), ((), ())),
            preferred_element_type=F32,
        )
        outer = mm(rightt_scr[at, :], left2_scr[...])
        for q in range(8):
            to = slice(128 * q, 128 * q + 128)
            grad_scr[at, to] = swap_blocks(grad[to]).astype(BF)
            outer_scr[to, at] = swap_blocks(outer[:, to]).astype(BF)
    final_out[...] = mm(outer_scr[...], scaled_scr[...])
    left_grad = mm(right_scr[...], grad_scr[...])
    right_grad = mm(grad_scr[...], leftt_scr[...])

    for q in range(8):
        at = slice(128 * q, 128 * q + 128)
        lin_scr[at, :] = (left_grad[:, at] * mask).astype(BF).astype(F32).T
    for k in range(8):
        rows = []
        for t in range(4 * k, 4 * k + 4):
            rows.append(right_grad[32 * t : 32 * t + 32] * mask_t[t : t + 1])
        at = slice(128 * k, 128 * k + 128)
        rin_scr[at, :] = jnp.concatenate(rows, axis=0).astype(BF)
        linc_scr[at, :] = jnp.concatenate(
            [lin_scr[pl.ds(t, 32, stride=32), :] for t in range(4 * k, 4 * k + 4)], axis=0
        ).astype(BF)

    total = jnp.zeros((128, 512), F32)
    for g in range(16):
        grads = jnp.concatenate(
            [linc_scr[64 * g : 64 * g + 64, :], rin_scr[64 * g : 64 * g + 64, :]], axis=0
        )
        total = total + mm(grads, rhs_scr[128 * g : 128 * g + 128, :])
    def fold(block):
        return block[0:32, 0:64] + block[32:64, 64:128]
    left_total, right_total = total[0:64], total[64:128]
    first_out[...] = fold(left_total[:, 0:128]).T
    second_out[...] = fold(right_total[:, 0:128]).T
    left_normed = fold(left_total[:, 128:256] + left_total[:, 256:384])
    right_normed = fold(right_total[:, 128:256] + right_total[:, 256:384])
    left_sum = fold(left_total[:, 384:512])
    right_sum = fold(right_total[:, 384:512])
    first_t, second_t = first.T, second.T
    gain_out[...] = jnp.sum(first_t * left_normed + second_t * right_normed, axis=0, keepdims=True)
    offset_out[...] = jnp.sum(first_t * left_sum + second_t * right_sum, axis=0, keepdims=True)

    back = project.astype(F32).T.astype(BF)
    contract_rows = (((0,), (0,)), ((), ()))
    for h in range(2):
        at = slice(128 * h, 128 * h + 128)
        d_normal = lax.dot_general(
            linc_scr[at, :], back[:128], contract_rows, preferred_element_type=F32
        ) + lax.dot_general(
            rin_scr[at, :], back[128:], contract_rows, preferred_element_type=F32
        )
        for half in range(2):
            g = 2 * h + half
            d_hat = d_normal[0:32, 128 * half : 128 * half + 128] * gain
            normed = normed_scr[128 * g : 128 * g + 32, :]
            result = inverse_own[128 * g : 128 * g + 32] * (
                d_hat
                - group_mean(d_hat, averager)
                - normed * group_mean(d_hat * normed, averager)
            )
            emb_out[:, 2 * g, :] = result[:, 0:64]
            emb_out[:, 2 * g + 1, :] = result[:, 64:128]


def vmem(count):
    return [pl.BlockSpec(memory_space=pltpu.VMEM)] * count


def gathered_body(
    n_row,
    n_col,
    homolog_embedding,
    presence_indicator,
    coupling_change_derivative,
    standardizer_scale,
    standardizer_shift,
    first_projection_matrix,
    second_projection_matrix,
    final_projection_matrix,
):
    packed = pl.pallas_call(
        pack_kernel,
        out_shape=jax.ShapeDtypeStruct((224, 128), BF),
        in_specs=vmem(3),
        out_specs=pl.BlockSpec(memory_space=pltpu.VMEM),
    )(homolog_embedding, presence_indicator, coupling_change_derivative)

    blocks = {(0, 0): packed}
    for b in range(1, n_col):
        blocks[0, b] = lax.ppermute(packed, "col", [(k, k ^ b) for k in range(n_col)])
    step = n_row // 2
    while step:
        for (a, b), block in sorted(blocks.items()):
            blocks[a ^ step, b] = lax.ppermute(block, "row", [(k, k ^ step) for k in range(n_row)])
        step //= 2

    place = lax.bitwise_xor(lax.axis_index("row"), lax.axis_index("col")).astype(jnp.int32)
    shards, tokens, features = homolog_embedding.shape
    width = first_projection_matrix.shape[1]
    shape = lambda *dims: jax.ShapeDtypeStruct(dims, F32)
    outs = pl.pallas_call(
        functools.partial(part_kernel, n_row, n_col),
        out_shape=(
            shape(shards, tokens, features),
            shape(width * width, 128),
            shape(features, width),
            shape(features, width),
            shape(1, features),
            shape(1, features),
            shape(1, 128),
        ),
        in_specs=[pl.BlockSpec(memory_space=pltpu.SMEM)] + vmem(n_row * n_col + 5),
        out_specs=tuple(vmem(7)),
        scratch_shapes=[
            pltpu.VMEM((32, 32, 128), F32),
            pltpu.VMEM((2048, 128), F32),
            pltpu.VMEM((2048, 512), BF),
            pltpu.VMEM((1024, 128), F32),
            pltpu.VMEM((1024, 128), BF),
            pltpu.VMEM((128, 1024), BF),
            pltpu.VMEM((128, 1024), BF),
            pltpu.VMEM((1024, 128), BF),
            pltpu.VMEM((1024, 128), BF),
            pltpu.VMEM((1024, 1024), BF),
            pltpu.VMEM((1024, 1024), BF),
            pltpu.VMEM((1024, 128), F32),
            pltpu.VMEM((1024, 128), BF),
            pltpu.VMEM((1024, 128), BF),
        ],
        compiler_params=pltpu.CompilerParams(vmem_limit_bytes=48 * 1024 * 1024),
    )(
        place.reshape(1),
        *[blocks[a, b] for a in range(n_row) for b in range(n_col)],
        standardizer_scale.reshape(1, features),
        standardizer_shift.reshape(1, features),
        first_projection_matrix,
        second_projection_matrix,
        final_projection_matrix,
    )
    emb, final, first, second, gain, offset, bias = outs
    return emb, final, first, second, gain.reshape(-1), offset.reshape(-1), bias.reshape(-1)


def body(n_row, n_col, *arguments):
    msa, _, pair = arguments[:3]
    width = arguments[5].shape[1]
    fits = (
        n_row == 4
        and n_col == 4
        and msa.shape == (32, 8, 64)
        and pair.shape == (8, 8, 128)
        and width == 32
    )
    if fits:
        return gathered_body(n_row, n_col, *arguments)
    return sharded_body(*arguments)


def solution(mesh):
    placed = (
        P(("grp", "col"), "row", None),
        P(("grp", "col"), "row"),
        P(("grp", "row"), "col", None),
        P(),
        P(),
        P(),
        P(),
        P(),
    )
    return jax.shard_map(
        functools.partial(body, mesh.shape["row"], mesh.shape["col"]),
        mesh=mesh,
        in_specs=placed,
        out_specs=(
            P(("grp", "col"), "row", None),
            P("grp", None),
            P("grp", None),
            P("grp", None),
            P("grp"),
            P("grp"),
            P("grp"),
        ),
        check_vma=False,
    )
```

```python
import functools

import jax
import jax.numpy as jnp
from jax import lax
from jax.experimental import pallas as pl
from jax.experimental.pallas import tpu as pltpu
from jax.sharding import PartitionSpec as P

TOKB = 2


def standardizer_parts(homolog_embedding, standardizer_scale, standardizer_shift):
    incoming_entries = homolog_embedding.astype(jnp.float32)
    center = jnp.mean(incoming_entries, axis=-1, keepdims=True)
    varied = incoming_entries - center
    variance = jnp.mean(varied * varied, axis=-1, keepdims=True)
    reciprocal_spread = lax.rsqrt(variance + 1e-05)
    standardized_entries = varied * reciprocal_spread
    standardized_bfloat = (standardized_entries * standardizer_scale + standardizer_shift).astype(
        jnp.bfloat16
    )
    return (standardized_entries, reciprocal_spread, standardized_bfloat)


def sharded_body(
    homolog_embedding,
    presence_indicator,
    coupling_change_derivative,
    standardizer_scale,
    standardizer_shift,
    first_projection_matrix,
    second_projection_matrix,
    final_projection_matrix,
):
    shard_homolog_number, residue_line_number, feature_number = homolog_embedding.shape
    tok_cols = coupling_change_derivative.shape[1]
    width = first_projection_matrix.shape[1]
    standardized_entries, reciprocal_spread, standardized_bfloat = standardizer_parts(
        homolog_embedding, standardizer_scale, standardizer_shift
    )
    mask_single_precision = presence_indicator.astype(jnp.float32)
    mask_half_precision = presence_indicator.astype(jnp.bfloat16)
    left = (
        jnp.einsum(
            "sic,cp->sip",
            standardized_bfloat,
            first_projection_matrix,
            preferred_element_type=jnp.float32,
        )
        * mask_single_precision[..., None]
    ).astype(jnp.bfloat16)
    right = (
        jnp.einsum(
            "sic,cp->sip",
            standardized_bfloat,
            second_projection_matrix,
            preferred_element_type=jnp.float32,
        )
        * mask_single_precision[..., None]
    ).astype(jnp.bfloat16)
    left_flat = left.reshape(shard_homolog_number, residue_line_number * width)
    right_flat = right.reshape(shard_homolog_number, residue_line_number * width)
    left_all, mask_left = (
        lax.all_gather(left_flat, "col", axis=0, tiled=True),
        lax.all_gather(mask_half_precision, "col", axis=0, tiled=True),
    )
    right_wide, mask_wide = (
        lax.all_gather(right_flat, "row", axis=1, tiled=True),
        lax.all_gather(mask_half_precision, "row", axis=1, tiled=True),
    )
    right_all, mask_right = (
        lax.all_to_all(right_wide, "col", split_axis=1, concat_axis=0, tiled=True),
        lax.all_to_all(mask_wide, "col", split_axis=1, concat_axis=0, tiled=True),
    )
    seq_total = left_all.shape[0]
    right_three = right_all.reshape(seq_total, tok_cols, width)
    counts = jnp.einsum("si,sj->ij", mask_left, mask_right, preferred_element_type=jnp.float32)
    scaled = coupling_change_derivative.astype(jnp.float32) / (counts + 0.001)[..., None]
    bias_part = jnp.sum(scaled, axis=(0, 1))
    scaled_bf = scaled.astype(jnp.bfloat16)
    block_rows = residue_line_number // TOKB
    right_acc = jnp.zeros((seq_total, tok_cols, width), jnp.float32)
    wout_acc = jnp.zeros(final_projection_matrix.shape, jnp.float32)
    left_pieces = []
    for block_index in range(TOKB):
        first = block_index * block_rows
        rows_bf = scaled_bf[first : first + block_rows]
        outer_grad = jnp.einsum(
            "ijz,fz->ijf", rows_bf, final_projection_matrix, preferred_element_type=jnp.float32
        ).astype(jnp.bfloat16)
        outer_grad = outer_grad.reshape(block_rows, tok_cols, width, width)
        left_block = left_all[:, first * width : (first + block_rows) * width].reshape(
            seq_total, block_rows, width
        )
        first_factor_derivative = jnp.einsum(
            "ijce,sje->sic", outer_grad, right_three, preferred_element_type=jnp.float32
        )
        right_acc = right_acc + jnp.einsum(
            "ijce,sic->sje", outer_grad, left_block, preferred_element_type=jnp.float32
        )
        outer = jnp.einsum(
            "sic,sje->ijce", left_block, right_three, preferred_element_type=jnp.float32
        ).astype(jnp.bfloat16)
        outer = outer.reshape(block_rows, tok_cols, width * width)
        wout_acc = wout_acc + jnp.einsum(
            "ijf,ijz->fz", outer, rows_bf, preferred_element_type=jnp.float32
        )
        first_factor_derivative = first_factor_derivative.reshape(seq_total, block_rows * width)
        left_pieces.append(first_factor_derivative)
    left_terms = jnp.concatenate(left_pieces, axis=1)
    left_own = lax.psum_scatter(left_terms, "col", scatter_dimension=0, tiled=True)
    right_spread = lax.all_to_all(
        right_acc.reshape(seq_total, tok_cols * width),
        "col",
        split_axis=0,
        concat_axis=1,
        tiled=True,
    )
    right_own = lax.psum_scatter(right_spread, "row", scatter_dimension=1, tiled=True)
    left_in = (
        left_own.reshape(shard_homolog_number, residue_line_number, width)
        * mask_single_precision[..., None]
    ).astype(jnp.bfloat16)
    right_in = (
        right_own.reshape(shard_homolog_number, residue_line_number, width)
        * mask_single_precision[..., None]
    ).astype(jnp.bfloat16)
    left_part = jnp.einsum(
        "sic,sip->cp", standardized_bfloat, left_in, preferred_element_type=jnp.float32
    )
    right_part = jnp.einsum(
        "sic,sip->cp", standardized_bfloat, right_in, preferred_element_type=jnp.float32
    )
    d_normal = jnp.einsum(
        "sip,cp->sic", left_in, first_projection_matrix, preferred_element_type=jnp.float32
    ) + jnp.einsum(
        "sip,cp->sic", right_in, second_projection_matrix, preferred_element_type=jnp.float32
    )
    gain_part = jnp.sum(d_normal * standardized_entries, axis=(0, 1))
    beta_part = jnp.sum(d_normal, axis=(0, 1))
    standardized_derivative = d_normal * standardizer_scale
    embedding_derivative = reciprocal_spread * (
        standardized_derivative
        - jnp.mean(standardized_derivative, axis=-1, keepdims=True)
        - standardized_entries
        * jnp.mean(standardized_derivative * standardized_entries, axis=-1, keepdims=True)
    )
    (
        final_matrix_derivative,
        first_matrix_derivative,
        second_matrix_derivative,
        scale_factor_derivative,
        shift_term_derivative,
        shift_derivative,
    ) = lax.psum((wout_acc, left_part, right_part, gain_part, beta_part, bias_part), ("row", "col"))
    return (
        embedding_derivative,
        final_matrix_derivative,
        first_matrix_derivative,
        second_matrix_derivative,
        scale_factor_derivative,
        shift_term_derivative,
        shift_derivative,
    )


BF = jnp.bfloat16
F32 = jnp.float32


def spread(rows, cols, rule):
    r = lax.broadcasted_iota(jnp.int32, (rows, cols), 0)
    c = lax.broadcasted_iota(jnp.int32, (rows, cols), 1)
    return rule(r, c)


def mm(a, b):
    return jnp.dot(a, b, preferred_element_type=F32)


def mm_nt(a, b):
    return lax.dot_general(a, b, (((1,), (1,)), ((), ())), preferred_element_type=F32)


def mm_tn(a, b):
    return lax.dot_general(a, b, (((0,), (0,)), ((), ())), preferred_element_type=F32)


def swap_blocks(block):
    lane = lax.broadcasted_iota(jnp.int32, (32, 128), 1)
    upper = lane >= 64
    odd = (lane // 32) % 2 == 1
    piece = [block[32 * a : 32 * a + 32] for a in range(4)]
    for a in (0, 1):
        x, y = piece[a], piece[a + 2]
        piece[a] = jnp.where(upper, pltpu.roll(y, 64, 1), x)
        piece[a + 2] = jnp.where(upper, y, pltpu.roll(x, 64, 1))
    for a in (0, 2):
        x, y = piece[a], piece[a + 1]
        piece[a] = jnp.where(odd, pltpu.roll(y, 32, 1), x)
        piece[a + 1] = jnp.where(odd, y, pltpu.roll(x, 96, 1))
    return jnp.concatenate(piece, axis=0)


ABSENT = 1024.0


def pack_kernel(msa_ref, mask_ref, pair_ref, out_ref):
    msa = msa_ref[...].astype(F32)
    pick = spread(8, 512, lambda r, c: jnp.where(c // 64 == r, 1.0, 0.0)).astype(BF)
    present = mm_tn(mask_ref[...].astype(F32).astype(BF), pick) > 0.5
    for g in range(4):
        rows = jnp.concatenate([msa[:, 2 * g, :], msa[:, 2 * g + 1, :]], axis=1)
        out_ref[32 * g : 32 * g + 32, :] = jnp.where(
            present[:, 128 * g : 128 * g + 128], rows, ABSENT
        ).astype(BF)
    pair = pair_ref[...].astype(F32)
    for j in range(0, 8, 2):
        out_ref[128 + 8 * j : 144 + 8 * j, :] = jnp.concatenate(
            [pair[:, j, :], pair[:, j + 1, :]], axis=0
        ).astype(BF)


def weights_kernel(gain_ref, offset_ref, first_ref, second_ref, norm_out, back_out):
    norm_out[...] = jnp.concatenate(
        [
            jnp.concatenate([ref[...]] * 2, axis=1)
            for ref in (gain_ref, offset_ref, gain_ref, offset_ref) * 2
        ],
        axis=0,
    )
    for k, ref in enumerate((first_ref, second_ref)):
        wide = jnp.concatenate([ref[...].astype(F32)] * 4, axis=1)
        wide = jnp.concatenate([wide] * 4, axis=0)
        own = spread(128, 256, lambda r, c: r // 32 == c // 64)
        back_out[128 * k : 128 * k + 128, :] = jnp.where(own, wide, 0.0).astype(BF)


def part_kernel(n_row, n_col, place_ref, *refs):
    sets = refs[:n_row]
    (
        norm_ref, back_ref, first_ref, second_ref, final_hbm,
        emb_out, final_hbm_out, first_out, second_out, gain_out, offset_out, bias_out,
        pair_scr, normed_scr, rhs_scr, left_scr, leftt_scr, right_scr, rightt_scr,
        scaled_scr, grad_scr, outer_scr, lin_scr, linc_scr, rin_scr,
        final_ref, final_out, in_sem, out_sem,
    ) = refs[n_row:]
    final_in = pltpu.make_async_copy(final_hbm, final_ref, in_sem)
    final_in.start()
    place = place_ref[0]

    for a in range(n_row):
        for b in range(n_col):
            at = lax.bitwise_xor(place, b) * 8
            pair_scr[pl.ds(at, 8), 8 * a : 8 * a + 8, :] = (
                sets[a][b, 128:192, :].astype(F32).reshape(8, 8, 128)
            )

    gain = norm_ref[0:1, :]
    offset = norm_ref[1:2, :]
    averager = spread(128, 128, lambda r, c: jnp.where(r // 64 == c // 64, 1.0 / 64, 0.0)).astype(BF)
    lane = lax.broadcasted_iota(jnp.int32, (128, 128), 1)
    inverse_own = None
    found = jnp.zeros((128, 128), F32)
    for a in range(n_row):
        x = jnp.concatenate(
            [sets[a][b, 32 * g : 32 * g + 32, :] for g in range(4) for b in range(n_col)], axis=0
        )
        mean = mm(x, averager)
        present = mean < ABSENT / 2
        varied = x.astype(F32) - mean
        inverse = lax.rsqrt(mm((varied * varied).astype(BF), averager) + 1e-05)
        normed = varied * inverse
        if a == 0:
            inverse_own = inverse
            normed_scr[...] = normed
        rows = slice(512 * a, 512 * a + 512)
        normal = jnp.where(present, normed * gain + offset, 0.0).astype(BF)
        rhs_scr[rows, 0:128] = normal
        rhs_scr[rows, 128:256] = normed.astype(BF)
        here = jnp.where(present, 1.0, 0.0)
        for g in range(4):
            found = jnp.where(lane % 32 // 2 == 4 * a + g, here[128 * g : 128 * g + 128], found)
        for h in range(2):
            masked = jnp.concatenate(
                [normal[128 * g : 128 * g + 128] for g in (2 * h, 2 * h + 1)], axis=1
            )
            k = 2 * a + h
            at = slice(128 * k, 128 * k + 128)
            right_scr[:, at] = mm_nt(masked, back_ref[128:, :]).astype(BF)
            both = mm_nt(back_ref[...], masked)
            rightt_scr[at, :] = both[128:].astype(BF)
            left_scr[at, :] = both[:128]
    for q in range(8):
        leftt_scr[128 * q : 128 * q + 128, :] = jnp.concatenate(
            [left_scr[pl.ds(4 * q + c, 32, stride=32), :] for c in range(4)], axis=0
        ).astype(BF)

    turned = pltpu.roll(found, 64, 1)
    mask = jnp.where((lane % 2 == 0) == (lane < 64), found, turned)
    mask_t = mask.T

    bias = jnp.zeros((1, 128), F32)
    ones = jnp.ones((128, 128), BF)
    for p in range(8):
        both_on = jnp.concatenate(
            [mask_t[0:32] * mask_t[j : j + 1] for j in range(4 * p, 4 * p + 4)], axis=0
        ).astype(BF)
        counts = mm(both_on, ones)
        scaled = pair_scr[4 * p : 4 * p + 4].reshape(128, 128) / (counts + 0.001)
        bias = bias + jnp.sum(scaled, axis=0, keepdims=True)
        scaled_scr[128 * p : 128 * p + 128, :] = scaled.astype(BF)
    bias_out[...] = bias

    for n in range(4):
        outer = mm_nt(rightt_scr[...], leftt_scr[256 * n : 256 * n + 256, :]).astype(BF)
        for p in range(8):
            for q in range(2):
                outer_scr[256 * n + 128 * q : 256 * n + 128 * q + 128, 128 * p : 128 * p + 128] = (
                    swap_blocks(outer[128 * p : 128 * p + 128, 128 * q : 128 * q + 128])
                )
    final_out[...] = mm(outer_scr[...], scaled_scr[...])
    final_send = pltpu.make_async_copy(final_out, final_hbm_out, out_sem)
    final_send.start()

    final_in.wait()
    for n in range(4):
        grad = mm_nt(final_ref[...], scaled_scr[256 * n : 256 * n + 256, :]).astype(BF)
        for q in range(8):
            for p in range(2):
                grad_scr[256 * n + 128 * p : 256 * n + 128 * p + 128, 128 * q : 128 * q + 128] = (
                    swap_blocks(grad[128 * q : 128 * q + 128, 128 * p : 128 * p + 128])
                )
    left_grad = mm(right_scr[...], grad_scr[...])
    right_grad = mm(grad_scr[...], leftt_scr[...])

    identity = spread(128, 128, lambda r, c: jnp.where(r == c, 1.0, 0.0)).astype(BF)
    for q in range(8):
        at = slice(128 * q, 128 * q + 128)
        lin_scr[at, :] = mm_nt(identity, (left_grad[:, at] * mask).astype(BF))
    for k in range(8):
        rows = []
        for t in range(4 * k, 4 * k + 4):
            rows.append(right_grad[32 * t : 32 * t + 32] * mask_t[t : t + 1])
        at = slice(128 * k, 128 * k + 128)
        rin_scr[at, :] = jnp.concatenate(rows, axis=0).astype(BF)
        linc_scr[at, :] = jnp.concatenate(
            [lin_scr[pl.ds(t, 32, stride=32), :] for t in range(4 * k, 4 * k + 4)], axis=0
        ).astype(BF)

    total = jnp.zeros((128, 256), F32)
    sums = jnp.zeros((128, 128), F32)
    for g in range(16):
        grads = jnp.concatenate(
            [linc_scr[64 * g : 64 * g + 64, :], rin_scr[64 * g : 64 * g + 64, :]], axis=0
        )
        sums = sums + grads.astype(F32)
        total = total + mm(grads, rhs_scr[128 * g : 128 * g + 128, :])

    def fold(block):
        return block[0:32, 0:64] + block[32:64, 64:128]

    first_out[...] = fold(total[0:64, 0:128])
    second_out[...] = fold(total[64:128, 0:128])
    sums = jnp.sum(sums, axis=1, keepdims=True)
    left_sum = sums[0:32] + sums[32:64]
    right_sum = sums[64:96] + sums[96:128]
    first = first_ref[...].astype(F32)
    second = second_ref[...].astype(F32)
    gain_out[...] = jnp.sum(
        first * fold(total[0:64, 128:256]) + second * fold(total[64:128, 128:256]),
        axis=0, keepdims=True,
    )
    offset_out[...] = jnp.sum(first * left_sum + second * right_sum, axis=0, keepdims=True)

    for h in range(2):
        at = slice(128 * h, 128 * h + 128)
        d_normal = mm_tn(linc_scr[at, :], back_ref[:128, :]) + mm_tn(rin_scr[at, :], back_ref[128:, :])
        for half in range(2):
            g = 2 * h + half
            d_hat = d_normal[0:32, 128 * half : 128 * half + 128] * gain
            normed = normed_scr[128 * g : 128 * g + 32, :]
            result = inverse_own[128 * g : 128 * g + 32] * (
                d_hat
                - mm(d_hat.astype(BF), averager)
                - normed * mm((d_hat * normed).astype(BF), averager)
            )
            emb_out[:, 2 * g, :] = result[:, 0:64]
            emb_out[:, 2 * g + 1, :] = result[:, 64:128]
    final_send.wait()


def vmem(count):
    return [pl.BlockSpec(memory_space=pltpu.VMEM)] * count


def gathered_body(
    n_row,
    n_col,
    homolog_embedding,
    presence_indicator,
    coupling_change_derivative,
    standardizer_scale,
    standardizer_shift,
    first_projection_matrix,
    second_projection_matrix,
    final_projection_matrix,
):
    shards, tokens, features = homolog_embedding.shape
    width = first_projection_matrix.shape[1]
    shape = lambda *dims: jax.ShapeDtypeStruct(dims, F32)
    packed = pl.pallas_call(
        pack_kernel,
        out_shape=jax.ShapeDtypeStruct((192, 128), BF),
        in_specs=vmem(3),
        out_specs=vmem(1)[0],
    )(homolog_embedding, presence_indicator.T, coupling_change_derivative)
    norm, back = pl.pallas_call(
        weights_kernel,
        out_shape=(shape(8, 128), jax.ShapeDtypeStruct((256, 256), BF)),
        in_specs=vmem(4),
        out_specs=tuple(vmem(2)),
    )(
        standardizer_scale.reshape(1, features),
        standardizer_shift.reshape(1, features),
        first_projection_matrix.T,
        second_projection_matrix.T,
    )

    pieces = [packed] + [
        lax.ppermute(packed, "col", [(k, k ^ b) for k in range(n_col)]) for b in range(1, n_col)
    ]
    sets = {0: jnp.stack(pieces)}
    step = n_row // 2
    while step:
        for a, held in sorted(sets.items()):
            sets[a ^ step] = lax.ppermute(held, "row", [(k, k ^ step) for k in range(n_row)])
        step //= 2

    place = lax.bitwise_xor(lax.axis_index("row"), lax.axis_index("col")).astype(jnp.int32)
    hbm = pl.BlockSpec(memory_space=pltpu.HBM)
    outs = pl.pallas_call(
        functools.partial(part_kernel, n_row, n_col),
        out_shape=(
            shape(shards, tokens, features),
            shape(width * width, 128),
            shape(width, features),
            shape(width, features),
            shape(1, features),
            shape(1, features),
            shape(1, 128),
        ),
        in_specs=[pl.BlockSpec(memory_space=pltpu.SMEM)] + vmem(n_row + 4) + [hbm],
        out_specs=(*vmem(1), hbm, *vmem(5)),
        scratch_shapes=[
            pltpu.VMEM((32, 32, 128), F32),
            pltpu.VMEM((512, 128), F32),
            pltpu.VMEM((2048, 256), BF),
            pltpu.VMEM((1024, 128), F32),
            pltpu.VMEM((1024, 128), BF),
            pltpu.VMEM((128, 1024), BF),
            pltpu.VMEM((1024, 128), BF),
            pltpu.VMEM((1024, 128), BF),
            pltpu.VMEM((1024, 1024), BF),
            pltpu.VMEM((1024, 1024), BF),
            pltpu.VMEM((1024, 128), F32),
            pltpu.VMEM((1024, 128), BF),
            pltpu.VMEM((1024, 128), BF),
            pltpu.VMEM((1024, 128), BF),
            pltpu.VMEM((1024, 128), F32),
            pltpu.SemaphoreType.DMA,
            pltpu.SemaphoreType.DMA,
        ],
        compiler_params=pltpu.CompilerParams(vmem_limit_bytes=48 * 1024 * 1024),
    )(
        place.reshape(1),
        *[sets[a] for a in range(n_row)],
        norm,
        back,
        first_projection_matrix.T,
        second_projection_matrix.T,
        final_projection_matrix,
    )
    emb, final, first, second, gain, offset, bias = outs
    return emb, final, first.T, second.T, gain.reshape(-1), offset.reshape(-1), bias.reshape(-1)


def body(n_row, n_col, *arguments):
    msa, _, pair = arguments[:3]
    width = arguments[5].shape[1]
    fits = (
        n_row == 4
        and n_col == 4
        and msa.shape == (32, 8, 64)
        and pair.shape == (8, 8, 128)
        and width == 32
    )
    if fits:
        return gathered_body(n_row, n_col, *arguments)
    return sharded_body(*arguments)


def solution(mesh):
    placed = (
        P(("grp", "col"), "row", None),
        P(("grp", "col"), "row"),
        P(("grp", "row"), "col", None),
        P(),
        P(),
        P(),
        P(),
        P(),
    )
    return jax.shard_map(
        functools.partial(body, mesh.shape["row"], mesh.shape["col"]),
        mesh=mesh,
        in_specs=placed,
        out_specs=(
            P(("grp", "col"), "row", None),
            P("grp", None),
            P("grp", None),
            P("grp", None),
            P("grp"),
            P("grp"),
            P("grp"),
        ),
        check_vma=False,
    )
```

```python
import functools

import jax
import jax.numpy as jnp
from jax import lax
from jax.experimental import pallas as pl
from jax.experimental.pallas import tpu as pltpu
from jax.sharding import PartitionSpec as P

TOKB = 2


def standardizer_parts(homolog_embedding, standardizer_scale, standardizer_shift):
    incoming_entries = homolog_embedding.astype(jnp.float32)
    center = jnp.mean(incoming_entries, axis=-1, keepdims=True)
    varied = incoming_entries - center
    variance = jnp.mean(varied * varied, axis=-1, keepdims=True)
    reciprocal_spread = lax.rsqrt(variance + 1e-05)
    standardized_entries = varied * reciprocal_spread
    standardized_bfloat = (standardized_entries * standardizer_scale + standardizer_shift).astype(
        jnp.bfloat16
    )
    return (standardized_entries, reciprocal_spread, standardized_bfloat)


def sharded_body(
    homolog_embedding,
    presence_indicator,
    coupling_change_derivative,
    standardizer_scale,
    standardizer_shift,
    first_projection_matrix,
    second_projection_matrix,
    final_projection_matrix,
):
    shard_homolog_number, residue_line_number, feature_number = homolog_embedding.shape
    tok_cols = coupling_change_derivative.shape[1]
    width = first_projection_matrix.shape[1]
    standardized_entries, reciprocal_spread, standardized_bfloat = standardizer_parts(
        homolog_embedding, standardizer_scale, standardizer_shift
    )
    mask_single_precision = presence_indicator.astype(jnp.float32)
    mask_half_precision = presence_indicator.astype(jnp.bfloat16)
    left = (
        jnp.einsum(
            "sic,cp->sip",
            standardized_bfloat,
            first_projection_matrix,
            preferred_element_type=jnp.float32,
        )
        * mask_single_precision[..., None]
    ).astype(jnp.bfloat16)
    right = (
        jnp.einsum(
            "sic,cp->sip",
            standardized_bfloat,
            second_projection_matrix,
            preferred_element_type=jnp.float32,
        )
        * mask_single_precision[..., None]
    ).astype(jnp.bfloat16)
    left_flat = left.reshape(shard_homolog_number, residue_line_number * width)
    right_flat = right.reshape(shard_homolog_number, residue_line_number * width)
    left_all, mask_left = (
        lax.all_gather(left_flat, "col", axis=0, tiled=True),
        lax.all_gather(mask_half_precision, "col", axis=0, tiled=True),
    )
    right_wide, mask_wide = (
        lax.all_gather(right_flat, "row", axis=1, tiled=True),
        lax.all_gather(mask_half_precision, "row", axis=1, tiled=True),
    )
    right_all, mask_right = (
        lax.all_to_all(right_wide, "col", split_axis=1, concat_axis=0, tiled=True),
        lax.all_to_all(mask_wide, "col", split_axis=1, concat_axis=0, tiled=True),
    )
    seq_total = left_all.shape[0]
    right_three = right_all.reshape(seq_total, tok_cols, width)
    counts = jnp.einsum("si,sj->ij", mask_left, mask_right, preferred_element_type=jnp.float32)
    scaled = coupling_change_derivative.astype(jnp.float32) / (counts + 0.001)[..., None]
    bias_part = jnp.sum(scaled, axis=(0, 1))
    scaled_bf = scaled.astype(jnp.bfloat16)
    block_rows = residue_line_number // TOKB
    right_acc = jnp.zeros((seq_total, tok_cols, width), jnp.float32)
    wout_acc = jnp.zeros(final_projection_matrix.shape, jnp.float32)
    left_pieces = []
    for block_index in range(TOKB):
        first = block_index * block_rows
        rows_bf = scaled_bf[first : first + block_rows]
        outer_grad = jnp.einsum(
            "ijz,fz->ijf", rows_bf, final_projection_matrix, preferred_element_type=jnp.float32
        ).astype(jnp.bfloat16)
        outer_grad = outer_grad.reshape(block_rows, tok_cols, width, width)
        left_block = left_all[:, first * width : (first + block_rows) * width].reshape(
            seq_total, block_rows, width
        )
        first_factor_derivative = jnp.einsum(
            "ijce,sje->sic", outer_grad, right_three, preferred_element_type=jnp.float32
        )
        right_acc = right_acc + jnp.einsum(
            "ijce,sic->sje", outer_grad, left_block, preferred_element_type=jnp.float32
        )
        outer = jnp.einsum(
            "sic,sje->ijce", left_block, right_three, preferred_element_type=jnp.float32
        ).astype(jnp.bfloat16)
        outer = outer.reshape(block_rows, tok_cols, width * width)
        wout_acc = wout_acc + jnp.einsum(
            "ijf,ijz->fz", outer, rows_bf, preferred_element_type=jnp.float32
        )
        first_factor_derivative = first_factor_derivative.reshape(seq_total, block_rows * width)
        left_pieces.append(first_factor_derivative)
    left_terms = jnp.concatenate(left_pieces, axis=1)
    left_own = lax.psum_scatter(left_terms, "col", scatter_dimension=0, tiled=True)
    right_spread = lax.all_to_all(
        right_acc.reshape(seq_total, tok_cols * width),
        "col",
        split_axis=0,
        concat_axis=1,
        tiled=True,
    )
    right_own = lax.psum_scatter(right_spread, "row", scatter_dimension=1, tiled=True)
    left_in = (
        left_own.reshape(shard_homolog_number, residue_line_number, width)
        * mask_single_precision[..., None]
    ).astype(jnp.bfloat16)
    right_in = (
        right_own.reshape(shard_homolog_number, residue_line_number, width)
        * mask_single_precision[..., None]
    ).astype(jnp.bfloat16)
    left_part = jnp.einsum(
        "sic,sip->cp", standardized_bfloat, left_in, preferred_element_type=jnp.float32
    )
    right_part = jnp.einsum(
        "sic,sip->cp", standardized_bfloat, right_in, preferred_element_type=jnp.float32
    )
    d_normal = jnp.einsum(
        "sip,cp->sic", left_in, first_projection_matrix, preferred_element_type=jnp.float32
    ) + jnp.einsum(
        "sip,cp->sic", right_in, second_projection_matrix, preferred_element_type=jnp.float32
    )
    gain_part = jnp.sum(d_normal * standardized_entries, axis=(0, 1))
    beta_part = jnp.sum(d_normal, axis=(0, 1))
    standardized_derivative = d_normal * standardizer_scale
    embedding_derivative = reciprocal_spread * (
        standardized_derivative
        - jnp.mean(standardized_derivative, axis=-1, keepdims=True)
        - standardized_entries
        * jnp.mean(standardized_derivative * standardized_entries, axis=-1, keepdims=True)
    )
    (
        final_matrix_derivative,
        first_matrix_derivative,
        second_matrix_derivative,
        scale_factor_derivative,
        shift_term_derivative,
        shift_derivative,
    ) = lax.psum((wout_acc, left_part, right_part, gain_part, beta_part, bias_part), ("row", "col"))
    return (
        embedding_derivative,
        final_matrix_derivative,
        first_matrix_derivative,
        second_matrix_derivative,
        scale_factor_derivative,
        shift_term_derivative,
        shift_derivative,
    )


BF = jnp.bfloat16
F32 = jnp.float32


def spread(rows, cols, rule):
    r = lax.broadcasted_iota(jnp.int32, (rows, cols), 0)
    c = lax.broadcasted_iota(jnp.int32, (rows, cols), 1)
    return rule(r, c)


def mm(a, b):
    return jnp.dot(a, b, preferred_element_type=F32)


def mm_nt(a, b):
    return lax.dot_general(a, b, (((1,), (1,)), ((), ())), preferred_element_type=F32)


def mm_tn(a, b):
    return lax.dot_general(a, b, (((0,), (0,)), ((), ())), preferred_element_type=F32)


def swap_blocks(block):
    lane = lax.broadcasted_iota(jnp.int32, (32, 128), 1)
    upper = lane >= 64
    odd = (lane // 32) % 2 == 1
    piece = [block[32 * a : 32 * a + 32] for a in range(4)]
    for a in (0, 1):
        x, y = piece[a], piece[a + 2]
        piece[a] = jnp.where(upper, pltpu.roll(y, 64, 1), x)
        piece[a + 2] = jnp.where(upper, y, pltpu.roll(x, 64, 1))
    for a in (0, 2):
        x, y = piece[a], piece[a + 1]
        piece[a] = jnp.where(odd, pltpu.roll(y, 32, 1), x)
        piece[a + 1] = jnp.where(odd, y, pltpu.roll(x, 96, 1))
    return jnp.concatenate(piece, axis=0)


ABSENT = 1024.0


def pack_kernel(msa_ref, mask_ref, pair_ref, out_ref):
    msa = msa_ref[...].astype(F32)
    pick = spread(8, 512, lambda r, c: jnp.where(c // 64 == r, 1.0, 0.0)).astype(BF)
    present = mm_tn(mask_ref[...].astype(F32).astype(BF), pick) > 0.5
    for g in range(4):
        rows = jnp.concatenate([msa[:, 2 * g, :], msa[:, 2 * g + 1, :]], axis=1)
        out_ref[32 * g : 32 * g + 32, :] = jnp.where(
            present[:, 128 * g : 128 * g + 128], rows, ABSENT
        ).astype(BF)
    out_ref[128:192, :] = pair_ref[...].astype(F32).reshape(64, 128).astype(BF)


def weights_kernel(gain_ref, offset_ref, first_ref, second_ref, final_ref, norm_out, back_out, final_out, scr):
    norm_out[...] = jnp.concatenate(
        [
            jnp.concatenate([ref[...]] * 2, axis=1)
            for ref in (gain_ref, offset_ref, gain_ref, offset_ref) * 2
        ],
        axis=0,
    )
    for k, ref in enumerate((first_ref, second_ref)):
        wide = jnp.concatenate([ref[...].astype(F32)] * 4, axis=1)
        wide = jnp.concatenate([wide] * 4, axis=0)
        own = spread(128, 256, lambda r, c: r // 32 == c // 64)
        back_out[128 * k : 128 * k + 128, :] = jnp.where(own, wide, 0.0).astype(BF)
    scr[...] = final_ref[...].astype(F32)
    for e in range(32):
        final_out[32 * e : 32 * e + 32, :] = scr[pl.ds(e, 32, stride=32), :].astype(BF)


def averager_of():
    return spread(128, 128, lambda r, c: jnp.where(r // 64 == c // 64, 1.0 / 64, 0.0)).astype(BF)


def stage_kernel(
    n_col, a, place_ref, set_ref, norm_ref, back_ref, final_ref,
    rhs_out, left_out, leftt_out, rightt_out, grad_out, pair_out, found_out, *own_out
):
    place = place_ref[0]
    for b in range(n_col):
        at = pl.multiple_of(lax.bitwise_xor(place, b) * 8, 8)
        pair_out[:, pl.ds(at, 8), :] = set_ref[b, 128:192, :].astype(F32).reshape(8, 8, 128)

    gain = norm_ref[0:1, :]
    offset = norm_ref[1:2, :]
    averager = averager_of()
    x = jnp.concatenate(
        [set_ref[b, 32 * g : 32 * g + 32, :] for g in range(4) for b in range(n_col)], axis=0
    )
    mean = mm(x, averager)
    present = mean < ABSENT / 2
    varied = x.astype(F32) - mean
    inverse = lax.rsqrt(mm((varied * varied).astype(BF), averager) + 1e-05)
    normed = varied * inverse
    if own_out:
        for g in range(4):
            own_out[0][32 * g : 32 * g + 32, :] = normed[128 * g : 128 * g + 32]
            own_out[1][32 * g : 32 * g + 32, :] = inverse[128 * g : 128 * g + 32]
    normal = jnp.where(present, normed * gain + offset, 0.0).astype(BF)
    rhs_out[:, 0:128] = normal
    rhs_out[:, 128:256] = normed.astype(BF)
    here = jnp.where(present, 1.0, 0.0)
    lane = lax.broadcasted_iota(jnp.int32, (128, 128), 1)
    found = jnp.zeros((128, 128), F32)
    for g in range(4):
        found = jnp.where(lane % 32 // 2 == 4 * a + g, here[128 * g : 128 * g + 128], found)
    found_out[...] = found
    for h in range(2):
        masked = jnp.concatenate(
            [normal[128 * g : 128 * g + 128] for g in (2 * h, 2 * h + 1)], axis=1
        )
        at = slice(128 * h, 128 * h + 128)
        left_out[:, at] = mm_nt(masked, back_ref[:128, :]).astype(BF)
        both = mm_nt(back_ref[...], masked)
        leftt_out[at, :] = both[:128].astype(BF)
        rightt_out[at, :] = both[128:]

    grad = mm_nt(final_ref[...], pair_out[...].reshape(256, 128).astype(BF)).astype(BF)
    for q in range(8):
        for p in range(2):
            grad_out[128 * p : 128 * p + 128, 128 * q : 128 * q + 128] = swap_blocks(
                grad[128 * q : 128 * q + 128, 128 * p : 128 * p + 128]
            )


def part_kernel(n_row, *refs):
    stages = [refs[7 * a : 7 * a + 7] for a in range(n_row)]
    (
        normed_ref, inverse_ref, norm_ref, back_ref, first_ref, second_ref,
        emb_out, final_hbm_out, first_out, second_out, gain_out, offset_out, bias_out,
        right_scr, scaled_scr, grad_scr, outer_scr, wide_scr, linc_scr, rin_scr, rinc_scr,
        final_out, out_sem,
    ) = refs[7 * n_row :]
    gain = norm_ref[0:1, :]
    averager = averager_of()
    lane = lax.broadcasted_iota(jnp.int32, (128, 128), 1)

    found = sum(stage[6][...] for stage in stages)
    turned = pltpu.roll(found, 64, 1)
    mask = jnp.where((lane % 2 == 0) == (lane < 64), found, turned)
    mask_t = mask.T

    for a, stage in enumerate(stages):
        wide_scr[256 * a : 256 * a + 256, :] = stage[3][...]
    for e in range(32):
        right_scr[32 * e : 32 * e + 32, :] = wide_scr[pl.ds(e, 32, stride=32), :].astype(BF)

    bias = jnp.zeros((1, 128), F32)
    ones = jnp.ones((128, 128), BF)
    for p in range(8):
        both_on = jnp.concatenate(
            [mask_t[0:32] * mask_t[i : i + 1] for i in range(4 * p, 4 * p + 4)], axis=0
        ).astype(BF)
        counts = mm(both_on, ones)
        pair = stages[p // 2][5][4 * (p % 2) : 4 * (p % 2) + 4]
        scaled = pair.reshape(128, 128) / (counts + 0.001)
        bias = bias + jnp.sum(scaled, axis=0, keepdims=True)
        scaled_scr[128 * p : 128 * p + 128, :] = scaled.astype(BF)
    bias_out[...] = bias

    for a, stage in enumerate(stages):
        outer = mm_nt(stage[2][...], right_scr[...]).astype(BF)
        for p in range(2):
            for q in range(8):
                to = 256 * a + 128 * p
                outer_scr[128 * q : 128 * q + 128, to : to + 128] = swap_blocks(
                    outer[128 * p : 128 * p + 128, 128 * q : 128 * q + 128]
                )
    wide_scr[...] = mm(outer_scr[...], scaled_scr[...])
    for c in range(32):
        final_out[32 * c : 32 * c + 32, :] = wide_scr[pl.ds(c, 32, stride=32), :]
    final_send = pltpu.make_async_copy(final_out, final_hbm_out, out_sem)
    final_send.start()

    mask_bf = mask.astype(BF)
    share = 1.0 / (mm_tn(mask_bf, mask_bf)[0:32] + 0.001)
    for i in range(32):
        a, at = i // 8, 32 * (i % 8)
        for q in range(8):
            block = stages[a][4][at : at + 32, 128 * q : 128 * q + 128].astype(F32)
            grad_scr[32 * i : 32 * i + 32, 128 * q : 128 * q + 128] = (
                block * share[i : i + 1]
            ).astype(BF)
    left_grad = mm(grad_scr[...], right_scr[...])
    left = jnp.concatenate([stage[1][...] for stage in stages], axis=1)
    right_grad = mm(left, grad_scr[...])

    identity = spread(128, 128, lambda r, c: jnp.where(r == c, 1.0, 0.0)).astype(BF)
    for q in range(8):
        at = slice(128 * q, 128 * q + 128)
        rin_scr[at, :] = mm_nt(identity, (right_grad[:, at] * mask).astype(BF))
    for k in range(8):
        rows = []
        for t in range(4 * k, 4 * k + 4):
            rows.append(left_grad[32 * t : 32 * t + 32] * mask_t[t : t + 1])
        at = slice(128 * k, 128 * k + 128)
        linc_scr[at, :] = jnp.concatenate(rows, axis=0).astype(BF)
        rinc_scr[at, :] = jnp.concatenate(
            [rin_scr[pl.ds(t, 32, stride=32), :] for t in range(4 * k, 4 * k + 4)], axis=0
        ).astype(BF)

    total = jnp.zeros((128, 256), F32)
    sums = jnp.zeros((128, 128), F32)
    for g in range(16):
        grads = jnp.concatenate(
            [linc_scr[64 * g : 64 * g + 64, :], rinc_scr[64 * g : 64 * g + 64, :]], axis=0
        )
        sums = sums + grads.astype(F32)
        total = total + mm(grads, stages[g // 4][0][128 * (g % 4) : 128 * (g % 4) + 128, :])

    def fold(block):
        return block[0:32, 0:64] + block[32:64, 64:128]

    first_out[...] = fold(total[0:64, 0:128])
    second_out[...] = fold(total[64:128, 0:128])
    sums = jnp.sum(sums, axis=1, keepdims=True)
    left_sum = sums[0:32] + sums[32:64]
    right_sum = sums[64:96] + sums[96:128]
    first = first_ref[...].astype(F32)
    second = second_ref[...].astype(F32)
    gain_out[...] = jnp.sum(
        first * fold(total[0:64, 128:256]) + second * fold(total[64:128, 128:256]),
        axis=0, keepdims=True,
    )
    offset_out[...] = jnp.sum(first * left_sum + second * right_sum, axis=0, keepdims=True)

    for h in range(2):
        at = slice(128 * h, 128 * h + 128)
        d_normal = mm_tn(linc_scr[at, :], back_ref[:128, :]) + mm_tn(rinc_scr[at, :], back_ref[128:, :])
        for half in range(2):
            g = 2 * h + half
            d_hat = d_normal[0:32, 128 * half : 128 * half + 128] * gain
            normed = normed_ref[32 * g : 32 * g + 32, :]
            result = inverse_ref[32 * g : 32 * g + 32, :] * (
                d_hat
                - mm(d_hat.astype(BF), averager)
                - normed * mm((d_hat * normed).astype(BF), averager)
            )
            emb_out[:, 2 * g, :] = result[:, 0:64]
            emb_out[:, 2 * g + 1, :] = result[:, 64:128]
    final_send.wait()


def vmem(count):
    return [pl.BlockSpec(memory_space=pltpu.VMEM)] * count


LIMIT = pltpu.CompilerParams(vmem_limit_bytes=32 * 1024 * 1024)


def gathered_body(
    n_row,
    n_col,
    homolog_embedding,
    presence_indicator,
    coupling_change_derivative,
    standardizer_scale,
    standardizer_shift,
    first_projection_matrix,
    second_projection_matrix,
    final_projection_matrix,
):
    shards, tokens, features = homolog_embedding.shape
    width = first_projection_matrix.shape[1]
    first_t, second_t = first_projection_matrix.T, second_projection_matrix.T
    shape = lambda *dims: jax.ShapeDtypeStruct(dims, F32)
    held = lambda *dims: pltpu.VMEM(dims, F32)
    held_bf = lambda *dims: pltpu.VMEM(dims, BF)
    place = lax.bitwise_xor(lax.axis_index("row"), lax.axis_index("col"))
    place = place.astype(jnp.int32).reshape(1)
    packed = pl.pallas_call(
        pack_kernel,
        out_shape=held_bf(192, 128),
        in_specs=vmem(3),
        out_specs=vmem(1)[0],
    )(homolog_embedding, presence_indicator.T, coupling_change_derivative)
    pieces = [packed] + [
        lax.ppermute(packed, "col", [(k, k ^ b) for k in range(n_col)]) for b in range(1, n_col)
    ]
    weights = pl.pallas_call(
        weights_kernel,
        out_shape=(held(8, 128), held_bf(256, 256), held_bf(width * width, 128)),
        in_specs=vmem(5),
        out_specs=tuple(vmem(3)),
        scratch_shapes=[pltpu.VMEM((width * width, 128), F32)],
        compiler_params=LIMIT,
    )(
        standardizer_scale.reshape(1, features),
        standardizer_shift.reshape(1, features),
        first_t,
        second_t,
        final_projection_matrix,
    )
    pieces, weights = lax.optimization_barrier((pieces, weights))
    norm, back, final_turned = weights

    sets = {0: jnp.stack(pieces)}
    step = n_row // 2
    while step:
        for a, block in sorted(sets.items()):
            sets[a ^ step] = lax.ppermute(block, "row", [(k, k ^ step) for k in range(n_row)])
        step //= 2

    def stage(a):
        outs = [
            held_bf(512, 256), held_bf(128, 256), held_bf(256, 128), held(256, 128),
            held_bf(256, 1024), held(8, 32, 128), held(128, 128),
        ]
        if a == 0:
            outs += [held(128, 128)] * 2
        return pl.pallas_call(
            functools.partial(stage_kernel, n_col, a),
            out_shape=tuple(outs),
            in_specs=[pl.BlockSpec(memory_space=pltpu.SMEM)] + vmem(4),
            out_specs=tuple(vmem(len(outs))),
            compiler_params=LIMIT,
            cost_estimate=pl.CostEstimate(
                flops=1_000_000_000, bytes_accessed=4_000_000, transcendentals=0
            ),
        )(place, sets[a], norm, back, final_turned)

    stages = [stage(a) for a in range(n_row)]
    own = stages[0][7:]
    hbm = pl.BlockSpec(memory_space=pltpu.HBM)
    outs = pl.pallas_call(
        functools.partial(part_kernel, n_row),
        out_shape=(
            shape(shards, tokens, features),
            shape(width * width, 128),
            shape(width, features),
            shape(width, features),
            shape(1, features),
            shape(1, features),
            shape(1, 128),
        ),
        in_specs=vmem(7 * n_row + 6),
        out_specs=(*vmem(1), hbm, *vmem(5)),
        scratch_shapes=[
            pltpu.VMEM((1024, 128), BF),
            pltpu.VMEM((1024, 128), BF),
            pltpu.VMEM((1024, 1024), BF),
            pltpu.VMEM((1024, 1024), BF),
            pltpu.VMEM((1024, 128), F32),
            pltpu.VMEM((1024, 128), BF),
            pltpu.VMEM((1024, 128), F32),
            pltpu.VMEM((1024, 128), BF),
            pltpu.VMEM((1024, 128), F32),
            pltpu.SemaphoreType.DMA,
        ],
        compiler_params=LIMIT,
    )(*[x for s in stages for x in s[:7]], *own, norm, back, first_t, second_t)
    emb, final, first, second, gain, offset, bias = outs
    return emb, final, first.T, second.T, gain.reshape(-1), offset.reshape(-1), bias.reshape(-1)


def body(n_row, n_col, *arguments):
    msa, _, pair = arguments[:3]
    width = arguments[5].shape[1]
    fits = (
        n_row == 4
        and n_col == 4
        and msa.shape == (32, 8, 64)
        and pair.shape == (8, 8, 128)
        and width == 32
    )
    if fits:
        return gathered_body(n_row, n_col, *arguments)
    return sharded_body(*arguments)


def solution(mesh):
    placed = (
        P(("grp", "col"), "row", None),
        P(("grp", "col"), "row"),
        P(("grp", "row"), "col", None),
        P(),
        P(),
        P(),
        P(),
        P(),
    )
    return jax.shard_map(
        functools.partial(body, mesh.shape["row"], mesh.shape["col"]),
        mesh=mesh,
        in_specs=placed,
        out_specs=(
            P(("grp", "col"), "row", None),
            P("grp", None),
            P("grp", None),
            P("grp", None),
            P("grp"),
            P("grp"),
            P("grp"),
        ),
        check_vma=False,
    )
```

```python
import functools

import jax
import jax.numpy as jnp
from jax import lax
from jax.experimental import pallas as pl
from jax.experimental.pallas import tpu as pltpu
from jax.sharding import PartitionSpec as P

TOKB = 2


def standardizer_parts(homolog_embedding, standardizer_scale, standardizer_shift):
    incoming_entries = homolog_embedding.astype(jnp.float32)
    center = jnp.mean(incoming_entries, axis=-1, keepdims=True)
    varied = incoming_entries - center
    variance = jnp.mean(varied * varied, axis=-1, keepdims=True)
    reciprocal_spread = lax.rsqrt(variance + 1e-05)
    standardized_entries = varied * reciprocal_spread
    standardized_bfloat = (standardized_entries * standardizer_scale + standardizer_shift).astype(
        jnp.bfloat16
    )
    return (standardized_entries, reciprocal_spread, standardized_bfloat)


def sharded_body(
    homolog_embedding,
    presence_indicator,
    coupling_change_derivative,
    standardizer_scale,
    standardizer_shift,
    first_projection_matrix,
    second_projection_matrix,
    final_projection_matrix,
):
    shard_homolog_number, residue_line_number, feature_number = homolog_embedding.shape
    tok_cols = coupling_change_derivative.shape[1]
    width = first_projection_matrix.shape[1]
    standardized_entries, reciprocal_spread, standardized_bfloat = standardizer_parts(
        homolog_embedding, standardizer_scale, standardizer_shift
    )
    mask_single_precision = presence_indicator.astype(jnp.float32)
    mask_half_precision = presence_indicator.astype(jnp.bfloat16)
    left = (
        jnp.einsum(
            "sic,cp->sip",
            standardized_bfloat,
            first_projection_matrix,
            preferred_element_type=jnp.float32,
        )
        * mask_single_precision[..., None]
    ).astype(jnp.bfloat16)
    right = (
        jnp.einsum(
            "sic,cp->sip",
            standardized_bfloat,
            second_projection_matrix,
            preferred_element_type=jnp.float32,
        )
        * mask_single_precision[..., None]
    ).astype(jnp.bfloat16)
    left_flat = left.reshape(shard_homolog_number, residue_line_number * width)
    right_flat = right.reshape(shard_homolog_number, residue_line_number * width)
    left_all, mask_left = (
        lax.all_gather(left_flat, "col", axis=0, tiled=True),
        lax.all_gather(mask_half_precision, "col", axis=0, tiled=True),
    )
    right_wide, mask_wide = (
        lax.all_gather(right_flat, "row", axis=1, tiled=True),
        lax.all_gather(mask_half_precision, "row", axis=1, tiled=True),
    )
    right_all, mask_right = (
        lax.all_to_all(right_wide, "col", split_axis=1, concat_axis=0, tiled=True),
        lax.all_to_all(mask_wide, "col", split_axis=1, concat_axis=0, tiled=True),
    )
    seq_total = left_all.shape[0]
    right_three = right_all.reshape(seq_total, tok_cols, width)
    counts = jnp.einsum("si,sj->ij", mask_left, mask_right, preferred_element_type=jnp.float32)
    scaled = coupling_change_derivative.astype(jnp.float32) / (counts + 0.001)[..., None]
    bias_part = jnp.sum(scaled, axis=(0, 1))
    scaled_bf = scaled.astype(jnp.bfloat16)
    block_rows = residue_line_number // TOKB
    right_acc = jnp.zeros((seq_total, tok_cols, width), jnp.float32)
    wout_acc = jnp.zeros(final_projection_matrix.shape, jnp.float32)
    left_pieces = []
    for block_index in range(TOKB):
        first = block_index * block_rows
        rows_bf = scaled_bf[first : first + block_rows]
        outer_grad = jnp.einsum(
            "ijz,fz->ijf", rows_bf, final_projection_matrix, preferred_element_type=jnp.float32
        ).astype(jnp.bfloat16)
        outer_grad = outer_grad.reshape(block_rows, tok_cols, width, width)
        left_block = left_all[:, first * width : (first + block_rows) * width].reshape(
            seq_total, block_rows, width
        )
        first_factor_derivative = jnp.einsum(
            "ijce,sje->sic", outer_grad, right_three, preferred_element_type=jnp.float32
        )
        right_acc = right_acc + jnp.einsum(
            "ijce,sic->sje", outer_grad, left_block, preferred_element_type=jnp.float32
        )
        outer = jnp.einsum(
            "sic,sje->ijce", left_block, right_three, preferred_element_type=jnp.float32
        ).astype(jnp.bfloat16)
        outer = outer.reshape(block_rows, tok_cols, width * width)
        wout_acc = wout_acc + jnp.einsum(
            "ijf,ijz->fz", outer, rows_bf, preferred_element_type=jnp.float32
        )
        first_factor_derivative = first_factor_derivative.reshape(seq_total, block_rows * width)
        left_pieces.append(first_factor_derivative)
    left_terms = jnp.concatenate(left_pieces, axis=1)
    left_own = lax.psum_scatter(left_terms, "col", scatter_dimension=0, tiled=True)
    right_spread = lax.all_to_all(
        right_acc.reshape(seq_total, tok_cols * width),
        "col",
        split_axis=0,
        concat_axis=1,
        tiled=True,
    )
    right_own = lax.psum_scatter(right_spread, "row", scatter_dimension=1, tiled=True)
    left_in = (
        left_own.reshape(shard_homolog_number, residue_line_number, width)
        * mask_single_precision[..., None]
    ).astype(jnp.bfloat16)
    right_in = (
        right_own.reshape(shard_homolog_number, residue_line_number, width)
        * mask_single_precision[..., None]
    ).astype(jnp.bfloat16)
    left_part = jnp.einsum(
        "sic,sip->cp", standardized_bfloat, left_in, preferred_element_type=jnp.float32
    )
    right_part = jnp.einsum(
        "sic,sip->cp", standardized_bfloat, right_in, preferred_element_type=jnp.float32
    )
    d_normal = jnp.einsum(
        "sip,cp->sic", left_in, first_projection_matrix, preferred_element_type=jnp.float32
    ) + jnp.einsum(
        "sip,cp->sic", right_in, second_projection_matrix, preferred_element_type=jnp.float32
    )
    gain_part = jnp.sum(d_normal * standardized_entries, axis=(0, 1))
    beta_part = jnp.sum(d_normal, axis=(0, 1))
    standardized_derivative = d_normal * standardizer_scale
    embedding_derivative = reciprocal_spread * (
        standardized_derivative
        - jnp.mean(standardized_derivative, axis=-1, keepdims=True)
        - standardized_entries
        * jnp.mean(standardized_derivative * standardized_entries, axis=-1, keepdims=True)
    )
    (
        final_matrix_derivative,
        first_matrix_derivative,
        second_matrix_derivative,
        scale_factor_derivative,
        shift_term_derivative,
        shift_derivative,
    ) = lax.psum((wout_acc, left_part, right_part, gain_part, beta_part, bias_part), ("row", "col"))
    return (
        embedding_derivative,
        final_matrix_derivative,
        first_matrix_derivative,
        second_matrix_derivative,
        scale_factor_derivative,
        shift_term_derivative,
        shift_derivative,
    )


BF = jnp.bfloat16
F32 = jnp.float32


def spread(rows, cols, rule):
    r = lax.broadcasted_iota(jnp.int32, (rows, cols), 0)
    c = lax.broadcasted_iota(jnp.int32, (rows, cols), 1)
    return rule(r, c)


def mm(a, b):
    return jnp.dot(a, b, preferred_element_type=F32)


def mm_nt(a, b):
    return lax.dot_general(a, b, (((1,), (1,)), ((), ())), preferred_element_type=F32)


def mm_tn(a, b):
    return lax.dot_general(a, b, (((0,), (0,)), ((), ())), preferred_element_type=F32)


def swap_blocks(block):
    lane = lax.broadcasted_iota(jnp.int32, (32, 128), 1)
    upper = lane >= 64
    odd = (lane // 32) % 2 == 1
    piece = [block[32 * a : 32 * a + 32] for a in range(4)]
    for a in (0, 1):
        x, y = piece[a], piece[a + 2]
        piece[a] = jnp.where(upper, pltpu.roll(y, 64, 1), x)
        piece[a + 2] = jnp.where(upper, y, pltpu.roll(x, 64, 1))
    for a in (0, 2):
        x, y = piece[a], piece[a + 1]
        piece[a] = jnp.where(odd, pltpu.roll(y, 32, 1), x)
        piece[a + 1] = jnp.where(odd, y, pltpu.roll(x, 96, 1))
    return jnp.concatenate(piece, axis=0)


ABSENT = 1024.0


def pack_kernel(msa_ref, mask_ref, pair_ref, out_ref):
    msa = msa_ref[...].astype(F32)
    pick = spread(8, 512, lambda r, c: jnp.where(c // 64 == r, 1.0, 0.0)).astype(BF)
    present = mm_tn(mask_ref[...].astype(F32).astype(BF), pick) > 0.5
    for g in range(4):
        rows = jnp.concatenate([msa[:, 2 * g, :], msa[:, 2 * g + 1, :]], axis=1)
        out_ref[32 * g : 32 * g + 32, :] = jnp.where(
            present[:, 128 * g : 128 * g + 128], rows, ABSENT
        ).astype(BF)
    out_ref[128:192, :] = pair_ref[...].astype(F32).reshape(64, 128).astype(BF)


def weights_kernel(*refs):
    sources, (norm_out, back_out, final_out), held, scr, sems = refs[:5], refs[5:8], refs[8:13], refs[13], refs[14]
    copies = [pltpu.make_async_copy(sources[k], held[k], sems.at[k]) for k in range(5)]
    for copy in copies:
        copy.start()
    for copy in copies:
        copy.wait()
    gain_ref, offset_ref, first_ref, second_ref, final_ref = held
    norm_out[...] = jnp.concatenate(
        [
            jnp.concatenate([ref[...]] * 2, axis=1)
            for ref in (gain_ref, offset_ref, gain_ref, offset_ref) * 2
        ],
        axis=0,
    )
    for k, ref in enumerate((first_ref, second_ref)):
        wide = jnp.concatenate([ref[...].astype(F32)] * 4, axis=1)
        wide = jnp.concatenate([wide] * 4, axis=0)
        own = spread(128, 256, lambda r, c: r // 32 == c // 64)
        back_out[128 * k : 128 * k + 128, :] = jnp.where(own, wide, 0.0).astype(BF)
    scr[...] = final_ref[...].astype(F32)
    for e in range(32):
        final_out[32 * e : 32 * e + 32, :] = scr[pl.ds(e, 32, stride=32), :].astype(BF)


def averager_of():
    return spread(128, 128, lambda r, c: jnp.where(r // 64 == c // 64, 1.0 / 64, 0.0)).astype(BF)


def stage_kernel(
    n_col, a, place_ref, even_ref, odd_ref, norm_ref, back_ref, final_ref,
    rhs_out, left_out, leftt_out, rightt_out, grad_out, pair_out, found_out, *own_out
):
    place = place_ref[0]
    blocks = [(even_ref, odd_ref)[b % 2].at[b // 2] for b in range(n_col)]
    for b in range(n_col):
        at = pl.multiple_of(lax.bitwise_xor(place, b) * 8, 8)
        pair_out[:, pl.ds(at, 8), :] = blocks[b][128:192, :].astype(F32).reshape(8, 8, 128)

    gain = norm_ref[0:1, :]
    offset = norm_ref[1:2, :]
    averager = averager_of()
    x = jnp.concatenate(
        [blocks[b][32 * g : 32 * g + 32, :] for g in range(4) for b in range(n_col)], axis=0
    )
    mean = mm(x, averager)
    present = mean < ABSENT / 2
    varied = x.astype(F32) - mean
    inverse = lax.rsqrt(mm((varied * varied).astype(BF), averager) + 1e-05)
    normed = varied * inverse
    if own_out:
        for g in range(4):
            own_out[0][32 * g : 32 * g + 32, :] = normed[128 * g : 128 * g + 32]
            own_out[1][32 * g : 32 * g + 32, :] = inverse[128 * g : 128 * g + 32]
    normal = jnp.where(present, normed * gain + offset, 0.0).astype(BF)
    rhs_out[:, 0:128] = normal
    rhs_out[:, 128:256] = normed.astype(BF)
    here = jnp.where(present, 1.0, 0.0)
    lane = lax.broadcasted_iota(jnp.int32, (128, 128), 1)
    found = jnp.zeros((128, 128), F32)
    for g in range(4):
        found = jnp.where(lane % 32 // 2 == 4 * a + g, here[128 * g : 128 * g + 128], found)
    found_out[...] = found
    for h in range(2):
        masked = jnp.concatenate(
            [normal[128 * g : 128 * g + 128] for g in (2 * h, 2 * h + 1)], axis=1
        )
        at = slice(128 * h, 128 * h + 128)
        left_out[:, at] = mm_nt(masked, back_ref[:128, :]).astype(BF)
        both = mm_nt(back_ref[...], masked)
        leftt_out[at, :] = both[:128].astype(BF)
        rightt_out[at, :] = both[128:]

    grad = mm_nt(final_ref[...], pair_out[...].reshape(256, 128).astype(BF)).astype(BF)
    for q in range(8):
        for p in range(2):
            grad_out[128 * p : 128 * p + 128, 128 * q : 128 * q + 128] = swap_blocks(
                grad[128 * q : 128 * q + 128, 128 * p : 128 * p + 128]
            )


def part_kernel(n_row, *refs):
    stages = [refs[7 * a : 7 * a + 7] for a in range(n_row)]
    (
        normed_ref, inverse_ref, norm_ref, back_ref, first_ref, second_ref,
        emb_out, final_hbm_out, first_out, second_out, gain_out, offset_out, bias_out,
        right_scr, scaled_scr, grad_scr, outer_scr, wide_scr, linc_scr, rin_scr, rinc_scr,
        final_out, out_sem,
    ) = refs[7 * n_row :]
    gain = norm_ref[0:1, :]
    averager = averager_of()
    lane = lax.broadcasted_iota(jnp.int32, (128, 128), 1)

    found = sum(stage[6][...] for stage in stages)
    turned = pltpu.roll(found, 64, 1)
    mask = jnp.where((lane % 2 == 0) == (lane < 64), found, turned)
    mask_t = mask.T

    for a, stage in enumerate(stages):
        wide_scr[256 * a : 256 * a + 256, :] = stage[3][...]
    for e in range(32):
        right_scr[32 * e : 32 * e + 32, :] = wide_scr[pl.ds(e, 32, stride=32), :].astype(BF)

    bias = jnp.zeros((1, 128), F32)
    ones = jnp.ones((128, 128), BF)
    for p in range(8):
        both_on = jnp.concatenate(
            [mask_t[0:32] * mask_t[i : i + 1] for i in range(4 * p, 4 * p + 4)], axis=0
        ).astype(BF)
        counts = mm(both_on, ones)
        pair = stages[p // 2][5][4 * (p % 2) : 4 * (p % 2) + 4]
        scaled = pair.reshape(128, 128) / (counts + 0.001)
        bias = bias + jnp.sum(scaled, axis=0, keepdims=True)
        scaled_scr[128 * p : 128 * p + 128, :] = scaled.astype(BF)
    bias_out[...] = bias

    for a, stage in enumerate(stages):
        outer = mm_nt(stage[2][...], right_scr[...]).astype(BF)
        for p in range(2):
            for q in range(8):
                to = 256 * a + 128 * p
                outer_scr[128 * q : 128 * q + 128, to : to + 128] = swap_blocks(
                    outer[128 * p : 128 * p + 128, 128 * q : 128 * q + 128]
                )
    wide_scr[...] = mm(outer_scr[...], scaled_scr[...])
    for c in range(32):
        final_out[32 * c : 32 * c + 32, :] = wide_scr[pl.ds(c, 32, stride=32), :]
    final_send = pltpu.make_async_copy(final_out, final_hbm_out, out_sem)
    final_send.start()

    mask_bf = mask.astype(BF)
    share = 1.0 / (mm_tn(mask_bf, mask_bf)[0:32] + 0.001)
    for i in range(32):
        a, at = i // 8, 32 * (i % 8)
        for q in range(8):
            block = stages[a][4][at : at + 32, 128 * q : 128 * q + 128].astype(F32)
            grad_scr[32 * i : 32 * i + 32, 128 * q : 128 * q + 128] = (
                block * share[i : i + 1]
            ).astype(BF)
    left_grad = mm(grad_scr[...], right_scr[...])
    left = jnp.concatenate([stage[1][...] for stage in stages], axis=1)
    right_grad = mm(left, grad_scr[...])

    identity = spread(128, 128, lambda r, c: jnp.where(r == c, 1.0, 0.0)).astype(BF)
    for q in range(8):
        at = slice(128 * q, 128 * q + 128)
        rin_scr[at, :] = mm_nt(identity, (right_grad[:, at] * mask).astype(BF))
    for k in range(8):
        rows = []
        for t in range(4 * k, 4 * k + 4):
            rows.append(left_grad[32 * t : 32 * t + 32] * mask_t[t : t + 1])
        at = slice(128 * k, 128 * k + 128)
        linc_scr[at, :] = jnp.concatenate(rows, axis=0).astype(BF)
        rinc_scr[at, :] = jnp.concatenate(
            [rin_scr[pl.ds(t, 32, stride=32), :] for t in range(4 * k, 4 * k + 4)], axis=0
        ).astype(BF)

    total = jnp.zeros((128, 256), F32)
    sums = jnp.zeros((128, 128), F32)
    for g in range(16):
        grads = jnp.concatenate(
            [linc_scr[64 * g : 64 * g + 64, :], rinc_scr[64 * g : 64 * g + 64, :]], axis=0
        )
        sums = sums + grads.astype(F32)
        total = total + mm(grads, stages[g // 4][0][128 * (g % 4) : 128 * (g % 4) + 128, :])

    def fold(block):
        return block[0:32, 0:64] + block[32:64, 64:128]

    first_out[...] = fold(total[0:64, 0:128])
    second_out[...] = fold(total[64:128, 0:128])
    sums = jnp.sum(sums, axis=1, keepdims=True)
    left_sum = sums[0:32] + sums[32:64]
    right_sum = sums[64:96] + sums[96:128]
    first = first_ref[...].astype(F32)
    second = second_ref[...].astype(F32)
    gain_out[...] = jnp.sum(
        first * fold(total[0:64, 128:256]) + second * fold(total[64:128, 128:256]),
        axis=0, keepdims=True,
    )
    offset_out[...] = jnp.sum(first * left_sum + second * right_sum, axis=0, keepdims=True)

    for h in range(2):
        at = slice(128 * h, 128 * h + 128)
        d_normal = mm_tn(linc_scr[at, :], back_ref[:128, :]) + mm_tn(rinc_scr[at, :], back_ref[128:, :])
        for half in range(2):
            g = 2 * h + half
            d_hat = d_normal[0:32, 128 * half : 128 * half + 128] * gain
            normed = normed_ref[32 * g : 32 * g + 32, :]
            result = inverse_ref[32 * g : 32 * g + 32, :] * (
                d_hat
                - mm(d_hat.astype(BF), averager)
                - normed * mm((d_hat * normed).astype(BF), averager)
            )
            emb_out[:, 2 * g, :] = result[:, 0:64]
            emb_out[:, 2 * g + 1, :] = result[:, 64:128]
    final_send.wait()


def vmem(count):
    return [pl.BlockSpec(memory_space=pltpu.VMEM)] * count


LIMIT = pltpu.CompilerParams(vmem_limit_bytes=32 * 1024 * 1024)


def gathered_body(
    n_row,
    n_col,
    homolog_embedding,
    presence_indicator,
    coupling_change_derivative,
    standardizer_scale,
    standardizer_shift,
    first_projection_matrix,
    second_projection_matrix,
    final_projection_matrix,
):
    shards, tokens, features = homolog_embedding.shape
    width = first_projection_matrix.shape[1]
    first_t, second_t = first_projection_matrix.T, second_projection_matrix.T
    shape = lambda *dims: jax.ShapeDtypeStruct(dims, F32)
    held = lambda *dims: pltpu.VMEM(dims, F32)
    held_bf = lambda *dims: pltpu.VMEM(dims, BF)
    hbm = pl.BlockSpec(memory_space=pltpu.HBM)
    place = lax.bitwise_xor(lax.axis_index("row"), lax.axis_index("col"))
    place = place.astype(jnp.int32).reshape(1)
    packed = pl.pallas_call(
        pack_kernel,
        out_shape=held_bf(192, 128),
        in_specs=vmem(3),
        out_specs=vmem(1)[0],
    )(homolog_embedding, presence_indicator.T, coupling_change_derivative)
    far = lax.ppermute(packed, "col", [(k, k ^ 2) for k in range(n_col)])
    weights = pl.pallas_call(
        weights_kernel,
        out_shape=(held(8, 128), held_bf(256, 256), held_bf(width * width, 128)),
        in_specs=[hbm] * 5,
        out_specs=tuple(vmem(3)),
        scratch_shapes=[
            pltpu.VMEM((1, features), F32),
            pltpu.VMEM((1, features), F32),
            pltpu.VMEM((width, features), BF),
            pltpu.VMEM((width, features), BF),
            pltpu.VMEM((width * width, 128), BF),
            pltpu.VMEM((width * width, 128), F32),
            pltpu.SemaphoreType.DMA((5,)),
        ],
        compiler_params=LIMIT,
    )(
        standardizer_scale.reshape(1, features),
        standardizer_shift.reshape(1, features),
        first_t,
        second_t,
        final_projection_matrix,
    )
    far, weights = lax.optimization_barrier((far, weights))
    norm, back, final_turned = weights

    def over(axis, size, step, array):
        return lax.ppermute(array, axis, [(k, k ^ step) for k in range(size)])

    even = jnp.stack([packed, far])
    odd = over("col", n_col, 1, even)
    chip_even = over("row", n_row, 2, even)
    chip_odd = over("row", n_row, 2, odd)
    core = over("row", n_row, 1, jnp.stack([even, odd]))

    def stage(a, even, odd):
        outs = [
            held_bf(512, 256), held_bf(128, 256), held_bf(256, 128), held(256, 128),
            held_bf(256, 1024), held(8, 32, 128), held(128, 128),
        ]
        if a == 0:
            outs += [held(128, 128)] * 2
        return pl.pallas_call(
            functools.partial(stage_kernel, n_col, a),
            out_shape=tuple(outs),
            in_specs=[pl.BlockSpec(memory_space=pltpu.SMEM)] + vmem(5),
            out_specs=tuple(vmem(len(outs))),
            compiler_params=LIMIT,
            cost_estimate=pl.CostEstimate(
                flops=1_000_000_000, bytes_accessed=4_000_000, transcendentals=0
            ),
        )(place, even, odd, norm, back, final_turned)

    own_stage = stage(0, even, odd)
    core_stage = stage(1, core[0], core[1])
    chip = jnp.stack([chip_even, chip_odd])
    chip, own_stage, core_stage = lax.optimization_barrier((chip, own_stage, core_stage))
    both = over("row", n_row, 1, chip)
    stages = [own_stage, core_stage, stage(2, chip[0], chip[1]), stage(3, both[0], both[1])]
    own = stages[0][7:]
    outs = pl.pallas_call(
        functools.partial(part_kernel, n_row),
        out_shape=(
            shape(shards, tokens, features),
            shape(width * width, 128),
            shape(width, features),
            shape(width, features),
            shape(1, features),
            shape(1, features),
            shape(1, 128),
        ),
        in_specs=vmem(7 * n_row + 6),
        out_specs=(*vmem(1), hbm, *vmem(5)),
        scratch_shapes=[
            pltpu.VMEM((1024, 128), BF),
            pltpu.VMEM((1024, 128), BF),
            pltpu.VMEM((1024, 1024), BF),
            pltpu.VMEM((1024, 1024), BF),
            pltpu.VMEM((1024, 128), F32),
            pltpu.VMEM((1024, 128), BF),
            pltpu.VMEM((1024, 128), F32),
            pltpu.VMEM((1024, 128), BF),
            pltpu.VMEM((1024, 128), F32),
            pltpu.SemaphoreType.DMA,
        ],
        compiler_params=LIMIT,
    )(*[x for s in stages for x in s[:7]], *own, norm, back, first_t, second_t)
    emb, final, first, second, gain, offset, bias = outs
    return emb, final, first.T, second.T, gain.reshape(-1), offset.reshape(-1), bias.reshape(-1)


def body(n_row, n_col, *arguments):
    msa, _, pair = arguments[:3]
    width = arguments[5].shape[1]
    fits = (
        n_row == 4
        and n_col == 4
        and msa.shape == (32, 8, 64)
        and pair.shape == (8, 8, 128)
        and width == 32
    )
    if fits:
        return gathered_body(n_row, n_col, *arguments)
    return sharded_body(*arguments)


def solution(mesh):
    placed = (
        P(("grp", "col"), "row", None),
        P(("grp", "col"), "row"),
        P(("grp", "row"), "col", None),
        P(),
        P(),
        P(),
        P(),
        P(),
    )
    return jax.shard_map(
        functools.partial(body, mesh.shape["row"], mesh.shape["col"]),
        mesh=mesh,
        in_specs=placed,
        out_specs=(
            P(("grp", "col"), "row", None),
            P("grp", None),
            P("grp", None),
            P("grp", None),
            P("grp"),
            P("grp"),
            P("grp"),
        ),
        check_vma=False,
    )
```

```python
import functools

import jax
import jax.numpy as jnp
from jax import lax
from jax.experimental import pallas as pl
from jax.experimental.pallas import tpu as pltpu
from jax.sharding import PartitionSpec as P

TOKB = 2


def standardizer_parts(homolog_embedding, standardizer_scale, standardizer_shift):
    incoming_entries = homolog_embedding.astype(jnp.float32)
    center = jnp.mean(incoming_entries, axis=-1, keepdims=True)
    varied = incoming_entries - center
    variance = jnp.mean(varied * varied, axis=-1, keepdims=True)
    reciprocal_spread = lax.rsqrt(variance + 1e-05)
    standardized_entries = varied * reciprocal_spread
    standardized_bfloat = (standardized_entries * standardizer_scale + standardizer_shift).astype(
        jnp.bfloat16
    )
    return (standardized_entries, reciprocal_spread, standardized_bfloat)


def sharded_body(
    homolog_embedding,
    presence_indicator,
    coupling_change_derivative,
    standardizer_scale,
    standardizer_shift,
    first_projection_matrix,
    second_projection_matrix,
    final_projection_matrix,
):
    shard_homolog_number, residue_line_number, feature_number = homolog_embedding.shape
    tok_cols = coupling_change_derivative.shape[1]
    width = first_projection_matrix.shape[1]
    standardized_entries, reciprocal_spread, standardized_bfloat = standardizer_parts(
        homolog_embedding, standardizer_scale, standardizer_shift
    )
    mask_single_precision = presence_indicator.astype(jnp.float32)
    mask_half_precision = presence_indicator.astype(jnp.bfloat16)
    left = (
        jnp.einsum(
            "sic,cp->sip",
            standardized_bfloat,
            first_projection_matrix,
            preferred_element_type=jnp.float32,
        )
        * mask_single_precision[..., None]
    ).astype(jnp.bfloat16)
    right = (
        jnp.einsum(
            "sic,cp->sip",
            standardized_bfloat,
            second_projection_matrix,
            preferred_element_type=jnp.float32,
        )
        * mask_single_precision[..., None]
    ).astype(jnp.bfloat16)
    left_flat = left.reshape(shard_homolog_number, residue_line_number * width)
    right_flat = right.reshape(shard_homolog_number, residue_line_number * width)
    left_all, mask_left = (
        lax.all_gather(left_flat, "col", axis=0, tiled=True),
        lax.all_gather(mask_half_precision, "col", axis=0, tiled=True),
    )
    right_wide, mask_wide = (
        lax.all_gather(right_flat, "row", axis=1, tiled=True),
        lax.all_gather(mask_half_precision, "row", axis=1, tiled=True),
    )
    right_all, mask_right = (
        lax.all_to_all(right_wide, "col", split_axis=1, concat_axis=0, tiled=True),
        lax.all_to_all(mask_wide, "col", split_axis=1, concat_axis=0, tiled=True),
    )
    seq_total = left_all.shape[0]
    right_three = right_all.reshape(seq_total, tok_cols, width)
    counts = jnp.einsum("si,sj->ij", mask_left, mask_right, preferred_element_type=jnp.float32)
    scaled = coupling_change_derivative.astype(jnp.float32) / (counts + 0.001)[..., None]
    bias_part = jnp.sum(scaled, axis=(0, 1))
    scaled_bf = scaled.astype(jnp.bfloat16)
    block_rows = residue_line_number // TOKB
    right_acc = jnp.zeros((seq_total, tok_cols, width), jnp.float32)
    wout_acc = jnp.zeros(final_projection_matrix.shape, jnp.float32)
    left_pieces = []
    for block_index in range(TOKB):
        first = block_index * block_rows
        rows_bf = scaled_bf[first : first + block_rows]
        outer_grad = jnp.einsum(
            "ijz,fz->ijf", rows_bf, final_projection_matrix, preferred_element_type=jnp.float32
        ).astype(jnp.bfloat16)
        outer_grad = outer_grad.reshape(block_rows, tok_cols, width, width)
        left_block = left_all[:, first * width : (first + block_rows) * width].reshape(
            seq_total, block_rows, width
        )
        first_factor_derivative = jnp.einsum(
            "ijce,sje->sic", outer_grad, right_three, preferred_element_type=jnp.float32
        )
        right_acc = right_acc + jnp.einsum(
            "ijce,sic->sje", outer_grad, left_block, preferred_element_type=jnp.float32
        )
        outer = jnp.einsum(
            "sic,sje->ijce", left_block, right_three, preferred_element_type=jnp.float32
        ).astype(jnp.bfloat16)
        outer = outer.reshape(block_rows, tok_cols, width * width)
        wout_acc = wout_acc + jnp.einsum(
            "ijf,ijz->fz", outer, rows_bf, preferred_element_type=jnp.float32
        )
        first_factor_derivative = first_factor_derivative.reshape(seq_total, block_rows * width)
        left_pieces.append(first_factor_derivative)
    left_terms = jnp.concatenate(left_pieces, axis=1)
    left_own = lax.psum_scatter(left_terms, "col", scatter_dimension=0, tiled=True)
    right_spread = lax.all_to_all(
        right_acc.reshape(seq_total, tok_cols * width),
        "col",
        split_axis=0,
        concat_axis=1,
        tiled=True,
    )
    right_own = lax.psum_scatter(right_spread, "row", scatter_dimension=1, tiled=True)
    left_in = (
        left_own.reshape(shard_homolog_number, residue_line_number, width)
        * mask_single_precision[..., None]
    ).astype(jnp.bfloat16)
    right_in = (
        right_own.reshape(shard_homolog_number, residue_line_number, width)
        * mask_single_precision[..., None]
    ).astype(jnp.bfloat16)
    left_part = jnp.einsum(
        "sic,sip->cp", standardized_bfloat, left_in, preferred_element_type=jnp.float32
    )
    right_part = jnp.einsum(
        "sic,sip->cp", standardized_bfloat, right_in, preferred_element_type=jnp.float32
    )
    d_normal = jnp.einsum(
        "sip,cp->sic", left_in, first_projection_matrix, preferred_element_type=jnp.float32
    ) + jnp.einsum(
        "sip,cp->sic", right_in, second_projection_matrix, preferred_element_type=jnp.float32
    )
    gain_part = jnp.sum(d_normal * standardized_entries, axis=(0, 1))
    beta_part = jnp.sum(d_normal, axis=(0, 1))
    standardized_derivative = d_normal * standardizer_scale
    embedding_derivative = reciprocal_spread * (
        standardized_derivative
        - jnp.mean(standardized_derivative, axis=-1, keepdims=True)
        - standardized_entries
        * jnp.mean(standardized_derivative * standardized_entries, axis=-1, keepdims=True)
    )
    (
        final_matrix_derivative,
        first_matrix_derivative,
        second_matrix_derivative,
        scale_factor_derivative,
        shift_term_derivative,
        shift_derivative,
    ) = lax.psum((wout_acc, left_part, right_part, gain_part, beta_part, bias_part), ("row", "col"))
    return (
        embedding_derivative,
        final_matrix_derivative,
        first_matrix_derivative,
        second_matrix_derivative,
        scale_factor_derivative,
        shift_term_derivative,
        shift_derivative,
    )


BF = jnp.bfloat16
F32 = jnp.float32


def spread(rows, cols, rule):
    r = lax.broadcasted_iota(jnp.int32, (rows, cols), 0)
    c = lax.broadcasted_iota(jnp.int32, (rows, cols), 1)
    return rule(r, c)


def mm(a, b):
    return jnp.dot(a, b, preferred_element_type=F32)


def mm_nt(a, b):
    return lax.dot_general(a, b, (((1,), (1,)), ((), ())), preferred_element_type=F32)


def mm_tn(a, b):
    return lax.dot_general(a, b, (((0,), (0,)), ((), ())), preferred_element_type=F32)


def swap_blocks(block):
    lane = lax.broadcasted_iota(jnp.int32, (32, 128), 1)
    upper = lane >= 64
    odd = (lane // 32) % 2 == 1
    piece = [block[32 * a : 32 * a + 32] for a in range(4)]
    for a in (0, 1):
        x, y = piece[a], piece[a + 2]
        piece[a] = jnp.where(upper, pltpu.roll(y, 64, 1), x)
        piece[a + 2] = jnp.where(upper, y, pltpu.roll(x, 64, 1))
    for a in (0, 2):
        x, y = piece[a], piece[a + 1]
        piece[a] = jnp.where(odd, pltpu.roll(y, 32, 1), x)
        piece[a + 1] = jnp.where(odd, y, pltpu.roll(x, 96, 1))
    return jnp.concatenate(piece, axis=0)


ABSENT = 1024.0


def pack_kernel(msa_ref, mask_ref, pair_ref, out_ref):
    msa = msa_ref[...].astype(F32)
    pick = spread(8, 512, lambda r, c: jnp.where(c // 64 == r, 1.0, 0.0)).astype(BF)
    present = mm_tn(mask_ref[...].astype(F32).astype(BF), pick) > 0.5
    for g in range(4):
        rows = jnp.concatenate([msa[:, 2 * g, :], msa[:, 2 * g + 1, :]], axis=1)
        out_ref[32 * g : 32 * g + 32, :] = jnp.where(
            present[:, 128 * g : 128 * g + 128], rows, ABSENT
        ).astype(BF)
    out_ref[128:192, :] = pair_ref[...].astype(F32).reshape(64, 128).astype(BF)


def weights_kernel(*refs):
    sources, (norm_out, back_out, final_out), held, scr, sems = refs[:5], refs[5:8], refs[8:13], refs[13], refs[14]
    copies = [pltpu.make_async_copy(sources[k], held[k], sems.at[k]) for k in range(5)]
    for copy in copies:
        copy.start()
    for copy in copies:
        copy.wait()
    gain_ref, offset_ref, first_ref, second_ref, final_ref = held
    norm_out[...] = jnp.concatenate(
        [
            jnp.concatenate([ref[...]] * 2, axis=1)
            for ref in (gain_ref, offset_ref, gain_ref, offset_ref) * 2
        ],
        axis=0,
    )
    for k, ref in enumerate((first_ref, second_ref)):
        wide = jnp.concatenate([ref[...].astype(F32)] * 4, axis=1)
        wide = jnp.concatenate([wide] * 4, axis=0)
        own = spread(128, 256, lambda r, c: r // 32 == c // 64)
        back_out[128 * k : 128 * k + 128, :] = jnp.where(own, wide, 0.0).astype(BF)
    scr[...] = final_ref[...].astype(F32)
    for e in range(32):
        final_out[32 * e : 32 * e + 32, :] = scr[pl.ds(e, 32, stride=32), :].astype(BF)


def averager_of():
    return spread(128, 128, lambda r, c: jnp.where(r // 64 == c // 64, 1.0 / 64, 0.0)).astype(BF)


def stage_kernel(
    n_col, a, place_ref, set_ref, norm_ref, back_ref, final_ref,
    rhs_out, left_out, leftt_out, rightt_out, grad_out, pair_out, found_out, *rest
):
    *own_out, turn_scr = rest
    place = place_ref[0]
    for b in range(n_col):
        at = pl.multiple_of(lax.bitwise_xor(place, b) * 8, 8)
        pair_out[:, pl.ds(at, 8), :] = set_ref[b, 128:192, :].astype(F32).reshape(8, 8, 128)

    gain = norm_ref[0:1, :]
    offset = norm_ref[1:2, :]
    averager = averager_of()
    x = jnp.concatenate(
        [set_ref[b, 32 * g : 32 * g + 32, :] for g in range(4) for b in range(n_col)], axis=0
    )
    mean = mm(x, averager)
    present = mean < ABSENT / 2
    varied = x.astype(F32) - mean
    inverse = lax.rsqrt(mm((varied * varied).astype(BF), averager) + 1e-05)
    normed = varied * inverse
    if own_out:
        for g in range(4):
            own_out[0][32 * g : 32 * g + 32, :] = normed[128 * g : 128 * g + 32]
            own_out[1][32 * g : 32 * g + 32, :] = inverse[128 * g : 128 * g + 32]
    normal = jnp.where(present, normed * gain + offset, 0.0).astype(BF)
    rhs_out[:, 0:128] = normal
    rhs_out[:, 128:256] = normed.astype(BF)
    here = jnp.where(present, 1.0, 0.0)
    lane = lax.broadcasted_iota(jnp.int32, (128, 128), 1)
    found = jnp.zeros((128, 128), F32)
    for g in range(4):
        found = jnp.where(lane % 32 // 2 == 4 * a + g, here[128 * g : 128 * g + 128], found)
    found_out[...] = found
    for h in range(2):
        masked = jnp.concatenate(
            [normal[128 * g : 128 * g + 128] for g in (2 * h, 2 * h + 1)], axis=1
        )
        at = slice(128 * h, 128 * h + 128)
        left_out[:, at] = mm_nt(masked, back_ref[:128, :]).astype(BF)
        both = mm_nt(back_ref[...], masked)
        leftt_out[at, :] = both[:128].astype(BF)
        turn_scr[at, :] = both[128:]

    for e in range(32):
        rightt_out[e] = turn_scr[pl.ds(e, 8, stride=32), :]

    grad = mm_nt(final_ref[...], pair_out[...].reshape(256, 128).astype(BF)).astype(BF)
    for q in range(8):
        for p in range(2):
            grad_out[128 * p : 128 * p + 128, 128 * q : 128 * q + 128] = swap_blocks(
                grad[128 * q : 128 * q + 128, 128 * p : 128 * p + 128]
            )


def part_kernel(n_row, *refs):
    stages = [refs[7 * a : 7 * a + 7] for a in range(n_row)]
    (
        normed_ref, inverse_ref, norm_ref, back_ref, first_ref, second_ref,
        emb_out, final_hbm_out, first_out, second_out, gain_out, offset_out, bias_out,
        right_scr, scaled_scr, grad_scr, outer_scr, wide_scr, linc_scr, rin_scr, rinc_scr,
        final_out, out_sem,
    ) = refs[7 * n_row :]
    gain = norm_ref[0:1, :]
    averager = averager_of()
    lane = lax.broadcasted_iota(jnp.int32, (128, 128), 1)

    found = sum(stage[6][...] for stage in stages)
    turned = pltpu.roll(found, 64, 1)
    mask = jnp.where((lane % 2 == 0) == (lane < 64), found, turned)
    mask_t = mask.T

    for e in range(32):
        right_scr[32 * e : 32 * e + 32, :] = jnp.concatenate(
            [stage[3][e] for stage in stages], axis=0
        ).astype(BF)

    bias = jnp.zeros((1, 128), F32)
    ones = jnp.ones((128, 128), BF)
    for p in range(8):
        both_on = jnp.concatenate(
            [mask_t[0:32] * mask_t[i : i + 1] for i in range(4 * p, 4 * p + 4)], axis=0
        ).astype(BF)
        counts = mm(both_on, ones)
        pair = stages[p // 2][5][4 * (p % 2) : 4 * (p % 2) + 4]
        scaled = pair.reshape(128, 128) / (counts + 0.001)
        bias = bias + jnp.sum(scaled, axis=0, keepdims=True)
        scaled_scr[128 * p : 128 * p + 128, :] = scaled.astype(BF)
    bias_out[...] = bias

    for a, stage in enumerate(stages):
        outer = mm_nt(stage[2][...], right_scr[...]).astype(BF)
        for p in range(2):
            for q in range(8):
                to = 256 * a + 128 * p
                outer_scr[128 * q : 128 * q + 128, to : to + 128] = swap_blocks(
                    outer[128 * p : 128 * p + 128, 128 * q : 128 * q + 128]
                )
    wide_scr[...] = mm(outer_scr[...], scaled_scr[...])
    for c in range(32):
        final_out[32 * c : 32 * c + 32, :] = wide_scr[pl.ds(c, 32, stride=32), :]
    final_send = pltpu.make_async_copy(final_out, final_hbm_out, out_sem)
    final_send.start()

    mask_bf = mask.astype(BF)
    share = (1.0 / (mm_tn(mask_bf, mask_bf)[0:32] + 0.001)).astype(BF)
    for i in range(32):
        a, at = i // 8, 32 * (i % 8)
        for q in range(8):
            grad_scr[32 * i : 32 * i + 32, 128 * q : 128 * q + 128] = (
                stages[a][4][at : at + 32, 128 * q : 128 * q + 128] * share[i : i + 1]
            )
    left_grad = mm(grad_scr[...], right_scr[...])
    left = jnp.concatenate([stage[1][...] for stage in stages], axis=1)
    right_grad = mm(left, grad_scr[...])

    identity = spread(128, 128, lambda r, c: jnp.where(r == c, 1.0, 0.0)).astype(BF)
    for q in range(8):
        at = slice(128 * q, 128 * q + 128)
        rin_scr[at, :] = mm_nt(identity, (right_grad[:, at] * mask).astype(BF))
    for k in range(8):
        rows = []
        for t in range(4 * k, 4 * k + 4):
            rows.append(left_grad[32 * t : 32 * t + 32] * mask_t[t : t + 1])
        at = slice(128 * k, 128 * k + 128)
        linc_scr[at, :] = jnp.concatenate(rows, axis=0).astype(BF)
        rinc_scr[at, :] = jnp.concatenate(
            [rin_scr[pl.ds(t, 32, stride=32), :] for t in range(4 * k, 4 * k + 4)], axis=0
        ).astype(BF)

    total = jnp.zeros((128, 256), F32)
    sums = jnp.zeros((128, 128), F32)
    for g in range(16):
        grads = jnp.concatenate(
            [linc_scr[64 * g : 64 * g + 64, :], rinc_scr[64 * g : 64 * g + 64, :]], axis=0
        )
        sums = sums + grads.astype(F32)
        total = total + mm(grads, stages[g // 4][0][128 * (g % 4) : 128 * (g % 4) + 128, :])

    def fold(block):
        return block[0:32, 0:64] + block[32:64, 64:128]

    first_out[...] = fold(total[0:64, 0:128])
    second_out[...] = fold(total[64:128, 0:128])
    sums = jnp.sum(sums, axis=1, keepdims=True)
    left_sum = sums[0:32] + sums[32:64]
    right_sum = sums[64:96] + sums[96:128]
    first = first_ref[...].astype(F32)
    second = second_ref[...].astype(F32)
    gain_out[...] = jnp.sum(
        first * fold(total[0:64, 128:256]) + second * fold(total[64:128, 128:256]),
        axis=0, keepdims=True,
    )
    offset_out[...] = jnp.sum(first * left_sum + second * right_sum, axis=0, keepdims=True)

    for h in range(2):
        at = slice(128 * h, 128 * h + 128)
        d_normal = mm_tn(linc_scr[at, :], back_ref[:128, :]) + mm_tn(rinc_scr[at, :], back_ref[128:, :])
        for half in range(2):
            g = 2 * h + half
            d_hat = d_normal[0:32, 128 * half : 128 * half + 128] * gain
            normed = normed_ref[32 * g : 32 * g + 32, :]
            result = inverse_ref[32 * g : 32 * g + 32, :] * (
                d_hat
                - mm(d_hat.astype(BF), averager)
                - normed * mm((d_hat * normed).astype(BF), averager)
            )
            emb_out[:, 2 * g, :] = result[:, 0:64]
            emb_out[:, 2 * g + 1, :] = result[:, 64:128]
    final_send.wait()


def vmem(count):
    return [pl.BlockSpec(memory_space=pltpu.VMEM)] * count


LIMIT = pltpu.CompilerParams(vmem_limit_bytes=32 * 1024 * 1024)


def gathered_body(
    n_row,
    n_col,
    homolog_embedding,
    presence_indicator,
    coupling_change_derivative,
    standardizer_scale,
    standardizer_shift,
    first_projection_matrix,
    second_projection_matrix,
    final_projection_matrix,
):
    shards, tokens, features = homolog_embedding.shape
    width = first_projection_matrix.shape[1]
    first_t, second_t = first_projection_matrix.T, second_projection_matrix.T
    shape = lambda *dims: jax.ShapeDtypeStruct(dims, F32)
    held = lambda *dims: pltpu.VMEM(dims, F32)
    held_bf = lambda *dims: pltpu.VMEM(dims, BF)
    hbm = pl.BlockSpec(memory_space=pltpu.HBM)
    place = lax.bitwise_xor(lax.axis_index("row"), lax.axis_index("col"))
    place = place.astype(jnp.int32).reshape(1)
    packed = pl.pallas_call(
        pack_kernel,
        out_shape=held_bf(192, 128),
        in_specs=vmem(3),
        out_specs=vmem(1)[0],
    )(homolog_embedding, presence_indicator.T, coupling_change_derivative)
    def over(axis, size, step, array):
        return lax.ppermute(array, axis, [(k, k ^ step) for k in range(size)])

    pieces = [packed] + [over("col", n_col, b, packed) for b in range(1, n_col)]
    weights = pl.pallas_call(
        weights_kernel,
        out_shape=(held(8, 128), held_bf(256, 256), held_bf(width * width, 128)),
        in_specs=[hbm] * 5,
        out_specs=tuple(vmem(3)),
        scratch_shapes=[
            pltpu.VMEM((1, features), F32),
            pltpu.VMEM((1, features), F32),
            pltpu.VMEM((width, features), BF),
            pltpu.VMEM((width, features), BF),
            pltpu.VMEM((width * width, 128), BF),
            pltpu.VMEM((width * width, 128), F32),
            pltpu.SemaphoreType.DMA((5,)),
        ],
        compiler_params=LIMIT,
    )(
        standardizer_scale.reshape(1, features),
        standardizer_shift.reshape(1, features),
        first_t,
        second_t,
        final_projection_matrix,
    )
    pieces, weights = lax.optimization_barrier((pieces, weights))
    norm, back, final_turned = weights
    own = jnp.stack(pieces)
    chip = over("row", n_row, 2, own)
    core = over("row", n_row, 1, own)

    def stage(a, block):
        outs = [
            held_bf(512, 256), held_bf(128, 256), held_bf(256, 128), held(width, 8, 128),
            held_bf(256, 1024), held(8, 32, 128), held(128, 128),
        ]
        if a == 0:
            outs += [held(128, 128)] * 2
        return pl.pallas_call(
            functools.partial(stage_kernel, n_col, a),
            out_shape=tuple(outs),
            in_specs=[pl.BlockSpec(memory_space=pltpu.SMEM)] + vmem(4),
            out_specs=tuple(vmem(len(outs))),
            scratch_shapes=[pltpu.VMEM((256, 128), F32)],
            compiler_params=LIMIT,
            cost_estimate=pl.CostEstimate(
                flops=1_000_000_000, bytes_accessed=4_000_000, transcendentals=0
            ),
        )(place, block, norm, back, final_turned)

    own_stage = stage(0, own)
    core_stage = stage(1, core)
    chip, own_stage, core_stage = lax.optimization_barrier((chip, own_stage, core_stage))
    both = over("row", n_row, 1, chip)
    stages = [own_stage, core_stage, stage(2, chip), stage(3, both)]
    own_norm = stages[0][7:]
    outs = pl.pallas_call(
        functools.partial(part_kernel, n_row),
        out_shape=(
            shape(shards, tokens, features),
            shape(width * width, 128),
            shape(width, features),
            shape(width, features),
            shape(1, features),
            shape(1, features),
            shape(1, 128),
        ),
        in_specs=vmem(7 * n_row + 6),
        out_specs=(*vmem(1), hbm, *vmem(5)),
        scratch_shapes=[
            pltpu.VMEM((1024, 128), BF),
            pltpu.VMEM((1024, 128), BF),
            pltpu.VMEM((1024, 1024), BF),
            pltpu.VMEM((1024, 1024), BF),
            pltpu.VMEM((1024, 128), F32),
            pltpu.VMEM((1024, 128), BF),
            pltpu.VMEM((1024, 128), F32),
            pltpu.VMEM((1024, 128), BF),
            pltpu.VMEM((1024, 128), F32),
            pltpu.SemaphoreType.DMA,
        ],
        compiler_params=LIMIT,
    )(*[x for s in stages for x in s[:7]], *own_norm, norm, back, first_t, second_t)
    emb, final, first, second, gain, offset, bias = outs
    return emb, final, first.T, second.T, gain.reshape(-1), offset.reshape(-1), bias.reshape(-1)


def body(n_row, n_col, *arguments):
    msa, _, pair = arguments[:3]
    width = arguments[5].shape[1]
    fits = (
        n_row == 4
        and n_col == 4
        and msa.shape == (32, 8, 64)
        and pair.shape == (8, 8, 128)
        and width == 32
    )
    if fits:
        return gathered_body(n_row, n_col, *arguments)
    return sharded_body(*arguments)


def solution(mesh):
    placed = (
        P(("grp", "col"), "row", None),
        P(("grp", "col"), "row"),
        P(("grp", "row"), "col", None),
        P(),
        P(),
        P(),
        P(),
        P(),
    )
    return jax.shard_map(
        functools.partial(body, mesh.shape["row"], mesh.shape["col"]),
        mesh=mesh,
        in_specs=placed,
        out_specs=(
            P(("grp", "col"), "row", None),
            P("grp", None),
            P("grp", None),
            P("grp", None),
            P("grp"),
            P("grp"),
            P("grp"),
        ),
        check_vma=False,
    )
```

```python
import functools

import jax
import jax.numpy as jnp
from jax import lax
from jax.experimental import pallas as pl
from jax.experimental.pallas import tpu as pltpu
from jax.sharding import PartitionSpec as P

TOKB = 2


def standardizer_parts(homolog_embedding, standardizer_scale, standardizer_shift):
    incoming_entries = homolog_embedding.astype(jnp.float32)
    center = jnp.mean(incoming_entries, axis=-1, keepdims=True)
    varied = incoming_entries - center
    variance = jnp.mean(varied * varied, axis=-1, keepdims=True)
    reciprocal_spread = lax.rsqrt(variance + 1e-05)
    standardized_entries = varied * reciprocal_spread
    standardized_bfloat = (standardized_entries * standardizer_scale + standardizer_shift).astype(
        jnp.bfloat16
    )
    return (standardized_entries, reciprocal_spread, standardized_bfloat)


def sharded_body(
    homolog_embedding,
    presence_indicator,
    coupling_change_derivative,
    standardizer_scale,
    standardizer_shift,
    first_projection_matrix,
    second_projection_matrix,
    final_projection_matrix,
):
    shard_homolog_number, residue_line_number, feature_number = homolog_embedding.shape
    tok_cols = coupling_change_derivative.shape[1]
    width = first_projection_matrix.shape[1]
    standardized_entries, reciprocal_spread, standardized_bfloat = standardizer_parts(
        homolog_embedding, standardizer_scale, standardizer_shift
    )
    mask_single_precision = presence_indicator.astype(jnp.float32)
    mask_half_precision = presence_indicator.astype(jnp.bfloat16)
    left = (
        jnp.einsum(
            "sic,cp->sip",
            standardized_bfloat,
            first_projection_matrix,
            preferred_element_type=jnp.float32,
        )
        * mask_single_precision[..., None]
    ).astype(jnp.bfloat16)
    right = (
        jnp.einsum(
            "sic,cp->sip",
            standardized_bfloat,
            second_projection_matrix,
            preferred_element_type=jnp.float32,
        )
        * mask_single_precision[..., None]
    ).astype(jnp.bfloat16)
    left_flat = left.reshape(shard_homolog_number, residue_line_number * width)
    right_flat = right.reshape(shard_homolog_number, residue_line_number * width)
    left_all, mask_left = (
        lax.all_gather(left_flat, "col", axis=0, tiled=True),
        lax.all_gather(mask_half_precision, "col", axis=0, tiled=True),
    )
    right_wide, mask_wide = (
        lax.all_gather(right_flat, "row", axis=1, tiled=True),
        lax.all_gather(mask_half_precision, "row", axis=1, tiled=True),
    )
    right_all, mask_right = (
        lax.all_to_all(right_wide, "col", split_axis=1, concat_axis=0, tiled=True),
        lax.all_to_all(mask_wide, "col", split_axis=1, concat_axis=0, tiled=True),
    )
    seq_total = left_all.shape[0]
    right_three = right_all.reshape(seq_total, tok_cols, width)
    counts = jnp.einsum("si,sj->ij", mask_left, mask_right, preferred_element_type=jnp.float32)
    scaled = coupling_change_derivative.astype(jnp.float32) / (counts + 0.001)[..., None]
    bias_part = jnp.sum(scaled, axis=(0, 1))
    scaled_bf = scaled.astype(jnp.bfloat16)
    block_rows = residue_line_number // TOKB
    right_acc = jnp.zeros((seq_total, tok_cols, width), jnp.float32)
    wout_acc = jnp.zeros(final_projection_matrix.shape, jnp.float32)
    left_pieces = []
    for block_index in range(TOKB):
        first = block_index * block_rows
        rows_bf = scaled_bf[first : first + block_rows]
        outer_grad = jnp.einsum(
            "ijz,fz->ijf", rows_bf, final_projection_matrix, preferred_element_type=jnp.float32
        ).astype(jnp.bfloat16)
        outer_grad = outer_grad.reshape(block_rows, tok_cols, width, width)
        left_block = left_all[:, first * width : (first + block_rows) * width].reshape(
            seq_total, block_rows, width
        )
        first_factor_derivative = jnp.einsum(
            "ijce,sje->sic", outer_grad, right_three, preferred_element_type=jnp.float32
        )
        right_acc = right_acc + jnp.einsum(
            "ijce,sic->sje", outer_grad, left_block, preferred_element_type=jnp.float32
        )
        outer = jnp.einsum(
            "sic,sje->ijce", left_block, right_three, preferred_element_type=jnp.float32
        ).astype(jnp.bfloat16)
        outer = outer.reshape(block_rows, tok_cols, width * width)
        wout_acc = wout_acc + jnp.einsum(
            "ijf,ijz->fz", outer, rows_bf, preferred_element_type=jnp.float32
        )
        first_factor_derivative = first_factor_derivative.reshape(seq_total, block_rows * width)
        left_pieces.append(first_factor_derivative)
    left_terms = jnp.concatenate(left_pieces, axis=1)
    left_own = lax.psum_scatter(left_terms, "col", scatter_dimension=0, tiled=True)
    right_spread = lax.all_to_all(
        right_acc.reshape(seq_total, tok_cols * width),
        "col",
        split_axis=0,
        concat_axis=1,
        tiled=True,
    )
    right_own = lax.psum_scatter(right_spread, "row", scatter_dimension=1, tiled=True)
    left_in = (
        left_own.reshape(shard_homolog_number, residue_line_number, width)
        * mask_single_precision[..., None]
    ).astype(jnp.bfloat16)
    right_in = (
        right_own.reshape(shard_homolog_number, residue_line_number, width)
        * mask_single_precision[..., None]
    ).astype(jnp.bfloat16)
    left_part = jnp.einsum(
        "sic,sip->cp", standardized_bfloat, left_in, preferred_element_type=jnp.float32
    )
    right_part = jnp.einsum(
        "sic,sip->cp", standardized_bfloat, right_in, preferred_element_type=jnp.float32
    )
    d_normal = jnp.einsum(
        "sip,cp->sic", left_in, first_projection_matrix, preferred_element_type=jnp.float32
    ) + jnp.einsum(
        "sip,cp->sic", right_in, second_projection_matrix, preferred_element_type=jnp.float32
    )
    gain_part = jnp.sum(d_normal * standardized_entries, axis=(0, 1))
    beta_part = jnp.sum(d_normal, axis=(0, 1))
    standardized_derivative = d_normal * standardizer_scale
    embedding_derivative = reciprocal_spread * (
        standardized_derivative
        - jnp.mean(standardized_derivative, axis=-1, keepdims=True)
        - standardized_entries
        * jnp.mean(standardized_derivative * standardized_entries, axis=-1, keepdims=True)
    )
    (
        final_matrix_derivative,
        first_matrix_derivative,
        second_matrix_derivative,
        scale_factor_derivative,
        shift_term_derivative,
        shift_derivative,
    ) = lax.psum((wout_acc, left_part, right_part, gain_part, beta_part, bias_part), ("row", "col"))
    return (
        embedding_derivative,
        final_matrix_derivative,
        first_matrix_derivative,
        second_matrix_derivative,
        scale_factor_derivative,
        shift_term_derivative,
        shift_derivative,
    )


BF = jnp.bfloat16
F32 = jnp.float32


def spread(rows, cols, rule):
    r = lax.broadcasted_iota(jnp.int32, (rows, cols), 0)
    c = lax.broadcasted_iota(jnp.int32, (rows, cols), 1)
    return rule(r, c)


def mm(a, b):
    return jnp.dot(a, b, preferred_element_type=F32)


def mm_nt(a, b):
    return lax.dot_general(a, b, (((1,), (1,)), ((), ())), preferred_element_type=F32)


def mm_tn(a, b):
    return lax.dot_general(a, b, (((0,), (0,)), ((), ())), preferred_element_type=F32)


def swap_blocks(block):
    lane = lax.broadcasted_iota(jnp.int32, (32, 128), 1)
    upper = lane >= 64
    odd = (lane // 32) % 2 == 1
    piece = [block[32 * a : 32 * a + 32] for a in range(4)]
    for a in (0, 1):
        x, y = piece[a], piece[a + 2]
        piece[a] = jnp.where(upper, pltpu.roll(y, 64, 1), x)
        piece[a + 2] = jnp.where(upper, y, pltpu.roll(x, 64, 1))
    for a in (0, 2):
        x, y = piece[a], piece[a + 1]
        piece[a] = jnp.where(odd, pltpu.roll(y, 32, 1), x)
        piece[a + 1] = jnp.where(odd, y, pltpu.roll(x, 96, 1))
    return jnp.concatenate(piece, axis=0)


ABSENT = 1024.0


def pack_kernel(msa_ref, mask_ref, pair_ref, out_ref):
    msa = msa_ref[...].astype(F32)
    pick = spread(8, 512, lambda r, c: jnp.where(c // 64 == r, 1.0, 0.0)).astype(BF)
    present = mm_tn(mask_ref[...].astype(F32).astype(BF), pick) > 0.5
    for g in range(4):
        rows = jnp.concatenate([msa[:, 2 * g, :], msa[:, 2 * g + 1, :]], axis=1)
        out_ref[32 * g : 32 * g + 32, :] = jnp.where(
            present[:, 128 * g : 128 * g + 128], rows, ABSENT
        ).astype(BF)
    out_ref[128:192, :] = pair_ref[...].astype(F32).reshape(64, 128).astype(BF)


def weights_kernel(*refs):
    sources, (norm_out, back_out, final_out), held, scr, sems = refs[:5], refs[5:8], refs[8:13], refs[13], refs[14]
    copies = [pltpu.make_async_copy(sources[k], held[k], sems.at[k]) for k in range(5)]
    for copy in copies:
        copy.start()
    for copy in copies:
        copy.wait()
    gain_ref, offset_ref, first_ref, second_ref, final_ref = held
    norm_out[...] = jnp.concatenate(
        [
            jnp.concatenate([ref[...]] * 2, axis=1)
            for ref in (gain_ref, offset_ref, gain_ref, offset_ref) * 2
        ],
        axis=0,
    )
    for k, ref in enumerate((first_ref, second_ref)):
        wide = jnp.concatenate([ref[...].astype(F32)] * 4, axis=1)
        wide = jnp.concatenate([wide] * 4, axis=0)
        own = spread(128, 256, lambda r, c: r // 32 == c // 64)
        back_out[128 * k : 128 * k + 128, :] = jnp.where(own, wide, 0.0).astype(BF)
    scr[...] = final_ref[...].astype(F32)
    for e in range(32):
        final_out[32 * e : 32 * e + 32, :] = scr[pl.ds(e, 32, stride=32), :].astype(BF)


def averager_of():
    return spread(128, 128, lambda r, c: jnp.where(r // 64 == c // 64, 1.0 / 64, 0.0)).astype(BF)


def stage_kernel(
    n_col, a, place_ref, set_ref, norm_ref, back_ref, final_ref,
    rhs_out, left_out, leftt_out, rightt_out, grad_out, pair_out, found_out, *rest
):
    *own_out, turn_scr = rest
    for b in range(n_col):
        source = lax.rem(place_ref[1] + n_col - b, n_col)
        at = pl.multiple_of(lax.bitwise_xor(place_ref[0], source) * 8, 8)
        pair_out[:, pl.ds(at, 8), :] = set_ref[b, 128:192, :].astype(F32).reshape(8, 8, 128)

    gain = norm_ref[0:1, :]
    offset = norm_ref[1:2, :]
    averager = averager_of()
    x = jnp.concatenate(
        [set_ref[b, 32 * g : 32 * g + 32, :] for g in range(4) for b in range(n_col)], axis=0
    )
    mean = mm(x, averager)
    present = mean < ABSENT / 2
    varied = x.astype(F32) - mean
    inverse = lax.rsqrt(mm((varied * varied).astype(BF), averager) + 1e-05)
    normed = varied * inverse
    if own_out:
        for g in range(4):
            own_out[0][32 * g : 32 * g + 32, :] = normed[128 * g : 128 * g + 32]
            own_out[1][32 * g : 32 * g + 32, :] = inverse[128 * g : 128 * g + 32]
    normal = jnp.where(present, normed * gain + offset, 0.0).astype(BF)
    rhs_out[:, 0:128] = normal
    rhs_out[:, 128:256] = normed.astype(BF)
    here = jnp.where(present, 1.0, 0.0)
    lane = lax.broadcasted_iota(jnp.int32, (128, 128), 1)
    found = jnp.zeros((128, 128), F32)
    for g in range(4):
        found = jnp.where(lane % 32 // 2 == 4 * a + g, here[128 * g : 128 * g + 128], found)
    found_out[...] = found
    for h in range(2):
        masked = jnp.concatenate(
            [normal[128 * g : 128 * g + 128] for g in (2 * h, 2 * h + 1)], axis=1
        )
        at = slice(128 * h, 128 * h + 128)
        left_out[:, at] = mm_nt(masked, back_ref[:128, :]).astype(BF)
        both = mm_nt(back_ref[...], masked)
        leftt_out[at, :] = both[:128].astype(BF)
        turn_scr[at, :] = both[128:]

    for e in range(32):
        rightt_out[e] = turn_scr[pl.ds(e, 8, stride=32), :]

    grad = mm_nt(final_ref[...], pair_out[...].reshape(256, 128).astype(BF)).astype(BF)
    for q in range(8):
        for p in range(2):
            grad_out[128 * p : 128 * p + 128, 128 * q : 128 * q + 128] = swap_blocks(
                grad[128 * q : 128 * q + 128, 128 * p : 128 * p + 128]
            )


def part_kernel(n_row, *refs):
    stages = [refs[7 * a : 7 * a + 7] for a in range(n_row)]
    (
        normed_ref, inverse_ref, norm_ref, back_ref, first_ref, second_ref,
        emb_out, final_hbm_out, first_out, second_out, gain_out, offset_out, bias_out,
        right_scr, scaled_scr, grad_scr, outer_scr, wide_scr, linc_scr, rin_scr, rinc_scr,
        final_out, out_sem,
    ) = refs[7 * n_row :]
    gain = norm_ref[0:1, :]
    averager = averager_of()
    lane = lax.broadcasted_iota(jnp.int32, (128, 128), 1)

    found = sum(stage[6][...] for stage in stages)
    turned = pltpu.roll(found, 64, 1)
    mask = jnp.where((lane % 2 == 0) == (lane < 64), found, turned)
    mask_t = mask.T

    for e in range(32):
        right_scr[32 * e : 32 * e + 32, :] = jnp.concatenate(
            [stage[3][e] for stage in stages], axis=0
        ).astype(BF)

    bias = jnp.zeros((1, 128), F32)
    ones = jnp.ones((128, 128), BF)
    for p in range(8):
        both_on = jnp.concatenate(
            [mask_t[0:32] * mask_t[i : i + 1] for i in range(4 * p, 4 * p + 4)], axis=0
        ).astype(BF)
        counts = mm(both_on, ones)
        pair = stages[p // 2][5][4 * (p % 2) : 4 * (p % 2) + 4]
        scaled = pair.reshape(128, 128) / (counts + 0.001)
        bias = bias + jnp.sum(scaled, axis=0, keepdims=True)
        scaled_scr[128 * p : 128 * p + 128, :] = scaled.astype(BF)
    bias_out[...] = bias

    for a, stage in enumerate(stages):
        outer = mm_nt(stage[2][...], right_scr[...]).astype(BF)
        for p in range(2):
            for q in range(8):
                to = 256 * a + 128 * p
                outer_scr[128 * q : 128 * q + 128, to : to + 128] = swap_blocks(
                    outer[128 * p : 128 * p + 128, 128 * q : 128 * q + 128]
                )
    wide_scr[...] = mm(outer_scr[...], scaled_scr[...])
    for c in range(32):
        final_out[32 * c : 32 * c + 32, :] = wide_scr[pl.ds(c, 32, stride=32), :]
    final_send = pltpu.make_async_copy(final_out, final_hbm_out, out_sem)
    final_send.start()

    mask_bf = mask.astype(BF)
    share = (1.0 / (mm_tn(mask_bf, mask_bf)[0:32] + 0.001)).astype(BF)
    for i in range(32):
        a, at = i // 8, 32 * (i % 8)
        for q in range(8):
            grad_scr[32 * i : 32 * i + 32, 128 * q : 128 * q + 128] = (
                stages[a][4][at : at + 32, 128 * q : 128 * q + 128] * share[i : i + 1]
            )
    left_grad = mm(grad_scr[...], right_scr[...])
    left = jnp.concatenate([stage[1][...] for stage in stages], axis=1)
    right_grad = mm(left, grad_scr[...])

    identity = spread(128, 128, lambda r, c: jnp.where(r == c, 1.0, 0.0)).astype(BF)
    for q in range(8):
        at = slice(128 * q, 128 * q + 128)
        rin_scr[at, :] = mm_nt(identity, (right_grad[:, at] * mask).astype(BF))
    for k in range(8):
        rows = []
        for t in range(4 * k, 4 * k + 4):
            rows.append(left_grad[32 * t : 32 * t + 32] * mask_t[t : t + 1])
        at = slice(128 * k, 128 * k + 128)
        linc_scr[at, :] = jnp.concatenate(rows, axis=0).astype(BF)
        rinc_scr[at, :] = jnp.concatenate(
            [rin_scr[pl.ds(t, 32, stride=32), :] for t in range(4 * k, 4 * k + 4)], axis=0
        ).astype(BF)

    total = jnp.zeros((128, 256), F32)
    sums = jnp.zeros((128, 128), F32)
    for g in range(16):
        grads = jnp.concatenate(
            [linc_scr[64 * g : 64 * g + 64, :], rinc_scr[64 * g : 64 * g + 64, :]], axis=0
        )
        sums = sums + grads.astype(F32)
        total = total + mm(grads, stages[g // 4][0][128 * (g % 4) : 128 * (g % 4) + 128, :])

    def fold(block):
        return block[0:32, 0:64] + block[32:64, 64:128]

    first_out[...] = fold(total[0:64, 0:128])
    second_out[...] = fold(total[64:128, 0:128])
    sums = jnp.sum(sums, axis=1, keepdims=True)
    left_sum = sums[0:32] + sums[32:64]
    right_sum = sums[64:96] + sums[96:128]
    first = first_ref[...].astype(F32)
    second = second_ref[...].astype(F32)
    gain_out[...] = jnp.sum(
        first * fold(total[0:64, 128:256]) + second * fold(total[64:128, 128:256]),
        axis=0, keepdims=True,
    )
    offset_out[...] = jnp.sum(first * left_sum + second * right_sum, axis=0, keepdims=True)

    for h in range(2):
        at = slice(128 * h, 128 * h + 128)
        d_normal = mm_tn(linc_scr[at, :], back_ref[:128, :]) + mm_tn(rinc_scr[at, :], back_ref[128:, :])
        for half in range(2):
            g = 2 * h + half
            d_hat = d_normal[0:32, 128 * half : 128 * half + 128] * gain
            normed = normed_ref[32 * g : 32 * g + 32, :]
            result = inverse_ref[32 * g : 32 * g + 32, :] * (
                d_hat
                - mm(d_hat.astype(BF), averager)
                - normed * mm((d_hat * normed).astype(BF), averager)
            )
            emb_out[:, 2 * g, :] = result[:, 0:64]
            emb_out[:, 2 * g + 1, :] = result[:, 64:128]
    final_send.wait()


def vmem(count):
    return [pl.BlockSpec(memory_space=pltpu.VMEM)] * count


LIMIT = pltpu.CompilerParams(vmem_limit_bytes=32 * 1024 * 1024)


def gathered_body(
    n_row,
    n_col,
    homolog_embedding,
    presence_indicator,
    coupling_change_derivative,
    standardizer_scale,
    standardizer_shift,
    first_projection_matrix,
    second_projection_matrix,
    final_projection_matrix,
):
    shards, tokens, features = homolog_embedding.shape
    width = first_projection_matrix.shape[1]
    first_t, second_t = first_projection_matrix.T, second_projection_matrix.T
    shape = lambda *dims: jax.ShapeDtypeStruct(dims, F32)
    held = lambda *dims: pltpu.VMEM(dims, F32)
    held_bf = lambda *dims: pltpu.VMEM(dims, BF)
    hbm = pl.BlockSpec(memory_space=pltpu.HBM)
    place = jnp.stack([lax.axis_index("row"), lax.axis_index("col")]).astype(jnp.int32)
    packed = pl.pallas_call(
        pack_kernel,
        out_shape=held_bf(192, 128),
        in_specs=vmem(3),
        out_specs=vmem(1)[0],
    )(homolog_embedding, presence_indicator.T, coupling_change_derivative)
    def over(axis, size, step, array):
        return lax.ppermute(array, axis, [(k, k ^ step) for k in range(size)])

    pieces = [
        lax.ppermute(packed, "col", [(k, (k + b) % n_col) for k in range(n_col)])
        for b in reversed(range(1, n_col))
    ]
    pieces = [packed] + pieces[::-1]
    weights = pl.pallas_call(
        weights_kernel,
        out_shape=(held(8, 128), held_bf(256, 256), held_bf(width * width, 128)),
        in_specs=[hbm] * 5,
        out_specs=tuple(vmem(3)),
        scratch_shapes=[
            pltpu.VMEM((1, features), F32),
            pltpu.VMEM((1, features), F32),
            pltpu.VMEM((width, features), BF),
            pltpu.VMEM((width, features), BF),
            pltpu.VMEM((width * width, 128), BF),
            pltpu.VMEM((width * width, 128), F32),
            pltpu.SemaphoreType.DMA((5,)),
        ],
        compiler_params=LIMIT,
    )(
        standardizer_scale.reshape(1, features),
        standardizer_shift.reshape(1, features),
        first_t,
        second_t,
        final_projection_matrix,
    )
    pieces, weights = lax.optimization_barrier((pieces, weights))
    norm, back, final_turned = weights
    own = jnp.stack(pieces)
    chip = over("row", n_row, 2, own)
    core = over("row", n_row, 1, own)

    def stage(a, block):
        outs = [
            held_bf(512, 256), held_bf(128, 256), held_bf(256, 128), held(width, 8, 128),
            held_bf(256, 1024), held(8, 32, 128), held(128, 128),
        ]
        if a == 0:
            outs += [held(128, 128)] * 2
        return pl.pallas_call(
            functools.partial(stage_kernel, n_col, a),
            out_shape=tuple(outs),
            in_specs=[pl.BlockSpec(memory_space=pltpu.SMEM)] + vmem(4),
            out_specs=tuple(vmem(len(outs))),
            scratch_shapes=[pltpu.VMEM((256, 128), F32)],
            compiler_params=LIMIT,
            cost_estimate=pl.CostEstimate(
                flops=1_000_000_000, bytes_accessed=4_000_000, transcendentals=0
            ),
        )(place, block, norm, back, final_turned)

    own_stage = stage(0, own)
    core_stage = stage(1, core)
    chip, own_stage = lax.optimization_barrier((chip, own_stage))
    both = over("row", n_row, 1, chip)
    stages = [own_stage, core_stage, stage(2, chip), stage(3, both)]
    own_norm = stages[0][7:]
    outs = pl.pallas_call(
        functools.partial(part_kernel, n_row),
        out_shape=(
            shape(shards, tokens, features),
            shape(width * width, 128),
            shape(width, features),
            shape(width, features),
            shape(1, features),
            shape(1, features),
            shape(1, 128),
        ),
        in_specs=vmem(7 * n_row + 6),
        out_specs=(*vmem(1), hbm, *vmem(5)),
        scratch_shapes=[
            pltpu.VMEM((1024, 128), BF),
            pltpu.VMEM((1024, 128), BF),
            pltpu.VMEM((1024, 1024), BF),
            pltpu.VMEM((1024, 1024), BF),
            pltpu.VMEM((1024, 128), F32),
            pltpu.VMEM((1024, 128), BF),
            pltpu.VMEM((1024, 128), F32),
            pltpu.VMEM((1024, 128), BF),
            pltpu.VMEM((1024, 128), F32),
            pltpu.SemaphoreType.DMA,
        ],
        compiler_params=LIMIT,
    )(*[x for s in stages for x in s[:7]], *own_norm, norm, back, first_t, second_t)
    emb, final, first, second, gain, offset, bias = outs
    return emb, final, first.T, second.T, gain.reshape(-1), offset.reshape(-1), bias.reshape(-1)


def body(n_row, n_col, *arguments):
    msa, _, pair = arguments[:3]
    width = arguments[5].shape[1]
    fits = (
        n_row == 4
        and n_col == 4
        and msa.shape == (32, 8, 64)
        and pair.shape == (8, 8, 128)
        and width == 32
    )
    if fits:
        return gathered_body(n_row, n_col, *arguments)
    return sharded_body(*arguments)


def solution(mesh):
    placed = (
        P(("grp", "col"), "row", None),
        P(("grp", "col"), "row"),
        P(("grp", "row"), "col", None),
        P(),
        P(),
        P(),
        P(),
        P(),
    )
    return jax.shard_map(
        functools.partial(body, mesh.shape["row"], mesh.shape["col"]),
        mesh=mesh,
        in_specs=placed,
        out_specs=(
            P(("grp", "col"), "row", None),
            P("grp", None),
            P("grp", None),
            P("grp", None),
            P("grp"),
            P("grp"),
            P("grp"),
        ),
        check_vma=False,
    )
```

```python
import functools

import jax
import jax.numpy as jnp
from jax import lax
from jax.experimental import pallas as pl
from jax.experimental.pallas import tpu as pltpu
from jax.sharding import PartitionSpec as P

TOKB = 2


def standardizer_parts(homolog_embedding, standardizer_scale, standardizer_shift):
    incoming_entries = homolog_embedding.astype(jnp.float32)
    center = jnp.mean(incoming_entries, axis=-1, keepdims=True)
    varied = incoming_entries - center
    variance = jnp.mean(varied * varied, axis=-1, keepdims=True)
    reciprocal_spread = lax.rsqrt(variance + 1e-05)
    standardized_entries = varied * reciprocal_spread
    standardized_bfloat = (standardized_entries * standardizer_scale + standardizer_shift).astype(
        jnp.bfloat16
    )
    return (standardized_entries, reciprocal_spread, standardized_bfloat)


def sharded_body(
    homolog_embedding,
    presence_indicator,
    coupling_change_derivative,
    standardizer_scale,
    standardizer_shift,
    first_projection_matrix,
    second_projection_matrix,
    final_projection_matrix,
):
    shard_homolog_number, residue_line_number, feature_number = homolog_embedding.shape
    tok_cols = coupling_change_derivative.shape[1]
    width = first_projection_matrix.shape[1]
    standardized_entries, reciprocal_spread, standardized_bfloat = standardizer_parts(
        homolog_embedding, standardizer_scale, standardizer_shift
    )
    mask_single_precision = presence_indicator.astype(jnp.float32)
    mask_half_precision = presence_indicator.astype(jnp.bfloat16)
    left = (
        jnp.einsum(
            "sic,cp->sip",
            standardized_bfloat,
            first_projection_matrix,
            preferred_element_type=jnp.float32,
        )
        * mask_single_precision[..., None]
    ).astype(jnp.bfloat16)
    right = (
        jnp.einsum(
            "sic,cp->sip",
            standardized_bfloat,
            second_projection_matrix,
            preferred_element_type=jnp.float32,
        )
        * mask_single_precision[..., None]
    ).astype(jnp.bfloat16)
    left_flat = left.reshape(shard_homolog_number, residue_line_number * width)
    right_flat = right.reshape(shard_homolog_number, residue_line_number * width)
    left_all, mask_left = (
        lax.all_gather(left_flat, "col", axis=0, tiled=True),
        lax.all_gather(mask_half_precision, "col", axis=0, tiled=True),
    )
    right_wide, mask_wide = (
        lax.all_gather(right_flat, "row", axis=1, tiled=True),
        lax.all_gather(mask_half_precision, "row", axis=1, tiled=True),
    )
    right_all, mask_right = (
        lax.all_to_all(right_wide, "col", split_axis=1, concat_axis=0, tiled=True),
        lax.all_to_all(mask_wide, "col", split_axis=1, concat_axis=0, tiled=True),
    )
    seq_total = left_all.shape[0]
    right_three = right_all.reshape(seq_total, tok_cols, width)
    counts = jnp.einsum("si,sj->ij", mask_left, mask_right, preferred_element_type=jnp.float32)
    scaled = coupling_change_derivative.astype(jnp.float32) / (counts + 0.001)[..., None]
    bias_part = jnp.sum(scaled, axis=(0, 1))
    scaled_bf = scaled.astype(jnp.bfloat16)
    block_rows = residue_line_number // TOKB
    right_acc = jnp.zeros((seq_total, tok_cols, width), jnp.float32)
    wout_acc = jnp.zeros(final_projection_matrix.shape, jnp.float32)
    left_pieces = []
    for block_index in range(TOKB):
        first = block_index * block_rows
        rows_bf = scaled_bf[first : first + block_rows]
        outer_grad = jnp.einsum(
            "ijz,fz->ijf", rows_bf, final_projection_matrix, preferred_element_type=jnp.float32
        ).astype(jnp.bfloat16)
        outer_grad = outer_grad.reshape(block_rows, tok_cols, width, width)
        left_block = left_all[:, first * width : (first + block_rows) * width].reshape(
            seq_total, block_rows, width
        )
        first_factor_derivative = jnp.einsum(
            "ijce,sje->sic", outer_grad, right_three, preferred_element_type=jnp.float32
        )
        right_acc = right_acc + jnp.einsum(
            "ijce,sic->sje", outer_grad, left_block, preferred_element_type=jnp.float32
        )
        outer = jnp.einsum(
            "sic,sje->ijce", left_block, right_three, preferred_element_type=jnp.float32
        ).astype(jnp.bfloat16)
        outer = outer.reshape(block_rows, tok_cols, width * width)
        wout_acc = wout_acc + jnp.einsum(
            "ijf,ijz->fz", outer, rows_bf, preferred_element_type=jnp.float32
        )
        first_factor_derivative = first_factor_derivative.reshape(seq_total, block_rows * width)
        left_pieces.append(first_factor_derivative)
    left_terms = jnp.concatenate(left_pieces, axis=1)
    left_own = lax.psum_scatter(left_terms, "col", scatter_dimension=0, tiled=True)
    right_spread = lax.all_to_all(
        right_acc.reshape(seq_total, tok_cols * width),
        "col",
        split_axis=0,
        concat_axis=1,
        tiled=True,
    )
    right_own = lax.psum_scatter(right_spread, "row", scatter_dimension=1, tiled=True)
    left_in = (
        left_own.reshape(shard_homolog_number, residue_line_number, width)
        * mask_single_precision[..., None]
    ).astype(jnp.bfloat16)
    right_in = (
        right_own.reshape(shard_homolog_number, residue_line_number, width)
        * mask_single_precision[..., None]
    ).astype(jnp.bfloat16)
    left_part = jnp.einsum(
        "sic,sip->cp", standardized_bfloat, left_in, preferred_element_type=jnp.float32
    )
    right_part = jnp.einsum(
        "sic,sip->cp", standardized_bfloat, right_in, preferred_element_type=jnp.float32
    )
    d_normal = jnp.einsum(
        "sip,cp->sic", left_in, first_projection_matrix, preferred_element_type=jnp.float32
    ) + jnp.einsum(
        "sip,cp->sic", right_in, second_projection_matrix, preferred_element_type=jnp.float32
    )
    gain_part = jnp.sum(d_normal * standardized_entries, axis=(0, 1))
    beta_part = jnp.sum(d_normal, axis=(0, 1))
    standardized_derivative = d_normal * standardizer_scale
    embedding_derivative = reciprocal_spread * (
        standardized_derivative
        - jnp.mean(standardized_derivative, axis=-1, keepdims=True)
        - standardized_entries
        * jnp.mean(standardized_derivative * standardized_entries, axis=-1, keepdims=True)
    )
    (
        final_matrix_derivative,
        first_matrix_derivative,
        second_matrix_derivative,
        scale_factor_derivative,
        shift_term_derivative,
        shift_derivative,
    ) = lax.psum((wout_acc, left_part, right_part, gain_part, beta_part, bias_part), ("row", "col"))
    return (
        embedding_derivative,
        final_matrix_derivative,
        first_matrix_derivative,
        second_matrix_derivative,
        scale_factor_derivative,
        shift_term_derivative,
        shift_derivative,
    )


BF = jnp.bfloat16
F32 = jnp.float32


def spread(rows, cols, rule):
    r = lax.broadcasted_iota(jnp.int32, (rows, cols), 0)
    c = lax.broadcasted_iota(jnp.int32, (rows, cols), 1)
    return rule(r, c)


def mm(a, b):
    return jnp.dot(a, b, preferred_element_type=F32)


def mm_nt(a, b):
    return lax.dot_general(a, b, (((1,), (1,)), ((), ())), preferred_element_type=F32)


def mm_tn(a, b):
    return lax.dot_general(a, b, (((0,), (0,)), ((), ())), preferred_element_type=F32)


def swap_blocks(block):
    lane = lax.broadcasted_iota(jnp.int32, (32, 128), 1)
    upper = lane >= 64
    odd = (lane // 32) % 2 == 1
    piece = [block[32 * a : 32 * a + 32] for a in range(4)]
    for a in (0, 1):
        x, y = piece[a], piece[a + 2]
        piece[a] = jnp.where(upper, pltpu.roll(y, 64, 1), x)
        piece[a + 2] = jnp.where(upper, y, pltpu.roll(x, 64, 1))
    for a in (0, 2):
        x, y = piece[a], piece[a + 1]
        piece[a] = jnp.where(odd, pltpu.roll(y, 32, 1), x)
        piece[a + 1] = jnp.where(odd, y, pltpu.roll(x, 96, 1))
    return jnp.concatenate(piece, axis=0)


ABSENT = 1024.0


def pack_kernel(msa_ref, mask_ref, pair_ref, out_ref):
    msa = msa_ref[...].astype(F32)
    pick = spread(8, 512, lambda r, c: jnp.where(c // 64 == r, 1.0, 0.0)).astype(BF)
    present = mm_tn(mask_ref[...].astype(F32).astype(BF), pick) > 0.5
    for g in range(4):
        rows = jnp.concatenate([msa[:, 2 * g, :], msa[:, 2 * g + 1, :]], axis=1)
        out_ref[32 * g : 32 * g + 32, :] = jnp.where(
            present[:, 128 * g : 128 * g + 128], rows, ABSENT
        ).astype(BF)
    out_ref[128:192, :] = pair_ref[...].astype(F32).reshape(64, 128).astype(BF)


def weights_kernel(*refs):
    sources, (norm_out, back_out, final_out), held, scr, sems = refs[:5], refs[5:8], refs[8:13], refs[13], refs[14]
    copies = [pltpu.make_async_copy(sources[k], held[k], sems.at[k]) for k in range(5)]
    for copy in copies:
        copy.start()
    for copy in copies:
        copy.wait()
    gain_ref, offset_ref, first_ref, second_ref, final_ref = held
    norm_out[...] = jnp.concatenate(
        [
            jnp.concatenate([ref[...]] * 2, axis=1)
            for ref in (gain_ref, offset_ref, gain_ref, offset_ref) * 2
        ],
        axis=0,
    )
    for k, ref in enumerate((first_ref, second_ref)):
        wide = jnp.concatenate([ref[...].astype(F32)] * 4, axis=1)
        wide = jnp.concatenate([wide] * 4, axis=0)
        own = spread(128, 256, lambda r, c: r // 32 == c // 64)
        back_out[128 * k : 128 * k + 128, :] = jnp.where(own, wide, 0.0).astype(BF)
    scr[...] = final_ref[...].astype(F32)
    for e in range(32):
        final_out[32 * e : 32 * e + 32, :] = scr[pl.ds(e, 32, stride=32), :].astype(BF)


def averager_of():
    return spread(128, 128, lambda r, c: jnp.where(r // 64 == c // 64, 1.0 / 64, 0.0)).astype(BF)


def stage_kernel(
    n_col, a, place_ref, set_ref, norm_ref, back_ref, final_ref,
    rhs_out, left_out, leftt_out, rightt_out, grad_out, pair_out, found_out, *rest
):
    *own_out, turn_scr = rest
    for b in range(n_col):
        at = pl.multiple_of(lax.bitwise_xor(place_ref[0], b) * 8, 8)
        pair_out[:, pl.ds(at, 8), :] = set_ref[b, 128:192, :].astype(F32).reshape(8, 8, 128)

    gain = norm_ref[0:1, :]
    offset = norm_ref[1:2, :]
    averager = averager_of()
    x = jnp.concatenate(
        [set_ref[b, 32 * g : 32 * g + 32, :] for g in range(4) for b in range(n_col)], axis=0
    )
    mean = mm(x, averager)
    present = mean < ABSENT / 2
    varied = x.astype(F32) - mean
    inverse = lax.rsqrt(mm((varied * varied).astype(BF), averager) + 1e-05)
    normed = varied * inverse
    if own_out:
        for g in range(4):
            own_out[0][32 * g : 32 * g + 32, :] = normed[128 * g : 128 * g + 32]
            own_out[1][32 * g : 32 * g + 32, :] = inverse[128 * g : 128 * g + 32]
    normal = jnp.where(present, normed * gain + offset, 0.0).astype(BF)
    rhs_out[:, 0:128] = normal
    rhs_out[:, 128:256] = normed.astype(BF)
    here = jnp.where(present, 1.0, 0.0)
    lane = lax.broadcasted_iota(jnp.int32, (128, 128), 1)
    found = jnp.zeros((128, 128), F32)
    for g in range(4):
        found = jnp.where(lane % 32 // 2 == 4 * a + g, here[128 * g : 128 * g + 128], found)
    found_out[...] = found
    for h in range(2):
        masked = jnp.concatenate(
            [normal[128 * g : 128 * g + 128] for g in (2 * h, 2 * h + 1)], axis=1
        )
        at = slice(128 * h, 128 * h + 128)
        left_out[:, at] = mm_nt(masked, back_ref[:128, :]).astype(BF)
        both = mm_nt(back_ref[...], masked)
        leftt_out[at, :] = both[:128].astype(BF)
        turn_scr[at, :] = both[128:]

    for e in range(32):
        rightt_out[e] = turn_scr[pl.ds(e, 8, stride=32), :]

    grad = mm_nt(final_ref[...], pair_out[...].reshape(256, 128).astype(BF)).astype(BF)
    for q in range(8):
        for p in range(2):
            grad_out[128 * p : 128 * p + 128, 128 * q : 128 * q + 128] = swap_blocks(
                grad[128 * q : 128 * q + 128, 128 * p : 128 * p + 128]
            )


def part_kernel(n_row, *refs):
    stages = [refs[7 * a : 7 * a + 7] for a in range(n_row)]
    (
        normed_ref, inverse_ref, norm_ref, back_ref, first_ref, second_ref,
        emb_out, final_hbm_out, first_out, second_out, gain_out, offset_out, bias_out,
        right_scr, scaled_scr, grad_scr, outer_scr, wide_scr, linc_scr, rin_scr, rinc_scr,
        final_out, out_sem,
    ) = refs[7 * n_row :]
    gain = norm_ref[0:1, :]
    averager = averager_of()
    lane = lax.broadcasted_iota(jnp.int32, (128, 128), 1)

    found = sum(stage[6][...] for stage in stages)
    turned = pltpu.roll(found, 64, 1)
    mask = jnp.where((lane % 2 == 0) == (lane < 64), found, turned)
    mask_t = mask.T

    for e in range(32):
        right_scr[32 * e : 32 * e + 32, :] = jnp.concatenate(
            [stage[3][e] for stage in stages], axis=0
        ).astype(BF)

    bias = jnp.zeros((1, 128), F32)
    ones = jnp.ones((128, 128), BF)
    for p in range(8):
        both_on = jnp.concatenate(
            [mask_t[0:32] * mask_t[i : i + 1] for i in range(4 * p, 4 * p + 4)], axis=0
        ).astype(BF)
        counts = mm(both_on, ones)
        pair = stages[p // 2][5][4 * (p % 2) : 4 * (p % 2) + 4]
        scaled = pair.reshape(128, 128) / (counts + 0.001)
        bias = bias + jnp.sum(scaled, axis=0, keepdims=True)
        scaled_scr[128 * p : 128 * p + 128, :] = scaled.astype(BF)
    bias_out[...] = bias

    for a, stage in enumerate(stages):
        outer = mm_nt(stage[2][...], right_scr[...]).astype(BF)
        for p in range(2):
            for q in range(8):
                to = 256 * a + 128 * p
                outer_scr[128 * q : 128 * q + 128, to : to + 128] = swap_blocks(
                    outer[128 * p : 128 * p + 128, 128 * q : 128 * q + 128]
                )
    wide_scr[...] = mm(outer_scr[...], scaled_scr[...])
    for c in range(32):
        final_out[32 * c : 32 * c + 32, :] = wide_scr[pl.ds(c, 32, stride=32), :]
    final_send = pltpu.make_async_copy(final_out, final_hbm_out, out_sem)
    final_send.start()

    mask_bf = mask.astype(BF)
    share = (1.0 / (mm_tn(mask_bf, mask_bf)[0:32] + 0.001)).astype(BF)
    for i in range(32):
        a, at = i // 8, 32 * (i % 8)
        for q in range(8):
            grad_scr[32 * i : 32 * i + 32, 128 * q : 128 * q + 128] = (
                stages[a][4][at : at + 32, 128 * q : 128 * q + 128] * share[i : i + 1]
            )
    left_grad = mm(grad_scr[...], right_scr[...])
    left = jnp.concatenate([stage[1][...] for stage in stages], axis=1)
    right_grad = mm(left, grad_scr[...])

    identity = spread(128, 128, lambda r, c: jnp.where(r == c, 1.0, 0.0)).astype(BF)
    for q in range(8):
        at = slice(128 * q, 128 * q + 128)
        rin_scr[at, :] = mm_nt(identity, (right_grad[:, at] * mask).astype(BF))
    for k in range(8):
        rows = []
        for t in range(4 * k, 4 * k + 4):
            rows.append(left_grad[32 * t : 32 * t + 32] * mask_t[t : t + 1])
        at = slice(128 * k, 128 * k + 128)
        linc_scr[at, :] = jnp.concatenate(rows, axis=0).astype(BF)
        rinc_scr[at, :] = jnp.concatenate(
            [rin_scr[pl.ds(t, 32, stride=32), :] for t in range(4 * k, 4 * k + 4)], axis=0
        ).astype(BF)

    total = jnp.zeros((128, 256), F32)
    sums = jnp.zeros((128, 128), F32)
    for g in range(16):
        grads = jnp.concatenate(
            [linc_scr[64 * g : 64 * g + 64, :], rinc_scr[64 * g : 64 * g + 64, :]], axis=0
        )
        sums = sums + grads.astype(F32)
        total = total + mm(grads, stages[g // 4][0][128 * (g % 4) : 128 * (g % 4) + 128, :])

    def fold(block):
        return block[0:32, 0:64] + block[32:64, 64:128]

    first_out[...] = fold(total[0:64, 0:128])
    second_out[...] = fold(total[64:128, 0:128])
    sums = jnp.sum(sums, axis=1, keepdims=True)
    left_sum = sums[0:32] + sums[32:64]
    right_sum = sums[64:96] + sums[96:128]
    first = first_ref[...].astype(F32)
    second = second_ref[...].astype(F32)
    gain_out[...] = jnp.sum(
        first * fold(total[0:64, 128:256]) + second * fold(total[64:128, 128:256]),
        axis=0, keepdims=True,
    )
    offset_out[...] = jnp.sum(first * left_sum + second * right_sum, axis=0, keepdims=True)

    for h in range(2):
        at = slice(128 * h, 128 * h + 128)
        d_normal = mm_tn(linc_scr[at, :], back_ref[:128, :]) + mm_tn(rinc_scr[at, :], back_ref[128:, :])
        for half in range(2):
            g = 2 * h + half
            d_hat = d_normal[0:32, 128 * half : 128 * half + 128] * gain
            normed = normed_ref[32 * g : 32 * g + 32, :]
            result = inverse_ref[32 * g : 32 * g + 32, :] * (
                d_hat
                - mm(d_hat.astype(BF), averager)
                - normed * mm((d_hat * normed).astype(BF), averager)
            )
            emb_out[:, 2 * g, :] = result[:, 0:64]
            emb_out[:, 2 * g + 1, :] = result[:, 64:128]
    final_send.wait()


def vmem(count):
    return [pl.BlockSpec(memory_space=pltpu.VMEM)] * count


LIMIT = pltpu.CompilerParams(vmem_limit_bytes=32 * 1024 * 1024)


def gathered_body(
    n_row,
    n_col,
    homolog_embedding,
    presence_indicator,
    coupling_change_derivative,
    standardizer_scale,
    standardizer_shift,
    first_projection_matrix,
    second_projection_matrix,
    final_projection_matrix,
):
    shards, tokens, features = homolog_embedding.shape
    width = first_projection_matrix.shape[1]
    first_t, second_t = first_projection_matrix.T, second_projection_matrix.T
    shape = lambda *dims: jax.ShapeDtypeStruct(dims, F32)
    held = lambda *dims: pltpu.VMEM(dims, F32)
    held_bf = lambda *dims: pltpu.VMEM(dims, BF)
    hbm = pl.BlockSpec(memory_space=pltpu.HBM)
    place = lax.bitwise_xor(lax.axis_index("row"), lax.axis_index("col"))
    place = place.astype(jnp.int32).reshape(1)
    packed = pl.pallas_call(
        pack_kernel,
        out_shape=held_bf(192, 128),
        in_specs=vmem(3),
        out_specs=vmem(1)[0],
    )(homolog_embedding, presence_indicator.T, coupling_change_derivative)
    def over(axis, size, step, array):
        return lax.ppermute(array, axis, [(k, k ^ step) for k in range(size)])

    pieces = [packed] + [over("col", n_col, b, packed) for b in range(1, n_col)]
    chip_first = over("row", n_row, 2, packed)
    rest = jnp.stack(pieces[1:])
    chip_rest = over("row", n_row, 2, rest)
    weights = pl.pallas_call(
        weights_kernel,
        out_shape=(held(8, 128), held_bf(256, 256), held_bf(width * width, 128)),
        in_specs=[hbm] * 5,
        out_specs=tuple(vmem(3)),
        scratch_shapes=[
            pltpu.VMEM((1, features), F32),
            pltpu.VMEM((1, features), F32),
            pltpu.VMEM((width, features), BF),
            pltpu.VMEM((width, features), BF),
            pltpu.VMEM((width * width, 128), BF),
            pltpu.VMEM((width * width, 128), F32),
            pltpu.SemaphoreType.DMA((5,)),
        ],
        compiler_params=LIMIT,
    )(
        *[
            pltpu.with_memory_space_constraint(x, pltpu.HBM)
            for x in (
                standardizer_scale.reshape(1, features),
                standardizer_shift.reshape(1, features),
                first_t,
                second_t,
                final_projection_matrix,
            )
        ]
    )
    norm, back, final_turned = weights
    own = jnp.concatenate([packed[None], rest])
    own, chip_first = lax.optimization_barrier((own, chip_first))
    core = over("row", n_row, 1, own)

    def stage(a, block):
        outs = [
            held_bf(512, 256), held_bf(128, 256), held_bf(256, 128), held(width, 8, 128),
            held_bf(256, 1024), held(8, 32, 128), held(128, 128),
        ]
        if a == 0:
            outs += [held(128, 128)] * 2
        return pl.pallas_call(
            functools.partial(stage_kernel, n_col, a),
            out_shape=tuple(outs),
            in_specs=[pl.BlockSpec(memory_space=pltpu.SMEM)] + vmem(4),
            out_specs=tuple(vmem(len(outs))),
            scratch_shapes=[pltpu.VMEM((256, 128), F32)],
            compiler_params=LIMIT,
            cost_estimate=pl.CostEstimate(
                flops=1_000_000_000, bytes_accessed=4_000_000, transcendentals=0
            ),
        )(place, block, norm, back, final_turned)

    own_stage = stage(0, own)
    core_stage = stage(1, core)
    chip = jnp.concatenate([chip_first[None], chip_rest])
    chip, own_stage = lax.optimization_barrier((chip, own_stage))
    both = over("row", n_row, 1, chip)
    stages = [own_stage, core_stage, stage(2, chip), stage(3, both)]
    own_norm = stages[0][7:]
    outs = pl.pallas_call(
        functools.partial(part_kernel, n_row),
        out_shape=(
            shape(shards, tokens, features),
            shape(width * width, 128),
            shape(width, features),
            shape(width, features),
            shape(1, features),
            shape(1, features),
            shape(1, 128),
        ),
        in_specs=vmem(7 * n_row + 6),
        out_specs=(*vmem(1), hbm, *vmem(5)),
        scratch_shapes=[
            pltpu.VMEM((1024, 128), BF),
            pltpu.VMEM((1024, 128), BF),
            pltpu.VMEM((1024, 1024), BF),
            pltpu.VMEM((1024, 1024), BF),
            pltpu.VMEM((1024, 128), F32),
            pltpu.VMEM((1024, 128), BF),
            pltpu.VMEM((1024, 128), F32),
            pltpu.VMEM((1024, 128), BF),
            pltpu.VMEM((1024, 128), F32),
            pltpu.SemaphoreType.DMA,
        ],
        compiler_params=LIMIT,
    )(*[x for s in stages for x in s[:7]], *own_norm, norm, back, first_t, second_t)
    emb, final, first, second, gain, offset, bias = outs
    return emb, final, first.T, second.T, gain.reshape(-1), offset.reshape(-1), bias.reshape(-1)


def body(n_row, n_col, *arguments):
    msa, _, pair = arguments[:3]
    width = arguments[5].shape[1]
    fits = (
        n_row == 4
        and n_col == 4
        and msa.shape == (32, 8, 64)
        and pair.shape == (8, 8, 128)
        and width == 32
    )
    if fits:
        return gathered_body(n_row, n_col, *arguments)
    return sharded_body(*arguments)


def solution(mesh):
    placed = (
        P(("grp", "col"), "row", None),
        P(("grp", "col"), "row"),
        P(("grp", "row"), "col", None),
        P(),
        P(),
        P(),
        P(),
        P(),
    )
    return jax.shard_map(
        functools.partial(body, mesh.shape["row"], mesh.shape["col"]),
        mesh=mesh,
        in_specs=placed,
        out_specs=(
            P(("grp", "col"), "row", None),
            P("grp", None),
            P("grp", None),
            P("grp", None),
            P("grp"),
            P("grp"),
            P("grp"),
        ),
        check_vma=False,
    )
```

```python
import functools

import jax
import jax.numpy as jnp
from jax import lax
from jax.experimental import pallas as pl
from jax.experimental.pallas import tpu as pltpu
from jax.sharding import PartitionSpec as P

TOKB = 2


def standardizer_parts(homolog_embedding, standardizer_scale, standardizer_shift):
    incoming_entries = homolog_embedding.astype(jnp.float32)
    center = jnp.mean(incoming_entries, axis=-1, keepdims=True)
    varied = incoming_entries - center
    variance = jnp.mean(varied * varied, axis=-1, keepdims=True)
    reciprocal_spread = lax.rsqrt(variance + 1e-05)
    standardized_entries = varied * reciprocal_spread
    standardized_bfloat = (standardized_entries * standardizer_scale + standardizer_shift).astype(
        jnp.bfloat16
    )
    return (standardized_entries, reciprocal_spread, standardized_bfloat)


def sharded_body(
    homolog_embedding,
    presence_indicator,
    coupling_change_derivative,
    standardizer_scale,
    standardizer_shift,
    first_projection_matrix,
    second_projection_matrix,
    final_projection_matrix,
):
    shard_homolog_number, residue_line_number, feature_number = homolog_embedding.shape
    tok_cols = coupling_change_derivative.shape[1]
    width = first_projection_matrix.shape[1]
    standardized_entries, reciprocal_spread, standardized_bfloat = standardizer_parts(
        homolog_embedding, standardizer_scale, standardizer_shift
    )
    mask_single_precision = presence_indicator.astype(jnp.float32)
    mask_half_precision = presence_indicator.astype(jnp.bfloat16)
    left = (
        jnp.einsum(
            "sic,cp->sip",
            standardized_bfloat,
            first_projection_matrix,
            preferred_element_type=jnp.float32,
        )
        * mask_single_precision[..., None]
    ).astype(jnp.bfloat16)
    right = (
        jnp.einsum(
            "sic,cp->sip",
            standardized_bfloat,
            second_projection_matrix,
            preferred_element_type=jnp.float32,
        )
        * mask_single_precision[..., None]
    ).astype(jnp.bfloat16)
    left_flat = left.reshape(shard_homolog_number, residue_line_number * width)
    right_flat = right.reshape(shard_homolog_number, residue_line_number * width)
    left_all, mask_left = (
        lax.all_gather(left_flat, "col", axis=0, tiled=True),
        lax.all_gather(mask_half_precision, "col", axis=0, tiled=True),
    )
    right_wide, mask_wide = (
        lax.all_gather(right_flat, "row", axis=1, tiled=True),
        lax.all_gather(mask_half_precision, "row", axis=1, tiled=True),
    )
    right_all, mask_right = (
        lax.all_to_all(right_wide, "col", split_axis=1, concat_axis=0, tiled=True),
        lax.all_to_all(mask_wide, "col", split_axis=1, concat_axis=0, tiled=True),
    )
    seq_total = left_all.shape[0]
    right_three = right_all.reshape(seq_total, tok_cols, width)
    counts = jnp.einsum("si,sj->ij", mask_left, mask_right, preferred_element_type=jnp.float32)
    scaled = coupling_change_derivative.astype(jnp.float32) / (counts + 0.001)[..., None]
    bias_part = jnp.sum(scaled, axis=(0, 1))
    scaled_bf = scaled.astype(jnp.bfloat16)
    block_rows = residue_line_number // TOKB
    right_acc = jnp.zeros((seq_total, tok_cols, width), jnp.float32)
    wout_acc = jnp.zeros(final_projection_matrix.shape, jnp.float32)
    left_pieces = []
    for block_index in range(TOKB):
        first = block_index * block_rows
        rows_bf = scaled_bf[first : first + block_rows]
        outer_grad = jnp.einsum(
            "ijz,fz->ijf", rows_bf, final_projection_matrix, preferred_element_type=jnp.float32
        ).astype(jnp.bfloat16)
        outer_grad = outer_grad.reshape(block_rows, tok_cols, width, width)
        left_block = left_all[:, first * width : (first + block_rows) * width].reshape(
            seq_total, block_rows, width
        )
        first_factor_derivative = jnp.einsum(
            "ijce,sje->sic", outer_grad, right_three, preferred_element_type=jnp.float32
        )
        right_acc = right_acc + jnp.einsum(
            "ijce,sic->sje", outer_grad, left_block, preferred_element_type=jnp.float32
        )
        outer = jnp.einsum(
            "sic,sje->ijce", left_block, right_three, preferred_element_type=jnp.float32
        ).astype(jnp.bfloat16)
        outer = outer.reshape(block_rows, tok_cols, width * width)
        wout_acc = wout_acc + jnp.einsum(
            "ijf,ijz->fz", outer, rows_bf, preferred_element_type=jnp.float32
        )
        first_factor_derivative = first_factor_derivative.reshape(seq_total, block_rows * width)
        left_pieces.append(first_factor_derivative)
    left_terms = jnp.concatenate(left_pieces, axis=1)
    left_own = lax.psum_scatter(left_terms, "col", scatter_dimension=0, tiled=True)
    right_spread = lax.all_to_all(
        right_acc.reshape(seq_total, tok_cols * width),
        "col",
        split_axis=0,
        concat_axis=1,
        tiled=True,
    )
    right_own = lax.psum_scatter(right_spread, "row", scatter_dimension=1, tiled=True)
    left_in = (
        left_own.reshape(shard_homolog_number, residue_line_number, width)
        * mask_single_precision[..., None]
    ).astype(jnp.bfloat16)
    right_in = (
        right_own.reshape(shard_homolog_number, residue_line_number, width)
        * mask_single_precision[..., None]
    ).astype(jnp.bfloat16)
    left_part = jnp.einsum(
        "sic,sip->cp", standardized_bfloat, left_in, preferred_element_type=jnp.float32
    )
    right_part = jnp.einsum(
        "sic,sip->cp", standardized_bfloat, right_in, preferred_element_type=jnp.float32
    )
    d_normal = jnp.einsum(
        "sip,cp->sic", left_in, first_projection_matrix, preferred_element_type=jnp.float32
    ) + jnp.einsum(
        "sip,cp->sic", right_in, second_projection_matrix, preferred_element_type=jnp.float32
    )
    gain_part = jnp.sum(d_normal * standardized_entries, axis=(0, 1))
    beta_part = jnp.sum(d_normal, axis=(0, 1))
    standardized_derivative = d_normal * standardizer_scale
    embedding_derivative = reciprocal_spread * (
        standardized_derivative
        - jnp.mean(standardized_derivative, axis=-1, keepdims=True)
        - standardized_entries
        * jnp.mean(standardized_derivative * standardized_entries, axis=-1, keepdims=True)
    )
    (
        final_matrix_derivative,
        first_matrix_derivative,
        second_matrix_derivative,
        scale_factor_derivative,
        shift_term_derivative,
        shift_derivative,
    ) = lax.psum((wout_acc, left_part, right_part, gain_part, beta_part, bias_part), ("row", "col"))
    return (
        embedding_derivative,
        final_matrix_derivative,
        first_matrix_derivative,
        second_matrix_derivative,
        scale_factor_derivative,
        shift_term_derivative,
        shift_derivative,
    )


BF = jnp.bfloat16
F32 = jnp.float32


def spread(rows, cols, rule):
    r = lax.broadcasted_iota(jnp.int32, (rows, cols), 0)
    c = lax.broadcasted_iota(jnp.int32, (rows, cols), 1)
    return rule(r, c)


def mm(a, b):
    return jnp.dot(a, b, preferred_element_type=F32)


def mm_nt(a, b):
    return lax.dot_general(a, b, (((1,), (1,)), ((), ())), preferred_element_type=F32)


def mm_tn(a, b):
    return lax.dot_general(a, b, (((0,), (0,)), ((), ())), preferred_element_type=F32)


def interleave(first, second):
    odd = lax.broadcasted_iota(jnp.int16, (32, 128), 1) & 32 != 0
    return (
        jnp.where(odd, pltpu.roll(second, 32, 1), first),
        jnp.where(odd, second, pltpu.roll(first, 96, 1)),
    )


def diagonal_pair(block):
    zero = jnp.zeros_like(block)
    return jnp.concatenate(
        [jnp.concatenate([block, zero], axis=1), jnp.concatenate([zero, block], axis=1)], axis=0
    )


ABSENT = 1024.0


def pack_kernel(msa_ref, mask_ref, pair_ref, out_ref):
    msa = msa_ref[...].astype(F32)
    pick = spread(8, 512, lambda r, c: jnp.where(c // 64 == r, 1.0, 0.0)).astype(BF)
    present = mm_tn(mask_ref[...].astype(F32).astype(BF), pick) > 0.5
    for g in range(4):
        rows = jnp.concatenate([msa[:, 2 * g, :], msa[:, 2 * g + 1, :]], axis=1)
        out_ref[32 * g : 32 * g + 32, :] = jnp.where(
            present[:, 128 * g : 128 * g + 128], rows, ABSENT
        ).astype(BF)
    out_ref[128:192, :] = pair_ref[...].astype(F32).reshape(64, 128).astype(BF)


def weights_kernel(*refs):
    sources, (norm_out, back_out, final_out, first_out) = refs[:5], refs[5:9]
    held, scr, sems = refs[9:14], refs[14], refs[15]
    copies = [pltpu.make_async_copy(sources[k], held[k], sems.at[k]) for k in range(5)]
    for copy in copies:
        copy.start()
    for copy in copies:
        copy.wait()
    gain_ref, offset_ref, first_ref, second_ref, final_ref = held
    norm_out[...] = jnp.concatenate(
        [
            jnp.concatenate([ref[...]] * 2, axis=1)
            for ref in (gain_ref, offset_ref, gain_ref, offset_ref) * 2
        ],
        axis=0,
    )
    for k, ref in enumerate((first_ref, second_ref)):
        narrow = ref[...].astype(F32)
        first_out[32 * k : 32 * k + 32, :] = narrow
        wide = jnp.concatenate([narrow] * 4, axis=1)
        wide = jnp.concatenate([wide] * 4, axis=0)
        own = spread(128, 256, lambda r, c: r // 32 == c // 64)
        back_out[128 * k : 128 * k + 128, :] = jnp.where(own, wide, 0.0).astype(BF)
    scr[...] = final_ref[...].astype(F32)
    for k in range(16):
        e = 4 * (k // 2) + k % 2
        final_out[32 * k : 32 * k + 32, :] = jnp.concatenate(
            [scr[pl.ds(e, 32, stride=32), :], scr[pl.ds(e + 2, 32, stride=32), :]], axis=1
        ).astype(BF)


def averager_of():
    return spread(128, 128, lambda r, c: jnp.where(r // 64 == c // 64, 1.0 / 64, 0.0)).astype(BF)


def stage_kernel(
    n_col, a, place_ref, set_ref, norm_ref, back_ref, final_ref,
    rhs_out, left_out, leftt_out, rightt_out, grad_out, pair_out, found_out, *rest
):
    *own_out, turn_scr = rest
    for b in range(n_col):
        at = pl.multiple_of(lax.bitwise_xor(place_ref[0], b) * 8, 8)
        pair_out[:, pl.ds(at, 8), :] = set_ref[b, 128:192, :].astype(F32).reshape(8, 8, 128)

    gain = norm_ref[0:1, :]
    offset = norm_ref[1:2, :]
    averager = averager_of()
    x = jnp.concatenate(
        [set_ref[b, 32 * g : 32 * g + 32, :] for g in range(4) for b in range(n_col)], axis=0
    )
    mean = mm(x, averager)
    present = mean < ABSENT / 2
    varied = x.astype(F32) - mean
    inverse = lax.rsqrt(mm((varied * varied).astype(BF), averager) + 1e-05)
    normed = varied * inverse
    if own_out:
        for g in range(4):
            own_out[0][32 * g : 32 * g + 32, :] = normed[128 * g : 128 * g + 32]
            own_out[1][32 * g : 32 * g + 32, :] = inverse[128 * g : 128 * g + 32]
    normal = jnp.where(present, normed * gain + offset, 0.0).astype(BF)
    rhs_out[:, 0:128] = normal
    rhs_out[:, 128:256] = normed.astype(BF)
    here = jnp.where(present, 1.0, 0.0)
    lane = lax.broadcasted_iota(jnp.int32, (128, 128), 1)
    found = jnp.zeros((128, 128), F32)
    for g in range(4):
        found = jnp.where(lane % 32 // 2 == 4 * a + g, here[128 * g : 128 * g + 128], found)
    found_out[...] = found
    for h in range(2):
        masked = jnp.concatenate(
            [normal[128 * g : 128 * g + 128] for g in (2 * h, 2 * h + 1)], axis=1
        )
        at = slice(128 * h, 128 * h + 128)
        left_out[:, at] = mm_nt(masked, back_ref[:128, :]).astype(BF)
        both = mm_nt(back_ref[...], masked)
        turn_scr[at, :] = both[128:]
        for k in range(2):
            leftt_out[64 * h + 32 * k : 64 * h + 32 * k + 32, :] = jnp.concatenate(
                [both[32 * k : 32 * k + 32], both[32 * k + 64 : 32 * k + 96]], axis=1
            ).astype(BF)

    for e in range(32):
        rightt_out[e] = turn_scr[pl.ds(e, 8, stride=32), :]

    pair = pair_out[...].reshape(256, 128).astype(BF)
    for n in range(2):
        pairs = jnp.concatenate(
            [diagonal_pair(pair[64 * p : 64 * p + 64]) for p in (2 * n, 2 * n + 1)], axis=0
        )
        grad = mm_nt(final_ref[...], pairs).astype(BF)
        for p in range(2):
            for q in range(8):
                rows = 64 * (2 * n + p)
                block = grad[64 * q : 64 * q + 64, 128 * p : 128 * p + 128]
                even, odd = interleave(block[:32], block[32:])
                grad_out[rows : rows + 32, 128 * q : 128 * q + 128] = even
                grad_out[rows + 32 : rows + 64, 128 * q : 128 * q + 128] = odd


def part_kernel(n_row, n_col, place_ref, last_ref, *refs):
    stages = [refs[7 * a : 7 * a + 7] for a in range(n_row - 1)]
    (
        normed_ref, inverse_ref, norm_ref, back_ref, final_ref, first_ref,
        emb_out, final_hbm_out, first_out, second_out, gain_out, offset_out, bias_out,
        right_scr, scaled_scr, grad_scr, outer_scr, wide_scr, rin_scr, all_scr,
        final_out, out_sem, turn_scr,
    ) = refs[7 * (n_row - 1) : -7]
    stages.append(refs[-7:])
    stage_kernel(
        n_col, n_row - 1, place_ref, last_ref, norm_ref, back_ref, final_ref, *stages[-1], turn_scr
    )
    gain = norm_ref[0:1, :]
    averager = averager_of()
    lane = lax.broadcasted_iota(jnp.int32, (128, 128), 1)

    found = sum(stage[6][...] for stage in stages)
    turned = pltpu.roll(found, 64, 1)
    mask = jnp.where((lane % 2 == 0) == (lane < 64), found, turned)
    mask_t = mask.T

    for e in range(32):
        right_scr[32 * e : 32 * e + 32, :] = jnp.concatenate(
            [stage[3][e] for stage in stages], axis=0
        ).astype(BF)

    mask_bf = mask.astype(BF)
    share = (1.0 / (mm_tn(mask_bf, mask_bf)[0:32] + 0.001)).astype(BF)
    for i in range(32):
        a, at = i // 8, 32 * (i % 8)
        for q in range(8):
            grad_scr[32 * i : 32 * i + 32, 128 * q : 128 * q + 128] = (
                stages[a][4][at : at + 32, 128 * q : 128 * q + 128] * share[i : i + 1]
            )
    left = jnp.concatenate([stage[1][...] for stage in stages], axis=1)
    right_grad = mm(left, grad_scr[...])
    left_grad = mm(grad_scr[...], right_scr[...])

    identity = spread(128, 128, lambda r, c: jnp.where(r == c, 1.0, 0.0)).astype(BF)
    for q in range(8):
        at = slice(128 * q, 128 * q + 128)
        rin_scr[at, :] = mm_nt(identity, (right_grad[:, at] * mask).astype(BF))
    for t in range(32):
        at = slice(128 * (t // 2), 128 * (t // 2) + 128)
        row = 32 * (t % 2)
        all_scr[row : row + 32, at] = (
            left_grad[32 * t : 32 * t + 32] * mask_t[t : t + 1]
        ).astype(BF)
        all_scr[row + 64 : row + 96, at] = rin_scr[pl.ds(t, 32, stride=32), :].astype(BF)

    bias = jnp.zeros((1, 128), F32)
    ones = jnp.ones((128, 128), BF)
    for p in range(8):
        both_on = jnp.concatenate(
            [mask_t[0:32] * mask_t[i : i + 1] for i in range(4 * p, 4 * p + 4)], axis=0
        ).astype(BF)
        counts = mm(both_on, ones)
        pair = stages[p // 2][5][4 * (p % 2) : 4 * (p % 2) + 4]
        scaled = pair.reshape(128, 128) / (counts + 0.001)
        bias = bias + jnp.sum(scaled, axis=0, keepdims=True)
        scaled_scr[128 * p : 128 * p + 128, :] = scaled.astype(BF)
    bias_out[...] = bias

    left_t = jnp.concatenate([stage[2][...] for stage in stages], axis=0)
    for n in range(8):
        rights = jnp.concatenate(
            [diagonal_pair(right_scr[64 * p : 64 * p + 64, :]) for p in (2 * n, 2 * n + 1)], axis=0
        )
        outer = mm_nt(left_t, rights).astype(BF)
        for p in range(2):
            for q in range(8):
                rows = 64 * (2 * n + p)
                block = outer[64 * q : 64 * q + 64, 128 * p : 128 * p + 128]
                even, odd = interleave(block[:32], block[32:])
                outer_scr[rows : rows + 32, 128 * q : 128 * q + 128] = even
                outer_scr[rows + 32 : rows + 64, 128 * q : 128 * q + 128] = odd
    wide_scr[...] = mm(outer_scr[...], scaled_scr[...])
    for c in range(32):
        final_out[32 * c : 32 * c + 32, :] = wide_scr[pl.ds(c, 32, stride=32), :]
    final_send = pltpu.make_async_copy(final_out, final_hbm_out, out_sem)
    final_send.start()

    total = mm(
        all_scr[...], jnp.concatenate([stage[0][...] for stage in stages], axis=0)
    )
    sums = all_scr[:, 0:128].astype(F32)
    for g in range(1, 16):
        sums = sums + all_scr[:, 128 * g : 128 * g + 128].astype(F32)

    def fold(block):
        return block[0:32, 0:64] + block[32:64, 64:128]

    first_out[...] = fold(total[0:64, 0:128])
    second_out[...] = fold(total[64:128, 0:128])
    sums = jnp.sum(sums, axis=1, keepdims=True)
    left_sum = sums[0:32] + sums[32:64]
    right_sum = sums[64:96] + sums[96:128]
    first, second = first_ref[0:32, :], first_ref[32:64, :]
    gain_out[...] = jnp.sum(
        first * fold(total[0:64, 128:256]) + second * fold(total[64:128, 128:256]),
        axis=0, keepdims=True,
    )
    offset_out[...] = jnp.sum(first * left_sum + second * right_sum, axis=0, keepdims=True)

    d_hat = []
    for h in range(2):
        sides = [
            jnp.concatenate(
                [all_scr[row : row + 64, 128 * g : 128 * g + 128] for g in (2 * h, 2 * h + 1)], axis=0
            )
            for row in (0, 64)
        ]
        d_normal = mm_tn(jnp.concatenate(sides, axis=0), back_ref[...])
        d_hat += [d_normal[0:32, 0:128] * gain, d_normal[0:32, 128:256] * gain]
    d_hat = jnp.concatenate(d_hat, axis=0)
    normed = normed_ref[...]
    means = mm(jnp.concatenate([d_hat, d_hat * normed], axis=0).astype(BF), averager)
    result = inverse_ref[...] * (d_hat - means[:128] - normed * means[128:])
    for g in range(4):
        emb_out[:, 2 * g, :] = result[32 * g : 32 * g + 32, 0:64]
        emb_out[:, 2 * g + 1, :] = result[32 * g : 32 * g + 32, 64:128]
    final_send.wait()


def vmem(count):
    return [pl.BlockSpec(memory_space=pltpu.VMEM)] * count


LIMIT = pltpu.CompilerParams(vmem_limit_bytes=32 * 1024 * 1024)


def gathered_body(
    n_row,
    n_col,
    homolog_embedding,
    presence_indicator,
    coupling_change_derivative,
    standardizer_scale,
    standardizer_shift,
    first_projection_matrix,
    second_projection_matrix,
    final_projection_matrix,
):
    shards, tokens, features = homolog_embedding.shape
    width = first_projection_matrix.shape[1]
    first_t, second_t = first_projection_matrix.T, second_projection_matrix.T
    shape = lambda *dims: jax.ShapeDtypeStruct(dims, F32)
    held = lambda *dims: pltpu.VMEM(dims, F32)
    held_bf = lambda *dims: pltpu.VMEM(dims, BF)
    hbm = pl.BlockSpec(memory_space=pltpu.HBM)
    place = lax.bitwise_xor(lax.axis_index("row"), lax.axis_index("col"))
    place = place.astype(jnp.int32).reshape(1)
    packed = pl.pallas_call(
        pack_kernel,
        out_shape=held_bf(192, 128),
        in_specs=vmem(3),
        out_specs=vmem(1)[0],
    )(homolog_embedding, presence_indicator.T, coupling_change_derivative)
    def over(axis, size, step, array):
        return lax.ppermute(array, axis, [(k, k ^ step) for k in range(size)])

    pieces = [packed] + [over("col", n_col, b, packed) for b in range(1, n_col)]
    chip_first = over("row", n_row, 2, packed)
    rest = jnp.stack(pieces[1:])
    chip_rest = over("row", n_row, 2, rest)
    weights = pl.pallas_call(
        weights_kernel,
        out_shape=(
            held(8, 128), held_bf(256, 256), held_bf(width * width // 2, 256), held(2 * width, features),
        ),
        in_specs=[hbm] * 5,
        out_specs=tuple(vmem(4)),
        scratch_shapes=[
            pltpu.VMEM((1, features), F32),
            pltpu.VMEM((1, features), F32),
            pltpu.VMEM((width, features), BF),
            pltpu.VMEM((width, features), BF),
            pltpu.VMEM((width * width, 128), BF),
            pltpu.VMEM((width * width, 128), F32),
            pltpu.SemaphoreType.DMA((5,)),
        ],
        compiler_params=LIMIT,
    )(
        *[
            pltpu.with_memory_space_constraint(x, pltpu.HBM)
            for x in (
                standardizer_scale.reshape(1, features),
                standardizer_shift.reshape(1, features),
                first_t,
                second_t,
                final_projection_matrix,
            )
        ]
    )
    norm, back, final_turned, first = weights
    own = jnp.concatenate([packed[None], rest])
    own, chip_first = lax.optimization_barrier((own, chip_first))
    core = over("row", n_row, 1, own)

    stage_outs = [
        held_bf(512, 256), held_bf(128, 256), held_bf(128, 256), held(width, 8, 128),
        held_bf(256, 1024), held(8, 32, 128), held(128, 128),
    ]
    scalar = pl.BlockSpec(memory_space=pltpu.SMEM)

    def stage(a, block):
        outs = stage_outs + [held(128, 128)] * 2 * (a == 0)
        return pl.pallas_call(
            functools.partial(stage_kernel, n_col, a),
            out_shape=tuple(outs),
            in_specs=[scalar] + vmem(4),
            out_specs=tuple(vmem(len(outs))),
            scratch_shapes=[pltpu.VMEM((256, 128), F32)],
            compiler_params=LIMIT,
            cost_estimate=pl.CostEstimate(
                flops=1_000_000_000, bytes_accessed=4_000_000, transcendentals=0
            ),
        )(place, block, norm, back, final_turned)

    own_stage = stage(0, own)
    core_stage = stage(1, core)
    chip = jnp.concatenate([chip_first[None], chip_rest])
    chip, own_stage = lax.optimization_barrier((chip, own_stage))
    both = over("row", n_row, 1, chip)
    stages = [own_stage[:7], core_stage, stage(2, chip)]
    outs = pl.pallas_call(
        functools.partial(part_kernel, n_row, n_col),
        out_shape=(
            shape(shards, tokens, features),
            shape(width * width, 128),
            shape(width, features),
            shape(width, features),
            shape(1, features),
            shape(1, features),
            shape(1, 128),
        ),
        in_specs=[scalar] + vmem(7 * (n_row - 1) + 7),
        out_specs=(*vmem(1), hbm, *vmem(5)),
        scratch_shapes=[
            pltpu.VMEM((1024, 128), BF),
            pltpu.VMEM((1024, 128), BF),
            pltpu.VMEM((1024, 1024), BF),
            pltpu.VMEM((1024, 1024), BF),
            pltpu.VMEM((1024, 128), F32),
            pltpu.VMEM((1024, 128), F32),
            pltpu.VMEM((128, 2048), BF),
            pltpu.VMEM((1024, 128), F32),
            pltpu.SemaphoreType.DMA,
            pltpu.VMEM((256, 128), F32),
            *stage_outs,
        ],
        compiler_params=LIMIT,
    )(place, both, *[x for s in stages for x in s], *own_stage[7:], norm, back, final_turned, first)
    emb, final, first, second, gain, offset, bias = outs
    return emb, final, first.T, second.T, gain.reshape(-1), offset.reshape(-1), bias.reshape(-1)


def body(n_row, n_col, *arguments):
    msa, _, pair = arguments[:3]
    width = arguments[5].shape[1]
    fits = (
        n_row == 4
        and n_col == 4
        and msa.shape == (32, 8, 64)
        and pair.shape == (8, 8, 128)
        and width == 32
    )
    if fits:
        return gathered_body(n_row, n_col, *arguments)
    return sharded_body(*arguments)


def solution(mesh):
    placed = (
        P(("grp", "col"), "row", None),
        P(("grp", "col"), "row"),
        P(("grp", "row"), "col", None),
        P(),
        P(),
        P(),
        P(),
        P(),
    )
    return jax.shard_map(
        functools.partial(body, mesh.shape["row"], mesh.shape["col"]),
        mesh=mesh,
        in_specs=placed,
        out_specs=(
            P(("grp", "col"), "row", None),
            P("grp", None),
            P("grp", None),
            P("grp", None),
            P("grp"),
            P("grp"),
            P("grp"),
        ),
        check_vma=False,
    )
```

```python
import functools

import jax
import jax.numpy as jnp
from jax import lax
from jax.experimental import pallas as pl
from jax.experimental.pallas import tpu as pltpu
from jax.sharding import PartitionSpec as P

TOKB = 2


def standardizer_parts(homolog_embedding, standardizer_scale, standardizer_shift):
    incoming_entries = homolog_embedding.astype(jnp.float32)
    center = jnp.mean(incoming_entries, axis=-1, keepdims=True)
    varied = incoming_entries - center
    variance = jnp.mean(varied * varied, axis=-1, keepdims=True)
    reciprocal_spread = lax.rsqrt(variance + 1e-05)
    standardized_entries = varied * reciprocal_spread
    standardized_bfloat = (standardized_entries * standardizer_scale + standardizer_shift).astype(
        jnp.bfloat16
    )
    return (standardized_entries, reciprocal_spread, standardized_bfloat)


def sharded_body(
    homolog_embedding,
    presence_indicator,
    coupling_change_derivative,
    standardizer_scale,
    standardizer_shift,
    first_projection_matrix,
    second_projection_matrix,
    final_projection_matrix,
):
    shard_homolog_number, residue_line_number, feature_number = homolog_embedding.shape
    tok_cols = coupling_change_derivative.shape[1]
    width = first_projection_matrix.shape[1]
    standardized_entries, reciprocal_spread, standardized_bfloat = standardizer_parts(
        homolog_embedding, standardizer_scale, standardizer_shift
    )
    mask_single_precision = presence_indicator.astype(jnp.float32)
    mask_half_precision = presence_indicator.astype(jnp.bfloat16)
    left = (
        jnp.einsum(
            "sic,cp->sip",
            standardized_bfloat,
            first_projection_matrix,
            preferred_element_type=jnp.float32,
        )
        * mask_single_precision[..., None]
    ).astype(jnp.bfloat16)
    right = (
        jnp.einsum(
            "sic,cp->sip",
            standardized_bfloat,
            second_projection_matrix,
            preferred_element_type=jnp.float32,
        )
        * mask_single_precision[..., None]
    ).astype(jnp.bfloat16)
    left_flat = left.reshape(shard_homolog_number, residue_line_number * width)
    right_flat = right.reshape(shard_homolog_number, residue_line_number * width)
    left_all, mask_left = (
        lax.all_gather(left_flat, "col", axis=0, tiled=True),
        lax.all_gather(mask_half_precision, "col", axis=0, tiled=True),
    )
    right_wide, mask_wide = (
        lax.all_gather(right_flat, "row", axis=1, tiled=True),
        lax.all_gather(mask_half_precision, "row", axis=1, tiled=True),
    )
    right_all, mask_right = (
        lax.all_to_all(right_wide, "col", split_axis=1, concat_axis=0, tiled=True),
        lax.all_to_all(mask_wide, "col", split_axis=1, concat_axis=0, tiled=True),
    )
    seq_total = left_all.shape[0]
    right_three = right_all.reshape(seq_total, tok_cols, width)
    counts = jnp.einsum("si,sj->ij", mask_left, mask_right, preferred_element_type=jnp.float32)
    scaled = coupling_change_derivative.astype(jnp.float32) / (counts + 0.001)[..., None]
    bias_part = jnp.sum(scaled, axis=(0, 1))
    scaled_bf = scaled.astype(jnp.bfloat16)
    block_rows = residue_line_number // TOKB
    right_acc = jnp.zeros((seq_total, tok_cols, width), jnp.float32)
    wout_acc = jnp.zeros(final_projection_matrix.shape, jnp.float32)
    left_pieces = []
    for block_index in range(TOKB):
        first = block_index * block_rows
        rows_bf = scaled_bf[first : first + block_rows]
        outer_grad = jnp.einsum(
            "ijz,fz->ijf", rows_bf, final_projection_matrix, preferred_element_type=jnp.float32
        ).astype(jnp.bfloat16)
        outer_grad = outer_grad.reshape(block_rows, tok_cols, width, width)
        left_block = left_all[:, first * width : (first + block_rows) * width].reshape(
            seq_total, block_rows, width
        )
        first_factor_derivative = jnp.einsum(
            "ijce,sje->sic", outer_grad, right_three, preferred_element_type=jnp.float32
        )
        right_acc = right_acc + jnp.einsum(
            "ijce,sic->sje", outer_grad, left_block, preferred_element_type=jnp.float32
        )
        outer = jnp.einsum(
            "sic,sje->ijce", left_block, right_three, preferred_element_type=jnp.float32
        ).astype(jnp.bfloat16)
        outer = outer.reshape(block_rows, tok_cols, width * width)
        wout_acc = wout_acc + jnp.einsum(
            "ijf,ijz->fz", outer, rows_bf, preferred_element_type=jnp.float32
        )
        first_factor_derivative = first_factor_derivative.reshape(seq_total, block_rows * width)
        left_pieces.append(first_factor_derivative)
    left_terms = jnp.concatenate(left_pieces, axis=1)
    left_own = lax.psum_scatter(left_terms, "col", scatter_dimension=0, tiled=True)
    right_spread = lax.all_to_all(
        right_acc.reshape(seq_total, tok_cols * width),
        "col",
        split_axis=0,
        concat_axis=1,
        tiled=True,
    )
    right_own = lax.psum_scatter(right_spread, "row", scatter_dimension=1, tiled=True)
    left_in = (
        left_own.reshape(shard_homolog_number, residue_line_number, width)
        * mask_single_precision[..., None]
    ).astype(jnp.bfloat16)
    right_in = (
        right_own.reshape(shard_homolog_number, residue_line_number, width)
        * mask_single_precision[..., None]
    ).astype(jnp.bfloat16)
    left_part = jnp.einsum(
        "sic,sip->cp", standardized_bfloat, left_in, preferred_element_type=jnp.float32
    )
    right_part = jnp.einsum(
        "sic,sip->cp", standardized_bfloat, right_in, preferred_element_type=jnp.float32
    )
    d_normal = jnp.einsum(
        "sip,cp->sic", left_in, first_projection_matrix, preferred_element_type=jnp.float32
    ) + jnp.einsum(
        "sip,cp->sic", right_in, second_projection_matrix, preferred_element_type=jnp.float32
    )
    gain_part = jnp.sum(d_normal * standardized_entries, axis=(0, 1))
    beta_part = jnp.sum(d_normal, axis=(0, 1))
    standardized_derivative = d_normal * standardizer_scale
    embedding_derivative = reciprocal_spread * (
        standardized_derivative
        - jnp.mean(standardized_derivative, axis=-1, keepdims=True)
        - standardized_entries
        * jnp.mean(standardized_derivative * standardized_entries, axis=-1, keepdims=True)
    )
    (
        final_matrix_derivative,
        first_matrix_derivative,
        second_matrix_derivative,
        scale_factor_derivative,
        shift_term_derivative,
        shift_derivative,
    ) = lax.psum((wout_acc, left_part, right_part, gain_part, beta_part, bias_part), ("row", "col"))
    return (
        embedding_derivative,
        final_matrix_derivative,
        first_matrix_derivative,
        second_matrix_derivative,
        scale_factor_derivative,
        shift_term_derivative,
        shift_derivative,
    )


BF = jnp.bfloat16
F32 = jnp.float32


def spread(rows, cols, rule):
    r = lax.broadcasted_iota(jnp.int32, (rows, cols), 0)
    c = lax.broadcasted_iota(jnp.int32, (rows, cols), 1)
    return rule(r, c)


def mm(a, b):
    return jnp.dot(a, b, preferred_element_type=F32)


def mm_nt(a, b):
    return lax.dot_general(a, b, (((1,), (1,)), ((), ())), preferred_element_type=F32)


def mm_tn(a, b):
    return lax.dot_general(a, b, (((0,), (0,)), ((), ())), preferred_element_type=F32)


def interleave(first, second):
    odd = lax.broadcasted_iota(jnp.int16, (32, 128), 1) & 32 != 0
    return (
        jnp.where(odd, pltpu.roll(second, 32, 1), first),
        jnp.where(odd, second, pltpu.roll(first, 96, 1)),
    )


def diagonal_pair(block):
    zero = jnp.zeros_like(block)
    return jnp.concatenate(
        [jnp.concatenate([block, zero], axis=1), jnp.concatenate([zero, block], axis=1)], axis=0
    )


ABSENT = 1024.0


def pack_kernel(msa_ref, mask_ref, pair_ref, out_ref):
    msa = msa_ref[...].astype(F32)
    pick = spread(8, 512, lambda r, c: jnp.where(c // 64 == r, 1.0, 0.0)).astype(BF)
    present = mm_tn(mask_ref[...].astype(F32).astype(BF), pick) > 0.5
    for g in range(4):
        rows = jnp.concatenate([msa[:, 2 * g, :], msa[:, 2 * g + 1, :]], axis=1)
        out_ref[32 * g : 32 * g + 32, :] = jnp.where(
            present[:, 128 * g : 128 * g + 128], rows, ABSENT
        ).astype(BF)
    out_ref[128:192, :] = pair_ref[...].astype(F32).reshape(64, 128).astype(BF)


def weights_kernel(*refs):
    sources, (norm_out, back_out, final_out, first_out) = refs[:5], refs[5:9]
    held, scr, sems = refs[9:14], refs[14], refs[15]
    copies = [pltpu.make_async_copy(sources[k], held[k], sems.at[k]) for k in range(5)]
    for copy in copies:
        copy.start()
    for copy in copies:
        copy.wait()
    gain_ref, offset_ref, first_ref, second_ref, final_ref = held
    norm_out[...] = jnp.concatenate(
        [
            jnp.concatenate([ref[...]] * 2, axis=1)
            for ref in (gain_ref, offset_ref, gain_ref, offset_ref) * 2
        ],
        axis=0,
    )
    for k, ref in enumerate((first_ref, second_ref)):
        narrow = ref[...].astype(F32)
        first_out[32 * k : 32 * k + 32, :] = narrow
        wide = jnp.concatenate([narrow] * 4, axis=1)
        wide = jnp.concatenate([wide] * 4, axis=0)
        own = spread(128, 256, lambda r, c: r // 32 == c // 64)
        back_out[128 * k : 128 * k + 128, :] = jnp.where(own, wide, 0.0).astype(BF)
    scr[...] = final_ref[...].astype(F32)
    for k in range(16):
        e = 4 * (k // 2) + k % 2
        final_out[32 * k : 32 * k + 32, :] = jnp.concatenate(
            [scr[pl.ds(e, 32, stride=32), :], scr[pl.ds(e + 2, 32, stride=32), :]], axis=1
        ).astype(BF)


def averager_of():
    return spread(128, 128, lambda r, c: jnp.where(r // 64 == c // 64, 1.0 / 64, 0.0)).astype(BF)


ORDER = (0, 1, 3, 2)


def stage_kernel(
    n_col, a, place_ref, set_ref, norm_ref, back_ref, final_ref,
    rhs_out, left_out, leftt_out, rightt_out, grad_out, pair_out, found_out, *rest
):
    *own_out, turn_scr = rest
    for b in range(n_col):
        at = pl.multiple_of(lax.bitwise_xor(place_ref[0], ORDER[b]) * 8, 8)
        pair_out[:, pl.ds(at, 8), :] = set_ref[b, 128:192, :].astype(F32).reshape(8, 8, 128)

    gain = norm_ref[0:1, :]
    offset = norm_ref[1:2, :]
    averager = averager_of()
    x = jnp.concatenate(
        [set_ref[b, 32 * g : 32 * g + 32, :] for g in range(4) for b in range(n_col)], axis=0
    )
    mean = mm(x, averager)
    present = mean < ABSENT / 2
    varied = x.astype(F32) - mean
    inverse = lax.rsqrt(mm((varied * varied).astype(BF), averager) + 1e-05)
    normed = varied * inverse
    if own_out:
        for g in range(4):
            own_out[0][32 * g : 32 * g + 32, :] = normed[128 * g : 128 * g + 32]
            own_out[1][32 * g : 32 * g + 32, :] = inverse[128 * g : 128 * g + 32]
    normal = jnp.where(present, normed * gain + offset, 0.0).astype(BF)
    rhs_out[:, 0:128] = normal
    rhs_out[:, 128:256] = normed.astype(BF)
    here = jnp.where(present, 1.0, 0.0)
    lane = lax.broadcasted_iota(jnp.int32, (128, 128), 1)
    found = jnp.zeros((128, 128), F32)
    for g in range(4):
        found = jnp.where(lane % 32 // 2 == 4 * a + g, here[128 * g : 128 * g + 128], found)
    found_out[...] = found
    for h in range(2):
        masked = jnp.concatenate(
            [normal[128 * g : 128 * g + 128] for g in (2 * h, 2 * h + 1)], axis=1
        )
        at = slice(128 * h, 128 * h + 128)
        left_out[:, at] = mm_nt(masked, back_ref[:128, :]).astype(BF)
        both = mm_nt(back_ref[...], masked)
        turn_scr[at, :] = both[128:]
        for k in range(2):
            leftt_out[64 * h + 32 * k : 64 * h + 32 * k + 32, :] = jnp.concatenate(
                [both[32 * k : 32 * k + 32], both[32 * k + 64 : 32 * k + 96]], axis=1
            ).astype(BF)

    for e in range(32):
        rightt_out[e] = turn_scr[pl.ds(e, 8, stride=32), :]

    pair = pair_out[...].reshape(256, 128).astype(BF)
    for n in range(2):
        pairs = jnp.concatenate(
            [diagonal_pair(pair[64 * p : 64 * p + 64]) for p in (2 * n, 2 * n + 1)], axis=0
        )
        grad = mm_nt(final_ref[...], pairs).astype(BF)
        for p in range(2):
            for q in range(8):
                rows = 64 * (2 * n + p)
                block = grad[64 * q : 64 * q + 64, 128 * p : 128 * p + 128]
                even, odd = interleave(block[:32], block[32:])
                grad_out[rows : rows + 32, 128 * q : 128 * q + 128] = even
                grad_out[rows + 32 : rows + 64, 128 * q : 128 * q + 128] = odd


def part_kernel(n_row, n_col, place_ref, last_ref, *refs):
    stages = [refs[7 * a : 7 * a + 7] for a in range(n_row - 1)]
    (
        normed_ref, inverse_ref, norm_ref, back_ref, final_ref, first_ref,
        emb_out, final_hbm_out, first_out, second_out, gain_out, offset_out, bias_out,
        right_scr, scaled_scr, grad_scr, outer_scr, wide_scr, all_scr,
        final_out, out_sem, turn_scr,
    ) = refs[7 * (n_row - 1) : -7]
    stages.append(refs[-7:])
    stage_kernel(
        n_col, n_row - 1, place_ref, last_ref, norm_ref, back_ref, final_ref, *stages[-1], turn_scr
    )
    gain = norm_ref[0:1, :]
    averager = averager_of()
    lane = lax.broadcasted_iota(jnp.int32, (128, 128), 1)

    found = sum(stage[6][...] for stage in stages)
    turned = pltpu.roll(found, 64, 1)
    mask = jnp.where((lane % 2 == 0) == (lane < 64), found, turned)
    mask_t = mask.T

    for e in range(32):
        right_scr[32 * e : 32 * e + 32, :] = jnp.concatenate(
            [stage[3][e] for stage in stages], axis=0
        ).astype(BF)

    mask_bf = mask.astype(BF)
    share = (1.0 / (mm_tn(mask_bf, mask_bf)[0:32] + 0.001)).astype(BF)
    for i in range(32):
        a, at = i // 8, 32 * (i % 8)
        for q in range(8):
            grad_scr[32 * i : 32 * i + 32, 128 * q : 128 * q + 128] = (
                stages[a][4][at : at + 32, 128 * q : 128 * q + 128] * share[i : i + 1]
            )
    left = jnp.concatenate([stage[1][...] for stage in stages], axis=1)
    right_grad = mm(left, grad_scr[...])
    left_grad = mm(grad_scr[...], right_scr[...])

    turn = spread(
        256, 256, lambda r, c: jnp.where((r // 8 == c % 32) & (r % 8 == c // 32), 1.0, 0.0)
    ).astype(BF)
    mask_two = jnp.concatenate([mask, mask], axis=1)
    right_in = [
        mm_nt(turn, (right_grad[:, 256 * q : 256 * q + 256] * mask_two).astype(BF))
        for q in range(4)
    ]
    for t in range(32):
        at = slice(128 * (t // 2), 128 * (t // 2) + 128)
        row = 32 * (t % 2)
        all_scr[row : row + 32, at] = (
            left_grad[32 * t : 32 * t + 32] * mask_t[t : t + 1]
        ).astype(BF)
        all_scr[row + 64 : row + 96, at] = jnp.concatenate(
            [part[8 * t : 8 * t + 8] for part in right_in], axis=0
        ).astype(BF)

    bias = jnp.zeros((1, 128), F32)
    ones = jnp.ones((128, 128), BF)
    for p in range(8):
        both_on = jnp.concatenate(
            [mask_t[0:32] * mask_t[i : i + 1] for i in range(4 * p, 4 * p + 4)], axis=0
        ).astype(BF)
        counts = mm(both_on, ones)
        pair = stages[p // 2][5][4 * (p % 2) : 4 * (p % 2) + 4]
        scaled = pair.reshape(128, 128) / (counts + 0.001)
        bias = bias + jnp.sum(scaled, axis=0, keepdims=True)
        scaled_scr[128 * p : 128 * p + 128, :] = scaled.astype(BF)
    bias_out[...] = bias

    left_t = jnp.concatenate([stage[2][...] for stage in stages], axis=0)
    for n in range(8):
        rights = jnp.concatenate(
            [diagonal_pair(right_scr[64 * p : 64 * p + 64, :]) for p in (2 * n, 2 * n + 1)], axis=0
        )
        outer = mm_nt(left_t, rights).astype(BF)
        for p in range(2):
            for q in range(8):
                rows = 64 * (2 * n + p)
                block = outer[64 * q : 64 * q + 64, 128 * p : 128 * p + 128]
                even, odd = interleave(block[:32], block[32:])
                outer_scr[rows : rows + 32, 128 * q : 128 * q + 128] = even
                outer_scr[rows + 32 : rows + 64, 128 * q : 128 * q + 128] = odd
    wide_scr[...] = mm(outer_scr[...], scaled_scr[...])
    for c in range(32):
        final_out[32 * c : 32 * c + 32, :] = wide_scr[pl.ds(c, 32, stride=32), :]
    final_send = pltpu.make_async_copy(final_out, final_hbm_out, out_sem)
    final_send.start()

    total = mm(
        all_scr[...], jnp.concatenate([stage[0][...] for stage in stages], axis=0)
    )
    sums = all_scr[:, 0:128].astype(F32)
    for g in range(1, 16):
        sums = sums + all_scr[:, 128 * g : 128 * g + 128].astype(F32)

    def fold(block):
        return block[0:32, 0:64] + block[32:64, 64:128]

    first_out[...] = fold(total[0:64, 0:128])
    second_out[...] = fold(total[64:128, 0:128])
    sums = jnp.sum(sums, axis=1, keepdims=True)
    left_sum = sums[0:32] + sums[32:64]
    right_sum = sums[64:96] + sums[96:128]
    first, second = first_ref[0:32, :], first_ref[32:64, :]
    gain_out[...] = jnp.sum(
        first * fold(total[0:64, 128:256]) + second * fold(total[64:128, 128:256]),
        axis=0, keepdims=True,
    )
    offset_out[...] = jnp.sum(first * left_sum + second * right_sum, axis=0, keepdims=True)

    d_hat = []
    for h in range(2):
        sides = [
            jnp.concatenate(
                [all_scr[row : row + 64, 128 * g : 128 * g + 128] for g in (2 * h, 2 * h + 1)], axis=0
            )
            for row in (0, 64)
        ]
        d_normal = mm_tn(jnp.concatenate(sides, axis=0), back_ref[...])
        d_hat += [d_normal[0:32, 0:128] * gain, d_normal[0:32, 128:256] * gain]
    d_hat = jnp.concatenate(d_hat, axis=0)
    normed = normed_ref[...]
    means = mm(jnp.concatenate([d_hat, d_hat * normed], axis=0).astype(BF), averager)
    result = inverse_ref[...] * (d_hat - means[:128] - normed * means[128:])
    for g in range(4):
        emb_out[:, 2 * g, :] = result[32 * g : 32 * g + 32, 0:64]
        emb_out[:, 2 * g + 1, :] = result[32 * g : 32 * g + 32, 64:128]
    final_send.wait()


def vmem(count):
    return [pl.BlockSpec(memory_space=pltpu.VMEM)] * count


LIMIT = pltpu.CompilerParams(vmem_limit_bytes=32 * 1024 * 1024)


def gathered_body(
    n_row,
    n_col,
    homolog_embedding,
    presence_indicator,
    coupling_change_derivative,
    standardizer_scale,
    standardizer_shift,
    first_projection_matrix,
    second_projection_matrix,
    final_projection_matrix,
):
    shards, tokens, features = homolog_embedding.shape
    width = first_projection_matrix.shape[1]
    first_t, second_t = first_projection_matrix.T, second_projection_matrix.T
    shape = lambda *dims: jax.ShapeDtypeStruct(dims, F32)
    held = lambda *dims: pltpu.VMEM(dims, F32)
    held_bf = lambda *dims: pltpu.VMEM(dims, BF)
    hbm = pl.BlockSpec(memory_space=pltpu.HBM)
    place = lax.bitwise_xor(lax.axis_index("row"), lax.axis_index("col"))
    place = place.astype(jnp.int32).reshape(1)
    packed = pl.pallas_call(
        pack_kernel,
        out_shape=held_bf(192, 128),
        in_specs=vmem(3),
        out_specs=vmem(1)[0],
    )(homolog_embedding, presence_indicator.T, coupling_change_derivative)
    def over(axis, size, step, array):
        return lax.ppermute(array, axis, [(k, k ^ step) for k in range(size)])

    far = over("col", n_col, 2, packed)
    last = over("col", n_col, 3, packed)
    near = over("col", n_col, 1, packed)
    front = jnp.stack([packed, near])
    chip_front = over("row", n_row, 2, front)
    rear = jnp.stack([last, far])
    chip_rear = over("row", n_row, 2, rear)
    rear, final_projection_matrix = lax.optimization_barrier((rear, final_projection_matrix))
    weights = pl.pallas_call(
        weights_kernel,
        out_shape=(
            held(8, 128), held_bf(256, 256), held_bf(width * width // 2, 256), held(2 * width, features),
        ),
        in_specs=[hbm] * 5,
        out_specs=tuple(vmem(4)),
        scratch_shapes=[
            pltpu.VMEM((1, features), F32),
            pltpu.VMEM((1, features), F32),
            pltpu.VMEM((width, features), BF),
            pltpu.VMEM((width, features), BF),
            pltpu.VMEM((width * width, 128), BF),
            pltpu.VMEM((width * width, 128), F32),
            pltpu.SemaphoreType.DMA((5,)),
        ],
        compiler_params=LIMIT,
    )(
        *[
            pltpu.with_memory_space_constraint(x, pltpu.HBM)
            for x in (
                standardizer_scale.reshape(1, features),
                standardizer_shift.reshape(1, features),
                first_t,
                second_t,
                final_projection_matrix,
            )
        ]
    )
    norm, back, final_turned, first = weights
    own = jnp.concatenate([front, rear])
    core = over("row", n_row, 1, own)
    stage_outs = [
        held_bf(512, 256), held_bf(128, 256), held_bf(128, 256), held(width, 8, 128),
        held_bf(256, 1024), held(8, 32, 128), held(128, 128),
    ]
    scalar = pl.BlockSpec(memory_space=pltpu.SMEM)

    def stage(a, block):
        outs = stage_outs + [held(128, 128)] * 2 * (a == 0)
        return pl.pallas_call(
            functools.partial(stage_kernel, n_col, a),
            out_shape=tuple(outs),
            in_specs=[scalar] + vmem(4),
            out_specs=tuple(vmem(len(outs))),
            scratch_shapes=[pltpu.VMEM((256, 128), F32)],
            compiler_params=LIMIT,
            cost_estimate=pl.CostEstimate(
                flops=1_000_000_000, bytes_accessed=4_000_000, transcendentals=0
            ),
        )(place, block, norm, back, final_turned)

    own_stage = stage(0, own)
    core_stage = stage(1, core)
    chip = jnp.concatenate([chip_front, chip_rear])
    chip, own_stage = lax.optimization_barrier((chip, own_stage))
    both = over("row", n_row, 1, chip)
    stages = [own_stage[:7], core_stage, stage(2, chip)]
    outs = pl.pallas_call(
        functools.partial(part_kernel, n_row, n_col),
        out_shape=(
            shape(shards, tokens, features),
            shape(width * width, 128),
            shape(width, features),
            shape(width, features),
            shape(1, features),
            shape(1, features),
            shape(1, 128),
        ),
        in_specs=[scalar] + vmem(7 * (n_row - 1) + 7),
        out_specs=(*vmem(1), hbm, *vmem(5)),
        scratch_shapes=[
            pltpu.VMEM((1024, 128), BF),
            pltpu.VMEM((1024, 128), BF),
            pltpu.VMEM((1024, 1024), BF),
            pltpu.VMEM((1024, 1024), BF),
            pltpu.VMEM((1024, 128), F32),
            pltpu.VMEM((128, 2048), BF),
            pltpu.VMEM((1024, 128), F32),
            pltpu.SemaphoreType.DMA,
            pltpu.VMEM((256, 128), F32),
            *stage_outs,
        ],
        compiler_params=LIMIT,
    )(place, both, *[x for s in stages for x in s], *own_stage[7:], norm, back, final_turned, first)
    emb, final, first, second, gain, offset, bias = outs
    return emb, final, first.T, second.T, gain.reshape(-1), offset.reshape(-1), bias.reshape(-1)


def body(n_row, n_col, *arguments):
    msa, _, pair = arguments[:3]
    width = arguments[5].shape[1]
    fits = (
        n_row == 4
        and n_col == 4
        and msa.shape == (32, 8, 64)
        and pair.shape == (8, 8, 128)
        and width == 32
    )
    if fits:
        return gathered_body(n_row, n_col, *arguments)
    return sharded_body(*arguments)


def solution(mesh):
    placed = (
        P(("grp", "col"), "row", None),
        P(("grp", "col"), "row"),
        P(("grp", "row"), "col", None),
        P(),
        P(),
        P(),
        P(),
        P(),
    )
    return jax.shard_map(
        functools.partial(body, mesh.shape["row"], mesh.shape["col"]),
        mesh=mesh,
        in_specs=placed,
        out_specs=(
            P(("grp", "col"), "row", None),
            P("grp", None),
            P("grp", None),
            P("grp", None),
            P("grp"),
            P("grp"),
            P("grp"),
        ),
        check_vma=False,
    )
```

```python
import functools

import jax
import jax.numpy as jnp
from jax import lax
from jax.experimental import pallas as pl
from jax.experimental.pallas import tpu as pltpu
from jax.sharding import PartitionSpec as P

TOKB = 2


def standardizer_parts(homolog_embedding, standardizer_scale, standardizer_shift):
    incoming_entries = homolog_embedding.astype(jnp.float32)
    center = jnp.mean(incoming_entries, axis=-1, keepdims=True)
    varied = incoming_entries - center
    variance = jnp.mean(varied * varied, axis=-1, keepdims=True)
    reciprocal_spread = lax.rsqrt(variance + 1e-05)
    standardized_entries = varied * reciprocal_spread
    standardized_bfloat = (standardized_entries * standardizer_scale + standardizer_shift).astype(
        jnp.bfloat16
    )
    return (standardized_entries, reciprocal_spread, standardized_bfloat)


def sharded_body(
    homolog_embedding,
    presence_indicator,
    coupling_change_derivative,
    standardizer_scale,
    standardizer_shift,
    first_projection_matrix,
    second_projection_matrix,
    final_projection_matrix,
):
    shard_homolog_number, residue_line_number, feature_number = homolog_embedding.shape
    tok_cols = coupling_change_derivative.shape[1]
    width = first_projection_matrix.shape[1]
    standardized_entries, reciprocal_spread, standardized_bfloat = standardizer_parts(
        homolog_embedding, standardizer_scale, standardizer_shift
    )
    mask_single_precision = presence_indicator.astype(jnp.float32)
    mask_half_precision = presence_indicator.astype(jnp.bfloat16)
    left = (
        jnp.einsum(
            "sic,cp->sip",
            standardized_bfloat,
            first_projection_matrix,
            preferred_element_type=jnp.float32,
        )
        * mask_single_precision[..., None]
    ).astype(jnp.bfloat16)
    right = (
        jnp.einsum(
            "sic,cp->sip",
            standardized_bfloat,
            second_projection_matrix,
            preferred_element_type=jnp.float32,
        )
        * mask_single_precision[..., None]
    ).astype(jnp.bfloat16)
    left_flat = left.reshape(shard_homolog_number, residue_line_number * width)
    right_flat = right.reshape(shard_homolog_number, residue_line_number * width)
    left_all, mask_left = (
        lax.all_gather(left_flat, "col", axis=0, tiled=True),
        lax.all_gather(mask_half_precision, "col", axis=0, tiled=True),
    )
    right_wide, mask_wide = (
        lax.all_gather(right_flat, "row", axis=1, tiled=True),
        lax.all_gather(mask_half_precision, "row", axis=1, tiled=True),
    )
    right_all, mask_right = (
        lax.all_to_all(right_wide, "col", split_axis=1, concat_axis=0, tiled=True),
        lax.all_to_all(mask_wide, "col", split_axis=1, concat_axis=0, tiled=True),
    )
    seq_total = left_all.shape[0]
    right_three = right_all.reshape(seq_total, tok_cols, width)
    counts = jnp.einsum("si,sj->ij", mask_left, mask_right, preferred_element_type=jnp.float32)
    scaled = coupling_change_derivative.astype(jnp.float32) / (counts + 0.001)[..., None]
    bias_part = jnp.sum(scaled, axis=(0, 1))
    scaled_bf = scaled.astype(jnp.bfloat16)
    block_rows = residue_line_number // TOKB
    right_acc = jnp.zeros((seq_total, tok_cols, width), jnp.float32)
    wout_acc = jnp.zeros(final_projection_matrix.shape, jnp.float32)
    left_pieces = []
    for block_index in range(TOKB):
        first = block_index * block_rows
        rows_bf = scaled_bf[first : first + block_rows]
        outer_grad = jnp.einsum(
            "ijz,fz->ijf", rows_bf, final_projection_matrix, preferred_element_type=jnp.float32
        ).astype(jnp.bfloat16)
        outer_grad = outer_grad.reshape(block_rows, tok_cols, width, width)
        left_block = left_all[:, first * width : (first + block_rows) * width].reshape(
            seq_total, block_rows, width
        )
        first_factor_derivative = jnp.einsum(
            "ijce,sje->sic", outer_grad, right_three, preferred_element_type=jnp.float32
        )
        right_acc = right_acc + jnp.einsum(
            "ijce,sic->sje", outer_grad, left_block, preferred_element_type=jnp.float32
        )
        outer = jnp.einsum(
            "sic,sje->ijce", left_block, right_three, preferred_element_type=jnp.float32
        ).astype(jnp.bfloat16)
        outer = outer.reshape(block_rows, tok_cols, width * width)
        wout_acc = wout_acc + jnp.einsum(
            "ijf,ijz->fz", outer, rows_bf, preferred_element_type=jnp.float32
        )
        first_factor_derivative = first_factor_derivative.reshape(seq_total, block_rows * width)
        left_pieces.append(first_factor_derivative)
    left_terms = jnp.concatenate(left_pieces, axis=1)
    left_own = lax.psum_scatter(left_terms, "col", scatter_dimension=0, tiled=True)
    right_spread = lax.all_to_all(
        right_acc.reshape(seq_total, tok_cols * width),
        "col",
        split_axis=0,
        concat_axis=1,
        tiled=True,
    )
    right_own = lax.psum_scatter(right_spread, "row", scatter_dimension=1, tiled=True)
    left_in = (
        left_own.reshape(shard_homolog_number, residue_line_number, width)
        * mask_single_precision[..., None]
    ).astype(jnp.bfloat16)
    right_in = (
        right_own.reshape(shard_homolog_number, residue_line_number, width)
        * mask_single_precision[..., None]
    ).astype(jnp.bfloat16)
    left_part = jnp.einsum(
        "sic,sip->cp", standardized_bfloat, left_in, preferred_element_type=jnp.float32
    )
    right_part = jnp.einsum(
        "sic,sip->cp", standardized_bfloat, right_in, preferred_element_type=jnp.float32
    )
    d_normal = jnp.einsum(
        "sip,cp->sic", left_in, first_projection_matrix, preferred_element_type=jnp.float32
    ) + jnp.einsum(
        "sip,cp->sic", right_in, second_projection_matrix, preferred_element_type=jnp.float32
    )
    gain_part = jnp.sum(d_normal * standardized_entries, axis=(0, 1))
    beta_part = jnp.sum(d_normal, axis=(0, 1))
    standardized_derivative = d_normal * standardizer_scale
    embedding_derivative = reciprocal_spread * (
        standardized_derivative
        - jnp.mean(standardized_derivative, axis=-1, keepdims=True)
        - standardized_entries
        * jnp.mean(standardized_derivative * standardized_entries, axis=-1, keepdims=True)
    )
    (
        final_matrix_derivative,
        first_matrix_derivative,
        second_matrix_derivative,
        scale_factor_derivative,
        shift_term_derivative,
        shift_derivative,
    ) = lax.psum((wout_acc, left_part, right_part, gain_part, beta_part, bias_part), ("row", "col"))
    return (
        embedding_derivative,
        final_matrix_derivative,
        first_matrix_derivative,
        second_matrix_derivative,
        scale_factor_derivative,
        shift_term_derivative,
        shift_derivative,
    )


BF = jnp.bfloat16
F32 = jnp.float32


def spread(rows, cols, rule):
    r = lax.broadcasted_iota(jnp.int32, (rows, cols), 0)
    c = lax.broadcasted_iota(jnp.int32, (rows, cols), 1)
    return rule(r, c)


def mm(a, b):
    return jnp.dot(a, b, preferred_element_type=F32)


def mm_nt(a, b):
    return lax.dot_general(a, b, (((1,), (1,)), ((), ())), preferred_element_type=F32)


def mm_tn(a, b):
    return lax.dot_general(a, b, (((0,), (0,)), ((), ())), preferred_element_type=F32)


def interleave(first, second):
    odd = lax.broadcasted_iota(jnp.int16, (32, 128), 1) & 32 != 0
    return (
        jnp.where(odd, pltpu.roll(second, 32, 1), first),
        jnp.where(odd, second, pltpu.roll(first, 96, 1)),
    )


def diagonal_pair(block):
    zero = jnp.zeros_like(block)
    return jnp.concatenate(
        [jnp.concatenate([block, zero], axis=1), jnp.concatenate([zero, block], axis=1)], axis=0
    )


ABSENT = 1024.0


def pack_kernel(msa_ref, mask_ref, pair_ref, out_ref):
    msa = msa_ref[...].astype(F32)
    pick = spread(8, 512, lambda r, c: jnp.where(c // 64 == r, 1.0, 0.0)).astype(BF)
    present = mm_tn(mask_ref[...].astype(F32).astype(BF), pick) > 0.5
    for g in range(4):
        rows = jnp.concatenate([msa[:, 2 * g, :], msa[:, 2 * g + 1, :]], axis=1)
        out_ref[32 * g : 32 * g + 32, :] = jnp.where(
            present[:, 128 * g : 128 * g + 128], rows, ABSENT
        ).astype(BF)
    out_ref[128:192, :] = pair_ref[...].astype(F32).reshape(64, 128).astype(BF)


def weights_kernel(*refs):
    sources, (norm_out, back_out, final_out, first_out) = refs[:5], refs[5:9]
    held, scr, sems = refs[9:14], refs[14], refs[15]
    copies = [pltpu.make_async_copy(sources[k], held[k], sems.at[k]) for k in range(5)]
    for copy in copies:
        copy.start()
    for copy in copies:
        copy.wait()
    gain_ref, offset_ref, first_ref, second_ref, final_ref = held
    norm_out[...] = jnp.concatenate(
        [
            jnp.concatenate([ref[...]] * 2, axis=1)
            for ref in (gain_ref, offset_ref, gain_ref, offset_ref) * 2
        ],
        axis=0,
    )
    for k, ref in enumerate((first_ref, second_ref)):
        narrow = ref[...].astype(F32)
        first_out[32 * k : 32 * k + 32, :] = narrow
        wide = jnp.concatenate([narrow] * 4, axis=1)
        wide = jnp.concatenate([wide] * 4, axis=0)
        own = spread(128, 256, lambda r, c: r // 32 == c // 64)
        back_out[128 * k : 128 * k + 128, :] = jnp.where(own, wide, 0.0).astype(BF)
    scr[...] = final_ref[...].astype(F32)
    for k in range(16):
        e = 4 * (k // 2) + k % 2
        final_out[32 * k : 32 * k + 32, :] = jnp.concatenate(
            [scr[pl.ds(e, 32, stride=32), :], scr[pl.ds(e + 2, 32, stride=32), :]], axis=1
        ).astype(BF)


def averager_of():
    return spread(128, 128, lambda r, c: jnp.where(r // 64 == c // 64, 1.0 / 64, 0.0)).astype(BF)


ORDER = (0, 3, 1, 2)


def stage_kernel(
    n_col, a, place_ref, set_ref, norm_ref, back_ref, final_ref,
    rhs_out, left_out, leftt_out, rightt_out, grad_out, pair_out, found_out, *rest
):
    *own_out, turn_scr = rest
    for b in range(n_col):
        at = pl.multiple_of(lax.bitwise_xor(place_ref[0], ORDER[b]) * 8, 8)
        pair_out[:, pl.ds(at, 8), :] = set_ref[b, 128:192, :].astype(F32).reshape(8, 8, 128)

    gain = norm_ref[0:1, :]
    offset = norm_ref[1:2, :]
    averager = averager_of()
    x = jnp.concatenate(
        [set_ref[b, 32 * g : 32 * g + 32, :] for g in range(4) for b in range(n_col)], axis=0
    )
    mean = mm(x, averager)
    present = mean < ABSENT / 2
    varied = x.astype(F32) - mean
    inverse = lax.rsqrt(mm((varied * varied).astype(BF), averager) + 1e-05)
    normed = varied * inverse
    if own_out:
        for g in range(4):
            own_out[0][32 * g : 32 * g + 32, :] = normed[128 * g : 128 * g + 32]
            own_out[1][32 * g : 32 * g + 32, :] = inverse[128 * g : 128 * g + 32]
    normal = jnp.where(present, normed * gain + offset, 0.0).astype(BF)
    rhs_out[:, 0:128] = normal
    rhs_out[:, 128:256] = normed.astype(BF)
    here = jnp.where(present, 1.0, 0.0)
    lane = lax.broadcasted_iota(jnp.int32, (128, 128), 1)
    found = jnp.zeros((128, 128), F32)
    for g in range(4):
        found = jnp.where(lane % 32 // 2 == 4 * a + g, here[128 * g : 128 * g + 128], found)
    found_out[...] = found
    for h in range(2):
        masked = jnp.concatenate(
            [normal[128 * g : 128 * g + 128] for g in (2 * h, 2 * h + 1)], axis=1
        )
        at = slice(128 * h, 128 * h + 128)
        left_out[:, at] = mm_nt(masked, back_ref[:128, :]).astype(BF)
        both = mm_nt(back_ref[...], masked)
        turn_scr[at, :] = both[128:]
        for k in range(2):
            leftt_out[64 * h + 32 * k : 64 * h + 32 * k + 32, :] = jnp.concatenate(
                [both[32 * k : 32 * k + 32], both[32 * k + 64 : 32 * k + 96]], axis=1
            ).astype(BF)

    for e in range(32):
        rightt_out[e] = turn_scr[pl.ds(e, 8, stride=32), :]

    pair = pair_out[...].reshape(256, 128).astype(BF)
    for n in range(2):
        pairs = jnp.concatenate(
            [diagonal_pair(pair[64 * p : 64 * p + 64]) for p in (2 * n, 2 * n + 1)], axis=0
        )
        grad = mm_nt(final_ref[...], pairs).astype(BF)
        for p in range(2):
            for q in range(8):
                rows = 64 * (2 * n + p)
                block = grad[64 * q : 64 * q + 64, 128 * p : 128 * p + 128]
                even, odd = interleave(block[:32], block[32:])
                grad_out[rows : rows + 32, 128 * q : 128 * q + 128] = even
                grad_out[rows + 32 : rows + 64, 128 * q : 128 * q + 128] = odd


def part_kernel(n_row, n_col, place_ref, last_ref, *refs):
    stages = [refs[7 * a : 7 * a + 7] for a in range(n_row - 1)]
    (
        normed_ref, inverse_ref, norm_ref, back_ref, final_ref, first_ref,
        emb_out, final_hbm_out, first_out, second_out, gain_out, offset_out, bias_out,
        right_scr, scaled_scr, grad_scr, outer_scr, wide_scr, all_scr,
        final_out, out_sem, turn_scr,
    ) = refs[7 * (n_row - 1) : -7]
    stages.append(refs[-7:])
    stage_kernel(
        n_col, n_row - 1, place_ref, last_ref, norm_ref, back_ref, final_ref, *stages[-1], turn_scr
    )
    gain = norm_ref[0:1, :]
    averager = averager_of()
    lane = lax.broadcasted_iota(jnp.int32, (128, 128), 1)

    found = sum(stage[6][...] for stage in stages)
    turned = pltpu.roll(found, 64, 1)
    mask = jnp.where((lane % 2 == 0) == (lane < 64), found, turned)
    mask_t = mask.T

    for e in range(32):
        right_scr[32 * e : 32 * e + 32, :] = jnp.concatenate(
            [stage[3][e] for stage in stages], axis=0
        ).astype(BF)

    mask_bf = mask.astype(BF)
    share = (1.0 / (mm_tn(mask_bf, mask_bf)[0:32] + 0.001)).astype(BF)
    for i in range(32):
        a, at = i // 8, 32 * (i % 8)
        for q in range(8):
            grad_scr[32 * i : 32 * i + 32, 128 * q : 128 * q + 128] = (
                stages[a][4][at : at + 32, 128 * q : 128 * q + 128] * share[i : i + 1]
            )
    left = jnp.concatenate([stage[1][...] for stage in stages], axis=1)
    right_grad = mm(left, grad_scr[...])
    left_grad = mm(grad_scr[...], right_scr[...])

    turn = spread(
        256, 256, lambda r, c: jnp.where((r // 8 == c % 32) & (r % 8 == c // 32), 1.0, 0.0)
    ).astype(BF)
    mask_two = jnp.concatenate([mask, mask], axis=1)
    right_in = [
        mm_nt(turn, (right_grad[:, 256 * q : 256 * q + 256] * mask_two).astype(BF))
        for q in range(4)
    ]
    for t in range(32):
        at = slice(128 * (t // 2), 128 * (t // 2) + 128)
        row = 32 * (t % 2)
        all_scr[row : row + 32, at] = (
            left_grad[32 * t : 32 * t + 32] * mask_t[t : t + 1]
        ).astype(BF)
        all_scr[row + 64 : row + 96, at] = jnp.concatenate(
            [part[8 * t : 8 * t + 8] for part in right_in], axis=0
        ).astype(BF)

    bias = jnp.zeros((1, 128), F32)
    ones = jnp.ones((128, 128), BF)
    for p in range(8):
        both_on = jnp.concatenate(
            [mask_t[0:32] * mask_t[i : i + 1] for i in range(4 * p, 4 * p + 4)], axis=0
        ).astype(BF)
        counts = mm(both_on, ones)
        pair = stages[p // 2][5][4 * (p % 2) : 4 * (p % 2) + 4]
        scaled = pair.reshape(128, 128) / (counts + 0.001)
        bias = bias + jnp.sum(scaled, axis=0, keepdims=True)
        scaled_scr[128 * p : 128 * p + 128, :] = scaled.astype(BF)
    bias_out[...] = bias

    left_t = jnp.concatenate([stage[2][...] for stage in stages], axis=0)
    for n in range(8):
        rights = jnp.concatenate(
            [diagonal_pair(right_scr[64 * p : 64 * p + 64, :]) for p in (2 * n, 2 * n + 1)], axis=0
        )
        outer = mm_nt(left_t, rights).astype(BF)
        for p in range(2):
            for q in range(8):
                rows = 64 * (2 * n + p)
                block = outer[64 * q : 64 * q + 64, 128 * p : 128 * p + 128]
                even, odd = interleave(block[:32], block[32:])
                outer_scr[rows : rows + 32, 128 * q : 128 * q + 128] = even
                outer_scr[rows + 32 : rows + 64, 128 * q : 128 * q + 128] = odd
    wide_scr[...] = mm(outer_scr[...], scaled_scr[...])
    for c in range(32):
        final_out[32 * c : 32 * c + 32, :] = wide_scr[pl.ds(c, 32, stride=32), :]
    final_send = pltpu.make_async_copy(final_out, final_hbm_out, out_sem)
    final_send.start()

    total = mm(
        all_scr[...], jnp.concatenate([stage[0][...] for stage in stages], axis=0)
    )
    sums = all_scr[:, 0:128].astype(F32)
    for g in range(1, 16):
        sums = sums + all_scr[:, 128 * g : 128 * g + 128].astype(F32)

    def fold(block):
        return block[0:32, 0:64] + block[32:64, 64:128]

    first_out[...] = fold(total[0:64, 0:128])
    second_out[...] = fold(total[64:128, 0:128])
    sums = jnp.sum(sums, axis=1, keepdims=True)
    left_sum = sums[0:32] + sums[32:64]
    right_sum = sums[64:96] + sums[96:128]
    first, second = first_ref[0:32, :], first_ref[32:64, :]
    gain_out[...] = jnp.sum(
        first * fold(total[0:64, 128:256]) + second * fold(total[64:128, 128:256]),
        axis=0, keepdims=True,
    )
    offset_out[...] = jnp.sum(first * left_sum + second * right_sum, axis=0, keepdims=True)

    d_hat = []
    for h in range(2):
        sides = [
            jnp.concatenate(
                [all_scr[row : row + 64, 128 * g : 128 * g + 128] for g in (2 * h, 2 * h + 1)], axis=0
            )
            for row in (0, 64)
        ]
        d_normal = mm_tn(jnp.concatenate(sides, axis=0), back_ref[...])
        d_hat += [d_normal[0:32, 0:128] * gain, d_normal[0:32, 128:256] * gain]
    d_hat = jnp.concatenate(d_hat, axis=0)
    normed = normed_ref[...]
    means = mm(jnp.concatenate([d_hat, d_hat * normed], axis=0).astype(BF), averager)
    result = inverse_ref[...] * (d_hat - means[:128] - normed * means[128:])
    for g in range(4):
        emb_out[:, 2 * g, :] = result[32 * g : 32 * g + 32, 0:64]
        emb_out[:, 2 * g + 1, :] = result[32 * g : 32 * g + 32, 64:128]
    final_send.wait()


def vmem(count):
    return [pl.BlockSpec(memory_space=pltpu.VMEM)] * count


LIMIT = pltpu.CompilerParams(vmem_limit_bytes=32 * 1024 * 1024)


def gathered_body(
    n_row,
    n_col,
    homolog_embedding,
    presence_indicator,
    coupling_change_derivative,
    standardizer_scale,
    standardizer_shift,
    first_projection_matrix,
    second_projection_matrix,
    final_projection_matrix,
):
    shards, tokens, features = homolog_embedding.shape
    width = first_projection_matrix.shape[1]
    first_t, second_t = first_projection_matrix.T, second_projection_matrix.T
    shape = lambda *dims: jax.ShapeDtypeStruct(dims, F32)
    held = lambda *dims: pltpu.VMEM(dims, F32)
    held_bf = lambda *dims: pltpu.VMEM(dims, BF)
    hbm = pl.BlockSpec(memory_space=pltpu.HBM)
    place = lax.bitwise_xor(lax.axis_index("row"), lax.axis_index("col"))
    place = place.astype(jnp.int32).reshape(1)
    packed = pl.pallas_call(
        pack_kernel,
        out_shape=held_bf(192, 128),
        in_specs=vmem(3),
        out_specs=vmem(1)[0],
    )(homolog_embedding, presence_indicator.T, coupling_change_derivative)
    def over(axis, size, step, array):
        return lax.ppermute(array, axis, [(k, k ^ step) for k in range(size)])

    far = over("col", n_col, 2, packed)
    near = over("col", n_col, 1, packed)
    last = over("col", n_col, 3, packed)
    front = jnp.stack([packed, last])
    chip_front = over("row", n_row, 2, front)
    rear = jnp.stack([near, far])
    chip_rear = over("row", n_row, 2, rear)
    front, final_projection_matrix = lax.optimization_barrier((front, final_projection_matrix))
    weights = pl.pallas_call(
        weights_kernel,
        out_shape=(
            held(8, 128), held_bf(256, 256), held_bf(width * width // 2, 256), held(2 * width, features),
        ),
        in_specs=[hbm] * 5,
        out_specs=tuple(vmem(4)),
        scratch_shapes=[
            pltpu.VMEM((1, features), F32),
            pltpu.VMEM((1, features), F32),
            pltpu.VMEM((width, features), BF),
            pltpu.VMEM((width, features), BF),
            pltpu.VMEM((width * width, 128), BF),
            pltpu.VMEM((width * width, 128), F32),
            pltpu.SemaphoreType.DMA((5,)),
        ],
        compiler_params=LIMIT,
    )(
        *[
            pltpu.with_memory_space_constraint(x, pltpu.HBM)
            for x in (
                standardizer_scale.reshape(1, features),
                standardizer_shift.reshape(1, features),
                first_t,
                second_t,
                final_projection_matrix,
            )
        ]
    )
    norm, back, final_turned, first = weights
    own = jnp.concatenate([front, rear])
    core = over("row", n_row, 1, own)
    stage_outs = [
        held_bf(512, 256), held_bf(128, 256), held_bf(128, 256), held(width, 8, 128),
        held_bf(256, 1024), held(8, 32, 128), held(128, 128),
    ]
    scalar = pl.BlockSpec(memory_space=pltpu.SMEM)

    def stage(a, block):
        outs = stage_outs + [held(128, 128)] * 2 * (a == 0)
        return pl.pallas_call(
            functools.partial(stage_kernel, n_col, a),
            out_shape=tuple(outs),
            in_specs=[scalar] + vmem(4),
            out_specs=tuple(vmem(len(outs))),
            scratch_shapes=[pltpu.VMEM((256, 128), F32)],
            compiler_params=LIMIT,
            cost_estimate=pl.CostEstimate(
                flops=1_000_000_000, bytes_accessed=4_000_000, transcendentals=0
            ),
        )(place, block, norm, back, final_turned)

    own_stage = stage(0, own)
    core_stage = stage(1, core)
    chip = jnp.concatenate([chip_front, chip_rear])
    chip, own_stage = lax.optimization_barrier((chip, own_stage))
    both = over("row", n_row, 1, chip)
    stages = [own_stage[:7], core_stage, stage(2, chip)]
    outs = pl.pallas_call(
        functools.partial(part_kernel, n_row, n_col),
        out_shape=(
            shape(shards, tokens, features),
            shape(width * width, 128),
            shape(width, features),
            shape(width, features),
            shape(1, features),
            shape(1, features),
            shape(1, 128),
        ),
        in_specs=[scalar] + vmem(7 * (n_row - 1) + 7),
        out_specs=(*vmem(1), hbm, *vmem(5)),
        scratch_shapes=[
            pltpu.VMEM((1024, 128), BF),
            pltpu.VMEM((1024, 128), BF),
            pltpu.VMEM((1024, 1024), BF),
            pltpu.VMEM((1024, 1024), BF),
            pltpu.VMEM((1024, 128), F32),
            pltpu.VMEM((128, 2048), BF),
            pltpu.VMEM((1024, 128), F32),
            pltpu.SemaphoreType.DMA,
            pltpu.VMEM((256, 128), F32),
            *stage_outs,
        ],
        compiler_params=LIMIT,
    )(place, both, *[x for s in stages for x in s], *own_stage[7:], norm, back, final_turned, first)
    emb, final, first, second, gain, offset, bias = outs
    return emb, final, first.T, second.T, gain.reshape(-1), offset.reshape(-1), bias.reshape(-1)


def body(n_row, n_col, *arguments):
    msa, _, pair = arguments[:3]
    width = arguments[5].shape[1]
    fits = (
        n_row == 4
        and n_col == 4
        and msa.shape == (32, 8, 64)
        and pair.shape == (8, 8, 128)
        and width == 32
    )
    if fits:
        return gathered_body(n_row, n_col, *arguments)
    return sharded_body(*arguments)


def solution(mesh):
    placed = (
        P(("grp", "col"), "row", None),
        P(("grp", "col"), "row"),
        P(("grp", "row"), "col", None),
        P(),
        P(),
        P(),
        P(),
        P(),
    )
    return jax.shard_map(
        functools.partial(body, mesh.shape["row"], mesh.shape["col"]),
        mesh=mesh,
        in_specs=placed,
        out_specs=(
            P(("grp", "col"), "row", None),
            P("grp", None),
            P("grp", None),
            P("grp", None),
            P("grp"),
            P("grp"),
            P("grp"),
        ),
        check_vma=False,
    )
```

```python
import functools

import jax
import jax.numpy as jnp
from jax import lax
from jax.experimental import pallas as pl
from jax.experimental.pallas import tpu as pltpu
from jax.sharding import PartitionSpec as P

TOKB = 2


def standardizer_parts(homolog_embedding, standardizer_scale, standardizer_shift):
    incoming_entries = homolog_embedding.astype(jnp.float32)
    center = jnp.mean(incoming_entries, axis=-1, keepdims=True)
    varied = incoming_entries - center
    variance = jnp.mean(varied * varied, axis=-1, keepdims=True)
    reciprocal_spread = lax.rsqrt(variance + 1e-05)
    standardized_entries = varied * reciprocal_spread
    standardized_bfloat = (standardized_entries * standardizer_scale + standardizer_shift).astype(
        jnp.bfloat16
    )
    return (standardized_entries, reciprocal_spread, standardized_bfloat)


def sharded_body(
    homolog_embedding,
    presence_indicator,
    coupling_change_derivative,
    standardizer_scale,
    standardizer_shift,
    first_projection_matrix,
    second_projection_matrix,
    final_projection_matrix,
):
    shard_homolog_number, residue_line_number, feature_number = homolog_embedding.shape
    tok_cols = coupling_change_derivative.shape[1]
    width = first_projection_matrix.shape[1]
    standardized_entries, reciprocal_spread, standardized_bfloat = standardizer_parts(
        homolog_embedding, standardizer_scale, standardizer_shift
    )
    mask_single_precision = presence_indicator.astype(jnp.float32)
    mask_half_precision = presence_indicator.astype(jnp.bfloat16)
    left = (
        jnp.einsum(
            "sic,cp->sip",
            standardized_bfloat,
            first_projection_matrix,
            preferred_element_type=jnp.float32,
        )
        * mask_single_precision[..., None]
    ).astype(jnp.bfloat16)
    right = (
        jnp.einsum(
            "sic,cp->sip",
            standardized_bfloat,
            second_projection_matrix,
            preferred_element_type=jnp.float32,
        )
        * mask_single_precision[..., None]
    ).astype(jnp.bfloat16)
    left_flat = left.reshape(shard_homolog_number, residue_line_number * width)
    right_flat = right.reshape(shard_homolog_number, residue_line_number * width)
    left_all, mask_left = (
        lax.all_gather(left_flat, "col", axis=0, tiled=True),
        lax.all_gather(mask_half_precision, "col", axis=0, tiled=True),
    )
    right_wide, mask_wide = (
        lax.all_gather(right_flat, "row", axis=1, tiled=True),
        lax.all_gather(mask_half_precision, "row", axis=1, tiled=True),
    )
    right_all, mask_right = (
        lax.all_to_all(right_wide, "col", split_axis=1, concat_axis=0, tiled=True),
        lax.all_to_all(mask_wide, "col", split_axis=1, concat_axis=0, tiled=True),
    )
    seq_total = left_all.shape[0]
    right_three = right_all.reshape(seq_total, tok_cols, width)
    counts = jnp.einsum("si,sj->ij", mask_left, mask_right, preferred_element_type=jnp.float32)
    scaled = coupling_change_derivative.astype(jnp.float32) / (counts + 0.001)[..., None]
    bias_part = jnp.sum(scaled, axis=(0, 1))
    scaled_bf = scaled.astype(jnp.bfloat16)
    block_rows = residue_line_number // TOKB
    right_acc = jnp.zeros((seq_total, tok_cols, width), jnp.float32)
    wout_acc = jnp.zeros(final_projection_matrix.shape, jnp.float32)
    left_pieces = []
    for block_index in range(TOKB):
        first = block_index * block_rows
        rows_bf = scaled_bf[first : first + block_rows]
        outer_grad = jnp.einsum(
            "ijz,fz->ijf", rows_bf, final_projection_matrix, preferred_element_type=jnp.float32
        ).astype(jnp.bfloat16)
        outer_grad = outer_grad.reshape(block_rows, tok_cols, width, width)
        left_block = left_all[:, first * width : (first + block_rows) * width].reshape(
            seq_total, block_rows, width
        )
        first_factor_derivative = jnp.einsum(
            "ijce,sje->sic", outer_grad, right_three, preferred_element_type=jnp.float32
        )
        right_acc = right_acc + jnp.einsum(
            "ijce,sic->sje", outer_grad, left_block, preferred_element_type=jnp.float32
        )
        outer = jnp.einsum(
            "sic,sje->ijce", left_block, right_three, preferred_element_type=jnp.float32
        ).astype(jnp.bfloat16)
        outer = outer.reshape(block_rows, tok_cols, width * width)
        wout_acc = wout_acc + jnp.einsum(
            "ijf,ijz->fz", outer, rows_bf, preferred_element_type=jnp.float32
        )
        first_factor_derivative = first_factor_derivative.reshape(seq_total, block_rows * width)
        left_pieces.append(first_factor_derivative)
    left_terms = jnp.concatenate(left_pieces, axis=1)
    left_own = lax.psum_scatter(left_terms, "col", scatter_dimension=0, tiled=True)
    right_spread = lax.all_to_all(
        right_acc.reshape(seq_total, tok_cols * width),
        "col",
        split_axis=0,
        concat_axis=1,
        tiled=True,
    )
    right_own = lax.psum_scatter(right_spread, "row", scatter_dimension=1, tiled=True)
    left_in = (
        left_own.reshape(shard_homolog_number, residue_line_number, width)
        * mask_single_precision[..., None]
    ).astype(jnp.bfloat16)
    right_in = (
        right_own.reshape(shard_homolog_number, residue_line_number, width)
        * mask_single_precision[..., None]
    ).astype(jnp.bfloat16)
    left_part = jnp.einsum(
        "sic,sip->cp", standardized_bfloat, left_in, preferred_element_type=jnp.float32
    )
    right_part = jnp.einsum(
        "sic,sip->cp", standardized_bfloat, right_in, preferred_element_type=jnp.float32
    )
    d_normal = jnp.einsum(
        "sip,cp->sic", left_in, first_projection_matrix, preferred_element_type=jnp.float32
    ) + jnp.einsum(
        "sip,cp->sic", right_in, second_projection_matrix, preferred_element_type=jnp.float32
    )
    gain_part = jnp.sum(d_normal * standardized_entries, axis=(0, 1))
    beta_part = jnp.sum(d_normal, axis=(0, 1))
    standardized_derivative = d_normal * standardizer_scale
    embedding_derivative = reciprocal_spread * (
        standardized_derivative
        - jnp.mean(standardized_derivative, axis=-1, keepdims=True)
        - standardized_entries
        * jnp.mean(standardized_derivative * standardized_entries, axis=-1, keepdims=True)
    )
    (
        final_matrix_derivative,
        first_matrix_derivative,
        second_matrix_derivative,
        scale_factor_derivative,
        shift_term_derivative,
        shift_derivative,
    ) = lax.psum((wout_acc, left_part, right_part, gain_part, beta_part, bias_part), ("row", "col"))
    return (
        embedding_derivative,
        final_matrix_derivative,
        first_matrix_derivative,
        second_matrix_derivative,
        scale_factor_derivative,
        shift_term_derivative,
        shift_derivative,
    )


BF = jnp.bfloat16
F32 = jnp.float32


def spread(rows, cols, rule):
    r = lax.broadcasted_iota(jnp.int32, (rows, cols), 0)
    c = lax.broadcasted_iota(jnp.int32, (rows, cols), 1)
    return rule(r, c)


def mm(a, b):
    return jnp.dot(a, b, preferred_element_type=F32)


def mm_nt(a, b):
    return lax.dot_general(a, b, (((1,), (1,)), ((), ())), preferred_element_type=F32)


def mm_tn(a, b):
    return lax.dot_general(a, b, (((0,), (0,)), ((), ())), preferred_element_type=F32)


def interleave(first, second):
    odd = lax.broadcasted_iota(jnp.int16, (32, 128), 1) & 32 != 0
    return (
        jnp.where(odd, pltpu.roll(second, 32, 1), first),
        jnp.where(odd, second, pltpu.roll(first, 96, 1)),
    )


def diagonal_pair(block):
    zero = jnp.zeros_like(block)
    return jnp.concatenate(
        [jnp.concatenate([block, zero], axis=1), jnp.concatenate([zero, block], axis=1)], axis=0
    )


ABSENT = 1024.0


def pack_kernel(msa_ref, mask_ref, pair_ref, out_ref):
    msa = msa_ref[...].astype(F32)
    pick = spread(8, 512, lambda r, c: jnp.where(c // 64 == r, 1.0, 0.0)).astype(BF)
    present = mm_tn(mask_ref[...].astype(F32).astype(BF), pick) > 0.5
    for g in range(4):
        rows = jnp.concatenate([msa[:, 2 * g, :], msa[:, 2 * g + 1, :]], axis=1)
        out_ref[32 * g : 32 * g + 32, :] = jnp.where(
            present[:, 128 * g : 128 * g + 128], rows, ABSENT
        ).astype(BF)
    out_ref[128:192, :] = pair_ref[...].astype(F32).reshape(64, 128).astype(BF)


def weights_kernel(*refs):
    sources, (norm_out, back_out, final_out, first_out) = refs[:5], refs[5:9]
    held, scr, sems = refs[9:14], refs[14], refs[15]
    copies = [pltpu.make_async_copy(sources[k], held[k], sems.at[k]) for k in range(5)]
    for copy in copies:
        copy.start()
    for copy in copies:
        copy.wait()
    gain_ref, offset_ref, first_ref, second_ref, final_ref = held
    norm_out[...] = jnp.concatenate(
        [
            jnp.concatenate([ref[...]] * 2, axis=1)
            for ref in (gain_ref, offset_ref, gain_ref, offset_ref) * 2
        ],
        axis=0,
    )
    for k, ref in enumerate((first_ref, second_ref)):
        narrow = ref[...].astype(F32)
        first_out[32 * k : 32 * k + 32, :] = narrow
        wide = jnp.concatenate([narrow] * 4, axis=1)
        wide = jnp.concatenate([wide] * 4, axis=0)
        own = spread(128, 256, lambda r, c: r // 32 == c // 64)
        back_out[128 * k : 128 * k + 128, :] = jnp.where(own, wide, 0.0).astype(BF)
    scr[...] = final_ref[...].astype(F32)
    for k in range(16):
        e = 4 * (k // 2) + k % 2
        final_out[32 * k : 32 * k + 32, :] = jnp.concatenate(
            [scr[pl.ds(e, 32, stride=32), :], scr[pl.ds(e + 2, 32, stride=32), :]], axis=1
        ).astype(BF)


def averager_of():
    return spread(128, 128, lambda r, c: jnp.where(r // 64 == c // 64, 1.0 / 64, 0.0)).astype(BF)


ORDER = (0, 3, 1, 2)


def stage_kernel(
    n_col, a, place_ref, set_ref, norm_ref, back_ref, final_ref,
    rhs_out, left_out, leftt_out, rightt_out, grad_out, pair_out, found_out, *rest
):
    *own_out, turn_scr = rest
    for b in range(n_col):
        at = pl.multiple_of(lax.bitwise_xor(place_ref[0], ORDER[b]) * 8, 8)
        pair_out[:, pl.ds(at, 8), :] = set_ref[b, 128:192, :].astype(F32).reshape(8, 8, 128)

    gain = norm_ref[0:1, :]
    offset = norm_ref[1:2, :]
    averager = averager_of()
    x = jnp.concatenate(
        [set_ref[b, 32 * g : 32 * g + 32, :] for g in range(4) for b in range(n_col)], axis=0
    )
    mean = mm(x, averager)
    present = mean < ABSENT / 2
    varied = x.astype(F32) - mean
    inverse = lax.rsqrt(mm((varied * varied).astype(BF), averager) + 1e-05)
    normed = varied * inverse
    if own_out:
        for g in range(4):
            own_out[0][32 * g : 32 * g + 32, :] = normed[128 * g : 128 * g + 32]
            own_out[1][32 * g : 32 * g + 32, :] = inverse[128 * g : 128 * g + 32]
    normal = jnp.where(present, normed * gain + offset, 0.0).astype(BF)
    rhs_out[:, 0:128] = normal
    rhs_out[:, 128:256] = normed.astype(BF)
    here = jnp.where(present, 1.0, 0.0)
    lane = lax.broadcasted_iota(jnp.int32, (128, 128), 1)
    found = jnp.zeros((128, 128), F32)
    for g in range(4):
        found = jnp.where(lane % 32 // 2 == 4 * a + g, here[128 * g : 128 * g + 128], found)
    found_out[...] = found
    for h in range(2):
        masked = jnp.concatenate(
            [normal[128 * g : 128 * g + 128] for g in (2 * h, 2 * h + 1)], axis=1
        )
        at = slice(128 * h, 128 * h + 128)
        left_out[:, at] = mm_nt(masked, back_ref[:128, :]).astype(BF)
        both = mm_nt(back_ref[...], masked)
        turn_scr[at, :] = both[128:]
        for k in range(2):
            leftt_out[64 * h + 32 * k : 64 * h + 32 * k + 32, :] = jnp.concatenate(
                [both[32 * k : 32 * k + 32], both[32 * k + 64 : 32 * k + 96]], axis=1
            ).astype(BF)

    for e in range(32):
        rightt_out[e] = turn_scr[pl.ds(e, 8, stride=32), :]

    pair = pair_out[...].reshape(256, 128).astype(BF)
    for n in range(2):
        pairs = jnp.concatenate(
            [diagonal_pair(pair[64 * p : 64 * p + 64]) for p in (2 * n, 2 * n + 1)], axis=0
        )
        grad = mm_nt(final_ref[...], pairs).astype(BF)
        for p in range(2):
            for q in range(8):
                rows = 64 * (2 * n + p)
                block = grad[64 * q : 64 * q + 64, 128 * p : 128 * p + 128]
                even, odd = interleave(block[:32], block[32:])
                grad_out[rows : rows + 32, 128 * q : 128 * q + 128] = even
                grad_out[rows + 32 : rows + 64, 128 * q : 128 * q + 128] = odd


def part_kernel(n_row, n_col, place_ref, last_ref, *refs):
    stages = [refs[7 * a : 7 * a + 7] for a in range(n_row - 1)]
    (
        normed_ref, inverse_ref, norm_ref, back_ref, final_ref, first_ref,
        emb_out, final_hbm_out, first_out, second_out, gain_out, offset_out, bias_out,
        right_scr, scaled_scr, grad_scr, outer_scr, all_scr,
        final_out, out_sem, turn_scr,
    ) = refs[7 * (n_row - 1) : -7]
    stages.append(refs[-7:])
    stage_kernel(
        n_col, n_row - 1, place_ref, last_ref, norm_ref, back_ref, final_ref, *stages[-1], turn_scr
    )
    gain = norm_ref[0:1, :]
    averager = averager_of()
    lane = lax.broadcasted_iota(jnp.int32, (128, 128), 1)

    found = sum(stage[6][...] for stage in stages)
    turned = pltpu.roll(found, 64, 1)
    mask = jnp.where((lane % 2 == 0) == (lane < 64), found, turned)
    mask_t = mask.T

    for e in range(32):
        right_scr[32 * e : 32 * e + 32, :] = jnp.concatenate(
            [stage[3][e] for stage in stages], axis=0
        ).astype(BF)

    mask_bf = mask.astype(BF)
    share = 1.0 / (mm_tn(mask_bf, mask_bf)[0:32] + 0.001)
    share_bf = share.astype(BF)
    for i in range(32):
        a, at = i // 8, 32 * (i % 8)
        for q in range(8):
            grad_scr[32 * i : 32 * i + 32, 128 * q : 128 * q + 128] = (
                stages[a][4][at : at + 32, 128 * q : 128 * q + 128] * share_bf[i : i + 1]
            )
    left = jnp.concatenate([stage[1][...] for stage in stages], axis=1)
    right_grad = mm(left, grad_scr[...])
    left_grad = mm(grad_scr[...], right_scr[...])

    turn = spread(
        256, 256, lambda r, c: jnp.where((r // 8 == c % 32) & (r % 8 == c // 32), 1.0, 0.0)
    ).astype(BF)
    mask_two = jnp.concatenate([mask, mask], axis=1)
    right_in = [
        mm_nt(turn, (right_grad[:, 256 * q : 256 * q + 256] * mask_two).astype(BF))
        for q in range(4)
    ]
    for t in range(32):
        at = slice(128 * (t // 2), 128 * (t // 2) + 128)
        row = 32 * (t % 2)
        all_scr[row : row + 32, at] = (
            left_grad[32 * t : 32 * t + 32] * mask_t[t : t + 1]
        ).astype(BF)
        all_scr[row + 64 : row + 96, at] = jnp.concatenate(
            [part[8 * t : 8 * t + 8] for part in right_in], axis=0
        ).astype(BF)

    bias = jnp.zeros((32, 128), F32)
    zero = jnp.zeros((32, 128), BF)
    for k in range(16):
        for half in range(2):
            i = 4 * (k // 2) + k % 2 + 2 * half
            scaled = stages[i // 8][5][i % 8] * jnp.broadcast_to(share[:, i : i + 1], (32, 128))
            bias = bias + scaled
            scaled = scaled.astype(BF)
            at = 128 * k + 64 * half
            scaled_scr[at : at + 32, 0:128] = scaled
            scaled_scr[at : at + 32, 128:256] = zero
            scaled_scr[at + 32 : at + 64, 0:128] = zero
            scaled_scr[at + 32 : at + 64, 128:256] = scaled
    bias_out[...] = jnp.sum(bias, axis=0, keepdims=True)

    left_t = jnp.concatenate([stage[2][...] for stage in stages], axis=0)
    for n in range(8):
        rights = jnp.concatenate(
            [diagonal_pair(right_scr[64 * p : 64 * p + 64, :]) for p in (2 * n, 2 * n + 1)], axis=0
        )
        outer = mm_nt(left_t, rights).astype(BF)
        for p in range(2):
            rows = 32 * (2 * n + p)
            for k in range(16):
                outer_scr[rows : rows + 32, 128 * k : 128 * k + 128] = (
                    outer[32 * k : 32 * k + 32, 128 * p : 128 * p + 128]
                )
    final = mm(outer_scr[...], scaled_scr[...])
    for e in range(32):
        final_out[pl.ds(e, 32, stride=32), :] = (
            final[32 * (e // 2) : 32 * (e // 2) + 32, 128 * (e % 2) : 128 * (e % 2) + 128]
        )
    final_send = pltpu.make_async_copy(final_out, final_hbm_out, out_sem)
    final_send.start()

    total = mm(
        all_scr[...], jnp.concatenate([stage[0][...] for stage in stages], axis=0)
    )
    sums = all_scr[:, 0:128].astype(F32)
    for g in range(1, 16):
        sums = sums + all_scr[:, 128 * g : 128 * g + 128].astype(F32)

    def fold(block):
        return block[0:32, 0:64] + block[32:64, 64:128]

    first_out[...] = fold(total[0:64, 0:128])
    second_out[...] = fold(total[64:128, 0:128])
    sums = jnp.sum(sums, axis=1, keepdims=True)
    left_sum = sums[0:32] + sums[32:64]
    right_sum = sums[64:96] + sums[96:128]
    first, second = first_ref[0:32, :], first_ref[32:64, :]
    gain_out[...] = jnp.sum(
        first * fold(total[0:64, 128:256]) + second * fold(total[64:128, 128:256]),
        axis=0, keepdims=True,
    )
    offset_out[...] = jnp.sum(first * left_sum + second * right_sum, axis=0, keepdims=True)

    d_hat = []
    for h in range(2):
        sides = [
            jnp.concatenate(
                [all_scr[row : row + 64, 128 * g : 128 * g + 128] for g in (2 * h, 2 * h + 1)], axis=0
            )
            for row in (0, 64)
        ]
        d_normal = mm_tn(jnp.concatenate(sides, axis=0), back_ref[...])
        d_hat += [d_normal[0:32, 0:128] * gain, d_normal[0:32, 128:256] * gain]
    d_hat = jnp.concatenate(d_hat, axis=0)
    normed = normed_ref[...]
    means = mm(jnp.concatenate([d_hat, d_hat * normed], axis=0).astype(BF), averager)
    result = inverse_ref[...] * (d_hat - means[:128] - normed * means[128:])
    for g in range(4):
        emb_out[:, 2 * g, :] = result[32 * g : 32 * g + 32, 0:64]
        emb_out[:, 2 * g + 1, :] = result[32 * g : 32 * g + 32, 64:128]
    final_send.wait()


def vmem(count):
    return [pl.BlockSpec(memory_space=pltpu.VMEM)] * count


LIMIT = pltpu.CompilerParams(vmem_limit_bytes=32 * 1024 * 1024)


def gathered_body(
    n_row,
    n_col,
    homolog_embedding,
    presence_indicator,
    coupling_change_derivative,
    standardizer_scale,
    standardizer_shift,
    first_projection_matrix,
    second_projection_matrix,
    final_projection_matrix,
):
    shards, tokens, features = homolog_embedding.shape
    width = first_projection_matrix.shape[1]
    first_t, second_t = first_projection_matrix.T, second_projection_matrix.T
    shape = lambda *dims: jax.ShapeDtypeStruct(dims, F32)
    held = lambda *dims: pltpu.VMEM(dims, F32)
    held_bf = lambda *dims: pltpu.VMEM(dims, BF)
    hbm = pl.BlockSpec(memory_space=pltpu.HBM)
    place = lax.bitwise_xor(lax.axis_index("row"), lax.axis_index("col"))
    place = place.astype(jnp.int32).reshape(1)
    packed = pl.pallas_call(
        pack_kernel,
        out_shape=held_bf(192, 128),
        in_specs=vmem(3),
        out_specs=vmem(1)[0],
    )(homolog_embedding, presence_indicator.T, coupling_change_derivative)
    def over(axis, size, step, array):
        return lax.ppermute(array, axis, [(k, k ^ step) for k in range(size)])

    far = over("col", n_col, 2, packed)
    near = over("col", n_col, 1, packed)
    last = over("col", n_col, 3, packed)
    front = jnp.stack([packed, last])
    chip_front = over("row", n_row, 2, front)
    rear = jnp.stack([near, far])
    chip_rear = over("row", n_row, 2, rear)
    front, final_projection_matrix = lax.optimization_barrier((front, final_projection_matrix))
    weights = pl.pallas_call(
        weights_kernel,
        out_shape=(
            held(8, 128), held_bf(256, 256), held_bf(width * width // 2, 256), held(2 * width, features),
        ),
        in_specs=[hbm] * 5,
        out_specs=tuple(vmem(4)),
        scratch_shapes=[
            pltpu.VMEM((1, features), F32),
            pltpu.VMEM((1, features), F32),
            pltpu.VMEM((width, features), BF),
            pltpu.VMEM((width, features), BF),
            pltpu.VMEM((width * width, 128), BF),
            pltpu.VMEM((width * width, 128), F32),
            pltpu.SemaphoreType.DMA((5,)),
        ],
        compiler_params=LIMIT,
    )(
        *[
            pltpu.with_memory_space_constraint(x, pltpu.HBM)
            for x in (
                standardizer_scale.reshape(1, features),
                standardizer_shift.reshape(1, features),
                first_t,
                second_t,
                final_projection_matrix,
            )
        ]
    )
    norm, back, final_turned, first = weights
    own = jnp.concatenate([front, rear])
    core = over("row", n_row, 1, own)
    stage_outs = [
        held_bf(512, 256), held_bf(128, 256), held_bf(128, 256), held(width, 8, 128),
        held_bf(256, 1024), held(8, 32, 128), held(128, 128),
    ]
    scalar = pl.BlockSpec(memory_space=pltpu.SMEM)

    def stage(a, block):
        outs = stage_outs + [held(128, 128)] * 2 * (a == 0)
        return pl.pallas_call(
            functools.partial(stage_kernel, n_col, a),
            out_shape=tuple(outs),
            in_specs=[scalar] + vmem(4),
            out_specs=tuple(vmem(len(outs))),
            scratch_shapes=[pltpu.VMEM((256, 128), F32)],
            compiler_params=LIMIT,
            cost_estimate=pl.CostEstimate(
                flops=1_000_000_000, bytes_accessed=4_000_000, transcendentals=0
            ),
        )(place, block, norm, back, final_turned)

    own_stage = stage(0, own)
    core_stage = stage(1, core)
    chip = jnp.concatenate([chip_front, chip_rear])
    chip, own_stage = lax.optimization_barrier((chip, own_stage))
    both = over("row", n_row, 1, chip)
    stages = [own_stage[:7], core_stage, stage(2, chip)]
    outs = pl.pallas_call(
        functools.partial(part_kernel, n_row, n_col),
        out_shape=(
            shape(shards, tokens, features),
            shape(width * width, 128),
            shape(width, features),
            shape(width, features),
            shape(1, features),
            shape(1, features),
            shape(1, 128),
        ),
        in_specs=[scalar] + vmem(7 * (n_row - 1) + 7),
        out_specs=(*vmem(1), hbm, *vmem(5)),
        scratch_shapes=[
            pltpu.VMEM((1024, 128), BF),
            pltpu.VMEM((2048, 256), BF),
            pltpu.VMEM((1024, 1024), BF),
            pltpu.VMEM((512, 2048), BF),
            pltpu.VMEM((128, 2048), BF),
            pltpu.VMEM((1024, 128), F32),
            pltpu.SemaphoreType.DMA,
            pltpu.VMEM((256, 128), F32),
            *stage_outs,
        ],
        compiler_params=LIMIT,
    )(place, both, *[x for s in stages for x in s], *own_stage[7:], norm, back, final_turned, first)
    emb, final, first, second, gain, offset, bias = outs
    return emb, final, first.T, second.T, gain.reshape(-1), offset.reshape(-1), bias.reshape(-1)


def body(n_row, n_col, *arguments):
    msa, _, pair = arguments[:3]
    width = arguments[5].shape[1]
    fits = (
        n_row == 4
        and n_col == 4
        and msa.shape == (32, 8, 64)
        and pair.shape == (8, 8, 128)
        and width == 32
    )
    if fits:
        return gathered_body(n_row, n_col, *arguments)
    return sharded_body(*arguments)


def solution(mesh):
    placed = (
        P(("grp", "col"), "row", None),
        P(("grp", "col"), "row"),
        P(("grp", "row"), "col", None),
        P(),
        P(),
        P(),
        P(),
        P(),
    )
    return jax.shard_map(
        functools.partial(body, mesh.shape["row"], mesh.shape["col"]),
        mesh=mesh,
        in_specs=placed,
        out_specs=(
            P(("grp", "col"), "row", None),
            P("grp", None),
            P("grp", None),
            P("grp", None),
            P("grp"),
            P("grp"),
            P("grp"),
        ),
        check_vma=False,
    )
```

```python
import functools

import jax
import jax.numpy as jnp
from jax import lax
from jax.experimental import pallas as pl
from jax.experimental.pallas import tpu as pltpu
from jax.sharding import PartitionSpec as P

TOKB = 2


def standardizer_parts(homolog_embedding, standardizer_scale, standardizer_shift):
    incoming_entries = homolog_embedding.astype(jnp.float32)
    center = jnp.mean(incoming_entries, axis=-1, keepdims=True)
    varied = incoming_entries - center
    variance = jnp.mean(varied * varied, axis=-1, keepdims=True)
    reciprocal_spread = lax.rsqrt(variance + 1e-05)
    standardized_entries = varied * reciprocal_spread
    standardized_bfloat = (standardized_entries * standardizer_scale + standardizer_shift).astype(
        jnp.bfloat16
    )
    return (standardized_entries, reciprocal_spread, standardized_bfloat)


def sharded_body(
    homolog_embedding,
    presence_indicator,
    coupling_change_derivative,
    standardizer_scale,
    standardizer_shift,
    first_projection_matrix,
    second_projection_matrix,
    final_projection_matrix,
):
    shard_homolog_number, residue_line_number, feature_number = homolog_embedding.shape
    tok_cols = coupling_change_derivative.shape[1]
    width = first_projection_matrix.shape[1]
    standardized_entries, reciprocal_spread, standardized_bfloat = standardizer_parts(
        homolog_embedding, standardizer_scale, standardizer_shift
    )
    mask_single_precision = presence_indicator.astype(jnp.float32)
    mask_half_precision = presence_indicator.astype(jnp.bfloat16)
    left = (
        jnp.einsum(
            "sic,cp->sip",
            standardized_bfloat,
            first_projection_matrix,
            preferred_element_type=jnp.float32,
        )
        * mask_single_precision[..., None]
    ).astype(jnp.bfloat16)
    right = (
        jnp.einsum(
            "sic,cp->sip",
            standardized_bfloat,
            second_projection_matrix,
            preferred_element_type=jnp.float32,
        )
        * mask_single_precision[..., None]
    ).astype(jnp.bfloat16)
    left_flat = left.reshape(shard_homolog_number, residue_line_number * width)
    right_flat = right.reshape(shard_homolog_number, residue_line_number * width)
    left_all, mask_left = (
        lax.all_gather(left_flat, "col", axis=0, tiled=True),
        lax.all_gather(mask_half_precision, "col", axis=0, tiled=True),
    )
    right_wide, mask_wide = (
        lax.all_gather(right_flat, "row", axis=1, tiled=True),
        lax.all_gather(mask_half_precision, "row", axis=1, tiled=True),
    )
    right_all, mask_right = (
        lax.all_to_all(right_wide, "col", split_axis=1, concat_axis=0, tiled=True),
        lax.all_to_all(mask_wide, "col", split_axis=1, concat_axis=0, tiled=True),
    )
    seq_total = left_all.shape[0]
    right_three = right_all.reshape(seq_total, tok_cols, width)
    counts = jnp.einsum("si,sj->ij", mask_left, mask_right, preferred_element_type=jnp.float32)
    scaled = coupling_change_derivative.astype(jnp.float32) / (counts + 0.001)[..., None]
    bias_part = jnp.sum(scaled, axis=(0, 1))
    scaled_bf = scaled.astype(jnp.bfloat16)
    block_rows = residue_line_number // TOKB
    right_acc = jnp.zeros((seq_total, tok_cols, width), jnp.float32)
    wout_acc = jnp.zeros(final_projection_matrix.shape, jnp.float32)
    left_pieces = []
    for block_index in range(TOKB):
        first = block_index * block_rows
        rows_bf = scaled_bf[first : first + block_rows]
        outer_grad = jnp.einsum(
            "ijz,fz->ijf", rows_bf, final_projection_matrix, preferred_element_type=jnp.float32
        ).astype(jnp.bfloat16)
        outer_grad = outer_grad.reshape(block_rows, tok_cols, width, width)
        left_block = left_all[:, first * width : (first + block_rows) * width].reshape(
            seq_total, block_rows, width
        )
        first_factor_derivative = jnp.einsum(
            "ijce,sje->sic", outer_grad, right_three, preferred_element_type=jnp.float32
        )
        right_acc = right_acc + jnp.einsum(
            "ijce,sic->sje", outer_grad, left_block, preferred_element_type=jnp.float32
        )
        outer = jnp.einsum(
            "sic,sje->ijce", left_block, right_three, preferred_element_type=jnp.float32
        ).astype(jnp.bfloat16)
        outer = outer.reshape(block_rows, tok_cols, width * width)
        wout_acc = wout_acc + jnp.einsum(
            "ijf,ijz->fz", outer, rows_bf, preferred_element_type=jnp.float32
        )
        first_factor_derivative = first_factor_derivative.reshape(seq_total, block_rows * width)
        left_pieces.append(first_factor_derivative)
    left_terms = jnp.concatenate(left_pieces, axis=1)
    left_own = lax.psum_scatter(left_terms, "col", scatter_dimension=0, tiled=True)
    right_spread = lax.all_to_all(
        right_acc.reshape(seq_total, tok_cols * width),
        "col",
        split_axis=0,
        concat_axis=1,
        tiled=True,
    )
    right_own = lax.psum_scatter(right_spread, "row", scatter_dimension=1, tiled=True)
    left_in = (
        left_own.reshape(shard_homolog_number, residue_line_number, width)
        * mask_single_precision[..., None]
    ).astype(jnp.bfloat16)
    right_in = (
        right_own.reshape(shard_homolog_number, residue_line_number, width)
        * mask_single_precision[..., None]
    ).astype(jnp.bfloat16)
    left_part = jnp.einsum(
        "sic,sip->cp", standardized_bfloat, left_in, preferred_element_type=jnp.float32
    )
    right_part = jnp.einsum(
        "sic,sip->cp", standardized_bfloat, right_in, preferred_element_type=jnp.float32
    )
    d_normal = jnp.einsum(
        "sip,cp->sic", left_in, first_projection_matrix, preferred_element_type=jnp.float32
    ) + jnp.einsum(
        "sip,cp->sic", right_in, second_projection_matrix, preferred_element_type=jnp.float32
    )
    gain_part = jnp.sum(d_normal * standardized_entries, axis=(0, 1))
    beta_part = jnp.sum(d_normal, axis=(0, 1))
    standardized_derivative = d_normal * standardizer_scale
    embedding_derivative = reciprocal_spread * (
        standardized_derivative
        - jnp.mean(standardized_derivative, axis=-1, keepdims=True)
        - standardized_entries
        * jnp.mean(standardized_derivative * standardized_entries, axis=-1, keepdims=True)
    )
    (
        final_matrix_derivative,
        first_matrix_derivative,
        second_matrix_derivative,
        scale_factor_derivative,
        shift_term_derivative,
        shift_derivative,
    ) = lax.psum((wout_acc, left_part, right_part, gain_part, beta_part, bias_part), ("row", "col"))
    return (
        embedding_derivative,
        final_matrix_derivative,
        first_matrix_derivative,
        second_matrix_derivative,
        scale_factor_derivative,
        shift_term_derivative,
        shift_derivative,
    )


BF = jnp.bfloat16
F32 = jnp.float32


def spread(rows, cols, rule):
    r = lax.broadcasted_iota(jnp.int32, (rows, cols), 0)
    c = lax.broadcasted_iota(jnp.int32, (rows, cols), 1)
    return rule(r, c)


def mm(a, b):
    return jnp.dot(a, b, preferred_element_type=F32)


def mm_nt(a, b):
    return lax.dot_general(a, b, (((1,), (1,)), ((), ())), preferred_element_type=F32)


def mm_tn(a, b):
    return lax.dot_general(a, b, (((0,), (0,)), ((), ())), preferred_element_type=F32)


def interleave(first, second):
    odd = lax.broadcasted_iota(jnp.int16, (32, 128), 1) & 32 != 0
    return (
        jnp.where(odd, pltpu.roll(second, 32, 1), first),
        jnp.where(odd, second, pltpu.roll(first, 96, 1)),
    )


def diagonal_pair(block):
    zero = jnp.zeros_like(block)
    return jnp.concatenate(
        [jnp.concatenate([block, zero], axis=1), jnp.concatenate([zero, block], axis=1)], axis=0
    )


ABSENT = 1024.0


def pack_kernel(msa_ref, mask_ref, pair_ref, out_ref):
    msa = msa_ref[...].astype(F32)
    pick = spread(8, 512, lambda r, c: jnp.where(c // 64 == r, 1.0, 0.0)).astype(BF)
    present = mm_tn(mask_ref[...].astype(F32).astype(BF), pick) > 0.5
    for g in range(4):
        rows = jnp.concatenate([msa[:, 2 * g, :], msa[:, 2 * g + 1, :]], axis=1)
        out_ref[32 * g : 32 * g + 32, :] = jnp.where(
            present[:, 128 * g : 128 * g + 128], rows, ABSENT
        ).astype(BF)
    out_ref[128:192, :] = pair_ref[...].astype(F32).reshape(64, 128).astype(BF)


def weights_kernel(*refs):
    sources, (norm_out, back_out, final_out, first_out) = refs[:5], refs[5:9]
    held, scr, sems = refs[9:14], refs[14], refs[15]
    copies = [pltpu.make_async_copy(sources[k], held[k], sems.at[k]) for k in range(5)]
    for copy in copies:
        copy.start()
    for copy in copies:
        copy.wait()
    gain_ref, offset_ref, first_ref, second_ref, final_ref = held
    norm_out[...] = jnp.concatenate(
        [
            jnp.concatenate([ref[...]] * 2, axis=1)
            for ref in (gain_ref, offset_ref, gain_ref, offset_ref) * 2
        ],
        axis=0,
    )
    for k, ref in enumerate((first_ref, second_ref)):
        narrow = ref[...].astype(F32)
        first_out[32 * k : 32 * k + 32, :] = narrow
        wide = jnp.concatenate([narrow] * 4, axis=1)
        wide = jnp.concatenate([wide] * 4, axis=0)
        own = spread(128, 256, lambda r, c: r // 32 == c // 64)
        back_out[128 * k : 128 * k + 128, :] = jnp.where(own, wide, 0.0).astype(BF)
    scr[...] = final_ref[...].astype(F32)
    for k in range(16):
        e = 4 * (k // 2) + k % 2
        final_out[32 * k : 32 * k + 32, :] = jnp.concatenate(
            [scr[pl.ds(e, 32, stride=32), :], scr[pl.ds(e + 2, 32, stride=32), :]], axis=1
        ).astype(BF)


def averager_of():
    return spread(128, 128, lambda r, c: jnp.where(r // 64 == c // 64, 1.0 / 64, 0.0)).astype(BF)


ORDER = (0, 1, 2, 3)


def stage_kernel(
    n_col, a, place_ref, set_ref, norm_ref, back_ref, final_ref,
    rhs_out, left_out, leftt_out, rightt_out, grad_out, pair_out, found_out, *rest
):
    *own_out, turn_scr = rest
    for b in range(n_col):
        at = pl.multiple_of(lax.bitwise_xor(place_ref[0], ORDER[b]) * 8, 8)
        pair_out[:, pl.ds(at, 8), :] = set_ref[b, 128:192, :].astype(F32).reshape(8, 8, 128)

    gain = norm_ref[0:1, :]
    offset = norm_ref[1:2, :]
    averager = averager_of()
    x = jnp.concatenate(
        [set_ref[b, 32 * g : 32 * g + 32, :] for g in range(4) for b in range(n_col)], axis=0
    )
    mean = mm(x, averager)
    present = mean < ABSENT / 2
    varied = x.astype(F32) - mean
    inverse = lax.rsqrt(mm((varied * varied).astype(BF), averager) + 1e-05)
    normed = varied * inverse
    if own_out:
        for g in range(4):
            own_out[0][32 * g : 32 * g + 32, :] = normed[128 * g : 128 * g + 32]
            own_out[1][32 * g : 32 * g + 32, :] = inverse[128 * g : 128 * g + 32]
    normal = jnp.where(present, normed * gain + offset, 0.0).astype(BF)
    rhs_out[:, 0:128] = normal
    rhs_out[:, 128:256] = normed.astype(BF)
    here = jnp.where(present, 1.0, 0.0)
    lane = lax.broadcasted_iota(jnp.int32, (128, 128), 1)
    found = jnp.zeros((128, 128), F32)
    for g in range(4):
        found = jnp.where(lane % 32 // 2 == 4 * a + g, here[128 * g : 128 * g + 128], found)
    found_out[...] = found
    for h in range(2):
        masked = jnp.concatenate(
            [normal[128 * g : 128 * g + 128] for g in (2 * h, 2 * h + 1)], axis=1
        )
        at = slice(128 * h, 128 * h + 128)
        left_out[:, at] = mm_nt(masked, back_ref[:128, :]).astype(BF)
        both = mm_nt(back_ref[...], masked)
        turn_scr[at, :] = both[128:]
        for k in range(2):
            leftt_out[64 * h + 32 * k : 64 * h + 32 * k + 32, :] = jnp.concatenate(
                [both[32 * k : 32 * k + 32], both[32 * k + 64 : 32 * k + 96]], axis=1
            ).astype(BF)

    for e in range(32):
        rightt_out[e] = turn_scr[pl.ds(e, 8, stride=32), :]

    pair = pair_out[...].reshape(256, 128).astype(BF)
    for n in range(2):
        pairs = jnp.concatenate(
            [diagonal_pair(pair[64 * p : 64 * p + 64]) for p in (2 * n, 2 * n + 1)], axis=0
        )
        grad = mm_nt(final_ref[...], pairs).astype(BF)
        for p in range(2):
            for q in range(8):
                rows = 64 * (2 * n + p)
                block = grad[64 * q : 64 * q + 64, 128 * p : 128 * p + 128]
                even, odd = interleave(block[:32], block[32:])
                grad_out[rows : rows + 32, 128 * q : 128 * q + 128] = even
                grad_out[rows + 32 : rows + 64, 128 * q : 128 * q + 128] = odd


def part_kernel(n_row, n_col, place_ref, last_ref, *refs):
    stages = [refs[7 * a : 7 * a + 7] for a in range(n_row - 1)]
    (
        normed_ref, inverse_ref, norm_ref, back_ref, final_ref, first_ref,
        emb_out, final_hbm_out, first_out, second_out, gain_out, offset_out, bias_out,
        right_scr, scaled_scr, grad_scr, outer_scr, wide_scr, all_scr,
        final_out, out_sem, turn_scr,
    ) = refs[7 * (n_row - 1) : -7]
    stages.append(refs[-7:])
    stage_kernel(
        n_col, n_row - 1, place_ref, last_ref, norm_ref, back_ref, final_ref, *stages[-1], turn_scr
    )
    gain = norm_ref[0:1, :]
    averager = averager_of()
    lane = lax.broadcasted_iota(jnp.int32, (128, 128), 1)

    found = sum(stage[6][...] for stage in stages)
    turned = pltpu.roll(found, 64, 1)
    mask = jnp.where((lane % 2 == 0) == (lane < 64), found, turned)
    mask_t = mask.T

    for e in range(32):
        right_scr[32 * e : 32 * e + 32, :] = jnp.concatenate(
            [stage[3][e] for stage in stages], axis=0
        ).astype(BF)

    mask_bf = mask.astype(BF)
    share = (1.0 / (mm_tn(mask_bf, mask_bf)[0:32] + 0.001)).astype(BF)
    for i in range(32):
        a, at = i // 8, 32 * (i % 8)
        for q in range(8):
            grad_scr[32 * i : 32 * i + 32, 128 * q : 128 * q + 128] = (
                stages[a][4][at : at + 32, 128 * q : 128 * q + 128] * share[i : i + 1]
            )
    left = jnp.concatenate([stage[1][...] for stage in stages], axis=1)
    right_grad = mm(left, grad_scr[...])
    left_grad = mm(grad_scr[...], right_scr[...])

    turn = spread(
        256, 256, lambda r, c: jnp.where((r // 8 == c % 32) & (r % 8 == c // 32), 1.0, 0.0)
    ).astype(BF)
    mask_two = jnp.concatenate([mask, mask], axis=1)
    right_in = [
        mm_nt(turn, (right_grad[:, 256 * q : 256 * q + 256] * mask_two).astype(BF))
        for q in range(4)
    ]
    for t in range(32):
        at = slice(128 * (t // 2), 128 * (t // 2) + 128)
        row = 32 * (t % 2)
        all_scr[row : row + 32, at] = (
            left_grad[32 * t : 32 * t + 32] * mask_t[t : t + 1]
        ).astype(BF)
        all_scr[row + 64 : row + 96, at] = jnp.concatenate(
            [part[8 * t : 8 * t + 8] for part in right_in], axis=0
        ).astype(BF)

    bias = jnp.zeros((1, 128), F32)
    ones = jnp.ones((128, 128), BF)
    for p in range(8):
        both_on = jnp.concatenate(
            [mask_t[0:32] * mask_t[i : i + 1] for i in range(4 * p, 4 * p + 4)], axis=0
        ).astype(BF)
        counts = mm(both_on, ones)
        pair = stages[p // 2][5][4 * (p % 2) : 4 * (p % 2) + 4]
        scaled = pair.reshape(128, 128) / (counts + 0.001)
        bias = bias + jnp.sum(scaled, axis=0, keepdims=True)
        scaled_scr[128 * p : 128 * p + 128, :] = scaled.astype(BF)
    bias_out[...] = bias

    left_t = jnp.concatenate([stage[2][...] for stage in stages], axis=0)
    for n in range(8):
        rights = jnp.concatenate(
            [diagonal_pair(right_scr[64 * p : 64 * p + 64, :]) for p in (2 * n, 2 * n + 1)], axis=0
        )
        outer = mm_nt(left_t, rights).astype(BF)
        for p in range(2):
            for q in range(8):
                rows = 64 * (2 * n + p)
                block = outer[64 * q : 64 * q + 64, 128 * p : 128 * p + 128]
                even, odd = interleave(block[:32], block[32:])
                outer_scr[rows : rows + 32, 128 * q : 128 * q + 128] = even
                outer_scr[rows + 32 : rows + 64, 128 * q : 128 * q + 128] = odd
    wide_scr[...] = mm(outer_scr[...], scaled_scr[...])
    for c in range(32):
        final_out[32 * c : 32 * c + 32, :] = wide_scr[pl.ds(c, 32, stride=32), :]
    final_send = pltpu.make_async_copy(final_out, final_hbm_out, out_sem)
    final_send.start()

    total = mm(
        all_scr[...], jnp.concatenate([stage[0][...] for stage in stages], axis=0)
    )
    sums = all_scr[:, 0:128].astype(F32)
    for g in range(1, 16):
        sums = sums + all_scr[:, 128 * g : 128 * g + 128].astype(F32)

    def fold(block):
        return block[0:32, 0:64] + block[32:64, 64:128]

    first_out[...] = fold(total[0:64, 0:128])
    second_out[...] = fold(total[64:128, 0:128])
    sums = jnp.sum(sums, axis=1, keepdims=True)
    left_sum = sums[0:32] + sums[32:64]
    right_sum = sums[64:96] + sums[96:128]
    first, second = first_ref[0:32, :], first_ref[32:64, :]
    gain_out[...] = jnp.sum(
        first * fold(total[0:64, 128:256]) + second * fold(total[64:128, 128:256]),
        axis=0, keepdims=True,
    )
    offset_out[...] = jnp.sum(first * left_sum + second * right_sum, axis=0, keepdims=True)

    d_hat = []
    for h in range(2):
        sides = [
            jnp.concatenate(
                [all_scr[row : row + 64, 128 * g : 128 * g + 128] for g in (2 * h, 2 * h + 1)], axis=0
            )
            for row in (0, 64)
        ]
        d_normal = mm_tn(jnp.concatenate(sides, axis=0), back_ref[...])
        d_hat += [d_normal[0:32, 0:128] * gain, d_normal[0:32, 128:256] * gain]
    d_hat = jnp.concatenate(d_hat, axis=0)
    normed = normed_ref[...]
    means = mm(jnp.concatenate([d_hat, d_hat * normed], axis=0).astype(BF), averager)
    result = inverse_ref[...] * (d_hat - means[:128] - normed * means[128:])
    for g in range(4):
        emb_out[:, 2 * g, :] = result[32 * g : 32 * g + 32, 0:64]
        emb_out[:, 2 * g + 1, :] = result[32 * g : 32 * g + 32, 64:128]
    final_send.wait()


def vmem(count):
    return [pl.BlockSpec(memory_space=pltpu.VMEM)] * count


LIMIT = pltpu.CompilerParams(vmem_limit_bytes=32 * 1024 * 1024)


def gathered_body(
    n_row,
    n_col,
    homolog_embedding,
    presence_indicator,
    coupling_change_derivative,
    standardizer_scale,
    standardizer_shift,
    first_projection_matrix,
    second_projection_matrix,
    final_projection_matrix,
):
    shards, tokens, features = homolog_embedding.shape
    width = first_projection_matrix.shape[1]
    first_t, second_t = first_projection_matrix.T, second_projection_matrix.T
    shape = lambda *dims: jax.ShapeDtypeStruct(dims, F32)
    held = lambda *dims: pltpu.VMEM(dims, F32)
    held_bf = lambda *dims: pltpu.VMEM(dims, BF)
    hbm = pl.BlockSpec(memory_space=pltpu.HBM)
    place = lax.bitwise_xor(lax.axis_index("row"), lax.axis_index("col"))
    place = place.astype(jnp.int32).reshape(1)
    packed = pl.pallas_call(
        pack_kernel,
        out_shape=held_bf(192, 128),
        in_specs=vmem(3),
        out_specs=vmem(1)[0],
    )(homolog_embedding, presence_indicator.T, coupling_change_derivative)
    def over(axis, size, step, array):
        return lax.ppermute(array, axis, [(k, k ^ step) for k in range(size)])

    def send(*pairs):
        return lax.ppermute(packed, "col", pairs)

    up = send((0, 2), (1, 3))
    cross = send((2, 0), (3, 1), (0, 3))
    around, down = lax.optimization_barrier((send((0, 1), (1, 2), (2, 3), (3, 0)), send((1, 0), (2, 1), (3, 2))))
    here = lax.axis_index("col")
    near = jnp.where(here % 2 == 0, down, around)
    near, around, down = lax.optimization_barrier((near, around, down))
    far = jnp.where(here >= 2, up, cross)
    last = jnp.where(here == 1, down, jnp.where(here == 3, cross, around))
    front = jnp.stack([packed, near])
    chip_front = over("row", n_row, 2, front)
    rear = jnp.stack([far, last])
    chip_rear = over("row", n_row, 2, rear)
    front, final_projection_matrix = lax.optimization_barrier((front, final_projection_matrix))
    weights = pl.pallas_call(
        weights_kernel,
        out_shape=(
            held(8, 128), held_bf(256, 256), held_bf(width * width // 2, 256), held(2 * width, features),
        ),
        in_specs=[hbm] * 5,
        out_specs=tuple(vmem(4)),
        scratch_shapes=[
            pltpu.VMEM((1, features), F32),
            pltpu.VMEM((1, features), F32),
            pltpu.VMEM((width, features), BF),
            pltpu.VMEM((width, features), BF),
            pltpu.VMEM((width * width, 128), BF),
            pltpu.VMEM((width * width, 128), F32),
            pltpu.SemaphoreType.DMA((5,)),
        ],
        compiler_params=LIMIT,
    )(
        *[
            pltpu.with_memory_space_constraint(x, pltpu.HBM)
            for x in (
                standardizer_scale.reshape(1, features),
                standardizer_shift.reshape(1, features),
                first_t,
                second_t,
                final_projection_matrix,
            )
        ]
    )
    norm, back, final_turned, first = weights
    own = jnp.concatenate([front, rear])
    core = over("row", n_row, 1, own)
    stage_outs = [
        held_bf(512, 256), held_bf(128, 256), held_bf(128, 256), held(width, 8, 128),
        held_bf(256, 1024), held(8, 32, 128), held(128, 128),
    ]
    scalar = pl.BlockSpec(memory_space=pltpu.SMEM)

    def stage(a, block):
        outs = stage_outs + [held(128, 128)] * 2 * (a == 0)
        return pl.pallas_call(
            functools.partial(stage_kernel, n_col, a),
            out_shape=tuple(outs),
            in_specs=[scalar] + vmem(4),
            out_specs=tuple(vmem(len(outs))),
            scratch_shapes=[pltpu.VMEM((256, 128), F32)],
            compiler_params=LIMIT,
            cost_estimate=pl.CostEstimate(
                flops=1_000_000_000, bytes_accessed=4_000_000, transcendentals=0
            ),
        )(place, block, norm, back, final_turned)

    own_stage = stage(0, own)
    core_stage = stage(1, core)
    chip = jnp.concatenate([chip_front, chip_rear])
    chip, own_stage = lax.optimization_barrier((chip, own_stage))
    both = over("row", n_row, 1, chip)
    stages = [own_stage[:7], core_stage, stage(2, chip)]
    outs = pl.pallas_call(
        functools.partial(part_kernel, n_row, n_col),
        out_shape=(
            shape(shards, tokens, features),
            shape(width * width, 128),
            shape(width, features),
            shape(width, features),
            shape(1, features),
            shape(1, features),
            shape(1, 128),
        ),
        in_specs=[scalar] + vmem(7 * (n_row - 1) + 7),
        out_specs=(*vmem(1), hbm, *vmem(5)),
        scratch_shapes=[
            pltpu.VMEM((1024, 128), BF),
            pltpu.VMEM((1024, 128), BF),
            pltpu.VMEM((1024, 1024), BF),
            pltpu.VMEM((1024, 1024), BF),
            pltpu.VMEM((1024, 128), F32),
            pltpu.VMEM((128, 2048), BF),
            pltpu.VMEM((1024, 128), F32),
            pltpu.SemaphoreType.DMA,
            pltpu.VMEM((256, 128), F32),
            *stage_outs,
        ],
        compiler_params=LIMIT,
    )(place, both, *[x for s in stages for x in s], *own_stage[7:], norm, back, final_turned, first)
    emb, final, first, second, gain, offset, bias = outs
    return emb, final, first.T, second.T, gain.reshape(-1), offset.reshape(-1), bias.reshape(-1)


def body(n_row, n_col, *arguments):
    msa, _, pair = arguments[:3]
    width = arguments[5].shape[1]
    fits = (
        n_row == 4
        and n_col == 4
        and msa.shape == (32, 8, 64)
        and pair.shape == (8, 8, 128)
        and width == 32
    )
    if fits:
        return gathered_body(n_row, n_col, *arguments)
    return sharded_body(*arguments)


def solution(mesh):
    placed = (
        P(("grp", "col"), "row", None),
        P(("grp", "col"), "row"),
        P(("grp", "row"), "col", None),
        P(),
        P(),
        P(),
        P(),
        P(),
    )
    return jax.shard_map(
        functools.partial(body, mesh.shape["row"], mesh.shape["col"]),
        mesh=mesh,
        in_specs=placed,
        out_specs=(
            P(("grp", "col"), "row", None),
            P("grp", None),
            P("grp", None),
            P("grp", None),
            P("grp"),
            P("grp"),
            P("grp"),
        ),
        check_vma=False,
    )
```

```python
import functools

import jax
import jax.numpy as jnp
from jax import lax
from jax.experimental import pallas as pl
from jax.experimental.pallas import tpu as pltpu
from jax.sharding import PartitionSpec as P

TOKB = 2


def standardizer_parts(homolog_embedding, standardizer_scale, standardizer_shift):
    incoming_entries = homolog_embedding.astype(jnp.float32)
    center = jnp.mean(incoming_entries, axis=-1, keepdims=True)
    varied = incoming_entries - center
    variance = jnp.mean(varied * varied, axis=-1, keepdims=True)
    reciprocal_spread = lax.rsqrt(variance + 1e-05)
    standardized_entries = varied * reciprocal_spread
    standardized_bfloat = (standardized_entries * standardizer_scale + standardizer_shift).astype(
        jnp.bfloat16
    )
    return (standardized_entries, reciprocal_spread, standardized_bfloat)


def sharded_body(
    homolog_embedding,
    presence_indicator,
    coupling_change_derivative,
    standardizer_scale,
    standardizer_shift,
    first_projection_matrix,
    second_projection_matrix,
    final_projection_matrix,
):
    shard_homolog_number, residue_line_number, feature_number = homolog_embedding.shape
    tok_cols = coupling_change_derivative.shape[1]
    width = first_projection_matrix.shape[1]
    standardized_entries, reciprocal_spread, standardized_bfloat = standardizer_parts(
        homolog_embedding, standardizer_scale, standardizer_shift
    )
    mask_single_precision = presence_indicator.astype(jnp.float32)
    mask_half_precision = presence_indicator.astype(jnp.bfloat16)
    left = (
        jnp.einsum(
            "sic,cp->sip",
            standardized_bfloat,
            first_projection_matrix,
            preferred_element_type=jnp.float32,
        )
        * mask_single_precision[..., None]
    ).astype(jnp.bfloat16)
    right = (
        jnp.einsum(
            "sic,cp->sip",
            standardized_bfloat,
            second_projection_matrix,
            preferred_element_type=jnp.float32,
        )
        * mask_single_precision[..., None]
    ).astype(jnp.bfloat16)
    left_flat = left.reshape(shard_homolog_number, residue_line_number * width)
    right_flat = right.reshape(shard_homolog_number, residue_line_number * width)
    left_all, mask_left = (
        lax.all_gather(left_flat, "col", axis=0, tiled=True),
        lax.all_gather(mask_half_precision, "col", axis=0, tiled=True),
    )
    right_wide, mask_wide = (
        lax.all_gather(right_flat, "row", axis=1, tiled=True),
        lax.all_gather(mask_half_precision, "row", axis=1, tiled=True),
    )
    right_all, mask_right = (
        lax.all_to_all(right_wide, "col", split_axis=1, concat_axis=0, tiled=True),
        lax.all_to_all(mask_wide, "col", split_axis=1, concat_axis=0, tiled=True),
    )
    seq_total = left_all.shape[0]
    right_three = right_all.reshape(seq_total, tok_cols, width)
    counts = jnp.einsum("si,sj->ij", mask_left, mask_right, preferred_element_type=jnp.float32)
    scaled = coupling_change_derivative.astype(jnp.float32) / (counts + 0.001)[..., None]
    bias_part = jnp.sum(scaled, axis=(0, 1))
    scaled_bf = scaled.astype(jnp.bfloat16)
    block_rows = residue_line_number // TOKB
    right_acc = jnp.zeros((seq_total, tok_cols, width), jnp.float32)
    wout_acc = jnp.zeros(final_projection_matrix.shape, jnp.float32)
    left_pieces = []
    for block_index in range(TOKB):
        first = block_index * block_rows
        rows_bf = scaled_bf[first : first + block_rows]
        outer_grad = jnp.einsum(
            "ijz,fz->ijf", rows_bf, final_projection_matrix, preferred_element_type=jnp.float32
        ).astype(jnp.bfloat16)
        outer_grad = outer_grad.reshape(block_rows, tok_cols, width, width)
        left_block = left_all[:, first * width : (first + block_rows) * width].reshape(
            seq_total, block_rows, width
        )
        first_factor_derivative = jnp.einsum(
            "ijce,sje->sic", outer_grad, right_three, preferred_element_type=jnp.float32
        )
        right_acc = right_acc + jnp.einsum(
            "ijce,sic->sje", outer_grad, left_block, preferred_element_type=jnp.float32
        )
        outer = jnp.einsum(
            "sic,sje->ijce", left_block, right_three, preferred_element_type=jnp.float32
        ).astype(jnp.bfloat16)
        outer = outer.reshape(block_rows, tok_cols, width * width)
        wout_acc = wout_acc + jnp.einsum(
            "ijf,ijz->fz", outer, rows_bf, preferred_element_type=jnp.float32
        )
        first_factor_derivative = first_factor_derivative.reshape(seq_total, block_rows * width)
        left_pieces.append(first_factor_derivative)
    left_terms = jnp.concatenate(left_pieces, axis=1)
    left_own = lax.psum_scatter(left_terms, "col", scatter_dimension=0, tiled=True)
    right_spread = lax.all_to_all(
        right_acc.reshape(seq_total, tok_cols * width),
        "col",
        split_axis=0,
        concat_axis=1,
        tiled=True,
    )
    right_own = lax.psum_scatter(right_spread, "row", scatter_dimension=1, tiled=True)
    left_in = (
        left_own.reshape(shard_homolog_number, residue_line_number, width)
        * mask_single_precision[..., None]
    ).astype(jnp.bfloat16)
    right_in = (
        right_own.reshape(shard_homolog_number, residue_line_number, width)
        * mask_single_precision[..., None]
    ).astype(jnp.bfloat16)
    left_part = jnp.einsum(
        "sic,sip->cp", standardized_bfloat, left_in, preferred_element_type=jnp.float32
    )
    right_part = jnp.einsum(
        "sic,sip->cp", standardized_bfloat, right_in, preferred_element_type=jnp.float32
    )
    d_normal = jnp.einsum(
        "sip,cp->sic", left_in, first_projection_matrix, preferred_element_type=jnp.float32
    ) + jnp.einsum(
        "sip,cp->sic", right_in, second_projection_matrix, preferred_element_type=jnp.float32
    )
    gain_part = jnp.sum(d_normal * standardized_entries, axis=(0, 1))
    beta_part = jnp.sum(d_normal, axis=(0, 1))
    standardized_derivative = d_normal * standardizer_scale
    embedding_derivative = reciprocal_spread * (
        standardized_derivative
        - jnp.mean(standardized_derivative, axis=-1, keepdims=True)
        - standardized_entries
        * jnp.mean(standardized_derivative * standardized_entries, axis=-1, keepdims=True)
    )
    (
        final_matrix_derivative,
        first_matrix_derivative,
        second_matrix_derivative,
        scale_factor_derivative,
        shift_term_derivative,
        shift_derivative,
    ) = lax.psum((wout_acc, left_part, right_part, gain_part, beta_part, bias_part), ("row", "col"))
    return (
        embedding_derivative,
        final_matrix_derivative,
        first_matrix_derivative,
        second_matrix_derivative,
        scale_factor_derivative,
        shift_term_derivative,
        shift_derivative,
    )


BF = jnp.bfloat16
F32 = jnp.float32


def spread(rows, cols, rule):
    r = lax.broadcasted_iota(jnp.int32, (rows, cols), 0)
    c = lax.broadcasted_iota(jnp.int32, (rows, cols), 1)
    return rule(r, c)


def mm(a, b):
    return jnp.dot(a, b, preferred_element_type=F32)


def mm_nt(a, b):
    return lax.dot_general(a, b, (((1,), (1,)), ((), ())), preferred_element_type=F32)


def mm_tn(a, b):
    return lax.dot_general(a, b, (((0,), (0,)), ((), ())), preferred_element_type=F32)


def interleave(first, second):
    odd = lax.broadcasted_iota(jnp.int16, (32, 128), 1) & 32 != 0
    return (
        jnp.where(odd, pltpu.roll(second, 32, 1), first),
        jnp.where(odd, second, pltpu.roll(first, 96, 1)),
    )


def diagonal_pair(block):
    zero = jnp.zeros_like(block)
    return jnp.concatenate(
        [jnp.concatenate([block, zero], axis=1), jnp.concatenate([zero, block], axis=1)], axis=0
    )


ABSENT = 1024.0


def pack_kernel(msa_ref, mask_ref, pair_ref, out_ref):
    msa = msa_ref[...].astype(F32)
    pick = spread(8, 512, lambda r, c: jnp.where(c // 64 == r, 1.0, 0.0)).astype(BF)
    present = mm_tn(mask_ref[...].astype(F32).astype(BF), pick) > 0.5
    for g in range(4):
        rows = jnp.concatenate([msa[:, 2 * g, :], msa[:, 2 * g + 1, :]], axis=1)
        out_ref[32 * g : 32 * g + 32, :] = jnp.where(
            present[:, 128 * g : 128 * g + 128], rows, ABSENT
        ).astype(BF)
    out_ref[128:192, :] = pair_ref[...].astype(F32).reshape(64, 128).astype(BF)


def weights_kernel(*refs):
    sources, (norm_out, back_out, final_out, first_out) = refs[:5], refs[5:9]
    held, scr, sems = refs[9:14], refs[14], refs[15]
    copies = [pltpu.make_async_copy(sources[k], held[k], sems.at[k]) for k in range(5)]
    for copy in copies:
        copy.start()
    for copy in copies:
        copy.wait()
    gain_ref, offset_ref, first_ref, second_ref, final_ref = held
    norm_out[...] = jnp.concatenate(
        [
            jnp.concatenate([ref[...]] * 2, axis=1)
            for ref in (gain_ref, offset_ref, gain_ref, offset_ref) * 2
        ],
        axis=0,
    )
    for k, ref in enumerate((first_ref, second_ref)):
        narrow = ref[...].astype(F32)
        first_out[32 * k : 32 * k + 32, :] = narrow
        wide = jnp.concatenate([narrow] * 4, axis=1)
        wide = jnp.concatenate([wide] * 4, axis=0)
        own = spread(128, 256, lambda r, c: r // 32 == c // 64)
        back_out[128 * k : 128 * k + 128, :] = jnp.where(own, wide, 0.0).astype(BF)
    scr[...] = final_ref[...].astype(F32)
    for k in range(16):
        e = 4 * (k // 2) + k % 2
        final_out[32 * k : 32 * k + 32, :] = jnp.concatenate(
            [scr[pl.ds(e, 32, stride=32), :], scr[pl.ds(e + 2, 32, stride=32), :]], axis=1
        ).astype(BF)


def averager_of():
    return spread(128, 128, lambda r, c: jnp.where(r // 64 == c // 64, 1.0 / 64, 0.0)).astype(BF)


ORDER = (0, 3, 1, 2)


def stage_kernel(
    n_col, a, place_ref, set_ref, norm_ref, back_ref, final_ref,
    rhs_out, left_out, leftt_out, rightt_out, grad_out, pair_out, found_out, *rest
):
    *own_out, turn_scr = rest
    for b in range(n_col):
        at = pl.multiple_of(lax.bitwise_xor(place_ref[0], ORDER[b]) * 8, 8)
        pair_out[:, pl.ds(at, 8), :] = set_ref[b, 128:192, :].astype(F32).reshape(8, 8, 128)

    gain = norm_ref[0:1, :]
    offset = norm_ref[1:2, :]
    averager = averager_of()
    x = jnp.concatenate(
        [set_ref[b, 32 * g : 32 * g + 32, :] for g in range(4) for b in range(n_col)], axis=0
    )
    mean = mm(x, averager)
    present = mean < ABSENT / 2
    varied = x.astype(F32) - mean
    inverse = lax.rsqrt(mm((varied * varied).astype(BF), averager) + 1e-05)
    normed = varied * inverse
    if own_out:
        for g in range(4):
            own_out[0][32 * g : 32 * g + 32, :] = normed[128 * g : 128 * g + 32]
            own_out[1][32 * g : 32 * g + 32, :] = inverse[128 * g : 128 * g + 32]
    normal = jnp.where(present, normed * gain + offset, 0.0).astype(BF)
    rhs_out[:, 0:128] = normal
    rhs_out[:, 128:256] = normed.astype(BF)
    here = jnp.where(present, 1.0, 0.0)
    lane = lax.broadcasted_iota(jnp.int32, (128, 128), 1)
    found = jnp.zeros((128, 128), F32)
    for g in range(4):
        found = jnp.where(lane % 32 // 2 == 4 * a + g, here[128 * g : 128 * g + 128], found)
    found_out[...] = found
    for h in range(2):
        masked = jnp.concatenate(
            [normal[128 * g : 128 * g + 128] for g in (2 * h, 2 * h + 1)], axis=1
        )
        at = slice(128 * h, 128 * h + 128)
        left_out[:, at] = mm_nt(masked, back_ref[:128, :]).astype(BF)
        both = mm_nt(back_ref[...], masked)
        turn_scr[at, :] = both[128:]
        for k in range(2):
            leftt_out[64 * h + 32 * k : 64 * h + 32 * k + 32, :] = jnp.concatenate(
                [both[32 * k : 32 * k + 32], both[32 * k + 64 : 32 * k + 96]], axis=1
            ).astype(BF)

    for e in range(32):
        rightt_out[e] = turn_scr[pl.ds(e, 8, stride=32), :]

    pair = pair_out[...].reshape(256, 128).astype(BF)
    for n in range(2):
        pairs = jnp.concatenate(
            [diagonal_pair(pair[64 * p : 64 * p + 64]) for p in (2 * n, 2 * n + 1)], axis=0
        )
        grad = mm_nt(final_ref[...], pairs).astype(BF)
        for p in range(2):
            for q in range(8):
                rows = 64 * (2 * n + p)
                block = grad[64 * q : 64 * q + 64, 128 * p : 128 * p + 128]
                even, odd = interleave(block[:32], block[32:])
                grad_out[rows : rows + 32, 128 * q : 128 * q + 128] = even
                grad_out[rows + 32 : rows + 64, 128 * q : 128 * q + 128] = odd


def part_kernel(n_row, n_col, place_ref, last_ref, *refs):
    stages = [refs[7 * a : 7 * a + 7] for a in range(n_row - 1)]
    (
        normed_ref, inverse_ref, norm_ref, back_ref, final_ref, first_ref,
        emb_out, final_hbm_out, first_out, second_out, gain_out, offset_out, bias_out,
        right_scr, scaled_scr, grad_scr, outer_scr, all_scr,
        final_out, out_sem, turn_scr,
    ) = refs[7 * (n_row - 1) : -7]
    stages.append(refs[-7:])
    stage_kernel(
        n_col, n_row - 1, place_ref, last_ref, norm_ref, back_ref, final_ref, *stages[-1], turn_scr
    )
    gain = norm_ref[0:1, :]
    averager = averager_of()
    lane = lax.broadcasted_iota(jnp.int32, (128, 128), 1)

    found = sum(stage[6][...] for stage in stages)
    turned = pltpu.roll(found, 64, 1)
    mask = jnp.where((lane % 2 == 0) == (lane < 64), found, turned)
    mask_t = mask.T

    for e in range(32):
        right_scr[32 * e : 32 * e + 32, :] = jnp.concatenate(
            [stage[3][e] for stage in stages], axis=0
        ).astype(BF)

    mask_bf = mask.astype(BF)
    share = 1.0 / (mm_tn(mask_bf, mask_bf)[0:32] + 0.001)
    share_bf = share.astype(BF)
    for i in range(32):
        a, at = i // 8, 32 * (i % 8)
        for q in range(8):
            grad_scr[32 * i : 32 * i + 32, 128 * q : 128 * q + 128] = (
                stages[a][4][at : at + 32, 128 * q : 128 * q + 128] * share_bf[i : i + 1]
            )
    left = jnp.concatenate([stage[1][...] for stage in stages], axis=1)

    turn = spread(
        256, 256, lambda r, c: jnp.where((r // 8 == c % 32) & (r % 8 == c // 32), 1.0, 0.0)
    ).astype(BF)
    mask_two = jnp.concatenate([mask, mask], axis=1)
    for h in range(2):
        parts = []
        for q in (2 * h, 2 * h + 1):
            right_grad = mm(left, grad_scr[:, 256 * q : 256 * q + 256])
            parts.append(mm_nt(turn, (right_grad * mask_two).astype(BF)))
        for t in range(32):
            at = slice(128 * (t // 2), 128 * (t // 2) + 128)
            row = 64 + 32 * (t % 2) + 16 * h
            all_scr[row : row + 16, at] = jnp.concatenate(
                [part[8 * t : 8 * t + 8] for part in parts], axis=0
            ).astype(BF)
    for h in range(4):
        left_grad = mm(grad_scr[256 * h : 256 * h + 256, :], right_scr[...])
        for k in range(8):
            t = 8 * h + k
            at = slice(128 * (t // 2), 128 * (t // 2) + 128)
            row = 32 * (t % 2)
            all_scr[row : row + 32, at] = (
                left_grad[32 * k : 32 * k + 32] * mask_t[t : t + 1]
            ).astype(BF)

    bias = jnp.zeros((32, 128), F32)
    for i in range(32):
        scaled = stages[i // 8][5][i % 8] * jnp.broadcast_to(share[:, i : i + 1], (32, 128))
        bias = bias + scaled
        scaled_scr[32 * i : 32 * i + 32, :] = scaled.astype(BF)
    bias_out[...] = jnp.sum(bias, axis=0, keepdims=True)

    left_t = jnp.concatenate([stage[2][...] for stage in stages], axis=0)
    for n in range(8):
        rights = jnp.concatenate(
            [diagonal_pair(right_scr[64 * p : 64 * p + 64, :]) for p in (2 * n, 2 * n + 1)], axis=0
        )
        outer = mm_nt(left_t, rights).astype(BF)
        for p in range(2):
            for q in range(8):
                rows = 64 * (2 * n + p)
                block = outer[64 * q : 64 * q + 64, 128 * p : 128 * p + 128]
                even, odd = interleave(block[:32], block[32:])
                outer_scr[rows : rows + 32, 128 * q : 128 * q + 128] = even
                outer_scr[rows + 32 : rows + 64, 128 * q : 128 * q + 128] = odd
    for h in range(4):
        final = mm(outer_scr[256 * h : 256 * h + 256, :], scaled_scr[...])
        for k in range(8):
            final_out[pl.ds(8 * h + k, 32, stride=32), :] = final[32 * k : 32 * k + 32]
    final_send = pltpu.make_async_copy(final_out, final_hbm_out, out_sem)
    final_send.start()

    total = mm(
        all_scr[...], jnp.concatenate([stage[0][...] for stage in stages], axis=0)
    )
    sums = all_scr[:, 0:128].astype(F32)
    for g in range(1, 16):
        sums = sums + all_scr[:, 128 * g : 128 * g + 128].astype(F32)

    def fold(block):
        return block[0:32, 0:64] + block[32:64, 64:128]

    first_out[...] = fold(total[0:64, 0:128])
    second_out[...] = fold(total[64:128, 0:128])
    sums = jnp.sum(sums, axis=1, keepdims=True)
    left_sum = sums[0:32] + sums[32:64]
    right_sum = sums[64:96] + sums[96:128]
    first, second = first_ref[0:32, :], first_ref[32:64, :]
    gain_out[...] = jnp.sum(
        first * fold(total[0:64, 128:256]) + second * fold(total[64:128, 128:256]),
        axis=0, keepdims=True,
    )
    offset_out[...] = jnp.sum(first * left_sum + second * right_sum, axis=0, keepdims=True)

    d_hat = []
    for h in range(2):
        sides = [
            jnp.concatenate(
                [all_scr[row : row + 64, 128 * g : 128 * g + 128] for g in (2 * h, 2 * h + 1)], axis=0
            )
            for row in (0, 64)
        ]
        d_normal = mm_tn(jnp.concatenate(sides, axis=0), back_ref[...])
        d_hat += [d_normal[0:32, 0:128] * gain, d_normal[0:32, 128:256] * gain]
    d_hat = jnp.concatenate(d_hat, axis=0)
    normed = normed_ref[...]
    means = mm(jnp.concatenate([d_hat, d_hat * normed], axis=0).astype(BF), averager)
    result = inverse_ref[...] * (d_hat - means[:128] - normed * means[128:])
    for g in range(4):
        emb_out[:, 2 * g, :] = result[32 * g : 32 * g + 32, 0:64]
        emb_out[:, 2 * g + 1, :] = result[32 * g : 32 * g + 32, 64:128]
    final_send.wait()


def vmem(count):
    return [pl.BlockSpec(memory_space=pltpu.VMEM)] * count


LIMIT = pltpu.CompilerParams(vmem_limit_bytes=32 * 1024 * 1024)


def gathered_body(
    n_row,
    n_col,
    homolog_embedding,
    presence_indicator,
    coupling_change_derivative,
    standardizer_scale,
    standardizer_shift,
    first_projection_matrix,
    second_projection_matrix,
    final_projection_matrix,
):
    shards, tokens, features = homolog_embedding.shape
    width = first_projection_matrix.shape[1]
    first_t, second_t = first_projection_matrix.T, second_projection_matrix.T
    shape = lambda *dims: jax.ShapeDtypeStruct(dims, F32)
    held = lambda *dims: pltpu.VMEM(dims, F32)
    held_bf = lambda *dims: pltpu.VMEM(dims, BF)
    hbm = pl.BlockSpec(memory_space=pltpu.HBM)
    place = lax.bitwise_xor(lax.axis_index("row"), lax.axis_index("col"))
    place = place.astype(jnp.int32).reshape(1)
    packed = pl.pallas_call(
        pack_kernel,
        out_shape=held_bf(192, 128),
        in_specs=vmem(3),
        out_specs=vmem(1)[0],
    )(homolog_embedding, presence_indicator.T, coupling_change_derivative)
    def over(axis, size, step, array):
        return lax.ppermute(array, axis, [(k, k ^ step) for k in range(size)])

    far = over("col", n_col, 2, packed)
    near = over("col", n_col, 1, packed)
    last = over("col", n_col, 3, packed)
    front = jnp.stack([packed, last])
    chip_front = over("row", n_row, 2, front)
    rear = jnp.stack([near, far])
    chip_rear = over("row", n_row, 2, rear)
    front, final_projection_matrix = lax.optimization_barrier((front, final_projection_matrix))
    weights = pl.pallas_call(
        weights_kernel,
        out_shape=(
            held(8, 128), held_bf(256, 256), held_bf(width * width // 2, 256), held(2 * width, features),
        ),
        in_specs=[hbm] * 5,
        out_specs=tuple(vmem(4)),
        scratch_shapes=[
            pltpu.VMEM((1, features), F32),
            pltpu.VMEM((1, features), F32),
            pltpu.VMEM((width, features), BF),
            pltpu.VMEM((width, features), BF),
            pltpu.VMEM((width * width, 128), BF),
            pltpu.VMEM((width * width, 128), F32),
            pltpu.SemaphoreType.DMA((5,)),
        ],
        compiler_params=LIMIT,
    )(
        *[
            pltpu.with_memory_space_constraint(x, pltpu.HBM)
            for x in (
                standardizer_scale.reshape(1, features),
                standardizer_shift.reshape(1, features),
                first_t,
                second_t,
                final_projection_matrix,
            )
        ]
    )
    norm, back, final_turned, first = weights
    own = jnp.concatenate([front, rear])
    core = over("row", n_row, 1, own)
    stage_outs = [
        held_bf(512, 256), held_bf(128, 256), held_bf(128, 256), held(width, 8, 128),
        held_bf(256, 1024), held(8, 32, 128), held(128, 128),
    ]
    scalar = pl.BlockSpec(memory_space=pltpu.SMEM)

    def stage(a, block):
        outs = stage_outs + [held(128, 128)] * 2 * (a == 0)
        return pl.pallas_call(
            functools.partial(stage_kernel, n_col, a),
            out_shape=tuple(outs),
            in_specs=[scalar] + vmem(4),
            out_specs=tuple(vmem(len(outs))),
            scratch_shapes=[pltpu.VMEM((256, 128), F32)],
            compiler_params=LIMIT,
            cost_estimate=pl.CostEstimate(
                flops=1_000_000_000, bytes_accessed=4_000_000, transcendentals=0
            ),
        )(place, block, norm, back, final_turned)

    own_stage = stage(0, own)
    core_stage = stage(1, core)
    chip = jnp.concatenate([chip_front, chip_rear])
    chip, own_stage = lax.optimization_barrier((chip, own_stage))
    both = over("row", n_row, 1, chip)
    stages = [own_stage[:7], core_stage, stage(2, chip)]
    outs = pl.pallas_call(
        functools.partial(part_kernel, n_row, n_col),
        out_shape=(
            shape(shards, tokens, features),
            shape(width * width, 128),
            shape(width, features),
            shape(width, features),
            shape(1, features),
            shape(1, features),
            shape(1, 128),
        ),
        in_specs=[scalar] + vmem(7 * (n_row - 1) + 7),
        out_specs=(*vmem(1), hbm, *vmem(5)),
        scratch_shapes=[
            pltpu.VMEM((1024, 128), BF),
            pltpu.VMEM((1024, 128), BF),
            pltpu.VMEM((1024, 1024), BF),
            pltpu.VMEM((1024, 1024), BF),
            pltpu.VMEM((128, 2048), BF),
            pltpu.VMEM((1024, 128), F32),
            pltpu.SemaphoreType.DMA,
            pltpu.VMEM((256, 128), F32),
            *stage_outs,
        ],
        compiler_params=LIMIT,
    )(place, both, *[x for s in stages for x in s], *own_stage[7:], norm, back, final_turned, first)
    emb, final, first, second, gain, offset, bias = outs
    return emb, final, first.T, second.T, gain.reshape(-1), offset.reshape(-1), bias.reshape(-1)


def body(n_row, n_col, *arguments):
    msa, _, pair = arguments[:3]
    width = arguments[5].shape[1]
    fits = (
        n_row == 4
        and n_col == 4
        and msa.shape == (32, 8, 64)
        and pair.shape == (8, 8, 128)
        and width == 32
    )
    if fits:
        return gathered_body(n_row, n_col, *arguments)
    return sharded_body(*arguments)


def solution(mesh):
    placed = (
        P(("grp", "col"), "row", None),
        P(("grp", "col"), "row"),
        P(("grp", "row"), "col", None),
        P(),
        P(),
        P(),
        P(),
        P(),
    )
    return jax.shard_map(
        functools.partial(body, mesh.shape["row"], mesh.shape["col"]),
        mesh=mesh,
        in_specs=placed,
        out_specs=(
            P(("grp", "col"), "row", None),
            P("grp", None),
            P("grp", None),
            P("grp", None),
            P("grp"),
            P("grp"),
            P("grp"),
        ),
        check_vma=False,
    )
```

```python
import functools

import jax
import jax.numpy as jnp
from jax import lax
from jax.experimental import pallas as pl
from jax.experimental.pallas import tpu as pltpu
from jax.sharding import PartitionSpec as P

TOKB = 2


def standardizer_parts(homolog_embedding, standardizer_scale, standardizer_shift):
    incoming_entries = homolog_embedding.astype(jnp.float32)
    center = jnp.mean(incoming_entries, axis=-1, keepdims=True)
    varied = incoming_entries - center
    variance = jnp.mean(varied * varied, axis=-1, keepdims=True)
    reciprocal_spread = lax.rsqrt(variance + 1e-05)
    standardized_entries = varied * reciprocal_spread
    standardized_bfloat = (standardized_entries * standardizer_scale + standardizer_shift).astype(
        jnp.bfloat16
    )
    return (standardized_entries, reciprocal_spread, standardized_bfloat)


def sharded_body(
    homolog_embedding,
    presence_indicator,
    coupling_change_derivative,
    standardizer_scale,
    standardizer_shift,
    first_projection_matrix,
    second_projection_matrix,
    final_projection_matrix,
):
    shard_homolog_number, residue_line_number, feature_number = homolog_embedding.shape
    tok_cols = coupling_change_derivative.shape[1]
    width = first_projection_matrix.shape[1]
    standardized_entries, reciprocal_spread, standardized_bfloat = standardizer_parts(
        homolog_embedding, standardizer_scale, standardizer_shift
    )
    mask_single_precision = presence_indicator.astype(jnp.float32)
    mask_half_precision = presence_indicator.astype(jnp.bfloat16)
    left = (
        jnp.einsum(
            "sic,cp->sip",
            standardized_bfloat,
            first_projection_matrix,
            preferred_element_type=jnp.float32,
        )
        * mask_single_precision[..., None]
    ).astype(jnp.bfloat16)
    right = (
        jnp.einsum(
            "sic,cp->sip",
            standardized_bfloat,
            second_projection_matrix,
            preferred_element_type=jnp.float32,
        )
        * mask_single_precision[..., None]
    ).astype(jnp.bfloat16)
    left_flat = left.reshape(shard_homolog_number, residue_line_number * width)
    right_flat = right.reshape(shard_homolog_number, residue_line_number * width)
    left_all, mask_left = (
        lax.all_gather(left_flat, "col", axis=0, tiled=True),
        lax.all_gather(mask_half_precision, "col", axis=0, tiled=True),
    )
    right_wide, mask_wide = (
        lax.all_gather(right_flat, "row", axis=1, tiled=True),
        lax.all_gather(mask_half_precision, "row", axis=1, tiled=True),
    )
    right_all, mask_right = (
        lax.all_to_all(right_wide, "col", split_axis=1, concat_axis=0, tiled=True),
        lax.all_to_all(mask_wide, "col", split_axis=1, concat_axis=0, tiled=True),
    )
    seq_total = left_all.shape[0]
    right_three = right_all.reshape(seq_total, tok_cols, width)
    counts = jnp.einsum("si,sj->ij", mask_left, mask_right, preferred_element_type=jnp.float32)
    scaled = coupling_change_derivative.astype(jnp.float32) / (counts + 0.001)[..., None]
    bias_part = jnp.sum(scaled, axis=(0, 1))
    scaled_bf = scaled.astype(jnp.bfloat16)
    block_rows = residue_line_number // TOKB
    right_acc = jnp.zeros((seq_total, tok_cols, width), jnp.float32)
    wout_acc = jnp.zeros(final_projection_matrix.shape, jnp.float32)
    left_pieces = []
    for block_index in range(TOKB):
        first = block_index * block_rows
        rows_bf = scaled_bf[first : first + block_rows]
        outer_grad = jnp.einsum(
            "ijz,fz->ijf", rows_bf, final_projection_matrix, preferred_element_type=jnp.float32
        ).astype(jnp.bfloat16)
        outer_grad = outer_grad.reshape(block_rows, tok_cols, width, width)
        left_block = left_all[:, first * width : (first + block_rows) * width].reshape(
            seq_total, block_rows, width
        )
        first_factor_derivative = jnp.einsum(
            "ijce,sje->sic", outer_grad, right_three, preferred_element_type=jnp.float32
        )
        right_acc = right_acc + jnp.einsum(
            "ijce,sic->sje", outer_grad, left_block, preferred_element_type=jnp.float32
        )
        outer = jnp.einsum(
            "sic,sje->ijce", left_block, right_three, preferred_element_type=jnp.float32
        ).astype(jnp.bfloat16)
        outer = outer.reshape(block_rows, tok_cols, width * width)
        wout_acc = wout_acc + jnp.einsum(
            "ijf,ijz->fz", outer, rows_bf, preferred_element_type=jnp.float32
        )
        first_factor_derivative = first_factor_derivative.reshape(seq_total, block_rows * width)
        left_pieces.append(first_factor_derivative)
    left_terms = jnp.concatenate(left_pieces, axis=1)
    left_own = lax.psum_scatter(left_terms, "col", scatter_dimension=0, tiled=True)
    right_spread = lax.all_to_all(
        right_acc.reshape(seq_total, tok_cols * width),
        "col",
        split_axis=0,
        concat_axis=1,
        tiled=True,
    )
    right_own = lax.psum_scatter(right_spread, "row", scatter_dimension=1, tiled=True)
    left_in = (
        left_own.reshape(shard_homolog_number, residue_line_number, width)
        * mask_single_precision[..., None]
    ).astype(jnp.bfloat16)
    right_in = (
        right_own.reshape(shard_homolog_number, residue_line_number, width)
        * mask_single_precision[..., None]
    ).astype(jnp.bfloat16)
    left_part = jnp.einsum(
        "sic,sip->cp", standardized_bfloat, left_in, preferred_element_type=jnp.float32
    )
    right_part = jnp.einsum(
        "sic,sip->cp", standardized_bfloat, right_in, preferred_element_type=jnp.float32
    )
    d_normal = jnp.einsum(
        "sip,cp->sic", left_in, first_projection_matrix, preferred_element_type=jnp.float32
    ) + jnp.einsum(
        "sip,cp->sic", right_in, second_projection_matrix, preferred_element_type=jnp.float32
    )
    gain_part = jnp.sum(d_normal * standardized_entries, axis=(0, 1))
    beta_part = jnp.sum(d_normal, axis=(0, 1))
    standardized_derivative = d_normal * standardizer_scale
    embedding_derivative = reciprocal_spread * (
        standardized_derivative
        - jnp.mean(standardized_derivative, axis=-1, keepdims=True)
        - standardized_entries
        * jnp.mean(standardized_derivative * standardized_entries, axis=-1, keepdims=True)
    )
    (
        final_matrix_derivative,
        first_matrix_derivative,
        second_matrix_derivative,
        scale_factor_derivative,
        shift_term_derivative,
        shift_derivative,
    ) = lax.psum((wout_acc, left_part, right_part, gain_part, beta_part, bias_part), ("row", "col"))
    return (
        embedding_derivative,
        final_matrix_derivative,
        first_matrix_derivative,
        second_matrix_derivative,
        scale_factor_derivative,
        shift_term_derivative,
        shift_derivative,
    )


BF = jnp.bfloat16
F32 = jnp.float32


def spread(rows, cols, rule):
    r = lax.broadcasted_iota(jnp.int32, (rows, cols), 0)
    c = lax.broadcasted_iota(jnp.int32, (rows, cols), 1)
    return rule(r, c)


def mm(a, b):
    return jnp.dot(a, b, preferred_element_type=F32)


def mm_nt(a, b):
    return lax.dot_general(a, b, (((1,), (1,)), ((), ())), preferred_element_type=F32)


def mm_tn(a, b):
    return lax.dot_general(a, b, (((0,), (0,)), ((), ())), preferred_element_type=F32)


def interleave(first, second):
    odd = lax.broadcasted_iota(jnp.int16, (32, 128), 1) & 32 != 0
    return (
        jnp.where(odd, pltpu.roll(second, 32, 1), first),
        jnp.where(odd, second, pltpu.roll(first, 96, 1)),
    )


def diagonal_pair(block):
    zero = jnp.zeros_like(block)
    return jnp.concatenate(
        [jnp.concatenate([block, zero], axis=1), jnp.concatenate([zero, block], axis=1)], axis=0
    )


ABSENT = 1024.0


def pack_kernel(msa_ref, mask_ref, pair_ref, out_ref):
    msa = msa_ref[...].astype(F32)
    pick = spread(8, 512, lambda r, c: jnp.where(c // 64 == r, 1.0, 0.0)).astype(BF)
    present = mm_tn(mask_ref[...].astype(F32).astype(BF), pick) > 0.5
    for g in range(4):
        rows = jnp.concatenate([msa[:, 2 * g, :], msa[:, 2 * g + 1, :]], axis=1)
        out_ref[32 * g : 32 * g + 32, :] = jnp.where(
            present[:, 128 * g : 128 * g + 128], rows, ABSENT
        ).astype(BF)
    out_ref[128:192, :] = pair_ref[...].astype(F32).reshape(64, 128).astype(BF)


def weights_kernel(*refs):
    sources, (norm_out, back_out, final_out, first_out) = refs[:5], refs[5:9]
    held, scr, sems = refs[9:14], refs[14], refs[15]
    copies = [pltpu.make_async_copy(sources[k], held[k], sems.at[k]) for k in range(5)]
    for copy in copies:
        copy.start()
    for copy in copies:
        copy.wait()
    gain_ref, offset_ref, first_ref, second_ref, final_ref = held
    norm_out[...] = jnp.concatenate(
        [
            jnp.concatenate([ref[...]] * 2, axis=1)
            for ref in (gain_ref, offset_ref, gain_ref, offset_ref) * 2
        ],
        axis=0,
    )
    for k, ref in enumerate((first_ref, second_ref)):
        narrow = ref[...].astype(F32)
        first_out[32 * k : 32 * k + 32, :] = narrow
        wide = jnp.concatenate([narrow] * 4, axis=1)
        wide = jnp.concatenate([wide] * 4, axis=0)
        own = spread(128, 256, lambda r, c: r // 32 == c // 64)
        back_out[128 * k : 128 * k + 128, :] = jnp.where(own, wide, 0.0).astype(BF)
    scr[...] = final_ref[...].astype(F32)
    for k in range(16):
        e = 4 * (k // 2) + k % 2
        final_out[32 * k : 32 * k + 32, :] = jnp.concatenate(
            [scr[pl.ds(e, 32, stride=32), :], scr[pl.ds(e + 2, 32, stride=32), :]], axis=1
        ).astype(BF)


def averager_of():
    return spread(128, 128, lambda r, c: jnp.where(r // 64 == c // 64, 1.0 / 64, 0.0)).astype(BF)


ORDER = (0, 2, 1, 3)


def stage_kernel(
    n_col, a, place_ref, set_ref, norm_ref, back_ref, final_ref,
    rhs_out, left_out, leftt_out, rightt_out, grad_out, pair_out, found_out, *rest
):
    *own_out, turn_scr = rest
    for b in range(n_col):
        at = pl.multiple_of(lax.bitwise_xor(place_ref[0], ORDER[b]) * 8, 8)
        pair_out[:, pl.ds(at, 8), :] = set_ref[b, 128:192, :].astype(F32).reshape(8, 8, 128)

    gain = norm_ref[0:1, :]
    offset = norm_ref[1:2, :]
    averager = averager_of()
    x = jnp.concatenate(
        [set_ref[b, 32 * g : 32 * g + 32, :] for g in range(4) for b in range(n_col)], axis=0
    )
    mean = mm(x, averager)
    present = mean < ABSENT / 2
    varied = x.astype(F32) - mean
    inverse = lax.rsqrt(mm((varied * varied).astype(BF), averager) + 1e-05)
    normed = varied * inverse
    if own_out:
        for g in range(4):
            own_out[0][32 * g : 32 * g + 32, :] = normed[128 * g : 128 * g + 32]
            own_out[1][32 * g : 32 * g + 32, :] = inverse[128 * g : 128 * g + 32]
    normal = jnp.where(present, normed * gain + offset, 0.0).astype(BF)
    rhs_out[:, 0:128] = normal
    rhs_out[:, 128:256] = normed.astype(BF)
    here = jnp.where(present, 1.0, 0.0)
    lane = lax.broadcasted_iota(jnp.int32, (128, 128), 1)
    found = jnp.zeros((128, 128), F32)
    for g in range(4):
        found = jnp.where(lane % 32 // 2 == 4 * a + g, here[128 * g : 128 * g + 128], found)
    found_out[...] = found
    for h in range(2):
        masked = jnp.concatenate(
            [normal[128 * g : 128 * g + 128] for g in (2 * h, 2 * h + 1)], axis=1
        )
        at = slice(128 * h, 128 * h + 128)
        left_out[:, at] = mm_nt(masked, back_ref[:128, :]).astype(BF)
        both = mm_nt(back_ref[...], masked)
        turn_scr[at, :] = both[128:]
        for k in range(2):
            leftt_out[64 * h + 32 * k : 64 * h + 32 * k + 32, :] = jnp.concatenate(
                [both[32 * k : 32 * k + 32], both[32 * k + 64 : 32 * k + 96]], axis=1
            ).astype(BF)

    for e in range(32):
        rightt_out[e] = turn_scr[pl.ds(e, 8, stride=32), :]

    pair = pair_out[...].reshape(256, 128).astype(BF)
    for n in range(2):
        pairs = jnp.concatenate(
            [diagonal_pair(pair[64 * p : 64 * p + 64]) for p in (2 * n, 2 * n + 1)], axis=0
        )
        grad = mm_nt(final_ref[...], pairs).astype(BF)
        for p in range(2):
            for q in range(8):
                rows = 64 * (2 * n + p)
                block = grad[64 * q : 64 * q + 64, 128 * p : 128 * p + 128]
                even, odd = interleave(block[:32], block[32:])
                grad_out[rows : rows + 32, 128 * q : 128 * q + 128] = even
                grad_out[rows + 32 : rows + 64, 128 * q : 128 * q + 128] = odd


def part_kernel(n_row, n_col, place_ref, last_ref, *refs):
    stages = [refs[7 * a : 7 * a + 7] for a in range(n_row - 1)]
    (
        normed_ref, inverse_ref, norm_ref, back_ref, final_ref, first_ref,
        emb_out, final_hbm_out, first_out, second_out, gain_out, offset_out, bias_out,
        right_scr, scaled_scr, grad_scr, outer_scr, wide_scr, all_scr,
        final_out, out_sem, turn_scr,
    ) = refs[7 * (n_row - 1) : -7]
    stages.append(refs[-7:])
    stage_kernel(
        n_col, n_row - 1, place_ref, last_ref, norm_ref, back_ref, final_ref, *stages[-1], turn_scr
    )
    gain = norm_ref[0:1, :]
    averager = averager_of()
    lane = lax.broadcasted_iota(jnp.int32, (128, 128), 1)

    found = sum(stage[6][...] for stage in stages)
    turned = pltpu.roll(found, 64, 1)
    mask = jnp.where((lane % 2 == 0) == (lane < 64), found, turned)
    mask_t = mask.T

    for e in range(32):
        right_scr[32 * e : 32 * e + 32, :] = jnp.concatenate(
            [stage[3][e] for stage in stages], axis=0
        ).astype(BF)

    mask_bf = mask.astype(BF)
    share = (1.0 / (mm_tn(mask_bf, mask_bf)[0:32] + 0.001)).astype(BF)
    for i in range(32):
        a, at = i // 8, 32 * (i % 8)
        for q in range(8):
            grad_scr[32 * i : 32 * i + 32, 128 * q : 128 * q + 128] = (
                stages[a][4][at : at + 32, 128 * q : 128 * q + 128] * share[i : i + 1]
            )
    left = jnp.concatenate([stage[1][...] for stage in stages], axis=1)
    right_grad = mm(left, grad_scr[...])
    left_grad = mm(grad_scr[...], right_scr[...])

    turn = spread(
        256, 256, lambda r, c: jnp.where((r // 8 == c % 32) & (r % 8 == c // 32), 1.0, 0.0)
    ).astype(BF)
    mask_two = jnp.concatenate([mask, mask], axis=1)
    right_in = [
        mm_nt(turn, (right_grad[:, 256 * q : 256 * q + 256] * mask_two).astype(BF))
        for q in range(4)
    ]
    for t in range(32):
        at = slice(128 * (t // 2), 128 * (t // 2) + 128)
        row = 32 * (t % 2)
        all_scr[row : row + 32, at] = (
            left_grad[32 * t : 32 * t + 32] * mask_t[t : t + 1]
        ).astype(BF)
        all_scr[row + 64 : row + 96, at] = jnp.concatenate(
            [part[8 * t : 8 * t + 8] for part in right_in], axis=0
        ).astype(BF)

    bias = jnp.zeros((1, 128), F32)
    ones = jnp.ones((128, 128), BF)
    for p in range(8):
        both_on = jnp.concatenate(
            [mask_t[0:32] * mask_t[i : i + 1] for i in range(4 * p, 4 * p + 4)], axis=0
        ).astype(BF)
        counts = mm(both_on, ones)
        pair = stages[p // 2][5][4 * (p % 2) : 4 * (p % 2) + 4]
        scaled = pair.reshape(128, 128) / (counts + 0.001)
        bias = bias + jnp.sum(scaled, axis=0, keepdims=True)
        scaled_scr[128 * p : 128 * p + 128, :] = scaled.astype(BF)
    bias_out[...] = bias

    left_t = jnp.concatenate([stage[2][...] for stage in stages], axis=0)
    for n in range(8):
        rights = jnp.concatenate(
            [diagonal_pair(right_scr[64 * p : 64 * p + 64, :]) for p in (2 * n, 2 * n + 1)], axis=0
        )
        outer = mm_nt(left_t, rights).astype(BF)
        for p in range(2):
            for q in range(8):
                rows = 64 * (2 * n + p)
                block = outer[64 * q : 64 * q + 64, 128 * p : 128 * p + 128]
                even, odd = interleave(block[:32], block[32:])
                outer_scr[rows : rows + 32, 128 * q : 128 * q + 128] = even
                outer_scr[rows + 32 : rows + 64, 128 * q : 128 * q + 128] = odd
    wide_scr[...] = mm(outer_scr[...], scaled_scr[...])
    for c in range(32):
        final_out[32 * c : 32 * c + 32, :] = wide_scr[pl.ds(c, 32, stride=32), :]
    final_send = pltpu.make_async_copy(final_out, final_hbm_out, out_sem)
    final_send.start()

    total = mm(
        all_scr[...], jnp.concatenate([stage[0][...] for stage in stages], axis=0)
    )
    sums = all_scr[:, 0:128].astype(F32)
    for g in range(1, 16):
        sums = sums + all_scr[:, 128 * g : 128 * g + 128].astype(F32)

    def fold(block):
        return block[0:32, 0:64] + block[32:64, 64:128]

    first_out[...] = fold(total[0:64, 0:128])
    second_out[...] = fold(total[64:128, 0:128])
    sums = jnp.sum(sums, axis=1, keepdims=True)
    left_sum = sums[0:32] + sums[32:64]
    right_sum = sums[64:96] + sums[96:128]
    first, second = first_ref[0:32, :], first_ref[32:64, :]
    gain_out[...] = jnp.sum(
        first * fold(total[0:64, 128:256]) + second * fold(total[64:128, 128:256]),
        axis=0, keepdims=True,
    )
    offset_out[...] = jnp.sum(first * left_sum + second * right_sum, axis=0, keepdims=True)

    d_hat = []
    for h in range(2):
        sides = [
            jnp.concatenate(
                [all_scr[row : row + 64, 128 * g : 128 * g + 128] for g in (2 * h, 2 * h + 1)], axis=0
            )
            for row in (0, 64)
        ]
        d_normal = mm_tn(jnp.concatenate(sides, axis=0), back_ref[...])
        d_hat += [d_normal[0:32, 0:128] * gain, d_normal[0:32, 128:256] * gain]
    d_hat = jnp.concatenate(d_hat, axis=0)
    normed = normed_ref[...]
    means = mm(jnp.concatenate([d_hat, d_hat * normed], axis=0).astype(BF), averager)
    result = inverse_ref[...] * (d_hat - means[:128] - normed * means[128:])
    for g in range(4):
        emb_out[:, 2 * g, :] = result[32 * g : 32 * g + 32, 0:64]
        emb_out[:, 2 * g + 1, :] = result[32 * g : 32 * g + 32, 64:128]
    final_send.wait()


def vmem(count):
    return [pl.BlockSpec(memory_space=pltpu.VMEM)] * count


LIMIT = pltpu.CompilerParams(vmem_limit_bytes=32 * 1024 * 1024)


def gathered_body(
    n_row,
    n_col,
    homolog_embedding,
    presence_indicator,
    coupling_change_derivative,
    standardizer_scale,
    standardizer_shift,
    first_projection_matrix,
    second_projection_matrix,
    final_projection_matrix,
):
    shards, tokens, features = homolog_embedding.shape
    width = first_projection_matrix.shape[1]
    first_t, second_t = first_projection_matrix.T, second_projection_matrix.T
    shape = lambda *dims: jax.ShapeDtypeStruct(dims, F32)
    held = lambda *dims: pltpu.VMEM(dims, F32)
    held_bf = lambda *dims: pltpu.VMEM(dims, BF)
    hbm = pl.BlockSpec(memory_space=pltpu.HBM)
    place = lax.bitwise_xor(lax.axis_index("row"), lax.axis_index("col"))
    place = place.astype(jnp.int32).reshape(1)
    packed = pl.pallas_call(
        pack_kernel,
        out_shape=held_bf(192, 128),
        in_specs=vmem(3),
        out_specs=vmem(1)[0],
    )(homolog_embedding, presence_indicator.T, coupling_change_derivative)
    def over(axis, size, step, array):
        return lax.ppermute(array, axis, [(k, k ^ step) for k in range(size)])

    far = over("col", n_col, 2, packed)
    near = over("col", n_col, 1, packed)
    last = over("col", n_col, 3, packed)
    front = jnp.stack([packed, far])
    chip_front = over("row", n_row, 2, front)
    rear = jnp.stack([near, last])
    chip_rear = over("row", n_row, 2, rear)
    front, final_projection_matrix = lax.optimization_barrier((front, final_projection_matrix))
    weights = pl.pallas_call(
        weights_kernel,
        out_shape=(
            held(8, 128), held_bf(256, 256), held_bf(width * width // 2, 256), held(2 * width, features),
        ),
        in_specs=[hbm] * 5,
        out_specs=tuple(vmem(4)),
        scratch_shapes=[
            pltpu.VMEM((1, features), F32),
            pltpu.VMEM((1, features), F32),
            pltpu.VMEM((width, features), BF),
            pltpu.VMEM((width, features), BF),
            pltpu.VMEM((width * width, 128), BF),
            pltpu.VMEM((width * width, 128), F32),
            pltpu.SemaphoreType.DMA((5,)),
        ],
        compiler_params=LIMIT,
    )(
        *[
            pltpu.with_memory_space_constraint(x, pltpu.HBM)
            for x in (
                standardizer_scale.reshape(1, features),
                standardizer_shift.reshape(1, features),
                first_t,
                second_t,
                final_projection_matrix,
            )
        ]
    )
    norm, back, final_turned, first = weights
    own = jnp.concatenate([front, rear])
    core = over("row", n_row, 1, own)
    stage_outs = [
        held_bf(512, 256), held_bf(128, 256), held_bf(128, 256), held(width, 8, 128),
        held_bf(256, 1024), held(8, 32, 128), held(128, 128),
    ]
    scalar = pl.BlockSpec(memory_space=pltpu.SMEM)

    def stage(a, block):
        outs = stage_outs + [held(128, 128)] * 2 * (a == 0)
        return pl.pallas_call(
            functools.partial(stage_kernel, n_col, a),
            out_shape=tuple(outs),
            in_specs=[scalar] + vmem(4),
            out_specs=tuple(vmem(len(outs))),
            scratch_shapes=[pltpu.VMEM((256, 128), F32)],
            compiler_params=LIMIT,
            cost_estimate=pl.CostEstimate(
                flops=1_000_000_000, bytes_accessed=4_000_000, transcendentals=0
            ),
        )(place, block, norm, back, final_turned)

    own_stage = stage(0, own)
    core_stage = stage(1, core)
    chip = jnp.concatenate([chip_front, chip_rear])
    chip, own_stage = lax.optimization_barrier((chip, own_stage))
    both = over("row", n_row, 1, chip)
    stages = [own_stage[:7], core_stage, stage(2, chip)]
    outs = pl.pallas_call(
        functools.partial(part_kernel, n_row, n_col),
        out_shape=(
            shape(shards, tokens, features),
            shape(width * width, 128),
            shape(width, features),
            shape(width, features),
            shape(1, features),
            shape(1, features),
            shape(1, 128),
        ),
        in_specs=[scalar] + vmem(7 * (n_row - 1) + 7),
        out_specs=(*vmem(1), hbm, *vmem(5)),
        scratch_shapes=[
            pltpu.VMEM((1024, 128), BF),
            pltpu.VMEM((1024, 128), BF),
            pltpu.VMEM((1024, 1024), BF),
            pltpu.VMEM((1024, 1024), BF),
            pltpu.VMEM((1024, 128), F32),
            pltpu.VMEM((128, 2048), BF),
            pltpu.VMEM((1024, 128), F32),
            pltpu.SemaphoreType.DMA,
            pltpu.VMEM((256, 128), F32),
            *stage_outs,
        ],
        compiler_params=LIMIT,
    )(place, both, *[x for s in stages for x in s], *own_stage[7:], norm, back, final_turned, first)
    emb, final, first, second, gain, offset, bias = outs
    return emb, final, first.T, second.T, gain.reshape(-1), offset.reshape(-1), bias.reshape(-1)


def body(n_row, n_col, *arguments):
    msa, _, pair = arguments[:3]
    width = arguments[5].shape[1]
    fits = (
        n_row == 4
        and n_col == 4
        and msa.shape == (32, 8, 64)
        and pair.shape == (8, 8, 128)
        and width == 32
    )
    if fits:
        return gathered_body(n_row, n_col, *arguments)
    return sharded_body(*arguments)


def solution(mesh):
    placed = (
        P(("grp", "col"), "row", None),
        P(("grp", "col"), "row"),
        P(("grp", "row"), "col", None),
        P(),
        P(),
        P(),
        P(),
        P(),
    )
    return jax.shard_map(
        functools.partial(body, mesh.shape["row"], mesh.shape["col"]),
        mesh=mesh,
        in_specs=placed,
        out_specs=(
            P(("grp", "col"), "row", None),
            P("grp", None),
            P("grp", None),
            P("grp", None),
            P("grp"),
            P("grp"),
            P("grp"),
        ),
        check_vma=False,
    )
```

```python
import functools

import jax
import jax.numpy as jnp
from jax import lax
from jax.experimental import pallas as pl
from jax.experimental.pallas import tpu as pltpu
from jax.sharding import PartitionSpec as P

TOKB = 2


def standardizer_parts(homolog_embedding, standardizer_scale, standardizer_shift):
    incoming_entries = homolog_embedding.astype(jnp.float32)
    center = jnp.mean(incoming_entries, axis=-1, keepdims=True)
    varied = incoming_entries - center
    variance = jnp.mean(varied * varied, axis=-1, keepdims=True)
    reciprocal_spread = lax.rsqrt(variance + 1e-05)
    standardized_entries = varied * reciprocal_spread
    standardized_bfloat = (standardized_entries * standardizer_scale + standardizer_shift).astype(
        jnp.bfloat16
    )
    return (standardized_entries, reciprocal_spread, standardized_bfloat)


def sharded_body(
    homolog_embedding,
    presence_indicator,
    coupling_change_derivative,
    standardizer_scale,
    standardizer_shift,
    first_projection_matrix,
    second_projection_matrix,
    final_projection_matrix,
):
    shard_homolog_number, residue_line_number, feature_number = homolog_embedding.shape
    tok_cols = coupling_change_derivative.shape[1]
    width = first_projection_matrix.shape[1]
    standardized_entries, reciprocal_spread, standardized_bfloat = standardizer_parts(
        homolog_embedding, standardizer_scale, standardizer_shift
    )
    mask_single_precision = presence_indicator.astype(jnp.float32)
    mask_half_precision = presence_indicator.astype(jnp.bfloat16)
    left = (
        jnp.einsum(
            "sic,cp->sip",
            standardized_bfloat,
            first_projection_matrix,
            preferred_element_type=jnp.float32,
        )
        * mask_single_precision[..., None]
    ).astype(jnp.bfloat16)
    right = (
        jnp.einsum(
            "sic,cp->sip",
            standardized_bfloat,
            second_projection_matrix,
            preferred_element_type=jnp.float32,
        )
        * mask_single_precision[..., None]
    ).astype(jnp.bfloat16)
    left_flat = left.reshape(shard_homolog_number, residue_line_number * width)
    right_flat = right.reshape(shard_homolog_number, residue_line_number * width)
    left_all, mask_left = (
        lax.all_gather(left_flat, "col", axis=0, tiled=True),
        lax.all_gather(mask_half_precision, "col", axis=0, tiled=True),
    )
    right_wide, mask_wide = (
        lax.all_gather(right_flat, "row", axis=1, tiled=True),
        lax.all_gather(mask_half_precision, "row", axis=1, tiled=True),
    )
    right_all, mask_right = (
        lax.all_to_all(right_wide, "col", split_axis=1, concat_axis=0, tiled=True),
        lax.all_to_all(mask_wide, "col", split_axis=1, concat_axis=0, tiled=True),
    )
    seq_total = left_all.shape[0]
    right_three = right_all.reshape(seq_total, tok_cols, width)
    counts = jnp.einsum("si,sj->ij", mask_left, mask_right, preferred_element_type=jnp.float32)
    scaled = coupling_change_derivative.astype(jnp.float32) / (counts + 0.001)[..., None]
    bias_part = jnp.sum(scaled, axis=(0, 1))
    scaled_bf = scaled.astype(jnp.bfloat16)
    block_rows = residue_line_number // TOKB
    right_acc = jnp.zeros((seq_total, tok_cols, width), jnp.float32)
    wout_acc = jnp.zeros(final_projection_matrix.shape, jnp.float32)
    left_pieces = []
    for block_index in range(TOKB):
        first = block_index * block_rows
        rows_bf = scaled_bf[first : first + block_rows]
        outer_grad = jnp.einsum(
            "ijz,fz->ijf", rows_bf, final_projection_matrix, preferred_element_type=jnp.float32
        ).astype(jnp.bfloat16)
        outer_grad = outer_grad.reshape(block_rows, tok_cols, width, width)
        left_block = left_all[:, first * width : (first + block_rows) * width].reshape(
            seq_total, block_rows, width
        )
        first_factor_derivative = jnp.einsum(
            "ijce,sje->sic", outer_grad, right_three, preferred_element_type=jnp.float32
        )
        right_acc = right_acc + jnp.einsum(
            "ijce,sic->sje", outer_grad, left_block, preferred_element_type=jnp.float32
        )
        outer = jnp.einsum(
            "sic,sje->ijce", left_block, right_three, preferred_element_type=jnp.float32
        ).astype(jnp.bfloat16)
        outer = outer.reshape(block_rows, tok_cols, width * width)
        wout_acc = wout_acc + jnp.einsum(
            "ijf,ijz->fz", outer, rows_bf, preferred_element_type=jnp.float32
        )
        first_factor_derivative = first_factor_derivative.reshape(seq_total, block_rows * width)
        left_pieces.append(first_factor_derivative)
    left_terms = jnp.concatenate(left_pieces, axis=1)
    left_own = lax.psum_scatter(left_terms, "col", scatter_dimension=0, tiled=True)
    right_spread = lax.all_to_all(
        right_acc.reshape(seq_total, tok_cols * width),
        "col",
        split_axis=0,
        concat_axis=1,
        tiled=True,
    )
    right_own = lax.psum_scatter(right_spread, "row", scatter_dimension=1, tiled=True)
    left_in = (
        left_own.reshape(shard_homolog_number, residue_line_number, width)
        * mask_single_precision[..., None]
    ).astype(jnp.bfloat16)
    right_in = (
        right_own.reshape(shard_homolog_number, residue_line_number, width)
        * mask_single_precision[..., None]
    ).astype(jnp.bfloat16)
    left_part = jnp.einsum(
        "sic,sip->cp", standardized_bfloat, left_in, preferred_element_type=jnp.float32
    )
    right_part = jnp.einsum(
        "sic,sip->cp", standardized_bfloat, right_in, preferred_element_type=jnp.float32
    )
    d_normal = jnp.einsum(
        "sip,cp->sic", left_in, first_projection_matrix, preferred_element_type=jnp.float32
    ) + jnp.einsum(
        "sip,cp->sic", right_in, second_projection_matrix, preferred_element_type=jnp.float32
    )
    gain_part = jnp.sum(d_normal * standardized_entries, axis=(0, 1))
    beta_part = jnp.sum(d_normal, axis=(0, 1))
    standardized_derivative = d_normal * standardizer_scale
    embedding_derivative = reciprocal_spread * (
        standardized_derivative
        - jnp.mean(standardized_derivative, axis=-1, keepdims=True)
        - standardized_entries
        * jnp.mean(standardized_derivative * standardized_entries, axis=-1, keepdims=True)
    )
    (
        final_matrix_derivative,
        first_matrix_derivative,
        second_matrix_derivative,
        scale_factor_derivative,
        shift_term_derivative,
        shift_derivative,
    ) = lax.psum((wout_acc, left_part, right_part, gain_part, beta_part, bias_part), ("row", "col"))
    return (
        embedding_derivative,
        final_matrix_derivative,
        first_matrix_derivative,
        second_matrix_derivative,
        scale_factor_derivative,
        shift_term_derivative,
        shift_derivative,
    )


BF = jnp.bfloat16
F32 = jnp.float32


def spread(rows, cols, rule):
    r = lax.broadcasted_iota(jnp.int32, (rows, cols), 0)
    c = lax.broadcasted_iota(jnp.int32, (rows, cols), 1)
    return rule(r, c)


def mm(a, b):
    return jnp.dot(a, b, preferred_element_type=F32)


def mm_nt(a, b):
    return lax.dot_general(a, b, (((1,), (1,)), ((), ())), preferred_element_type=F32)


def mm_tn(a, b):
    return lax.dot_general(a, b, (((0,), (0,)), ((), ())), preferred_element_type=F32)


def interleave(first, second):
    odd = lax.broadcasted_iota(jnp.int16, (32, 128), 1) & 32 != 0
    return (
        jnp.where(odd, pltpu.roll(second, 32, 1), first),
        jnp.where(odd, second, pltpu.roll(first, 96, 1)),
    )


def swap_blocks(block):
    upper = lax.broadcasted_iota(jnp.int16, (32, 128), 1) & 64 != 0
    piece = [block[32 * a : 32 * a + 32] for a in range(4)]
    low = [jnp.where(upper, pltpu.roll(piece[a + 2], 64, 1), piece[a]) for a in range(2)]
    high = [jnp.where(upper, piece[a + 2], pltpu.roll(piece[a], 64, 1)) for a in range(2)]
    return jnp.concatenate([*interleave(*low), *interleave(*high)], axis=0)


def diagonal_pair(block):
    zero = jnp.zeros_like(block)
    return jnp.concatenate(
        [jnp.concatenate([block, zero], axis=1), jnp.concatenate([zero, block], axis=1)], axis=0
    )


ABSENT = 1024.0


def pack_kernel(msa_ref, mask_ref, pair_ref, out_ref):
    msa = msa_ref[...].astype(F32)
    pick = spread(8, 512, lambda r, c: jnp.where(c // 64 == r, 1.0, 0.0)).astype(BF)
    present = mm_tn(mask_ref[...].astype(F32).astype(BF), pick) > 0.5
    for g in range(4):
        rows = jnp.concatenate([msa[:, 2 * g, :], msa[:, 2 * g + 1, :]], axis=1)
        out_ref[32 * g : 32 * g + 32, :] = jnp.where(
            present[:, 128 * g : 128 * g + 128], rows, ABSENT
        ).astype(BF)
    out_ref[128:192, :] = pair_ref[...].astype(F32).reshape(64, 128).astype(BF)


def weights_kernel(*refs):
    sources, (norm_out, back_out, final_out, first_out) = refs[:5], refs[5:9]
    held, scr, sems = refs[9:14], refs[14], refs[15]
    copies = [pltpu.make_async_copy(sources[k], held[k], sems.at[k]) for k in range(5)]
    for copy in copies:
        copy.start()
    for copy in copies:
        copy.wait()
    gain_ref, offset_ref, first_ref, second_ref, final_ref = held
    norm_out[...] = jnp.concatenate(
        [
            jnp.concatenate([ref[...]] * 2, axis=1)
            for ref in (gain_ref, offset_ref, gain_ref, offset_ref) * 2
        ],
        axis=0,
    )
    for k, ref in enumerate((first_ref, second_ref)):
        narrow = ref[...].astype(F32)
        first_out[32 * k : 32 * k + 32, :] = narrow
        wide = jnp.concatenate([narrow] * 4, axis=1)
        wide = jnp.concatenate([wide] * 4, axis=0)
        own = spread(128, 256, lambda r, c: r // 32 == c // 64)
        back_out[128 * k : 128 * k + 128, :] = jnp.where(own, wide, 0.0).astype(BF)
    scr[...] = final_ref[...].astype(F32)
    for k in range(16):
        e = 4 * (k // 2) + k % 2
        final_out[32 * k : 32 * k + 32, :] = jnp.concatenate(
            [scr[pl.ds(e, 32, stride=32), :], scr[pl.ds(e + 2, 32, stride=32), :]], axis=1
        ).astype(BF)


def averager_of():
    return spread(128, 128, lambda r, c: jnp.where(r // 64 == c // 64, 1.0 / 64, 0.0)).astype(BF)


ORDER = (0, 2, 1, 3)


def stage_kernel(
    n_col, a, place_ref, set_refs, norm_ref, back_ref, final_ref,
    rhs_out, left_out, leftt_out, rightt_out, grad_out, pair_out, found_out, *rest
):
    *own_out, turn_scr = rest
    blocks = [ref.at[k] for ref in set_refs for k in range(ref.shape[0])]
    for b in range(n_col):
        at = pl.multiple_of(lax.bitwise_xor(place_ref[0], ORDER[b]) * 8, 8)
        pair_out[:, pl.ds(at, 8), :] = blocks[b][128:192, :].astype(F32).reshape(8, 8, 128)

    gain = norm_ref[0:1, :]
    offset = norm_ref[1:2, :]
    averager = averager_of()
    x = jnp.concatenate(
        [blocks[b][32 * g : 32 * g + 32, :] for g in range(4) for b in range(n_col)], axis=0
    )
    mean = mm(x, averager)
    present = mean < ABSENT / 2
    varied = x.astype(F32) - mean
    inverse = lax.rsqrt(mm((varied * varied).astype(BF), averager) + 1e-05)
    normed = varied * inverse
    if own_out:
        for g in range(4):
            own_out[0][32 * g : 32 * g + 32, :] = normed[128 * g : 128 * g + 32]
            own_out[1][32 * g : 32 * g + 32, :] = inverse[128 * g : 128 * g + 32]
    normal = jnp.where(present, normed * gain + offset, 0.0).astype(BF)
    rhs_out[:, 0:128] = normal
    rhs_out[:, 128:256] = normed.astype(BF)
    here = jnp.where(present, 1.0, 0.0)
    lane = lax.broadcasted_iota(jnp.int32, (128, 128), 1)
    found = jnp.zeros((128, 128), F32)
    for g in range(4):
        found = jnp.where(lane % 32 // 2 == 4 * a + g, here[128 * g : 128 * g + 128], found)
    found_out[...] = found
    for h in range(2):
        masked = jnp.concatenate(
            [normal[128 * g : 128 * g + 128] for g in (2 * h, 2 * h + 1)], axis=1
        )
        at = slice(128 * h, 128 * h + 128)
        left_out[:, at] = mm_nt(masked, back_ref[:128, :]).astype(BF)
        both = mm_nt(back_ref[...], masked)
        leftt_out[at, :] = both[:128].astype(BF)
        turn_scr[at, :] = both[128:]

    for e in range(32):
        rightt_out[e] = turn_scr[pl.ds(e, 8, stride=32), :]

    pair = pair_out[...].reshape(256, 128).astype(BF)
    for n in range(2):
        pairs = jnp.concatenate(
            [diagonal_pair(pair[64 * p : 64 * p + 64]) for p in (2 * n, 2 * n + 1)], axis=0
        )
        grad = mm_nt(final_ref[...], pairs).astype(BF)
        for p in range(2):
            for q in range(8):
                rows = 64 * (2 * n + p)
                block = grad[64 * q : 64 * q + 64, 128 * p : 128 * p + 128]
                even, odd = interleave(block[:32], block[32:])
                grad_out[rows : rows + 32, 128 * q : 128 * q + 128] = even
                grad_out[rows + 32 : rows + 64, 128 * q : 128 * q + 128] = odd


def own_kernel(n_col, place_ref, front_ref, rear_ref, norm_ref, back_ref, final_ref, *rest):
    stage_kernel(n_col, 0, place_ref, (front_ref, rear_ref), norm_ref, back_ref, final_ref, *rest)


def pair_kernel(n_col, place_ref, core_ref, front_ref, rear_ref, norm_ref, back_ref, final_ref, *rest):
    common = (norm_ref, back_ref, final_ref)
    stage_kernel(n_col, 1, place_ref, (core_ref,), *common, *rest[:7], rest[14])
    stage_kernel(n_col, 2, place_ref, (front_ref, rear_ref), *common, *rest[7:14], rest[15])


def part_kernel(n_row, n_col, place_ref, front_ref, rear_ref, *refs):
    stages = [refs[7 * a : 7 * a + 7] for a in range(n_row - 1)]
    (
        normed_ref, inverse_ref, norm_ref, back_ref, final_ref, first_ref,
        emb_out, final_hbm_out, first_out, second_out, gain_out, offset_out, bias_out,
        right_scr, rights_scr, scaled_scr, grad_scr, outer_scr, wide_scr, all_scr,
        final_out, out_sem, turn_scr,
    ) = refs[7 * (n_row - 1) : -7]
    stages.append(refs[-7:])
    stage_kernel(
        n_col, n_row - 1, place_ref, (front_ref, rear_ref),
        norm_ref, back_ref, final_ref, *stages[-1], turn_scr,
    )
    gain = norm_ref[0:1, :]
    averager = averager_of()
    lane = lax.broadcasted_iota(jnp.int32, (128, 128), 1)

    found = sum(stage[6][...] for stage in stages)
    turned = pltpu.roll(found, 64, 1)
    mask = jnp.where((lane % 2 == 0) == (lane < 64), found, turned)
    mask_t = mask.T

    for q in range(8):
        at = slice(128 * q, 128 * q + 128)
        block = jnp.concatenate(
            [stage[3][e] for e in range(4 * q, 4 * q + 4) for stage in stages], axis=0
        )
        right_scr[at, :] = block.astype(BF)
        rights_scr[:, at] = block.T.astype(BF)

    mask_bf = mask.astype(BF)
    share = (1.0 / (mm_tn(mask_bf, mask_bf)[0:32] + 0.001)).astype(BF)
    for i in range(32):
        a, at = i // 8, 32 * (i % 8)
        for q in range(8):
            grad_scr[32 * i : 32 * i + 32, 128 * q : 128 * q + 128] = (
                stages[a][4][at : at + 32, 128 * q : 128 * q + 128] * share[i : i + 1]
            )
    left = jnp.concatenate([stage[1][...] for stage in stages], axis=1)
    right_grad = mm(left, grad_scr[...])
    left_grad = mm(grad_scr[...], right_scr[...])

    turn = spread(
        256, 256, lambda r, c: jnp.where((r // 8 == c % 32) & (r % 8 == c // 32), 1.0, 0.0)
    ).astype(BF)
    mask_two = jnp.concatenate([mask, mask], axis=1)
    right_in = [
        mm_nt(turn, (right_grad[:, 256 * q : 256 * q + 256] * mask_two).astype(BF))
        for q in range(4)
    ]
    for t in range(32):
        at = slice(128 * (t // 2), 128 * (t // 2) + 128)
        row = 32 * (t % 2)
        all_scr[row : row + 32, at] = (
            left_grad[32 * t : 32 * t + 32] * mask_t[t : t + 1]
        ).astype(BF)
        all_scr[row + 64 : row + 96, at] = jnp.concatenate(
            [part[8 * t : 8 * t + 8] for part in right_in], axis=0
        ).astype(BF)

    bias = jnp.zeros((1, 128), F32)
    ones = jnp.ones((128, 128), BF)
    for p in range(8):
        both_on = jnp.concatenate(
            [mask_t[0:32] * mask_t[i : i + 1] for i in range(4 * p, 4 * p + 4)], axis=0
        ).astype(BF)
        counts = mm(both_on, ones)
        pair = stages[p // 2][5][4 * (p % 2) : 4 * (p % 2) + 4]
        scaled = pair.reshape(128, 128) / (counts + 0.001)
        bias = bias + jnp.sum(scaled, axis=0, keepdims=True)
        scaled_scr[128 * p : 128 * p + 128, :] = scaled.astype(BF)
    bias_out[...] = bias

    left_t = jnp.concatenate([stage[2][...] for stage in stages], axis=0)
    for n in range(4):
        outer = mm(left_t, rights_scr[:, 256 * n : 256 * n + 256]).astype(BF)
        for p in range(8):
            for q in range(2):
                rows = 256 * n + 128 * q
                outer_scr[rows : rows + 128, 128 * p : 128 * p + 128] = swap_blocks(
                    outer[128 * p : 128 * p + 128, 128 * q : 128 * q + 128]
                )
    wide_scr[...] = mm(outer_scr[...], scaled_scr[...])
    for c in range(32):
        final_out[32 * c : 32 * c + 32, :] = wide_scr[pl.ds(c, 32, stride=32), :]
    final_send = pltpu.make_async_copy(final_out, final_hbm_out, out_sem)
    final_send.start()

    total = mm(
        all_scr[...], jnp.concatenate([stage[0][...] for stage in stages], axis=0)
    )
    sums = all_scr[:, 0:128].astype(F32)
    for g in range(1, 16):
        sums = sums + all_scr[:, 128 * g : 128 * g + 128].astype(F32)

    def fold(block):
        return block[0:32, 0:64] + block[32:64, 64:128]

    first_out[...] = fold(total[0:64, 0:128])
    second_out[...] = fold(total[64:128, 0:128])
    sums = jnp.sum(sums, axis=1, keepdims=True)
    left_sum = sums[0:32] + sums[32:64]
    right_sum = sums[64:96] + sums[96:128]
    first, second = first_ref[0:32, :], first_ref[32:64, :]
    gain_out[...] = jnp.sum(
        first * fold(total[0:64, 128:256]) + second * fold(total[64:128, 128:256]),
        axis=0, keepdims=True,
    )
    offset_out[...] = jnp.sum(first * left_sum + second * right_sum, axis=0, keepdims=True)

    d_hat = []
    for h in range(2):
        sides = [
            jnp.concatenate(
                [all_scr[row : row + 64, 128 * g : 128 * g + 128] for g in (2 * h, 2 * h + 1)], axis=0
            )
            for row in (0, 64)
        ]
        d_normal = mm_tn(jnp.concatenate(sides, axis=0), back_ref[...])
        d_hat += [d_normal[0:32, 0:128] * gain, d_normal[0:32, 128:256] * gain]
    d_hat = jnp.concatenate(d_hat, axis=0)
    normed = normed_ref[...]
    means = mm(jnp.concatenate([d_hat, d_hat * normed], axis=0).astype(BF), averager)
    result = inverse_ref[...] * (d_hat - means[:128] - normed * means[128:])
    for g in range(4):
        emb_out[:, 2 * g, :] = result[32 * g : 32 * g + 32, 0:64]
        emb_out[:, 2 * g + 1, :] = result[32 * g : 32 * g + 32, 64:128]
    final_send.wait()


def vmem(count):
    return [pl.BlockSpec(memory_space=pltpu.VMEM)] * count


LIMIT = pltpu.CompilerParams(vmem_limit_bytes=32 * 1024 * 1024)


def gathered_body(
    n_row,
    n_col,
    homolog_embedding,
    presence_indicator,
    coupling_change_derivative,
    standardizer_scale,
    standardizer_shift,
    first_projection_matrix,
    second_projection_matrix,
    final_projection_matrix,
):
    shards, tokens, features = homolog_embedding.shape
    width = first_projection_matrix.shape[1]
    first_t, second_t = first_projection_matrix.T, second_projection_matrix.T
    shape = lambda *dims: jax.ShapeDtypeStruct(dims, F32)
    held = lambda *dims: pltpu.VMEM(dims, F32)
    held_bf = lambda *dims: pltpu.VMEM(dims, BF)
    hbm = pl.BlockSpec(memory_space=pltpu.HBM)
    place = lax.bitwise_xor(lax.axis_index("row"), lax.axis_index("col"))
    place = place.astype(jnp.int32).reshape(1)
    packed = pl.pallas_call(
        pack_kernel,
        out_shape=held_bf(192, 128),
        in_specs=vmem(3),
        out_specs=vmem(1)[0],
    )(homolog_embedding, presence_indicator.T, coupling_change_derivative)
    def over(axis, size, step, array):
        return lax.ppermute(array, axis, [(k, k ^ step) for k in range(size)])

    far = over("col", n_col, 2, packed)
    near = over("col", n_col, 1, packed)
    last = over("col", n_col, 3, packed)
    front = jnp.stack([packed, far])
    chip_front = over("row", n_row, 2, front)
    rear = jnp.stack([near, last])
    chip_rear = over("row", n_row, 2, rear)
    front, final_projection_matrix = lax.optimization_barrier((front, final_projection_matrix))
    weights = pl.pallas_call(
        weights_kernel,
        out_shape=(
            held(8, 128), held_bf(256, 256), held_bf(width * width // 2, 256), held(2 * width, features),
        ),
        in_specs=[hbm] * 5,
        out_specs=tuple(vmem(4)),
        scratch_shapes=[
            pltpu.VMEM((1, features), F32),
            pltpu.VMEM((1, features), F32),
            pltpu.VMEM((width, features), BF),
            pltpu.VMEM((width, features), BF),
            pltpu.VMEM((width * width, 128), BF),
            pltpu.VMEM((width * width, 128), F32),
            pltpu.SemaphoreType.DMA((5,)),
        ],
        compiler_params=LIMIT,
    )(
        *[
            pltpu.with_memory_space_constraint(x, pltpu.HBM)
            for x in (
                standardizer_scale.reshape(1, features),
                standardizer_shift.reshape(1, features),
                first_t,
                second_t,
                final_projection_matrix,
            )
        ]
    )
    norm, back, final_turned, first = weights
    own = jnp.concatenate([front, rear])
    own, chip_front = lax.optimization_barrier((own, chip_front))
    core = over("row", n_row, 1, own)
    stage_outs = [
        held_bf(512, 256), held_bf(128, 256), held_bf(256, 128), held(width, 8, 128),
        held_bf(256, 1024), held(8, 32, 128), held(128, 128),
    ]
    scalar = pl.BlockSpec(memory_space=pltpu.SMEM)

    def stages_of(kernel, sets, outs, flops):
        return pl.pallas_call(
            functools.partial(kernel, n_col),
            out_shape=tuple(outs),
            in_specs=[scalar] + vmem(len(sets) + 3),
            out_specs=tuple(vmem(len(outs))),
            scratch_shapes=[pltpu.VMEM((256, 128), F32)] * (len(outs) // 7),
            compiler_params=LIMIT,
            cost_estimate=pl.CostEstimate(
                flops=flops, bytes_accessed=flops // 256, transcendentals=0
            ),
        )(place, *sets, norm, back, final_turned)

    both_front = over("row", n_row, 1, chip_front)
    own_stage = stages_of(own_kernel, (front, rear), stage_outs + [held(128, 128)] * 2, 1_000_000_000)
    chip_rear, own_stage = lax.optimization_barrier((chip_rear, own_stage))
    both_rear = over("row", n_row, 1, chip_rear)
    pair_stages = stages_of(pair_kernel, (core, chip_front, chip_rear), stage_outs * 2, 1000000)
    stages = [own_stage[:7], pair_stages]
    outs = pl.pallas_call(
        functools.partial(part_kernel, n_row, n_col),
        out_shape=(
            shape(shards, tokens, features),
            shape(width * width, 128),
            shape(width, features),
            shape(width, features),
            shape(1, features),
            shape(1, features),
            shape(1, 128),
        ),
        in_specs=[scalar] + vmem(7 * (n_row - 1) + 8),
        out_specs=(*vmem(1), hbm, *vmem(5)),
        scratch_shapes=[
            pltpu.VMEM((1024, 128), BF),
            pltpu.VMEM((128, 1024), BF),
            pltpu.VMEM((1024, 128), BF),
            pltpu.VMEM((1024, 1024), BF),
            pltpu.VMEM((1024, 1024), BF),
            pltpu.VMEM((1024, 128), F32),
            pltpu.VMEM((128, 2048), BF),
            pltpu.VMEM((1024, 128), F32),
            pltpu.SemaphoreType.DMA,
            pltpu.VMEM((256, 128), F32),
            *stage_outs,
        ],
        compiler_params=LIMIT,
    )(place, both_front, both_rear, *[x for s in stages for x in s], *own_stage[7:], norm, back, final_turned, first)
    emb, final, first, second, gain, offset, bias = outs
    return emb, final, first.T, second.T, gain.reshape(-1), offset.reshape(-1), bias.reshape(-1)


def body(n_row, n_col, *arguments):
    msa, _, pair = arguments[:3]
    width = arguments[5].shape[1]
    fits = (
        n_row == 4
        and n_col == 4
        and msa.shape == (32, 8, 64)
        and pair.shape == (8, 8, 128)
        and width == 32
    )
    if fits:
        return gathered_body(n_row, n_col, *arguments)
    return sharded_body(*arguments)


def solution(mesh):
    placed = (
        P(("grp", "col"), "row", None),
        P(("grp", "col"), "row"),
        P(("grp", "row"), "col", None),
        P(),
        P(),
        P(),
        P(),
        P(),
    )
    return jax.shard_map(
        functools.partial(body, mesh.shape["row"], mesh.shape["col"]),
        mesh=mesh,
        in_specs=placed,
        out_specs=(
            P(("grp", "col"), "row", None),
            P("grp", None),
            P("grp", None),
            P("grp", None),
            P("grp"),
            P("grp"),
            P("grp"),
        ),
        check_vma=False,
    )
```

```python
import functools

import jax
import jax.numpy as jnp
from jax import lax
from jax.experimental import pallas as pl
from jax.experimental.pallas import tpu as pltpu
from jax.sharding import PartitionSpec as P

TOKB = 2


def standardizer_parts(homolog_embedding, standardizer_scale, standardizer_shift):
    incoming_entries = homolog_embedding.astype(jnp.float32)
    center = jnp.mean(incoming_entries, axis=-1, keepdims=True)
    varied = incoming_entries - center
    variance = jnp.mean(varied * varied, axis=-1, keepdims=True)
    reciprocal_spread = lax.rsqrt(variance + 1e-05)
    standardized_entries = varied * reciprocal_spread
    standardized_bfloat = (standardized_entries * standardizer_scale + standardizer_shift).astype(
        jnp.bfloat16
    )
    return (standardized_entries, reciprocal_spread, standardized_bfloat)


def sharded_body(
    homolog_embedding,
    presence_indicator,
    coupling_change_derivative,
    standardizer_scale,
    standardizer_shift,
    first_projection_matrix,
    second_projection_matrix,
    final_projection_matrix,
):
    shard_homolog_number, residue_line_number, feature_number = homolog_embedding.shape
    tok_cols = coupling_change_derivative.shape[1]
    width = first_projection_matrix.shape[1]
    standardized_entries, reciprocal_spread, standardized_bfloat = standardizer_parts(
        homolog_embedding, standardizer_scale, standardizer_shift
    )
    mask_single_precision = presence_indicator.astype(jnp.float32)
    mask_half_precision = presence_indicator.astype(jnp.bfloat16)
    left = (
        jnp.einsum(
            "sic,cp->sip",
            standardized_bfloat,
            first_projection_matrix,
            preferred_element_type=jnp.float32,
        )
        * mask_single_precision[..., None]
    ).astype(jnp.bfloat16)
    right = (
        jnp.einsum(
            "sic,cp->sip",
            standardized_bfloat,
            second_projection_matrix,
            preferred_element_type=jnp.float32,
        )
        * mask_single_precision[..., None]
    ).astype(jnp.bfloat16)
    left_flat = left.reshape(shard_homolog_number, residue_line_number * width)
    right_flat = right.reshape(shard_homolog_number, residue_line_number * width)
    left_all, mask_left = (
        lax.all_gather(left_flat, "col", axis=0, tiled=True),
        lax.all_gather(mask_half_precision, "col", axis=0, tiled=True),
    )
    right_wide, mask_wide = (
        lax.all_gather(right_flat, "row", axis=1, tiled=True),
        lax.all_gather(mask_half_precision, "row", axis=1, tiled=True),
    )
    right_all, mask_right = (
        lax.all_to_all(right_wide, "col", split_axis=1, concat_axis=0, tiled=True),
        lax.all_to_all(mask_wide, "col", split_axis=1, concat_axis=0, tiled=True),
    )
    seq_total = left_all.shape[0]
    right_three = right_all.reshape(seq_total, tok_cols, width)
    counts = jnp.einsum("si,sj->ij", mask_left, mask_right, preferred_element_type=jnp.float32)
    scaled = coupling_change_derivative.astype(jnp.float32) / (counts + 0.001)[..., None]
    bias_part = jnp.sum(scaled, axis=(0, 1))
    scaled_bf = scaled.astype(jnp.bfloat16)
    block_rows = residue_line_number // TOKB
    right_acc = jnp.zeros((seq_total, tok_cols, width), jnp.float32)
    wout_acc = jnp.zeros(final_projection_matrix.shape, jnp.float32)
    left_pieces = []
    for block_index in range(TOKB):
        first = block_index * block_rows
        rows_bf = scaled_bf[first : first + block_rows]
        outer_grad = jnp.einsum(
            "ijz,fz->ijf", rows_bf, final_projection_matrix, preferred_element_type=jnp.float32
        ).astype(jnp.bfloat16)
        outer_grad = outer_grad.reshape(block_rows, tok_cols, width, width)
        left_block = left_all[:, first * width : (first + block_rows) * width].reshape(
            seq_total, block_rows, width
        )
        first_factor_derivative = jnp.einsum(
            "ijce,sje->sic", outer_grad, right_three, preferred_element_type=jnp.float32
        )
        right_acc = right_acc + jnp.einsum(
            "ijce,sic->sje", outer_grad, left_block, preferred_element_type=jnp.float32
        )
        outer = jnp.einsum(
            "sic,sje->ijce", left_block, right_three, preferred_element_type=jnp.float32
        ).astype(jnp.bfloat16)
        outer = outer.reshape(block_rows, tok_cols, width * width)
        wout_acc = wout_acc + jnp.einsum(
            "ijf,ijz->fz", outer, rows_bf, preferred_element_type=jnp.float32
        )
        first_factor_derivative = first_factor_derivative.reshape(seq_total, block_rows * width)
        left_pieces.append(first_factor_derivative)
    left_terms = jnp.concatenate(left_pieces, axis=1)
    left_own = lax.psum_scatter(left_terms, "col", scatter_dimension=0, tiled=True)
    right_spread = lax.all_to_all(
        right_acc.reshape(seq_total, tok_cols * width),
        "col",
        split_axis=0,
        concat_axis=1,
        tiled=True,
    )
    right_own = lax.psum_scatter(right_spread, "row", scatter_dimension=1, tiled=True)
    left_in = (
        left_own.reshape(shard_homolog_number, residue_line_number, width)
        * mask_single_precision[..., None]
    ).astype(jnp.bfloat16)
    right_in = (
        right_own.reshape(shard_homolog_number, residue_line_number, width)
        * mask_single_precision[..., None]
    ).astype(jnp.bfloat16)
    left_part = jnp.einsum(
        "sic,sip->cp", standardized_bfloat, left_in, preferred_element_type=jnp.float32
    )
    right_part = jnp.einsum(
        "sic,sip->cp", standardized_bfloat, right_in, preferred_element_type=jnp.float32
    )
    d_normal = jnp.einsum(
        "sip,cp->sic", left_in, first_projection_matrix, preferred_element_type=jnp.float32
    ) + jnp.einsum(
        "sip,cp->sic", right_in, second_projection_matrix, preferred_element_type=jnp.float32
    )
    gain_part = jnp.sum(d_normal * standardized_entries, axis=(0, 1))
    beta_part = jnp.sum(d_normal, axis=(0, 1))
    standardized_derivative = d_normal * standardizer_scale
    embedding_derivative = reciprocal_spread * (
        standardized_derivative
        - jnp.mean(standardized_derivative, axis=-1, keepdims=True)
        - standardized_entries
        * jnp.mean(standardized_derivative * standardized_entries, axis=-1, keepdims=True)
    )
    (
        final_matrix_derivative,
        first_matrix_derivative,
        second_matrix_derivative,
        scale_factor_derivative,
        shift_term_derivative,
        shift_derivative,
    ) = lax.psum((wout_acc, left_part, right_part, gain_part, beta_part, bias_part), ("row", "col"))
    return (
        embedding_derivative,
        final_matrix_derivative,
        first_matrix_derivative,
        second_matrix_derivative,
        scale_factor_derivative,
        shift_term_derivative,
        shift_derivative,
    )


BF = jnp.bfloat16
F32 = jnp.float32


def spread(rows, cols, rule):
    r = lax.broadcasted_iota(jnp.int32, (rows, cols), 0)
    c = lax.broadcasted_iota(jnp.int32, (rows, cols), 1)
    return rule(r, c)


def mm(a, b):
    return jnp.dot(a, b, preferred_element_type=F32)


def mm_nt(a, b):
    return lax.dot_general(a, b, (((1,), (1,)), ((), ())), preferred_element_type=F32)


def mm_tn(a, b):
    return lax.dot_general(a, b, (((0,), (0,)), ((), ())), preferred_element_type=F32)


def diagonal(block, count):
    zero = jnp.zeros_like(block)
    return jnp.concatenate(
        [
            jnp.concatenate([block if a == b else zero for b in range(count)], axis=1)
            for a in range(count)
        ],
        axis=0,
    )


ABSENT = 1024.0


def pack_kernel(msa_ref, mask_ref, pair_ref, out_ref):
    msa = msa_ref[...].astype(F32)
    pick = spread(8, 512, lambda r, c: jnp.where(c // 64 == r, 1.0, 0.0)).astype(BF)
    present = mm_tn(mask_ref[...].astype(F32).astype(BF), pick) > 0.5
    for g in range(4):
        rows = jnp.concatenate([msa[:, 2 * g, :], msa[:, 2 * g + 1, :]], axis=1)
        out_ref[32 * g : 32 * g + 32, :] = jnp.where(
            present[:, 128 * g : 128 * g + 128], rows, ABSENT
        ).astype(BF)
    out_ref[128:192, :] = pair_ref[...].astype(F32).reshape(64, 128).astype(BF)


def weights_kernel(*refs):
    sources, (norm_out, back_out, final_out, first_out) = refs[:5], refs[5:9]
    held, scr, sems = refs[9:14], refs[14], refs[15]
    copies = [pltpu.make_async_copy(sources[k], held[k], sems.at[k]) for k in range(5)]
    for copy in copies:
        copy.start()
    for copy in copies:
        copy.wait()
    gain_ref, offset_ref, first_ref, second_ref, final_ref = held
    norm_out[...] = jnp.concatenate(
        [
            jnp.concatenate([ref[...]] * 2, axis=1)
            for ref in (gain_ref, offset_ref, gain_ref, offset_ref) * 2
        ],
        axis=0,
    )
    for k, ref in enumerate((first_ref, second_ref)):
        narrow = ref[...].astype(F32)
        first_out[32 * k : 32 * k + 32, :] = narrow
        wide = jnp.concatenate([narrow] * 4, axis=1)
        wide = jnp.concatenate([wide] * 4, axis=0)
        own = spread(128, 256, lambda r, c: r // 32 == c // 64)
        back_out[128 * k : 128 * k + 128, :] = jnp.where(own, wide, 0.0).astype(BF)
    scr[...] = final_ref[...].astype(F32)
    for q in range(8):
        final_out[32 * q : 32 * q + 32, :] = jnp.concatenate(
            [scr[pl.ds(e, 32, stride=32), :] for e in range(4 * q, 4 * q + 4)], axis=1
        ).astype(BF)


def averager_of():
    return spread(128, 128, lambda r, c: jnp.where(r // 64 == c // 64, 1.0 / 64, 0.0)).astype(BF)


ORDER = (0, 2, 1, 3)


def stage_kernel(
    n_col, a, place_ref, set_refs, norm_ref, back_ref, final_ref,
    rhs_out, left_out, leftt_out, rightt_out, grad_out, pair_out, found_out, *rest
):
    *own_out, turn_scr = rest
    blocks = [ref.at[k] for ref in set_refs for k in range(ref.shape[0])]
    for b in range(n_col):
        at = pl.multiple_of(lax.bitwise_xor(place_ref[0], ORDER[b]) * 8, 8)
        pair_out[:, pl.ds(at, 8), :] = blocks[b][128:192, :].astype(F32).reshape(8, 8, 128)

    gain = norm_ref[0:1, :]
    offset = norm_ref[1:2, :]
    averager = averager_of()
    x = jnp.concatenate(
        [blocks[b][32 * g : 32 * g + 32, :] for g in range(4) for b in range(n_col)], axis=0
    )
    mean = mm(x, averager)
    present = mean < ABSENT / 2
    varied = x.astype(F32) - mean
    inverse = lax.rsqrt(mm((varied * varied).astype(BF), averager) + 1e-05)
    normed = varied * inverse
    if own_out:
        for g in range(4):
            own_out[0][32 * g : 32 * g + 32, :] = normed[128 * g : 128 * g + 32]
            own_out[1][32 * g : 32 * g + 32, :] = inverse[128 * g : 128 * g + 32]
    normal = jnp.where(present, normed * gain + offset, 0.0).astype(BF)
    rhs_out[:, 0:128] = normal
    rhs_out[:, 128:256] = normed.astype(BF)
    here = jnp.where(present, 1.0, 0.0)
    lane = lax.broadcasted_iota(jnp.int32, (128, 128), 1)
    found = jnp.zeros((128, 128), F32)
    for g in range(4):
        found = jnp.where(lane % 32 // 2 == 4 * a + g, here[128 * g : 128 * g + 128], found)
    found_out[...] = found
    for h in range(2):
        masked = jnp.concatenate(
            [normal[128 * g : 128 * g + 128] for g in (2 * h, 2 * h + 1)], axis=1
        )
        at = slice(128 * h, 128 * h + 128)
        left_out[:, at] = mm_nt(masked, back_ref[:128, :]).astype(BF)
        both = mm_nt(back_ref[...], masked)
        turn_scr[at, :] = both[128:]
        for k in range(2):
            leftt_out[64 * h + 32 * k : 64 * h + 32 * k + 32, :] = jnp.concatenate(
                [both[32 * k : 32 * k + 32], both[32 * k + 64 : 32 * k + 96]], axis=1
            ).astype(BF)

    for e in range(32):
        rightt_out[e] = turn_scr[pl.ds(e, 8, stride=32), :]

    for n in range(4):
        pairs = jnp.concatenate(
            [diagonal(pair_out[i].astype(BF), 4) for i in (2 * n, 2 * n + 1)], axis=0
        )
        grad = mm_nt(final_ref[...], pairs).astype(BF)
        for i in range(2):
            rows = 32 * (2 * n + i)
            for q in range(8):
                grad_out[rows : rows + 32, 128 * q : 128 * q + 128] = (
                    grad[32 * q : 32 * q + 32, 128 * i : 128 * i + 128]
                )


def own_kernel(n_col, place_ref, front_ref, rear_ref, norm_ref, back_ref, final_ref, *rest):
    stage_kernel(n_col, 0, place_ref, (front_ref, rear_ref), norm_ref, back_ref, final_ref, *rest)


def pair_kernel(n_col, place_ref, core_ref, front_ref, rear_ref, norm_ref, back_ref, final_ref, *rest):
    common = (norm_ref, back_ref, final_ref)
    stage_kernel(n_col, 1, place_ref, (core_ref,), *common, *rest[:7], rest[14])
    stage_kernel(n_col, 2, place_ref, (front_ref, rear_ref), *common, *rest[7:14], rest[15])


def part_kernel(n_row, n_col, place_ref, front_ref, rear_ref, *refs):
    stages = [refs[7 * a : 7 * a + 7] for a in range(n_row - 1)]
    (
        normed_ref, inverse_ref, norm_ref, back_ref, final_ref, first_ref,
        emb_out, final_hbm_out, first_out, second_out, gain_out, offset_out, bias_out,
        right_scr, scaled_scr, grad_scr, outer_scr, wide_scr, all_scr,
        final_out, out_sem, turn_scr,
    ) = refs[7 * (n_row - 1) : -7]
    stages.append(refs[-7:])
    stage_kernel(
        n_col, n_row - 1, place_ref, (front_ref, rear_ref),
        norm_ref, back_ref, final_ref, *stages[-1], turn_scr,
    )
    gain = norm_ref[0:1, :]
    averager = averager_of()
    lane = lax.broadcasted_iota(jnp.int32, (128, 128), 1)

    found = sum(stage[6][...] for stage in stages)
    turned = pltpu.roll(found, 64, 1)
    mask = jnp.where((lane % 2 == 0) == (lane < 64), found, turned)
    mask_t = mask.T

    for e in range(32):
        right_scr[32 * e : 32 * e + 32, :] = jnp.concatenate(
            [stage[3][e] for stage in stages], axis=0
        ).astype(BF)

    mask_bf = mask.astype(BF)
    share = (1.0 / (mm_tn(mask_bf, mask_bf)[0:32] + 0.001)).astype(BF)
    for i in range(32):
        a, at = i // 8, 32 * (i % 8)
        for q in range(8):
            grad_scr[32 * i : 32 * i + 32, 128 * q : 128 * q + 128] = (
                stages[a][4][at : at + 32, 128 * q : 128 * q + 128] * share[i : i + 1]
            )
    left = jnp.concatenate([stage[1][...] for stage in stages], axis=1)
    right_grad = mm(left, grad_scr[...])
    left_grad = mm(grad_scr[...], right_scr[...])

    turn = spread(
        256, 256, lambda r, c: jnp.where((r // 8 == c % 32) & (r % 8 == c // 32), 1.0, 0.0)
    ).astype(BF)
    mask_two = jnp.concatenate([mask, mask], axis=1)
    right_in = [
        mm_nt(turn, (right_grad[:, 256 * q : 256 * q + 256] * mask_two).astype(BF))
        for q in range(4)
    ]
    for t in range(32):
        at = slice(128 * (t // 2), 128 * (t // 2) + 128)
        row = 32 * (t % 2)
        all_scr[row : row + 32, at] = (
            left_grad[32 * t : 32 * t + 32] * mask_t[t : t + 1]
        ).astype(BF)
        all_scr[row + 64 : row + 96, at] = jnp.concatenate(
            [part[8 * t : 8 * t + 8] for part in right_in], axis=0
        ).astype(BF)

    bias = jnp.zeros((1, 128), F32)
    ones = jnp.ones((128, 128), BF)
    zero = jnp.zeros((32, 128), BF)
    for p in range(8):
        both_on = jnp.concatenate(
            [mask_t[0:32] * mask_t[i : i + 1] for i in range(4 * p, 4 * p + 4)], axis=0
        ).astype(BF)
        counts = mm(both_on, ones)
        pair = stages[p // 2][5][4 * (p % 2) : 4 * (p % 2) + 4]
        scaled = pair.reshape(128, 128) / (counts + 0.001)
        bias = bias + jnp.sum(scaled, axis=0, keepdims=True)
        scaled = scaled.astype(BF)
        for k in range(4):
            at = 256 * p + 128 * (k % 2) + 64 * (k // 2)
            part = scaled[32 * k : 32 * k + 32]
            scaled_scr[at : at + 32, 0:128] = part
            scaled_scr[at : at + 32, 128:256] = zero
            scaled_scr[at + 32 : at + 64, 0:128] = zero
            scaled_scr[at + 32 : at + 64, 128:256] = part
    bias_out[...] = bias

    left_t = jnp.concatenate([stage[2][...] for stage in stages], axis=0)
    for n in range(8):
        rights = jnp.concatenate(
            [diagonal(right_scr[64 * p : 64 * p + 64, :], 2) for p in (2 * n, 2 * n + 1)], axis=0
        )
        outer = mm_nt(left_t, rights).astype(BF)
        for p in range(2):
            rows = 32 * (2 * n + p)
            for k in range(16):
                outer_scr[rows : rows + 32, 128 * k : 128 * k + 128] = (
                    outer[32 * k : 32 * k + 32, 128 * p : 128 * p + 128]
                )
    final = mm(outer_scr[...], scaled_scr[...])
    for e in range(32):
        wide_scr[32 * e : 32 * e + 32, :] = (
            final[32 * (e // 2) : 32 * (e // 2) + 32, 128 * (e % 2) : 128 * (e % 2) + 128]
        )
    for c in range(32):
        final_out[32 * c : 32 * c + 32, :] = wide_scr[pl.ds(c, 32, stride=32), :]
    final_send = pltpu.make_async_copy(final_out, final_hbm_out, out_sem)
    final_send.start()

    total = mm(
        all_scr[...], jnp.concatenate([stage[0][...] for stage in stages], axis=0)
    )
    sums = all_scr[:, 0:128].astype(F32)
    for g in range(1, 16):
        sums = sums + all_scr[:, 128 * g : 128 * g + 128].astype(F32)

    def fold(block):
        return block[0:32, 0:64] + block[32:64, 64:128]

    first_out[...] = fold(total[0:64, 0:128])
    second_out[...] = fold(total[64:128, 0:128])
    sums = jnp.sum(sums, axis=1, keepdims=True)
    left_sum = sums[0:32] + sums[32:64]
    right_sum = sums[64:96] + sums[96:128]
    first, second = first_ref[0:32, :], first_ref[32:64, :]
    gain_out[...] = jnp.sum(
        first * fold(total[0:64, 128:256]) + second * fold(total[64:128, 128:256]),
        axis=0, keepdims=True,
    )
    offset_out[...] = jnp.sum(first * left_sum + second * right_sum, axis=0, keepdims=True)

    d_hat = []
    for h in range(2):
        sides = [
            jnp.concatenate(
                [all_scr[row : row + 64, 128 * g : 128 * g + 128] for g in (2 * h, 2 * h + 1)], axis=0
            )
            for row in (0, 64)
        ]
        d_normal = mm_tn(jnp.concatenate(sides, axis=0), back_ref[...])
        d_hat += [d_normal[0:32, 0:128] * gain, d_normal[0:32, 128:256] * gain]
    d_hat = jnp.concatenate(d_hat, axis=0)
    normed = normed_ref[...]
    means = mm(jnp.concatenate([d_hat, d_hat * normed], axis=0).astype(BF), averager)
    result = inverse_ref[...] * (d_hat - means[:128] - normed * means[128:])
    for g in range(4):
        emb_out[:, 2 * g, :] = result[32 * g : 32 * g + 32, 0:64]
        emb_out[:, 2 * g + 1, :] = result[32 * g : 32 * g + 32, 64:128]
    final_send.wait()


def vmem(count):
    return [pl.BlockSpec(memory_space=pltpu.VMEM)] * count


LIMIT = pltpu.CompilerParams(vmem_limit_bytes=32 * 1024 * 1024)


def gathered_body(
    n_row,
    n_col,
    homolog_embedding,
    presence_indicator,
    coupling_change_derivative,
    standardizer_scale,
    standardizer_shift,
    first_projection_matrix,
    second_projection_matrix,
    final_projection_matrix,
):
    shards, tokens, features = homolog_embedding.shape
    width = first_projection_matrix.shape[1]
    first_t, second_t = first_projection_matrix.T, second_projection_matrix.T
    shape = lambda *dims: jax.ShapeDtypeStruct(dims, F32)
    held = lambda *dims: pltpu.VMEM(dims, F32)
    held_bf = lambda *dims: pltpu.VMEM(dims, BF)
    hbm = pl.BlockSpec(memory_space=pltpu.HBM)
    place = lax.bitwise_xor(lax.axis_index("row"), lax.axis_index("col"))
    place = place.astype(jnp.int32).reshape(1)
    packed = pl.pallas_call(
        pack_kernel,
        out_shape=held_bf(192, 128),
        in_specs=vmem(3),
        out_specs=vmem(1)[0],
    )(homolog_embedding, presence_indicator.T, coupling_change_derivative)
    def over(axis, size, step, array):
        return lax.ppermute(array, axis, [(k, k ^ step) for k in range(size)])

    far = over("col", n_col, 2, packed)
    near = over("col", n_col, 1, packed)
    last = over("col", n_col, 3, packed)
    front = jnp.stack([packed, far])
    chip_front = over("row", n_row, 2, front)
    rear = jnp.stack([near, last])
    chip_rear = over("row", n_row, 2, rear)
    front, final_projection_matrix = lax.optimization_barrier((front, final_projection_matrix))
    weights = pl.pallas_call(
        weights_kernel,
        out_shape=(
            held(8, 128), held_bf(256, 256), held_bf(width * width // 4, 512), held(2 * width, features),
        ),
        in_specs=[hbm] * 5,
        out_specs=tuple(vmem(4)),
        scratch_shapes=[
            pltpu.VMEM((1, features), F32),
            pltpu.VMEM((1, features), F32),
            pltpu.VMEM((width, features), BF),
            pltpu.VMEM((width, features), BF),
            pltpu.VMEM((width * width, 128), BF),
            pltpu.VMEM((width * width, 128), F32),
            pltpu.SemaphoreType.DMA((5,)),
        ],
        compiler_params=LIMIT,
    )(
        *[
            pltpu.with_memory_space_constraint(x, pltpu.HBM)
            for x in (
                standardizer_scale.reshape(1, features),
                standardizer_shift.reshape(1, features),
                first_t,
                second_t,
                final_projection_matrix,
            )
        ]
    )
    norm, back, final_turned, first = weights
    own = jnp.concatenate([front, rear])
    own, chip_front = lax.optimization_barrier((own, chip_front))
    core = over("row", n_row, 1, own)
    stage_outs = [
        held_bf(512, 256), held_bf(128, 256), held_bf(128, 256), held(width, 8, 128),
        held_bf(256, 1024), held(8, 32, 128), held(128, 128),
    ]
    scalar = pl.BlockSpec(memory_space=pltpu.SMEM)

    def stages_of(kernel, sets, outs, flops):
        return pl.pallas_call(
            functools.partial(kernel, n_col),
            out_shape=tuple(outs),
            in_specs=[scalar] + vmem(len(sets) + 3),
            out_specs=tuple(vmem(len(outs))),
            scratch_shapes=[pltpu.VMEM((256, 128), F32)] * (len(outs) // 7),
            compiler_params=LIMIT,
            cost_estimate=pl.CostEstimate(
                flops=flops, bytes_accessed=flops // 256, transcendentals=0
            ),
        )(place, *sets, norm, back, final_turned)

    both_front = over("row", n_row, 1, chip_front)
    own_stage = stages_of(own_kernel, (front, rear), stage_outs + [held(128, 128)] * 2, 1_000_000_000)
    chip_rear, own_stage = lax.optimization_barrier((chip_rear, own_stage))
    both_rear = over("row", n_row, 1, chip_rear)
    pair_stages = stages_of(pair_kernel, (core, chip_front, chip_rear), stage_outs * 2, 1000000)
    stages = [own_stage[:7], pair_stages]
    outs = pl.pallas_call(
        functools.partial(part_kernel, n_row, n_col),
        out_shape=(
            shape(shards, tokens, features),
            shape(width * width, 128),
            shape(width, features),
            shape(width, features),
            shape(1, features),
            shape(1, features),
            shape(1, 128),
        ),
        in_specs=[scalar] + vmem(7 * (n_row - 1) + 8),
        out_specs=(*vmem(1), hbm, *vmem(5)),
        scratch_shapes=[
            pltpu.VMEM((1024, 128), BF),
            pltpu.VMEM((2048, 256), BF),
            pltpu.VMEM((1024, 1024), BF),
            pltpu.VMEM((512, 2048), BF),
            pltpu.VMEM((1024, 128), F32),
            pltpu.VMEM((128, 2048), BF),
            pltpu.VMEM((1024, 128), F32),
            pltpu.SemaphoreType.DMA,
            pltpu.VMEM((256, 128), F32),
            *stage_outs,
        ],
        compiler_params=LIMIT,
    )(place, both_front, both_rear, *[x for s in stages for x in s], *own_stage[7:], norm, back, final_turned, first)
    emb, final, first, second, gain, offset, bias = outs
    return emb, final, first.T, second.T, gain.reshape(-1), offset.reshape(-1), bias.reshape(-1)


def body(n_row, n_col, *arguments):
    msa, _, pair = arguments[:3]
    width = arguments[5].shape[1]
    fits = (
        n_row == 4
        and n_col == 4
        and msa.shape == (32, 8, 64)
        and pair.shape == (8, 8, 128)
        and width == 32
    )
    if fits:
        return gathered_body(n_row, n_col, *arguments)
    return sharded_body(*arguments)


def solution(mesh):
    placed = (
        P(("grp", "col"), "row", None),
        P(("grp", "col"), "row"),
        P(("grp", "row"), "col", None),
        P(),
        P(),
        P(),
        P(),
        P(),
    )
    return jax.shard_map(
        functools.partial(body, mesh.shape["row"], mesh.shape["col"]),
        mesh=mesh,
        in_specs=placed,
        out_specs=(
            P(("grp", "col"), "row", None),
            P("grp", None),
            P("grp", None),
            P("grp", None),
            P("grp"),
            P("grp"),
            P("grp"),
        ),
        check_vma=False,
    )
```

```python
import functools

import jax
import jax.numpy as jnp
from jax import lax
from jax.experimental import pallas as pl
from jax.experimental.pallas import tpu as pltpu
from jax.sharding import PartitionSpec as P

TOKB = 2


def standardizer_parts(homolog_embedding, standardizer_scale, standardizer_shift):
    incoming_entries = homolog_embedding.astype(jnp.float32)
    center = jnp.mean(incoming_entries, axis=-1, keepdims=True)
    varied = incoming_entries - center
    variance = jnp.mean(varied * varied, axis=-1, keepdims=True)
    reciprocal_spread = lax.rsqrt(variance + 1e-05)
    standardized_entries = varied * reciprocal_spread
    standardized_bfloat = (standardized_entries * standardizer_scale + standardizer_shift).astype(
        jnp.bfloat16
    )
    return (standardized_entries, reciprocal_spread, standardized_bfloat)


def sharded_body(
    homolog_embedding,
    presence_indicator,
    coupling_change_derivative,
    standardizer_scale,
    standardizer_shift,
    first_projection_matrix,
    second_projection_matrix,
    final_projection_matrix,
):
    shard_homolog_number, residue_line_number, feature_number = homolog_embedding.shape
    tok_cols = coupling_change_derivative.shape[1]
    width = first_projection_matrix.shape[1]
    standardized_entries, reciprocal_spread, standardized_bfloat = standardizer_parts(
        homolog_embedding, standardizer_scale, standardizer_shift
    )
    mask_single_precision = presence_indicator.astype(jnp.float32)
    mask_half_precision = presence_indicator.astype(jnp.bfloat16)
    left = (
        jnp.einsum(
            "sic,cp->sip",
            standardized_bfloat,
            first_projection_matrix,
            preferred_element_type=jnp.float32,
        )
        * mask_single_precision[..., None]
    ).astype(jnp.bfloat16)
    right = (
        jnp.einsum(
            "sic,cp->sip",
            standardized_bfloat,
            second_projection_matrix,
            preferred_element_type=jnp.float32,
        )
        * mask_single_precision[..., None]
    ).astype(jnp.bfloat16)
    left_flat = left.reshape(shard_homolog_number, residue_line_number * width)
    right_flat = right.reshape(shard_homolog_number, residue_line_number * width)
    left_all, mask_left = (
        lax.all_gather(left_flat, "col", axis=0, tiled=True),
        lax.all_gather(mask_half_precision, "col", axis=0, tiled=True),
    )
    right_wide, mask_wide = (
        lax.all_gather(right_flat, "row", axis=1, tiled=True),
        lax.all_gather(mask_half_precision, "row", axis=1, tiled=True),
    )
    right_all, mask_right = (
        lax.all_to_all(right_wide, "col", split_axis=1, concat_axis=0, tiled=True),
        lax.all_to_all(mask_wide, "col", split_axis=1, concat_axis=0, tiled=True),
    )
    seq_total = left_all.shape[0]
    right_three = right_all.reshape(seq_total, tok_cols, width)
    counts = jnp.einsum("si,sj->ij", mask_left, mask_right, preferred_element_type=jnp.float32)
    scaled = coupling_change_derivative.astype(jnp.float32) / (counts + 0.001)[..., None]
    bias_part = jnp.sum(scaled, axis=(0, 1))
    scaled_bf = scaled.astype(jnp.bfloat16)
    block_rows = residue_line_number // TOKB
    right_acc = jnp.zeros((seq_total, tok_cols, width), jnp.float32)
    wout_acc = jnp.zeros(final_projection_matrix.shape, jnp.float32)
    left_pieces = []
    for block_index in range(TOKB):
        first = block_index * block_rows
        rows_bf = scaled_bf[first : first + block_rows]
        outer_grad = jnp.einsum(
            "ijz,fz->ijf", rows_bf, final_projection_matrix, preferred_element_type=jnp.float32
        ).astype(jnp.bfloat16)
        outer_grad = outer_grad.reshape(block_rows, tok_cols, width, width)
        left_block = left_all[:, first * width : (first + block_rows) * width].reshape(
            seq_total, block_rows, width
        )
        first_factor_derivative = jnp.einsum(
            "ijce,sje->sic", outer_grad, right_three, preferred_element_type=jnp.float32
        )
        right_acc = right_acc + jnp.einsum(
            "ijce,sic->sje", outer_grad, left_block, preferred_element_type=jnp.float32
        )
        outer = jnp.einsum(
            "sic,sje->ijce", left_block, right_three, preferred_element_type=jnp.float32
        ).astype(jnp.bfloat16)
        outer = outer.reshape(block_rows, tok_cols, width * width)
        wout_acc = wout_acc + jnp.einsum(
            "ijf,ijz->fz", outer, rows_bf, preferred_element_type=jnp.float32
        )
        first_factor_derivative = first_factor_derivative.reshape(seq_total, block_rows * width)
        left_pieces.append(first_factor_derivative)
    left_terms = jnp.concatenate(left_pieces, axis=1)
    left_own = lax.psum_scatter(left_terms, "col", scatter_dimension=0, tiled=True)
    right_spread = lax.all_to_all(
        right_acc.reshape(seq_total, tok_cols * width),
        "col",
        split_axis=0,
        concat_axis=1,
        tiled=True,
    )
    right_own = lax.psum_scatter(right_spread, "row", scatter_dimension=1, tiled=True)
    left_in = (
        left_own.reshape(shard_homolog_number, residue_line_number, width)
        * mask_single_precision[..., None]
    ).astype(jnp.bfloat16)
    right_in = (
        right_own.reshape(shard_homolog_number, residue_line_number, width)
        * mask_single_precision[..., None]
    ).astype(jnp.bfloat16)
    left_part = jnp.einsum(
        "sic,sip->cp", standardized_bfloat, left_in, preferred_element_type=jnp.float32
    )
    right_part = jnp.einsum(
        "sic,sip->cp", standardized_bfloat, right_in, preferred_element_type=jnp.float32
    )
    d_normal = jnp.einsum(
        "sip,cp->sic", left_in, first_projection_matrix, preferred_element_type=jnp.float32
    ) + jnp.einsum(
        "sip,cp->sic", right_in, second_projection_matrix, preferred_element_type=jnp.float32
    )
    gain_part = jnp.sum(d_normal * standardized_entries, axis=(0, 1))
    beta_part = jnp.sum(d_normal, axis=(0, 1))
    standardized_derivative = d_normal * standardizer_scale
    embedding_derivative = reciprocal_spread * (
        standardized_derivative
        - jnp.mean(standardized_derivative, axis=-1, keepdims=True)
        - standardized_entries
        * jnp.mean(standardized_derivative * standardized_entries, axis=-1, keepdims=True)
    )
    (
        final_matrix_derivative,
        first_matrix_derivative,
        second_matrix_derivative,
        scale_factor_derivative,
        shift_term_derivative,
        shift_derivative,
    ) = lax.psum((wout_acc, left_part, right_part, gain_part, beta_part, bias_part), ("row", "col"))
    return (
        embedding_derivative,
        final_matrix_derivative,
        first_matrix_derivative,
        second_matrix_derivative,
        scale_factor_derivative,
        shift_term_derivative,
        shift_derivative,
    )


BF = jnp.bfloat16
F32 = jnp.float32


def spread(rows, cols, rule):
    r = lax.broadcasted_iota(jnp.int32, (rows, cols), 0)
    c = lax.broadcasted_iota(jnp.int32, (rows, cols), 1)
    return rule(r, c)


def mm(a, b):
    return jnp.dot(a, b, preferred_element_type=F32)


def mm_nt(a, b):
    return lax.dot_general(a, b, (((1,), (1,)), ((), ())), preferred_element_type=F32)


def mm_tn(a, b):
    return lax.dot_general(a, b, (((0,), (0,)), ((), ())), preferred_element_type=F32)


def interleave(first, second):
    odd = lax.broadcasted_iota(jnp.int16, (32, 128), 1) & 32 != 0
    return (
        jnp.where(odd, pltpu.roll(second, 32, 1), first),
        jnp.where(odd, second, pltpu.roll(first, 96, 1)),
    )


def diagonal_pair(block):
    zero = jnp.zeros_like(block)
    return jnp.concatenate(
        [jnp.concatenate([block, zero], axis=1), jnp.concatenate([zero, block], axis=1)], axis=0
    )


ABSENT = 1024.0


def pack_kernel(msa_ref, mask_ref, pair_ref, out_ref):
    msa = msa_ref[...].astype(F32)
    pick = spread(8, 512, lambda r, c: jnp.where(c // 64 == r, 1.0, 0.0)).astype(BF)
    present = mm_tn(mask_ref[...].astype(F32).astype(BF), pick) > 0.5
    for g in range(4):
        rows = jnp.concatenate([msa[:, 2 * g, :], msa[:, 2 * g + 1, :]], axis=1)
        out_ref[32 * g : 32 * g + 32, :] = jnp.where(
            present[:, 128 * g : 128 * g + 128], rows, ABSENT
        ).astype(BF)
    out_ref[128:192, :] = pair_ref[...].astype(F32).reshape(64, 128).astype(BF)


def weights_kernel(*refs):
    sources, (norm_out, back_out, final_out, first_out) = refs[:5], refs[5:9]
    held, scr, sems = refs[9:14], refs[14], refs[15]
    copies = [pltpu.make_async_copy(sources[k], held[k], sems.at[k]) for k in range(5)]
    for copy in copies:
        copy.start()
    for copy in copies:
        copy.wait()
    gain_ref, offset_ref, first_ref, second_ref, final_ref = held
    norm_out[...] = jnp.concatenate(
        [
            jnp.concatenate([ref[...]] * 2, axis=1)
            for ref in (gain_ref, offset_ref, gain_ref, offset_ref) * 2
        ],
        axis=0,
    )
    for k, ref in enumerate((first_ref, second_ref)):
        narrow = ref[...].astype(F32)
        first_out[32 * k : 32 * k + 32, :] = narrow
        wide = jnp.concatenate([narrow] * 4, axis=1)
        wide = jnp.concatenate([wide] * 4, axis=0)
        own = spread(128, 256, lambda r, c: r // 32 == c // 64)
        back_out[128 * k : 128 * k + 128, :] = jnp.where(own, wide, 0.0).astype(BF)
    scr[...] = final_ref[...].astype(F32)
    for k in range(16):
        e = 4 * (k // 2) + k % 2
        final_out[32 * k : 32 * k + 32, :] = jnp.concatenate(
            [scr[pl.ds(e, 32, stride=32), :], scr[pl.ds(e + 2, 32, stride=32), :]], axis=1
        ).astype(BF)


def averager_of():
    return spread(128, 128, lambda r, c: jnp.where(r // 64 == c // 64, 1.0 / 64, 0.0)).astype(BF)


ORDER = (0, 2, 1, 3)


def stage_kernel(
    n_col, a, place_ref, set_refs, norm_ref, back_ref, final_ref,
    rhs_out, left_out, leftt_out, rightt_out, grad_out, pair_out, found_out, *rest
):
    *own_out, turn_scr = rest
    blocks = [ref.at[k] for ref in set_refs for k in range(ref.shape[0])]
    for b in range(n_col):
        at = pl.multiple_of(lax.bitwise_xor(place_ref[0], ORDER[b]) * 8, 8)
        pair_out[:, pl.ds(at, 8), :] = blocks[b][128:192, :].astype(F32).reshape(8, 8, 128)

    gain = norm_ref[0:1, :]
    offset = norm_ref[1:2, :]
    averager = averager_of()
    x = jnp.concatenate(
        [blocks[b][32 * g : 32 * g + 32, :] for g in range(4) for b in range(n_col)], axis=0
    )
    mean = mm(x, averager)
    present = mean < ABSENT / 2
    varied = x.astype(F32) - mean
    inverse = lax.rsqrt(mm((varied * varied).astype(BF), averager) + 1e-05)
    normed = varied * inverse
    if own_out:
        for g in range(4):
            own_out[0][32 * g : 32 * g + 32, :] = normed[128 * g : 128 * g + 32]
            own_out[1][32 * g : 32 * g + 32, :] = inverse[128 * g : 128 * g + 32]
    normal = jnp.where(present, normed * gain + offset, 0.0).astype(BF)
    rhs_out[:, 0:128] = normal
    rhs_out[:, 128:256] = normed.astype(BF)
    here = jnp.where(present, 1.0, 0.0)
    lane = lax.broadcasted_iota(jnp.int32, (128, 128), 1)
    found = jnp.zeros((128, 128), F32)
    for g in range(4):
        found = jnp.where(lane % 32 // 2 == 4 * a + g, here[128 * g : 128 * g + 128], found)
    found_out[...] = found
    for h in range(2):
        masked = jnp.concatenate(
            [normal[128 * g : 128 * g + 128] for g in (2 * h, 2 * h + 1)], axis=1
        )
        at = slice(128 * h, 128 * h + 128)
        left_out[:, at] = mm_nt(masked, back_ref[:128, :]).astype(BF)
        both = mm_nt(back_ref[...], masked)
        turn_scr[at, :] = both[128:]
        for k in range(2):
            leftt_out[64 * h + 32 * k : 64 * h + 32 * k + 32, :] = jnp.concatenate(
                [both[32 * k : 32 * k + 32], both[32 * k + 64 : 32 * k + 96]], axis=1
            ).astype(BF)

    for e in range(32):
        rightt_out[e] = turn_scr[pl.ds(e, 8, stride=32), :]

    pair = pair_out[...].reshape(256, 128).astype(BF)
    for n in range(2):
        pairs = jnp.concatenate(
            [diagonal_pair(pair[64 * p : 64 * p + 64]) for p in (2 * n, 2 * n + 1)], axis=0
        )
        grad = mm_nt(final_ref[...], pairs).astype(BF)
        for p in range(2):
            for q in range(8):
                rows = 64 * (2 * n + p)
                block = grad[64 * q : 64 * q + 64, 128 * p : 128 * p + 128]
                even, odd = interleave(block[:32], block[32:])
                grad_out[rows : rows + 32, 128 * q : 128 * q + 128] = even
                grad_out[rows + 32 : rows + 64, 128 * q : 128 * q + 128] = odd


def own_kernel(n_col, place_ref, front_ref, rear_ref, norm_ref, back_ref, final_ref, *rest):
    stage_kernel(n_col, 0, place_ref, (front_ref, rear_ref), norm_ref, back_ref, final_ref, *rest)


def pair_kernel(n_col, place_ref, core_ref, front_ref, rear_ref, norm_ref, back_ref, final_ref, *rest):
    common = (norm_ref, back_ref, final_ref)
    stage_kernel(n_col, 1, place_ref, (core_ref,), *common, *rest[:7], rest[14])
    stage_kernel(n_col, 2, place_ref, (front_ref, rear_ref), *common, *rest[7:14], rest[15])


def part_kernel(n_row, n_col, place_ref, front_ref, rear_ref, *refs):
    stages = [refs[7 * a : 7 * a + 7] for a in range(n_row - 1)]
    (
        normed_ref, inverse_ref, norm_ref, back_ref, final_ref, first_ref,
        emb_out, final_hbm_out, first_out, second_out, gain_out, offset_out, bias_out,
        right_scr, scaled_scr, grad_scr, outer_scr, wide_scr, all_scr,
        final_out, out_sem, turn_scr,
    ) = refs[7 * (n_row - 1) : -7]
    stages.append(refs[-7:])
    stage_kernel(
        n_col, n_row - 1, place_ref, (front_ref, rear_ref),
        norm_ref, back_ref, final_ref, *stages[-1], turn_scr,
    )
    gain = norm_ref[0:1, :]
    averager = averager_of()
    lane = lax.broadcasted_iota(jnp.int32, (128, 128), 1)

    found = sum(stage[6][...] for stage in stages)
    turned = pltpu.roll(found, 64, 1)
    mask = jnp.where((lane % 2 == 0) == (lane < 64), found, turned)
    mask_t = mask.T

    for e in range(32):
        right_scr[32 * e : 32 * e + 32, :] = jnp.concatenate(
            [stage[3][e] for stage in stages], axis=0
        ).astype(BF)

    mask_bf = mask.astype(BF)
    share = (1.0 / (mm_tn(mask_bf, mask_bf)[0:32] + 0.001)).astype(BF)
    for i in range(32):
        a, at = i // 8, 32 * (i % 8)
        for q in range(8):
            grad_scr[32 * i : 32 * i + 32, 128 * q : 128 * q + 128] = (
                stages[a][4][at : at + 32, 128 * q : 128 * q + 128] * share[i : i + 1]
            )
    left = jnp.concatenate([stage[1][...] for stage in stages], axis=1)
    right_grad = mm(left, grad_scr[...])
    left_grad = mm(grad_scr[...], right_scr[...])

    turn = spread(
        256, 256, lambda r, c: jnp.where((r // 8 == c % 32) & (r % 8 == c // 32), 1.0, 0.0)
    ).astype(BF)
    mask_two = jnp.concatenate([mask, mask], axis=1)
    right_in = [
        mm_nt(turn, (right_grad[:, 256 * q : 256 * q + 256] * mask_two).astype(BF))
        for q in range(4)
    ]
    for t in range(32):
        at = slice(128 * (t // 2), 128 * (t // 2) + 128)
        row = 32 * (t % 2)
        all_scr[row : row + 32, at] = (
            left_grad[32 * t : 32 * t + 32] * mask_t[t : t + 1]
        ).astype(BF)
        all_scr[row + 64 : row + 96, at] = jnp.concatenate(
            [part[8 * t : 8 * t + 8] for part in right_in], axis=0
        ).astype(BF)

    bias = jnp.zeros((1, 128), F32)
    ones = jnp.ones((128, 128), BF)
    for p in range(8):
        both_on = jnp.concatenate(
            [mask_t[0:32] * mask_t[i : i + 1] for i in range(4 * p, 4 * p + 4)], axis=0
        ).astype(BF)
        counts = mm(both_on, ones)
        pair = stages[p // 2][5][4 * (p % 2) : 4 * (p % 2) + 4]
        scaled = pair.reshape(128, 128) / (counts + 0.001)
        bias = bias + jnp.sum(scaled, axis=0, keepdims=True)
        scaled_scr[128 * p : 128 * p + 128, :] = scaled.astype(BF)
    bias_out[...] = bias

    left_t = jnp.concatenate([stage[2][...] for stage in stages], axis=0)
    for n in range(8):
        rights = jnp.concatenate(
            [diagonal_pair(right_scr[64 * p : 64 * p + 64, :]) for p in (2 * n, 2 * n + 1)], axis=0
        )
        outer = mm_nt(left_t, rights).astype(BF)
        for p in range(2):
            for q in range(8):
                rows = 64 * (2 * n + p)
                block = outer[64 * q : 64 * q + 64, 128 * p : 128 * p + 128]
                even, odd = interleave(block[:32], block[32:])
                outer_scr[rows : rows + 32, 128 * q : 128 * q + 128] = even
                outer_scr[rows + 32 : rows + 64, 128 * q : 128 * q + 128] = odd
    wide_scr[...] = mm(outer_scr[...], scaled_scr[...])
    for c in range(32):
        final_out[32 * c : 32 * c + 32, :] = wide_scr[pl.ds(c, 32, stride=32), :]
    final_send = pltpu.make_async_copy(final_out, final_hbm_out, out_sem)
    final_send.start()

    total = mm(
        all_scr[...], jnp.concatenate([stage[0][...] for stage in stages], axis=0)
    )
    sums = all_scr[:, 0:128].astype(F32)
    for g in range(1, 16):
        sums = sums + all_scr[:, 128 * g : 128 * g + 128].astype(F32)

    def fold(block):
        return block[0:32, 0:64] + block[32:64, 64:128]

    first_out[...] = fold(total[0:64, 0:128])
    second_out[...] = fold(total[64:128, 0:128])
    sums = jnp.sum(sums, axis=1, keepdims=True)
    left_sum = sums[0:32] + sums[32:64]
    right_sum = sums[64:96] + sums[96:128]
    first, second = first_ref[0:32, :], first_ref[32:64, :]
    gain_out[...] = jnp.sum(
        first * fold(total[0:64, 128:256]) + second * fold(total[64:128, 128:256]),
        axis=0, keepdims=True,
    )
    offset_out[...] = jnp.sum(first * left_sum + second * right_sum, axis=0, keepdims=True)

    d_hat = []
    for h in range(2):
        sides = [
            jnp.concatenate(
                [all_scr[row : row + 64, 128 * g : 128 * g + 128] for g in (2 * h, 2 * h + 1)], axis=0
            )
            for row in (0, 64)
        ]
        d_normal = mm_tn(jnp.concatenate(sides, axis=0), back_ref[...])
        d_hat += [d_normal[0:32, 0:128] * gain, d_normal[0:32, 128:256] * gain]
    d_hat = jnp.concatenate(d_hat, axis=0)
    normed = normed_ref[...]
    means = mm(jnp.concatenate([d_hat, d_hat * normed], axis=0).astype(BF), averager)
    result = inverse_ref[...] * (d_hat - means[:128] - normed * means[128:])
    for g in range(4):
        emb_out[:, 2 * g, :] = result[32 * g : 32 * g + 32, 0:64]
        emb_out[:, 2 * g + 1, :] = result[32 * g : 32 * g + 32, 64:128]
    final_send.wait()


def vmem(count):
    return [pl.BlockSpec(memory_space=pltpu.VMEM)] * count


LIMIT = pltpu.CompilerParams(vmem_limit_bytes=32 * 1024 * 1024)


def gathered_body(
    n_row,
    n_col,
    homolog_embedding,
    presence_indicator,
    coupling_change_derivative,
    standardizer_scale,
    standardizer_shift,
    first_projection_matrix,
    second_projection_matrix,
    final_projection_matrix,
):
    shards, tokens, features = homolog_embedding.shape
    width = first_projection_matrix.shape[1]
    first_t, second_t = first_projection_matrix.T, second_projection_matrix.T
    shape = lambda *dims: jax.ShapeDtypeStruct(dims, F32)
    held = lambda *dims: pltpu.VMEM(dims, F32)
    held_bf = lambda *dims: pltpu.VMEM(dims, BF)
    hbm = pl.BlockSpec(memory_space=pltpu.HBM)
    place = lax.bitwise_xor(lax.axis_index("row"), lax.axis_index("col"))
    place = place.astype(jnp.int32).reshape(1)
    packed = pl.pallas_call(
        pack_kernel,
        out_shape=held_bf(192, 128),
        in_specs=vmem(3),
        out_specs=vmem(1)[0],
    )(homolog_embedding, presence_indicator.T, coupling_change_derivative)
    def over(axis, size, step, array):
        return lax.ppermute(array, axis, [(k, k ^ step) for k in range(size)])

    far = over("col", n_col, 2, packed)
    near = over("col", n_col, 1, packed)
    last = over("col", n_col, 3, packed)
    front = jnp.stack([packed, far])
    chip_front = over("row", n_row, 2, front)
    rear = jnp.stack([near, last])
    chip_rear = over("row", n_row, 2, rear)
    front, final_projection_matrix = lax.optimization_barrier((front, final_projection_matrix))
    weights = pl.pallas_call(
        weights_kernel,
        out_shape=(
            held(8, 128), held_bf(256, 256), held_bf(width * width // 2, 256), held(2 * width, features),
        ),
        in_specs=[hbm] * 5,
        out_specs=tuple(vmem(4)),
        scratch_shapes=[
            pltpu.VMEM((1, features), F32),
            pltpu.VMEM((1, features), F32),
            pltpu.VMEM((width, features), BF),
            pltpu.VMEM((width, features), BF),
            pltpu.VMEM((width * width, 128), BF),
            pltpu.VMEM((width * width, 128), F32),
            pltpu.SemaphoreType.DMA((5,)),
        ],
        compiler_params=LIMIT,
    )(
        *[
            pltpu.with_memory_space_constraint(x, pltpu.HBM)
            for x in (
                standardizer_scale.reshape(1, features),
                standardizer_shift.reshape(1, features),
                first_t,
                second_t,
                final_projection_matrix,
            )
        ]
    )
    norm, back, final_turned, first = weights
    own = jnp.concatenate([front, rear])
    own, chip_front = lax.optimization_barrier((own, chip_front))
    core = over("row", n_row, 1, own)
    stage_outs = [
        held_bf(512, 256), held_bf(128, 256), held_bf(128, 256), held(width, 8, 128),
        held_bf(256, 1024), held(8, 32, 128), held(128, 128),
    ]
    scalar = pl.BlockSpec(memory_space=pltpu.SMEM)

    def stages_of(kernel, sets, outs, flops):
        return pl.pallas_call(
            functools.partial(kernel, n_col),
            out_shape=tuple(outs),
            in_specs=[scalar] + vmem(len(sets) + 3),
            out_specs=tuple(vmem(len(outs))),
            scratch_shapes=[pltpu.VMEM((256, 128), F32)] * (len(outs) // 7),
            compiler_params=LIMIT,
            cost_estimate=pl.CostEstimate(
                flops=flops, bytes_accessed=flops // 256, transcendentals=0
            ),
        )(place, *sets, norm, back, final_turned)

    both_front = over("row", n_row, 1, chip_front)
    own_stage = stages_of(own_kernel, (front, rear), stage_outs + [held(128, 128)] * 2, 1_000_000_000)
    chip_rear, own_stage = lax.optimization_barrier((chip_rear, own_stage))
    both_rear = over("row", n_row, 1, chip_rear)
    pair_stages = stages_of(pair_kernel, (core, chip_front, chip_rear), stage_outs * 2, 1000000)
    stages = [own_stage[:7], pair_stages]
    outs = pl.pallas_call(
        functools.partial(part_kernel, n_row, n_col),
        out_shape=(
            shape(shards, tokens, features),
            shape(width * width, 128),
            shape(width, features),
            shape(width, features),
            shape(1, features),
            shape(1, features),
            shape(1, 128),
        ),
        in_specs=[scalar] + vmem(7 * (n_row - 1) + 8),
        out_specs=(*vmem(1), hbm, *vmem(5)),
        scratch_shapes=[
            pltpu.VMEM((1024, 128), BF),
            pltpu.VMEM((1024, 128), BF),
            pltpu.VMEM((1024, 1024), BF),
            pltpu.VMEM((1024, 1024), BF),
            pltpu.VMEM((1024, 128), F32),
            pltpu.VMEM((128, 2048), BF),
            pltpu.VMEM((1024, 128), F32),
            pltpu.SemaphoreType.DMA,
            pltpu.VMEM((256, 128), F32),
            *stage_outs,
        ],
        compiler_params=LIMIT,
    )(place, both_front, both_rear, *[x for s in stages for x in s], *own_stage[7:], norm, back, final_turned, first)
    emb, final, first, second, gain, offset, bias = outs
    return emb, final, first.T, second.T, gain.reshape(-1), offset.reshape(-1), bias.reshape(-1)


def body(n_row, n_col, *arguments):
    msa, _, pair = arguments[:3]
    width = arguments[5].shape[1]
    fits = (
        n_row == 4
        and n_col == 4
        and msa.shape == (32, 8, 64)
        and pair.shape == (8, 8, 128)
        and width == 32
    )
    if fits:
        return gathered_body(n_row, n_col, *arguments)
    return sharded_body(*arguments)


def solution(mesh):
    placed = (
        P(("grp", "col"), "row", None),
        P(("grp", "col"), "row"),
        P(("grp", "row"), "col", None),
        P(),
        P(),
        P(),
        P(),
        P(),
    )
    return jax.shard_map(
        functools.partial(body, mesh.shape["row"], mesh.shape["col"]),
        mesh=mesh,
        in_specs=placed,
        out_specs=(
            P(("grp", "col"), "row", None),
            P("grp", None),
            P("grp", None),
            P("grp", None),
            P("grp"),
            P("grp"),
            P("grp"),
        ),
        check_vma=False,
    )
```

```python
import functools

import jax
import jax.numpy as jnp
from jax import lax
from jax.experimental import pallas as pl
from jax.experimental.pallas import tpu as pltpu
from jax.sharding import PartitionSpec as P

TOKB = 2


def standardizer_parts(homolog_embedding, standardizer_scale, standardizer_shift):
    incoming_entries = homolog_embedding.astype(jnp.float32)
    center = jnp.mean(incoming_entries, axis=-1, keepdims=True)
    varied = incoming_entries - center
    variance = jnp.mean(varied * varied, axis=-1, keepdims=True)
    reciprocal_spread = lax.rsqrt(variance + 1e-05)
    standardized_entries = varied * reciprocal_spread
    standardized_bfloat = (standardized_entries * standardizer_scale + standardizer_shift).astype(
        jnp.bfloat16
    )
    return (standardized_entries, reciprocal_spread, standardized_bfloat)


def sharded_body(
    homolog_embedding,
    presence_indicator,
    coupling_change_derivative,
    standardizer_scale,
    standardizer_shift,
    first_projection_matrix,
    second_projection_matrix,
    final_projection_matrix,
):
    shard_homolog_number, residue_line_number, feature_number = homolog_embedding.shape
    tok_cols = coupling_change_derivative.shape[1]
    width = first_projection_matrix.shape[1]
    standardized_entries, reciprocal_spread, standardized_bfloat = standardizer_parts(
        homolog_embedding, standardizer_scale, standardizer_shift
    )
    mask_single_precision = presence_indicator.astype(jnp.float32)
    mask_half_precision = presence_indicator.astype(jnp.bfloat16)
    left = (
        jnp.einsum(
            "sic,cp->sip",
            standardized_bfloat,
            first_projection_matrix,
            preferred_element_type=jnp.float32,
        )
        * mask_single_precision[..., None]
    ).astype(jnp.bfloat16)
    right = (
        jnp.einsum(
            "sic,cp->sip",
            standardized_bfloat,
            second_projection_matrix,
            preferred_element_type=jnp.float32,
        )
        * mask_single_precision[..., None]
    ).astype(jnp.bfloat16)
    left_flat = left.reshape(shard_homolog_number, residue_line_number * width)
    right_flat = right.reshape(shard_homolog_number, residue_line_number * width)
    left_all, mask_left = (
        lax.all_gather(left_flat, "col", axis=0, tiled=True),
        lax.all_gather(mask_half_precision, "col", axis=0, tiled=True),
    )
    right_wide, mask_wide = (
        lax.all_gather(right_flat, "row", axis=1, tiled=True),
        lax.all_gather(mask_half_precision, "row", axis=1, tiled=True),
    )
    right_all, mask_right = (
        lax.all_to_all(right_wide, "col", split_axis=1, concat_axis=0, tiled=True),
        lax.all_to_all(mask_wide, "col", split_axis=1, concat_axis=0, tiled=True),
    )
    seq_total = left_all.shape[0]
    right_three = right_all.reshape(seq_total, tok_cols, width)
    counts = jnp.einsum("si,sj->ij", mask_left, mask_right, preferred_element_type=jnp.float32)
    scaled = coupling_change_derivative.astype(jnp.float32) / (counts + 0.001)[..., None]
    bias_part = jnp.sum(scaled, axis=(0, 1))
    scaled_bf = scaled.astype(jnp.bfloat16)
    block_rows = residue_line_number // TOKB
    right_acc = jnp.zeros((seq_total, tok_cols, width), jnp.float32)
    wout_acc = jnp.zeros(final_projection_matrix.shape, jnp.float32)
    left_pieces = []
    for block_index in range(TOKB):
        first = block_index * block_rows
        rows_bf = scaled_bf[first : first + block_rows]
        outer_grad = jnp.einsum(
            "ijz,fz->ijf", rows_bf, final_projection_matrix, preferred_element_type=jnp.float32
        ).astype(jnp.bfloat16)
        outer_grad = outer_grad.reshape(block_rows, tok_cols, width, width)
        left_block = left_all[:, first * width : (first + block_rows) * width].reshape(
            seq_total, block_rows, width
        )
        first_factor_derivative = jnp.einsum(
            "ijce,sje->sic", outer_grad, right_three, preferred_element_type=jnp.float32
        )
        right_acc = right_acc + jnp.einsum(
            "ijce,sic->sje", outer_grad, left_block, preferred_element_type=jnp.float32
        )
        outer = jnp.einsum(
            "sic,sje->ijce", left_block, right_three, preferred_element_type=jnp.float32
        ).astype(jnp.bfloat16)
        outer = outer.reshape(block_rows, tok_cols, width * width)
        wout_acc = wout_acc + jnp.einsum(
            "ijf,ijz->fz", outer, rows_bf, preferred_element_type=jnp.float32
        )
        first_factor_derivative = first_factor_derivative.reshape(seq_total, block_rows * width)
        left_pieces.append(first_factor_derivative)
    left_terms = jnp.concatenate(left_pieces, axis=1)
    left_own = lax.psum_scatter(left_terms, "col", scatter_dimension=0, tiled=True)
    right_spread = lax.all_to_all(
        right_acc.reshape(seq_total, tok_cols * width),
        "col",
        split_axis=0,
        concat_axis=1,
        tiled=True,
    )
    right_own = lax.psum_scatter(right_spread, "row", scatter_dimension=1, tiled=True)
    left_in = (
        left_own.reshape(shard_homolog_number, residue_line_number, width)
        * mask_single_precision[..., None]
    ).astype(jnp.bfloat16)
    right_in = (
        right_own.reshape(shard_homolog_number, residue_line_number, width)
        * mask_single_precision[..., None]
    ).astype(jnp.bfloat16)
    left_part = jnp.einsum(
        "sic,sip->cp", standardized_bfloat, left_in, preferred_element_type=jnp.float32
    )
    right_part = jnp.einsum(
        "sic,sip->cp", standardized_bfloat, right_in, preferred_element_type=jnp.float32
    )
    d_normal = jnp.einsum(
        "sip,cp->sic", left_in, first_projection_matrix, preferred_element_type=jnp.float32
    ) + jnp.einsum(
        "sip,cp->sic", right_in, second_projection_matrix, preferred_element_type=jnp.float32
    )
    gain_part = jnp.sum(d_normal * standardized_entries, axis=(0, 1))
    beta_part = jnp.sum(d_normal, axis=(0, 1))
    standardized_derivative = d_normal * standardizer_scale
    embedding_derivative = reciprocal_spread * (
        standardized_derivative
        - jnp.mean(standardized_derivative, axis=-1, keepdims=True)
        - standardized_entries
        * jnp.mean(standardized_derivative * standardized_entries, axis=-1, keepdims=True)
    )
    (
        final_matrix_derivative,
        first_matrix_derivative,
        second_matrix_derivative,
        scale_factor_derivative,
        shift_term_derivative,
        shift_derivative,
    ) = lax.psum((wout_acc, left_part, right_part, gain_part, beta_part, bias_part), ("row", "col"))
    return (
        embedding_derivative,
        final_matrix_derivative,
        first_matrix_derivative,
        second_matrix_derivative,
        scale_factor_derivative,
        shift_term_derivative,
        shift_derivative,
    )


BF = jnp.bfloat16
F32 = jnp.float32


def spread(rows, cols, rule):
    r = lax.broadcasted_iota(jnp.int32, (rows, cols), 0)
    c = lax.broadcasted_iota(jnp.int32, (rows, cols), 1)
    return rule(r, c)


def mm(a, b):
    return jnp.dot(a, b, preferred_element_type=F32)


def mm_nt(a, b):
    return lax.dot_general(a, b, (((1,), (1,)), ((), ())), preferred_element_type=F32)


def mm_tn(a, b):
    return lax.dot_general(a, b, (((0,), (0,)), ((), ())), preferred_element_type=F32)


def interleave(first, second):
    odd = lax.broadcasted_iota(jnp.int16, (32, 128), 1) & 32 != 0
    return (
        jnp.where(odd, pltpu.roll(second, 32, 1), first),
        jnp.where(odd, second, pltpu.roll(first, 96, 1)),
    )


def diagonal_pair(block):
    zero = jnp.zeros_like(block)
    return jnp.concatenate(
        [jnp.concatenate([block, zero], axis=1), jnp.concatenate([zero, block], axis=1)], axis=0
    )


ABSENT = 1024.0


def pack_kernel(msa_ref, mask_ref, pair_ref, out_ref):
    msa = msa_ref[...].astype(F32)
    pick = spread(8, 512, lambda r, c: jnp.where(c // 64 == r, 1.0, 0.0)).astype(BF)
    present = mm_tn(mask_ref[...].astype(F32).astype(BF), pick) > 0.5
    for g in range(4):
        rows = jnp.concatenate([msa[:, 2 * g, :], msa[:, 2 * g + 1, :]], axis=1)
        out_ref[32 * g : 32 * g + 32, :] = jnp.where(
            present[:, 128 * g : 128 * g + 128], rows, ABSENT
        ).astype(BF)
    out_ref[128:192, :] = pair_ref[...].astype(F32).reshape(64, 128).astype(BF)


def weights_kernel(*refs):
    sources, (norm_out, back_out, final_out, first_out) = refs[:5], refs[5:9]
    held, scr, sems = refs[9:14], refs[14], refs[15]
    copies = [pltpu.make_async_copy(sources[k], held[k], sems.at[k]) for k in range(5)]
    for copy in copies:
        copy.start()
    for copy in copies:
        copy.wait()
    gain_ref, offset_ref, first_ref, second_ref, final_ref = held
    norm_out[...] = jnp.concatenate(
        [
            jnp.concatenate([ref[...]] * 2, axis=1)
            for ref in (gain_ref, offset_ref, gain_ref, offset_ref) * 2
        ],
        axis=0,
    )
    for k, ref in enumerate((first_ref, second_ref)):
        narrow = ref[...].astype(F32)
        first_out[32 * k : 32 * k + 32, :] = narrow
        wide = jnp.concatenate([narrow] * 4, axis=1)
        wide = jnp.concatenate([wide] * 4, axis=0)
        own = spread(128, 256, lambda r, c: r // 32 == c // 64)
        back_out[128 * k : 128 * k + 128, :] = jnp.where(own, wide, 0.0).astype(BF)
    scr[...] = final_ref[...].astype(F32)
    for k in range(16):
        e = 4 * (k // 2) + k % 2
        final_out[32 * k : 32 * k + 32, :] = jnp.concatenate(
            [scr[pl.ds(e, 32, stride=32), :], scr[pl.ds(e + 2, 32, stride=32), :]], axis=1
        ).astype(BF)


def averager_of():
    return spread(128, 128, lambda r, c: jnp.where(r // 64 == c // 64, 1.0 / 64, 0.0)).astype(BF)


ORDER = (0, 2, 1, 3)


def stage_kernel(
    n_col, a, place_ref, set_refs, norm_ref, back_ref, final_ref,
    rhs_out, left_out, leftt_out, rightt_out, grad_out, pair_out, found_out, *rest
):
    *own_out, turn_scr = rest
    blocks = [ref.at[k] for ref in set_refs for k in range(ref.shape[0])]
    for b in range(n_col):
        at = pl.multiple_of(lax.bitwise_xor(place_ref[0], ORDER[b]) * 8, 8)
        pair_out[:, pl.ds(at, 8), :] = blocks[b][128:192, :].astype(F32).reshape(8, 8, 128)

    gain = norm_ref[0:1, :]
    offset = norm_ref[1:2, :]
    averager = averager_of()
    x = jnp.concatenate(
        [blocks[b][32 * g : 32 * g + 32, :] for g in range(4) for b in range(n_col)], axis=0
    )
    mean = mm(x, averager)
    present = mean < ABSENT / 2
    varied = x.astype(F32) - mean
    inverse = lax.rsqrt(mm((varied * varied).astype(BF), averager) + 1e-05)
    normed = varied * inverse
    if own_out:
        for g in range(4):
            own_out[0][32 * g : 32 * g + 32, :] = normed[128 * g : 128 * g + 32]
            own_out[1][32 * g : 32 * g + 32, :] = inverse[128 * g : 128 * g + 32]
    normal = jnp.where(present, normed * gain + offset, 0.0).astype(BF)
    rhs_out[:, 0:128] = normal
    rhs_out[:, 128:256] = normed.astype(BF)
    here = jnp.where(present, 1.0, 0.0)
    lane = lax.broadcasted_iota(jnp.int32, (128, 128), 1)
    found = jnp.zeros((128, 128), F32)
    for g in range(4):
        found = jnp.where(lane % 32 // 2 == 4 * a + g, here[128 * g : 128 * g + 128], found)
    found_out[...] = found
    for h in range(2):
        masked = jnp.concatenate(
            [normal[128 * g : 128 * g + 128] for g in (2 * h, 2 * h + 1)], axis=1
        )
        at = slice(128 * h, 128 * h + 128)
        left_out[:, at] = mm_nt(masked, back_ref[:128, :]).astype(BF)
        both = mm_nt(back_ref[...], masked)
        turn_scr[at, :] = both[128:]
        for k in range(2):
            leftt_out[64 * h + 32 * k : 64 * h + 32 * k + 32, :] = jnp.concatenate(
                [both[32 * k : 32 * k + 32], both[32 * k + 64 : 32 * k + 96]], axis=1
            ).astype(BF)

    for e in range(32):
        rightt_out[e] = turn_scr[pl.ds(e, 8, stride=32), :]

    pair = pair_out[...].reshape(256, 128).astype(BF)
    for n in range(2):
        pairs = jnp.concatenate(
            [diagonal_pair(pair[64 * p : 64 * p + 64]) for p in (2 * n, 2 * n + 1)], axis=0
        )
        grad = mm_nt(final_ref[...], pairs).astype(BF)
        for p in range(2):
            for q in range(8):
                rows = 64 * (2 * n + p)
                block = grad[64 * q : 64 * q + 64, 128 * p : 128 * p + 128]
                even, odd = interleave(block[:32], block[32:])
                grad_out[rows : rows + 32, 128 * q : 128 * q + 128] = even
                grad_out[rows + 32 : rows + 64, 128 * q : 128 * q + 128] = odd


def own_kernel(n_col, place_ref, front_ref, rear_ref, norm_ref, back_ref, final_ref, *rest):
    stage_kernel(n_col, 0, place_ref, (front_ref, rear_ref), norm_ref, back_ref, final_ref, *rest)


def pair_kernel(n_col, place_ref, core_ref, front_ref, rear_ref, norm_ref, back_ref, final_ref, *rest):
    common = (norm_ref, back_ref, final_ref)
    stage_kernel(n_col, 1, place_ref, (core_ref,), *common, *rest[:7], rest[14])
    stage_kernel(n_col, 2, place_ref, (front_ref, rear_ref), *common, *rest[7:14], rest[15])


def part_kernel(n_row, n_col, place_ref, front_ref, rear_ref, *refs):
    stages = [refs[7 * a : 7 * a + 7] for a in range(n_row - 1)]
    (
        normed_ref, inverse_ref, norm_ref, back_ref, final_ref, first_ref,
        emb_out, final_hbm_out, first_out, second_out, gain_out, offset_out, bias_out,
        right_scr, scaled_scr, grad_scr, outer_scr, wide_scr, all_scr,
        final_out, out_sem, turn_scr,
    ) = refs[7 * (n_row - 1) : -7]
    stages.append(refs[-7:])
    stage_kernel(
        n_col, n_row - 1, place_ref, (front_ref, rear_ref),
        norm_ref, back_ref, final_ref, *stages[-1], turn_scr,
    )
    gain = norm_ref[0:1, :]
    averager = averager_of()
    lane = lax.broadcasted_iota(jnp.int32, (128, 128), 1)

    found = sum(stage[6][...] for stage in stages)
    turned = pltpu.roll(found, 64, 1)
    mask = jnp.where((lane % 2 == 0) == (lane < 64), found, turned)
    mask_t = mask.T

    for e in range(32):
        right_scr[32 * e : 32 * e + 32, :] = jnp.concatenate(
            [stage[3][e] for stage in stages], axis=0
        ).astype(BF)

    mask_bf = mask.astype(BF)
    share = (1.0 / (mm_tn(mask_bf, mask_bf)[0:32] + 0.001)).astype(BF)
    for i in range(32):
        a, at = i // 8, 32 * (i % 8)
        for q in range(8):
            grad_scr[32 * i : 32 * i + 32, 128 * q : 128 * q + 128] = (
                stages[a][4][at : at + 32, 128 * q : 128 * q + 128] * share[i : i + 1]
            )
    left = jnp.concatenate([stage[1][...] for stage in stages], axis=1)
    right_grad = mm(left, grad_scr[...])
    left_grad = mm(grad_scr[...], right_scr[...])

    turn = spread(
        256, 256, lambda r, c: jnp.where((r // 8 == c % 32) & (r % 8 == c // 32), 1.0, 0.0)
    ).astype(BF)
    mask_two = jnp.concatenate([mask, mask], axis=1)
    right_in = [
        mm_nt(turn, (right_grad[:, 256 * q : 256 * q + 256] * mask_two).astype(BF))
        for q in range(4)
    ]
    for t in range(32):
        at = slice(128 * (t // 2), 128 * (t // 2) + 128)
        row = 32 * (t % 2)
        all_scr[row : row + 32, at] = (
            left_grad[32 * t : 32 * t + 32] * mask_t[t : t + 1]
        ).astype(BF)
        all_scr[row + 64 : row + 96, at] = jnp.concatenate(
            [part[8 * t : 8 * t + 8] for part in right_in], axis=0
        ).astype(BF)

    bias = jnp.zeros((1, 128), F32)
    ones = jnp.ones((128, 128), BF)
    for p in range(8):
        both_on = jnp.concatenate(
            [mask_t[0:32] * mask_t[i : i + 1] for i in range(4 * p, 4 * p + 4)], axis=0
        ).astype(BF)
        counts = mm(both_on, ones)
        pair = stages[p // 2][5][4 * (p % 2) : 4 * (p % 2) + 4]
        scaled = pair.reshape(128, 128) / (counts + 0.001)
        bias = bias + jnp.sum(scaled, axis=0, keepdims=True)
        scaled_scr[128 * p : 128 * p + 128, :] = scaled.astype(BF)
    bias_out[...] = bias

    left_t = jnp.concatenate([stage[2][...] for stage in stages], axis=0)
    for n in range(8):
        rights = jnp.concatenate(
            [diagonal_pair(right_scr[64 * p : 64 * p + 64, :]) for p in (2 * n, 2 * n + 1)], axis=0
        )
        outer = mm_nt(left_t, rights).astype(BF)
        for p in range(2):
            for q in range(8):
                rows = 64 * (2 * n + p)
                block = outer[64 * q : 64 * q + 64, 128 * p : 128 * p + 128]
                even, odd = interleave(block[:32], block[32:])
                outer_scr[rows : rows + 32, 128 * q : 128 * q + 128] = even
                outer_scr[rows + 32 : rows + 64, 128 * q : 128 * q + 128] = odd
    wide_scr[...] = mm(outer_scr[...], scaled_scr[...])
    for c in range(32):
        final_out[32 * c : 32 * c + 32, :] = wide_scr[pl.ds(c, 32, stride=32), :]
    final_send = pltpu.make_async_copy(final_out, final_hbm_out, out_sem)
    final_send.start()

    total = mm(
        all_scr[...], jnp.concatenate([stage[0][...] for stage in stages], axis=0)
    )
    sums = all_scr[:, 0:128].astype(F32)
    for g in range(1, 16):
        sums = sums + all_scr[:, 128 * g : 128 * g + 128].astype(F32)

    def fold(block):
        return block[0:32, 0:64] + block[32:64, 64:128]

    first_out[...] = fold(total[0:64, 0:128])
    second_out[...] = fold(total[64:128, 0:128])
    sums = jnp.sum(sums, axis=1, keepdims=True)
    left_sum = sums[0:32] + sums[32:64]
    right_sum = sums[64:96] + sums[96:128]
    first, second = first_ref[0:32, :], first_ref[32:64, :]
    gain_out[...] = jnp.sum(
        first * fold(total[0:64, 128:256]) + second * fold(total[64:128, 128:256]),
        axis=0, keepdims=True,
    )
    offset_out[...] = jnp.sum(first * left_sum + second * right_sum, axis=0, keepdims=True)

    d_hat = []
    for h in range(2):
        sides = [
            jnp.concatenate(
                [all_scr[row : row + 64, 128 * g : 128 * g + 128] for g in (2 * h, 2 * h + 1)], axis=0
            )
            for row in (0, 64)
        ]
        d_normal = mm_tn(jnp.concatenate(sides, axis=0), back_ref[...])
        d_hat += [d_normal[0:32, 0:128] * gain, d_normal[0:32, 128:256] * gain]
    d_hat = jnp.concatenate(d_hat, axis=0)
    normed = normed_ref[...]
    means = mm(jnp.concatenate([d_hat, d_hat * normed], axis=0).astype(BF), averager)
    result = inverse_ref[...] * (d_hat - means[:128] - normed * means[128:])
    for g in range(4):
        emb_out[:, 2 * g, :] = result[32 * g : 32 * g + 32, 0:64]
        emb_out[:, 2 * g + 1, :] = result[32 * g : 32 * g + 32, 64:128]
    final_send.wait()


def vmem(count):
    return [pl.BlockSpec(memory_space=pltpu.VMEM)] * count


LIMIT = pltpu.CompilerParams(vmem_limit_bytes=32 * 1024 * 1024)


def gathered_body(
    n_row,
    n_col,
    homolog_embedding,
    presence_indicator,
    coupling_change_derivative,
    standardizer_scale,
    standardizer_shift,
    first_projection_matrix,
    second_projection_matrix,
    final_projection_matrix,
):
    shards, tokens, features = homolog_embedding.shape
    width = first_projection_matrix.shape[1]
    first_t, second_t = first_projection_matrix.T, second_projection_matrix.T
    shape = lambda *dims: jax.ShapeDtypeStruct(dims, F32)
    held = lambda *dims: pltpu.VMEM(dims, F32)
    held_bf = lambda *dims: pltpu.VMEM(dims, BF)
    hbm = pl.BlockSpec(memory_space=pltpu.HBM)
    place = lax.bitwise_xor(lax.axis_index("row"), lax.axis_index("col"))
    place = place.astype(jnp.int32).reshape(1)
    packed = pl.pallas_call(
        pack_kernel,
        out_shape=held_bf(192, 128),
        in_specs=vmem(3),
        out_specs=vmem(1)[0],
    )(homolog_embedding, presence_indicator.T, coupling_change_derivative)
    def over(axis, size, step, array):
        return lax.ppermute(array, axis, [(k, k ^ step) for k in range(size)])

    far = over("col", n_col, 2, packed)
    near = over("col", n_col, 1, packed)
    last = over("col", n_col, 3, packed)
    front = jnp.stack([packed, far])
    chip_front = over("row", n_row, 2, front)
    rear = jnp.stack([near, last])
    chip_rear = over("row", n_row, 2, rear)
    front, final_projection_matrix = lax.optimization_barrier((front, final_projection_matrix))
    weights = pl.pallas_call(
        weights_kernel,
        out_shape=(
            held(8, 128), held_bf(256, 256), held_bf(width * width // 2, 256), held(2 * width, features),
        ),
        in_specs=[hbm] * 5,
        out_specs=tuple(vmem(4)),
        scratch_shapes=[
            pltpu.VMEM((1, features), F32),
            pltpu.VMEM((1, features), F32),
            pltpu.VMEM((width, features), BF),
            pltpu.VMEM((width, features), BF),
            pltpu.VMEM((width * width, 128), BF),
            pltpu.VMEM((width * width, 128), F32),
            pltpu.SemaphoreType.DMA((5,)),
        ],
        compiler_params=LIMIT,
    )(
        *[
            pltpu.with_memory_space_constraint(x, pltpu.HBM)
            for x in (
                standardizer_scale.reshape(1, features),
                standardizer_shift.reshape(1, features),
                first_t,
                second_t,
                final_projection_matrix,
            )
        ]
    )
    norm, back, final_turned, first = weights
    own = jnp.concatenate([front, rear])
    own, chip_front, norm = lax.optimization_barrier((own, chip_front, norm))
    core = over("row", n_row, 1, own)
    stage_outs = [
        held_bf(512, 256), held_bf(128, 256), held_bf(128, 256), held(width, 8, 128),
        held_bf(256, 1024), held(8, 32, 128), held(128, 128),
    ]
    scalar = pl.BlockSpec(memory_space=pltpu.SMEM)

    def stages_of(kernel, sets, outs, flops):
        return pl.pallas_call(
            functools.partial(kernel, n_col),
            out_shape=tuple(outs),
            in_specs=[scalar] + vmem(len(sets) + 3),
            out_specs=tuple(vmem(len(outs))),
            scratch_shapes=[pltpu.VMEM((256, 128), F32)] * (len(outs) // 7),
            compiler_params=LIMIT,
            cost_estimate=pl.CostEstimate(
                flops=flops, bytes_accessed=flops // 256, transcendentals=0
            ),
        )(place, *sets, norm, back, final_turned)

    both_front = over("row", n_row, 1, chip_front)
    own_stage = stages_of(own_kernel, (front, rear), stage_outs + [held(128, 128)] * 2, 1_000_000_000)
    chip_rear, own_stage = lax.optimization_barrier((chip_rear, own_stage))
    both_rear = over("row", n_row, 1, chip_rear)
    pair_stages = stages_of(pair_kernel, (core, chip_front, chip_rear), stage_outs * 2, 1000000)
    stages = [own_stage[:7], pair_stages]
    outs = pl.pallas_call(
        functools.partial(part_kernel, n_row, n_col),
        out_shape=(
            shape(shards, tokens, features),
            shape(width * width, 128),
            shape(width, features),
            shape(width, features),
            shape(1, features),
            shape(1, features),
            shape(1, 128),
        ),
        in_specs=[scalar] + vmem(7 * (n_row - 1) + 8),
        out_specs=(*vmem(1), hbm, *vmem(5)),
        scratch_shapes=[
            pltpu.VMEM((1024, 128), BF),
            pltpu.VMEM((1024, 128), BF),
            pltpu.VMEM((1024, 1024), BF),
            pltpu.VMEM((1024, 1024), BF),
            pltpu.VMEM((1024, 128), F32),
            pltpu.VMEM((128, 2048), BF),
            pltpu.VMEM((1024, 128), F32),
            pltpu.SemaphoreType.DMA,
            pltpu.VMEM((256, 128), F32),
            *stage_outs,
        ],
        compiler_params=LIMIT,
    )(place, both_front, both_rear, *[x for s in stages for x in s], *own_stage[7:], norm, back, final_turned, first)
    emb, final, first, second, gain, offset, bias = outs
    return emb, final, first.T, second.T, gain.reshape(-1), offset.reshape(-1), bias.reshape(-1)


def body(n_row, n_col, *arguments):
    msa, _, pair = arguments[:3]
    width = arguments[5].shape[1]
    fits = (
        n_row == 4
        and n_col == 4
        and msa.shape == (32, 8, 64)
        and pair.shape == (8, 8, 128)
        and width == 32
    )
    if fits:
        return gathered_body(n_row, n_col, *arguments)
    return sharded_body(*arguments)


def solution(mesh):
    placed = (
        P(("grp", "col"), "row", None),
        P(("grp", "col"), "row"),
        P(("grp", "row"), "col", None),
        P(),
        P(),
        P(),
        P(),
        P(),
    )
    return jax.shard_map(
        functools.partial(body, mesh.shape["row"], mesh.shape["col"]),
        mesh=mesh,
        in_specs=placed,
        out_specs=(
            P(("grp", "col"), "row", None),
            P("grp", None),
            P("grp", None),
            P("grp", None),
            P("grp"),
            P("grp"),
            P("grp"),
        ),
        check_vma=False,
    )
```

```python
import functools

import jax
import jax.numpy as jnp
from jax import lax
from jax.experimental import pallas as pl
from jax.experimental.pallas import tpu as pltpu
from jax.sharding import PartitionSpec as P

TOKB = 2


def standardizer_parts(homolog_embedding, standardizer_scale, standardizer_shift):
    incoming_entries = homolog_embedding.astype(jnp.float32)
    center = jnp.mean(incoming_entries, axis=-1, keepdims=True)
    varied = incoming_entries - center
    variance = jnp.mean(varied * varied, axis=-1, keepdims=True)
    reciprocal_spread = lax.rsqrt(variance + 1e-05)
    standardized_entries = varied * reciprocal_spread
    standardized_bfloat = (standardized_entries * standardizer_scale + standardizer_shift).astype(
        jnp.bfloat16
    )
    return (standardized_entries, reciprocal_spread, standardized_bfloat)


def sharded_body(
    homolog_embedding,
    presence_indicator,
    coupling_change_derivative,
    standardizer_scale,
    standardizer_shift,
    first_projection_matrix,
    second_projection_matrix,
    final_projection_matrix,
):
    shard_homolog_number, residue_line_number, feature_number = homolog_embedding.shape
    tok_cols = coupling_change_derivative.shape[1]
    width = first_projection_matrix.shape[1]
    standardized_entries, reciprocal_spread, standardized_bfloat = standardizer_parts(
        homolog_embedding, standardizer_scale, standardizer_shift
    )
    mask_single_precision = presence_indicator.astype(jnp.float32)
    mask_half_precision = presence_indicator.astype(jnp.bfloat16)
    left = (
        jnp.einsum(
            "sic,cp->sip",
            standardized_bfloat,
            first_projection_matrix,
            preferred_element_type=jnp.float32,
        )
        * mask_single_precision[..., None]
    ).astype(jnp.bfloat16)
    right = (
        jnp.einsum(
            "sic,cp->sip",
            standardized_bfloat,
            second_projection_matrix,
            preferred_element_type=jnp.float32,
        )
        * mask_single_precision[..., None]
    ).astype(jnp.bfloat16)
    left_flat = left.reshape(shard_homolog_number, residue_line_number * width)
    right_flat = right.reshape(shard_homolog_number, residue_line_number * width)
    left_all, mask_left = (
        lax.all_gather(left_flat, "col", axis=0, tiled=True),
        lax.all_gather(mask_half_precision, "col", axis=0, tiled=True),
    )
    right_wide, mask_wide = (
        lax.all_gather(right_flat, "row", axis=1, tiled=True),
        lax.all_gather(mask_half_precision, "row", axis=1, tiled=True),
    )
    right_all, mask_right = (
        lax.all_to_all(right_wide, "col", split_axis=1, concat_axis=0, tiled=True),
        lax.all_to_all(mask_wide, "col", split_axis=1, concat_axis=0, tiled=True),
    )
    seq_total = left_all.shape[0]
    right_three = right_all.reshape(seq_total, tok_cols, width)
    counts = jnp.einsum("si,sj->ij", mask_left, mask_right, preferred_element_type=jnp.float32)
    scaled = coupling_change_derivative.astype(jnp.float32) / (counts + 0.001)[..., None]
    bias_part = jnp.sum(scaled, axis=(0, 1))
    scaled_bf = scaled.astype(jnp.bfloat16)
    block_rows = residue_line_number // TOKB
    right_acc = jnp.zeros((seq_total, tok_cols, width), jnp.float32)
    wout_acc = jnp.zeros(final_projection_matrix.shape, jnp.float32)
    left_pieces = []
    for block_index in range(TOKB):
        first = block_index * block_rows
        rows_bf = scaled_bf[first : first + block_rows]
        outer_grad = jnp.einsum(
            "ijz,fz->ijf", rows_bf, final_projection_matrix, preferred_element_type=jnp.float32
        ).astype(jnp.bfloat16)
        outer_grad = outer_grad.reshape(block_rows, tok_cols, width, width)
        left_block = left_all[:, first * width : (first + block_rows) * width].reshape(
            seq_total, block_rows, width
        )
        first_factor_derivative = jnp.einsum(
            "ijce,sje->sic", outer_grad, right_three, preferred_element_type=jnp.float32
        )
        right_acc = right_acc + jnp.einsum(
            "ijce,sic->sje", outer_grad, left_block, preferred_element_type=jnp.float32
        )
        outer = jnp.einsum(
            "sic,sje->ijce", left_block, right_three, preferred_element_type=jnp.float32
        ).astype(jnp.bfloat16)
        outer = outer.reshape(block_rows, tok_cols, width * width)
        wout_acc = wout_acc + jnp.einsum(
            "ijf,ijz->fz", outer, rows_bf, preferred_element_type=jnp.float32
        )
        first_factor_derivative = first_factor_derivative.reshape(seq_total, block_rows * width)
        left_pieces.append(first_factor_derivative)
    left_terms = jnp.concatenate(left_pieces, axis=1)
    left_own = lax.psum_scatter(left_terms, "col", scatter_dimension=0, tiled=True)
    right_spread = lax.all_to_all(
        right_acc.reshape(seq_total, tok_cols * width),
        "col",
        split_axis=0,
        concat_axis=1,
        tiled=True,
    )
    right_own = lax.psum_scatter(right_spread, "row", scatter_dimension=1, tiled=True)
    left_in = (
        left_own.reshape(shard_homolog_number, residue_line_number, width)
        * mask_single_precision[..., None]
    ).astype(jnp.bfloat16)
    right_in = (
        right_own.reshape(shard_homolog_number, residue_line_number, width)
        * mask_single_precision[..., None]
    ).astype(jnp.bfloat16)
    left_part = jnp.einsum(
        "sic,sip->cp", standardized_bfloat, left_in, preferred_element_type=jnp.float32
    )
    right_part = jnp.einsum(
        "sic,sip->cp", standardized_bfloat, right_in, preferred_element_type=jnp.float32
    )
    d_normal = jnp.einsum(
        "sip,cp->sic", left_in, first_projection_matrix, preferred_element_type=jnp.float32
    ) + jnp.einsum(
        "sip,cp->sic", right_in, second_projection_matrix, preferred_element_type=jnp.float32
    )
    gain_part = jnp.sum(d_normal * standardized_entries, axis=(0, 1))
    beta_part = jnp.sum(d_normal, axis=(0, 1))
    standardized_derivative = d_normal * standardizer_scale
    embedding_derivative = reciprocal_spread * (
        standardized_derivative
        - jnp.mean(standardized_derivative, axis=-1, keepdims=True)
        - standardized_entries
        * jnp.mean(standardized_derivative * standardized_entries, axis=-1, keepdims=True)
    )
    (
        final_matrix_derivative,
        first_matrix_derivative,
        second_matrix_derivative,
        scale_factor_derivative,
        shift_term_derivative,
        shift_derivative,
    ) = lax.psum((wout_acc, left_part, right_part, gain_part, beta_part, bias_part), ("row", "col"))
    return (
        embedding_derivative,
        final_matrix_derivative,
        first_matrix_derivative,
        second_matrix_derivative,
        scale_factor_derivative,
        shift_term_derivative,
        shift_derivative,
    )


BF = jnp.bfloat16
F32 = jnp.float32


def spread(rows, cols, rule):
    r = lax.broadcasted_iota(jnp.int32, (rows, cols), 0)
    c = lax.broadcasted_iota(jnp.int32, (rows, cols), 1)
    return rule(r, c)


def mm(a, b):
    return jnp.dot(a, b, preferred_element_type=F32)


def mm_nt(a, b):
    return lax.dot_general(a, b, (((1,), (1,)), ((), ())), preferred_element_type=F32)


def mm_tn(a, b):
    return lax.dot_general(a, b, (((0,), (0,)), ((), ())), preferred_element_type=F32)


def interleave(first, second):
    odd = lax.broadcasted_iota(jnp.int32, (32, 128), 1) & 32 != 0
    return (
        jnp.where(odd, pltpu.roll(second, 32, 1), first).astype(BF),
        jnp.where(odd, second, pltpu.roll(first, 96, 1)).astype(BF),
    )


def diagonal_pair(block):
    zero = jnp.zeros_like(block)
    return jnp.concatenate(
        [jnp.concatenate([block, zero], axis=1), jnp.concatenate([zero, block], axis=1)], axis=0
    )


ABSENT = 1024.0


def pack_kernel(msa_ref, mask_ref, pair_ref, out_ref):
    msa = msa_ref[...].astype(F32)
    pick = spread(8, 512, lambda r, c: jnp.where(c // 64 == r, 1.0, 0.0)).astype(BF)
    present = mm_tn(mask_ref[...].astype(F32).astype(BF), pick) > 0.5
    for g in range(4):
        rows = jnp.concatenate([msa[:, 2 * g, :], msa[:, 2 * g + 1, :]], axis=1)
        out_ref[32 * g : 32 * g + 32, :] = jnp.where(
            present[:, 128 * g : 128 * g + 128], rows, ABSENT
        ).astype(BF)
    out_ref[128:192, :] = pair_ref[...].astype(F32).reshape(64, 128).astype(BF)


def weights_kernel(*refs):
    sources, (norm_out, back_out, final_out, first_out) = refs[:5], refs[5:9]
    held, scr, sems = refs[9:14], refs[14], refs[15]
    copies = [pltpu.make_async_copy(sources[k], held[k], sems.at[k]) for k in range(5)]
    for copy in copies:
        copy.start()
    for copy in copies:
        copy.wait()
    gain_ref, offset_ref, first_ref, second_ref, final_ref = held
    norm_out[...] = jnp.concatenate(
        [
            jnp.concatenate([ref[...]] * 2, axis=1)
            for ref in (gain_ref, offset_ref, gain_ref, offset_ref) * 2
        ],
        axis=0,
    )
    for k, ref in enumerate((first_ref, second_ref)):
        narrow = ref[...].astype(F32)
        first_out[32 * k : 32 * k + 32, :] = narrow
        wide = jnp.concatenate([narrow] * 4, axis=1)
        wide = jnp.concatenate([wide] * 4, axis=0)
        own = spread(128, 256, lambda r, c: r // 32 == c // 64)
        back_out[128 * k : 128 * k + 128, :] = jnp.where(own, wide, 0.0).astype(BF)
    scr[...] = final_ref[...].astype(F32)
    for k in range(16):
        e = 4 * (k // 2) + k % 2
        final_out[32 * k : 32 * k + 32, :] = jnp.concatenate(
            [scr[pl.ds(e, 32, stride=32), :], scr[pl.ds(e + 2, 32, stride=32), :]], axis=1
        ).astype(BF)


def averager_of():
    return spread(128, 128, lambda r, c: jnp.where(r // 64 == c // 64, 1.0 / 64, 0.0)).astype(BF)


ORDER = (0, 2, 1, 3)


def stage_kernel(
    n_col, a, place_ref, set_refs, norm_ref, back_ref, final_ref,
    rhs_out, left_out, leftt_out, rightt_out, grad_out, pair_out, found_out, *rest
):
    *own_out, turn_scr = rest
    blocks = [ref.at[k] for ref in set_refs for k in range(ref.shape[0])]
    for b in range(n_col):
        at = pl.multiple_of(lax.bitwise_xor(place_ref[0], ORDER[b]) * 8, 8)
        pair_out[:, pl.ds(at, 8), :] = blocks[b][128:192, :].astype(F32).reshape(8, 8, 128)

    gain = norm_ref[0:1, :]
    offset = norm_ref[1:2, :]
    averager = averager_of()
    x = jnp.concatenate(
        [blocks[b][32 * g : 32 * g + 32, :] for g in range(4) for b in range(n_col)], axis=0
    )
    mean = mm(x, averager)
    present = mean < ABSENT / 2
    varied = x.astype(F32) - mean
    inverse = lax.rsqrt(mm((varied * varied).astype(BF), averager) + 1e-05)
    normed = varied * inverse
    if own_out:
        for g in range(4):
            own_out[0][32 * g : 32 * g + 32, :] = normed[128 * g : 128 * g + 32]
            own_out[1][32 * g : 32 * g + 32, :] = inverse[128 * g : 128 * g + 32]
    normal = jnp.where(present, normed * gain + offset, 0.0).astype(BF)
    rhs_out[:, 0:128] = normal
    rhs_out[:, 128:256] = normed.astype(BF)
    here = jnp.where(present, 1.0, 0.0)
    lane = lax.broadcasted_iota(jnp.int32, (128, 128), 1)
    found = jnp.zeros((128, 128), F32)
    for g in range(4):
        found = jnp.where(lane % 32 // 2 == 4 * a + g, here[128 * g : 128 * g + 128], found)
    found_out[...] = found
    for h in range(2):
        masked = jnp.concatenate(
            [normal[128 * g : 128 * g + 128] for g in (2 * h, 2 * h + 1)], axis=1
        )
        at = slice(128 * h, 128 * h + 128)
        left_out[:, at] = mm_nt(masked, back_ref[:128, :]).astype(BF)
        both = mm_nt(back_ref[...], masked)
        turn_scr[at, :] = both[128:]
        for k in range(2):
            leftt_out[64 * h + 32 * k : 64 * h + 32 * k + 32, :] = jnp.concatenate(
                [both[32 * k : 32 * k + 32], both[32 * k + 64 : 32 * k + 96]], axis=1
            ).astype(BF)

    for e in range(32):
        rightt_out[e] = turn_scr[pl.ds(e, 8, stride=32), :]

    pair = pair_out[...].reshape(256, 128).astype(BF)
    for n in range(2):
        pairs = jnp.concatenate(
            [diagonal_pair(pair[64 * p : 64 * p + 64]) for p in (2 * n, 2 * n + 1)], axis=0
        )
        grad = mm_nt(final_ref[...], pairs)
        for p in range(2):
            for q in range(8):
                rows = 64 * (2 * n + p)
                block = grad[64 * q : 64 * q + 64, 128 * p : 128 * p + 128]
                even, odd = interleave(block[:32], block[32:])
                grad_out[rows : rows + 32, 128 * q : 128 * q + 128] = even
                grad_out[rows + 32 : rows + 64, 128 * q : 128 * q + 128] = odd


def own_kernel(n_col, place_ref, front_ref, rear_ref, norm_ref, back_ref, final_ref, *rest):
    stage_kernel(n_col, 0, place_ref, (front_ref, rear_ref), norm_ref, back_ref, final_ref, *rest)


def pair_kernel(n_col, place_ref, core_ref, front_ref, rear_ref, norm_ref, back_ref, final_ref, *rest):
    common = (norm_ref, back_ref, final_ref)
    stage_kernel(n_col, 1, place_ref, (core_ref,), *common, *rest[:7], rest[14])
    stage_kernel(n_col, 2, place_ref, (front_ref, rear_ref), *common, *rest[7:14], rest[15])


def part_kernel(n_row, n_col, place_ref, front_ref, rear_ref, *refs):
    stages = [refs[7 * a : 7 * a + 7] for a in range(n_row - 1)]
    (
        normed_ref, inverse_ref, norm_ref, back_ref, final_ref, first_ref,
        emb_out, final_hbm_out, first_out, second_out, gain_out, offset_out, bias_out,
        right_scr, scaled_scr, grad_scr, outer_scr, wide_scr, all_scr,
        final_out, out_sem, turn_scr,
    ) = refs[7 * (n_row - 1) : -7]
    stages.append(refs[-7:])
    stage_kernel(
        n_col, n_row - 1, place_ref, (front_ref, rear_ref),
        norm_ref, back_ref, final_ref, *stages[-1], turn_scr,
    )
    gain = norm_ref[0:1, :]
    averager = averager_of()
    lane = lax.broadcasted_iota(jnp.int32, (128, 128), 1)

    found = sum(stage[6][...] for stage in stages)
    turned = pltpu.roll(found, 64, 1)
    mask = jnp.where((lane % 2 == 0) == (lane < 64), found, turned)
    mask_t = mask.T

    for e in range(32):
        right_scr[32 * e : 32 * e + 32, :] = jnp.concatenate(
            [stage[3][e] for stage in stages], axis=0
        ).astype(BF)

    mask_bf = mask.astype(BF)
    share = (1.0 / (mm_tn(mask_bf, mask_bf)[0:32] + 0.001)).astype(BF)
    for i in range(32):
        a, at = i // 8, 32 * (i % 8)
        for q in range(8):
            grad_scr[32 * i : 32 * i + 32, 128 * q : 128 * q + 128] = (
                stages[a][4][at : at + 32, 128 * q : 128 * q + 128] * share[i : i + 1]
            )
    left = jnp.concatenate([stage[1][...] for stage in stages], axis=1)
    right_grad = mm(left, grad_scr[...])
    left_grad = mm(grad_scr[...], right_scr[...])

    turn = spread(
        256, 256, lambda r, c: jnp.where((r // 8 == c % 32) & (r % 8 == c // 32), 1.0, 0.0)
    ).astype(BF)
    mask_two = jnp.concatenate([mask, mask], axis=1)
    right_in = [
        mm_nt(turn, (right_grad[:, 256 * q : 256 * q + 256] * mask_two).astype(BF))
        for q in range(4)
    ]
    for t in range(32):
        at = slice(128 * (t // 2), 128 * (t // 2) + 128)
        row = 32 * (t % 2)
        all_scr[row : row + 32, at] = (
            left_grad[32 * t : 32 * t + 32] * mask_t[t : t + 1]
        ).astype(BF)
        all_scr[row + 64 : row + 96, at] = jnp.concatenate(
            [part[8 * t : 8 * t + 8] for part in right_in], axis=0
        ).astype(BF)

    bias = jnp.zeros((1, 128), F32)
    ones = jnp.ones((128, 128), BF)
    for p in range(8):
        both_on = jnp.concatenate(
            [mask_t[0:32] * mask_t[i : i + 1] for i in range(4 * p, 4 * p + 4)], axis=0
        ).astype(BF)
        counts = mm(both_on, ones)
        pair = stages[p // 2][5][4 * (p % 2) : 4 * (p % 2) + 4]
        scaled = pair.reshape(128, 128) / (counts + 0.001)
        bias = bias + jnp.sum(scaled, axis=0, keepdims=True)
        scaled_scr[128 * p : 128 * p + 128, :] = scaled.astype(BF)
    bias_out[...] = bias

    left_t = jnp.concatenate([stage[2][...] for stage in stages], axis=0)
    for n in range(8):
        rights = jnp.concatenate(
            [diagonal_pair(right_scr[64 * p : 64 * p + 64, :]) for p in (2 * n, 2 * n + 1)], axis=0
        )
        outer = mm_nt(left_t, rights)
        for p in range(2):
            for q in range(8):
                rows = 64 * (2 * n + p)
                block = outer[64 * q : 64 * q + 64, 128 * p : 128 * p + 128]
                even, odd = interleave(block[:32], block[32:])
                outer_scr[rows : rows + 32, 128 * q : 128 * q + 128] = even
                outer_scr[rows + 32 : rows + 64, 128 * q : 128 * q + 128] = odd
    wide_scr[...] = mm(outer_scr[...], scaled_scr[...])
    for c in range(32):
        final_out[32 * c : 32 * c + 32, :] = wide_scr[pl.ds(c, 32, stride=32), :]
    final_send = pltpu.make_async_copy(final_out, final_hbm_out, out_sem)
    final_send.start()

    total = mm(
        all_scr[...], jnp.concatenate([stage[0][...] for stage in stages], axis=0)
    )
    sums = all_scr[:, 0:128].astype(F32)
    for g in range(1, 16):
        sums = sums + all_scr[:, 128 * g : 128 * g + 128].astype(F32)

    def fold(block):
        return block[0:32, 0:64] + block[32:64, 64:128]

    first_out[...] = fold(total[0:64, 0:128])
    second_out[...] = fold(total[64:128, 0:128])
    sums = jnp.sum(sums, axis=1, keepdims=True)
    left_sum = sums[0:32] + sums[32:64]
    right_sum = sums[64:96] + sums[96:128]
    first, second = first_ref[0:32, :], first_ref[32:64, :]
    gain_out[...] = jnp.sum(
        first * fold(total[0:64, 128:256]) + second * fold(total[64:128, 128:256]),
        axis=0, keepdims=True,
    )
    offset_out[...] = jnp.sum(first * left_sum + second * right_sum, axis=0, keepdims=True)

    d_hat = []
    for h in range(2):
        sides = [
            jnp.concatenate(
                [all_scr[row : row + 64, 128 * g : 128 * g + 128] for g in (2 * h, 2 * h + 1)], axis=0
            )
            for row in (0, 64)
        ]
        d_normal = mm_tn(jnp.concatenate(sides, axis=0), back_ref[...])
        d_hat += [d_normal[0:32, 0:128] * gain, d_normal[0:32, 128:256] * gain]
    d_hat = jnp.concatenate(d_hat, axis=0)
    normed = normed_ref[...]
    means = mm(jnp.concatenate([d_hat, d_hat * normed], axis=0).astype(BF), averager)
    result = inverse_ref[...] * (d_hat - means[:128] - normed * means[128:])
    for g in range(4):
        emb_out[:, 2 * g, :] = result[32 * g : 32 * g + 32, 0:64]
        emb_out[:, 2 * g + 1, :] = result[32 * g : 32 * g + 32, 64:128]
    final_send.wait()


def vmem(count):
    return [pl.BlockSpec(memory_space=pltpu.VMEM)] * count


LIMIT = pltpu.CompilerParams(vmem_limit_bytes=32 * 1024 * 1024)


def gathered_body(
    n_row,
    n_col,
    homolog_embedding,
    presence_indicator,
    coupling_change_derivative,
    standardizer_scale,
    standardizer_shift,
    first_projection_matrix,
    second_projection_matrix,
    final_projection_matrix,
):
    shards, tokens, features = homolog_embedding.shape
    width = first_projection_matrix.shape[1]
    first_t, second_t = first_projection_matrix.T, second_projection_matrix.T
    shape = lambda *dims: jax.ShapeDtypeStruct(dims, F32)
    held = lambda *dims: pltpu.VMEM(dims, F32)
    held_bf = lambda *dims: pltpu.VMEM(dims, BF)
    hbm = pl.BlockSpec(memory_space=pltpu.HBM)
    place = lax.bitwise_xor(lax.axis_index("row"), lax.axis_index("col"))
    place = place.astype(jnp.int32).reshape(1)
    packed = pl.pallas_call(
        pack_kernel,
        out_shape=held_bf(192, 128),
        in_specs=vmem(3),
        out_specs=vmem(1)[0],
    )(homolog_embedding, presence_indicator.T, coupling_change_derivative)
    def over(axis, size, step, array):
        return lax.ppermute(array, axis, [(k, k ^ step) for k in range(size)])

    far = over("col", n_col, 2, packed)
    near = over("col", n_col, 1, packed)
    last = over("col", n_col, 3, packed)
    front = jnp.stack([packed, far])
    chip_front = over("row", n_row, 2, front)
    rear = jnp.stack([near, last])
    chip_rear = over("row", n_row, 2, rear)
    front, final_projection_matrix = lax.optimization_barrier((front, final_projection_matrix))
    weights = pl.pallas_call(
        weights_kernel,
        out_shape=(
            held(8, 128), held_bf(256, 256), held_bf(width * width // 2, 256), held(2 * width, features),
        ),
        in_specs=[hbm] * 5,
        out_specs=tuple(vmem(4)),
        scratch_shapes=[
            pltpu.VMEM((1, features), F32),
            pltpu.VMEM((1, features), F32),
            pltpu.VMEM((width, features), BF),
            pltpu.VMEM((width, features), BF),
            pltpu.VMEM((width * width, 128), BF),
            pltpu.VMEM((width * width, 128), F32),
            pltpu.SemaphoreType.DMA((5,)),
        ],
        compiler_params=LIMIT,
    )(
        *[
            pltpu.with_memory_space_constraint(x, pltpu.HBM)
            for x in (
                standardizer_scale.reshape(1, features),
                standardizer_shift.reshape(1, features),
                first_t,
                second_t,
                final_projection_matrix,
            )
        ]
    )
    norm, back, final_turned, first = weights
    own = jnp.concatenate([front, rear])
    own, chip_front, norm = lax.optimization_barrier((own, chip_front, norm))
    core = over("row", n_row, 1, own)
    stage_outs = [
        held_bf(512, 256), held_bf(128, 256), held_bf(128, 256), held(width, 8, 128),
        held_bf(256, 1024), held(8, 32, 128), held(128, 128),
    ]
    scalar = pl.BlockSpec(memory_space=pltpu.SMEM)

    def stages_of(kernel, sets, outs, flops):
        return pl.pallas_call(
            functools.partial(kernel, n_col),
            out_shape=tuple(outs),
            in_specs=[scalar] + vmem(len(sets) + 3),
            out_specs=tuple(vmem(len(outs))),
            scratch_shapes=[pltpu.VMEM((256, 128), F32)] * (len(outs) // 7),
            compiler_params=LIMIT,
            cost_estimate=pl.CostEstimate(
                flops=flops, bytes_accessed=flops // 256, transcendentals=0
            ),
        )(place, *sets, norm, back, final_turned)

    both_front = over("row", n_row, 1, chip_front)
    own_stage = stages_of(own_kernel, (front, rear), stage_outs + [held(128, 128)] * 2, 1_000_000_000)
    chip_rear, own_stage = lax.optimization_barrier((chip_rear, own_stage))
    both_rear = over("row", n_row, 1, chip_rear)
    pair_stages = stages_of(pair_kernel, (core, chip_front, chip_rear), stage_outs * 2, 1000000)
    stages = [own_stage[:7], pair_stages]
    outs = pl.pallas_call(
        functools.partial(part_kernel, n_row, n_col),
        out_shape=(
            shape(shards, tokens, features),
            shape(width * width, 128),
            shape(width, features),
            shape(width, features),
            shape(1, features),
            shape(1, features),
            shape(1, 128),
        ),
        in_specs=[scalar] + vmem(7 * (n_row - 1) + 8),
        out_specs=(*vmem(1), hbm, *vmem(5)),
        scratch_shapes=[
            pltpu.VMEM((1024, 128), BF),
            pltpu.VMEM((1024, 128), BF),
            pltpu.VMEM((1024, 1024), BF),
            pltpu.VMEM((1024, 1024), BF),
            pltpu.VMEM((1024, 128), F32),
            pltpu.VMEM((128, 2048), BF),
            pltpu.VMEM((1024, 128), F32),
            pltpu.SemaphoreType.DMA,
            pltpu.VMEM((256, 128), F32),
            *stage_outs,
        ],
        compiler_params=LIMIT,
    )(place, both_front, both_rear, *[x for s in stages for x in s], *own_stage[7:], norm, back, final_turned, first)
    emb, final, first, second, gain, offset, bias = outs
    return emb, final, first.T, second.T, gain.reshape(-1), offset.reshape(-1), bias.reshape(-1)


def body(n_row, n_col, *arguments):
    msa, _, pair = arguments[:3]
    width = arguments[5].shape[1]
    fits = (
        n_row == 4
        and n_col == 4
        and msa.shape == (32, 8, 64)
        and pair.shape == (8, 8, 128)
        and width == 32
    )
    if fits:
        return gathered_body(n_row, n_col, *arguments)
    return sharded_body(*arguments)


def solution(mesh):
    placed = (
        P(("grp", "col"), "row", None),
        P(("grp", "col"), "row"),
        P(("grp", "row"), "col", None),
        P(),
        P(),
        P(),
        P(),
        P(),
    )
    return jax.shard_map(
        functools.partial(body, mesh.shape["row"], mesh.shape["col"]),
        mesh=mesh,
        in_specs=placed,
        out_specs=(
            P(("grp", "col"), "row", None),
            P("grp", None),
            P("grp", None),
            P("grp", None),
            P("grp"),
            P("grp"),
            P("grp"),
        ),
        check_vma=False,
    )
```

```python
import functools

import jax
import jax.numpy as jnp
from jax import lax
from jax.experimental import pallas as pl
from jax.experimental.pallas import tpu as pltpu
from jax.sharding import PartitionSpec as P

TOKB = 2


def standardizer_parts(homolog_embedding, standardizer_scale, standardizer_shift):
    incoming_entries = homolog_embedding.astype(jnp.float32)
    center = jnp.mean(incoming_entries, axis=-1, keepdims=True)
    varied = incoming_entries - center
    variance = jnp.mean(varied * varied, axis=-1, keepdims=True)
    reciprocal_spread = lax.rsqrt(variance + 1e-05)
    standardized_entries = varied * reciprocal_spread
    standardized_bfloat = (standardized_entries * standardizer_scale + standardizer_shift).astype(
        jnp.bfloat16
    )
    return (standardized_entries, reciprocal_spread, standardized_bfloat)


def sharded_body(
    homolog_embedding,
    presence_indicator,
    coupling_change_derivative,
    standardizer_scale,
    standardizer_shift,
    first_projection_matrix,
    second_projection_matrix,
    final_projection_matrix,
):
    shard_homolog_number, residue_line_number, feature_number = homolog_embedding.shape
    tok_cols = coupling_change_derivative.shape[1]
    width = first_projection_matrix.shape[1]
    standardized_entries, reciprocal_spread, standardized_bfloat = standardizer_parts(
        homolog_embedding, standardizer_scale, standardizer_shift
    )
    mask_single_precision = presence_indicator.astype(jnp.float32)
    mask_half_precision = presence_indicator.astype(jnp.bfloat16)
    left = (
        jnp.einsum(
            "sic,cp->sip",
            standardized_bfloat,
            first_projection_matrix,
            preferred_element_type=jnp.float32,
        )
        * mask_single_precision[..., None]
    ).astype(jnp.bfloat16)
    right = (
        jnp.einsum(
            "sic,cp->sip",
            standardized_bfloat,
            second_projection_matrix,
            preferred_element_type=jnp.float32,
        )
        * mask_single_precision[..., None]
    ).astype(jnp.bfloat16)
    left_flat = left.reshape(shard_homolog_number, residue_line_number * width)
    right_flat = right.reshape(shard_homolog_number, residue_line_number * width)
    left_all, mask_left = (
        lax.all_gather(left_flat, "col", axis=0, tiled=True),
        lax.all_gather(mask_half_precision, "col", axis=0, tiled=True),
    )
    right_wide, mask_wide = (
        lax.all_gather(right_flat, "row", axis=1, tiled=True),
        lax.all_gather(mask_half_precision, "row", axis=1, tiled=True),
    )
    right_all, mask_right = (
        lax.all_to_all(right_wide, "col", split_axis=1, concat_axis=0, tiled=True),
        lax.all_to_all(mask_wide, "col", split_axis=1, concat_axis=0, tiled=True),
    )
    seq_total = left_all.shape[0]
    right_three = right_all.reshape(seq_total, tok_cols, width)
    counts = jnp.einsum("si,sj->ij", mask_left, mask_right, preferred_element_type=jnp.float32)
    scaled = coupling_change_derivative.astype(jnp.float32) / (counts + 0.001)[..., None]
    bias_part = jnp.sum(scaled, axis=(0, 1))
    scaled_bf = scaled.astype(jnp.bfloat16)
    block_rows = residue_line_number // TOKB
    right_acc = jnp.zeros((seq_total, tok_cols, width), jnp.float32)
    wout_acc = jnp.zeros(final_projection_matrix.shape, jnp.float32)
    left_pieces = []
    for block_index in range(TOKB):
        first = block_index * block_rows
        rows_bf = scaled_bf[first : first + block_rows]
        outer_grad = jnp.einsum(
            "ijz,fz->ijf", rows_bf, final_projection_matrix, preferred_element_type=jnp.float32
        ).astype(jnp.bfloat16)
        outer_grad = outer_grad.reshape(block_rows, tok_cols, width, width)
        left_block = left_all[:, first * width : (first + block_rows) * width].reshape(
            seq_total, block_rows, width
        )
        first_factor_derivative = jnp.einsum(
            "ijce,sje->sic", outer_grad, right_three, preferred_element_type=jnp.float32
        )
        right_acc = right_acc + jnp.einsum(
            "ijce,sic->sje", outer_grad, left_block, preferred_element_type=jnp.float32
        )
        outer = jnp.einsum(
            "sic,sje->ijce", left_block, right_three, preferred_element_type=jnp.float32
        ).astype(jnp.bfloat16)
        outer = outer.reshape(block_rows, tok_cols, width * width)
        wout_acc = wout_acc + jnp.einsum(
            "ijf,ijz->fz", outer, rows_bf, preferred_element_type=jnp.float32
        )
        first_factor_derivative = first_factor_derivative.reshape(seq_total, block_rows * width)
        left_pieces.append(first_factor_derivative)
    left_terms = jnp.concatenate(left_pieces, axis=1)
    left_own = lax.psum_scatter(left_terms, "col", scatter_dimension=0, tiled=True)
    right_spread = lax.all_to_all(
        right_acc.reshape(seq_total, tok_cols * width),
        "col",
        split_axis=0,
        concat_axis=1,
        tiled=True,
    )
    right_own = lax.psum_scatter(right_spread, "row", scatter_dimension=1, tiled=True)
    left_in = (
        left_own.reshape(shard_homolog_number, residue_line_number, width)
        * mask_single_precision[..., None]
    ).astype(jnp.bfloat16)
    right_in = (
        right_own.reshape(shard_homolog_number, residue_line_number, width)
        * mask_single_precision[..., None]
    ).astype(jnp.bfloat16)
    left_part = jnp.einsum(
        "sic,sip->cp", standardized_bfloat, left_in, preferred_element_type=jnp.float32
    )
    right_part = jnp.einsum(
        "sic,sip->cp", standardized_bfloat, right_in, preferred_element_type=jnp.float32
    )
    d_normal = jnp.einsum(
        "sip,cp->sic", left_in, first_projection_matrix, preferred_element_type=jnp.float32
    ) + jnp.einsum(
        "sip,cp->sic", right_in, second_projection_matrix, preferred_element_type=jnp.float32
    )
    gain_part = jnp.sum(d_normal * standardized_entries, axis=(0, 1))
    beta_part = jnp.sum(d_normal, axis=(0, 1))
    standardized_derivative = d_normal * standardizer_scale
    embedding_derivative = reciprocal_spread * (
        standardized_derivative
        - jnp.mean(standardized_derivative, axis=-1, keepdims=True)
        - standardized_entries
        * jnp.mean(standardized_derivative * standardized_entries, axis=-1, keepdims=True)
    )
    (
        final_matrix_derivative,
        first_matrix_derivative,
        second_matrix_derivative,
        scale_factor_derivative,
        shift_term_derivative,
        shift_derivative,
    ) = lax.psum((wout_acc, left_part, right_part, gain_part, beta_part, bias_part), ("row", "col"))
    return (
        embedding_derivative,
        final_matrix_derivative,
        first_matrix_derivative,
        second_matrix_derivative,
        scale_factor_derivative,
        shift_term_derivative,
        shift_derivative,
    )


BF = jnp.bfloat16
F32 = jnp.float32


def spread(rows, cols, rule):
    r = lax.broadcasted_iota(jnp.int32, (rows, cols), 0)
    c = lax.broadcasted_iota(jnp.int32, (rows, cols), 1)
    return rule(r, c)


def mm(a, b):
    return jnp.dot(a, b, preferred_element_type=F32)


def mm_nt(a, b):
    return lax.dot_general(a, b, (((1,), (1,)), ((), ())), preferred_element_type=F32)


def mm_tn(a, b):
    return lax.dot_general(a, b, (((0,), (0,)), ((), ())), preferred_element_type=F32)


def interleave(first, second):
    odd = lax.broadcasted_iota(jnp.int16, (32, 128), 1) & 32 != 0
    return (
        jnp.where(odd, pltpu.roll(second, 32, 1), first),
        jnp.where(odd, second, pltpu.roll(first, 96, 1)),
    )


def diagonal_pair(block):
    zero = jnp.zeros_like(block)
    return jnp.concatenate(
        [jnp.concatenate([block, zero], axis=1), jnp.concatenate([zero, block], axis=1)], axis=0
    )


ABSENT = 1024.0


def pack_kernel(msa_ref, mask_ref, pair_ref, out_ref, scr):
    scr[...] = msa_ref[...].astype(F32).reshape(256, 64)
    pick = spread(8, 512, lambda r, c: jnp.where(c // 64 == r, 1.0, 0.0)).astype(BF)
    present = mm_tn(mask_ref[...].astype(F32).astype(BF), pick) > 0.5
    for g in range(4):
        rows = jnp.concatenate(
            [scr[pl.ds(t, 32, stride=8), :] for t in (2 * g, 2 * g + 1)], axis=1
        )
        out_ref[32 * g : 32 * g + 32, :] = jnp.where(
            present[:, 128 * g : 128 * g + 128], rows, ABSENT
        ).astype(BF)
    out_ref[128:192, :] = pair_ref[...].astype(F32).reshape(64, 128).astype(BF)


def weights_kernel(*refs):
    sources, (norm_out, back_out, final_out, first_out) = refs[:5], refs[5:9]
    held, scr, sems = refs[9:14], refs[14], refs[15]
    copies = [pltpu.make_async_copy(sources[k], held[k], sems.at[k]) for k in range(5)]
    for copy in copies:
        copy.start()
    for copy in copies:
        copy.wait()
    gain_ref, offset_ref, first_ref, second_ref, final_ref = held
    norm_out[...] = jnp.concatenate(
        [
            jnp.concatenate([ref[...]] * 2, axis=1)
            for ref in (gain_ref, offset_ref, gain_ref, offset_ref) * 2
        ],
        axis=0,
    )
    for k, ref in enumerate((first_ref, second_ref)):
        narrow = ref[...].astype(F32)
        first_out[32 * k : 32 * k + 32, :] = narrow
        wide = jnp.concatenate([narrow] * 4, axis=1)
        wide = jnp.concatenate([wide] * 4, axis=0)
        own = spread(128, 256, lambda r, c: r // 32 == c // 64)
        back_out[128 * k : 128 * k + 128, :] = jnp.where(own, wide, 0.0).astype(BF)
    scr[...] = final_ref[...].astype(F32)
    for k in range(16):
        e = 4 * (k // 2) + k % 2
        final_out[32 * k : 32 * k + 32, :] = jnp.concatenate(
            [scr[pl.ds(e, 32, stride=32), :], scr[pl.ds(e + 2, 32, stride=32), :]], axis=1
        ).astype(BF)


def averager_of():
    return spread(128, 128, lambda r, c: jnp.where(r // 64 == c // 64, 1.0 / 64, 0.0)).astype(BF)


ORDER = (0, 2, 1, 3)


def stage_kernel(
    n_col, a, place_ref, set_refs, norm_ref, back_ref, final_ref,
    rhs_out, left_out, leftt_out, rightt_out, grad_out, pair_out, found_out, *rest
):
    *own_out, turn_scr = rest
    blocks = [ref.at[k] for ref in set_refs for k in range(ref.shape[0])]
    for b in range(n_col):
        at = pl.multiple_of(lax.bitwise_xor(place_ref[0], ORDER[b]) * 8, 8)
        pair_out[:, pl.ds(at, 8), :] = blocks[b][128:192, :].astype(F32).reshape(8, 8, 128)

    gain = norm_ref[0:1, :]
    offset = norm_ref[1:2, :]
    averager = averager_of()
    x = jnp.concatenate(
        [blocks[b][32 * g : 32 * g + 32, :] for g in range(4) for b in range(n_col)], axis=0
    )
    mean = mm(x, averager)
    present = mean < ABSENT / 2
    varied = x.astype(F32) - mean
    inverse = lax.rsqrt(mm((varied * varied).astype(BF), averager) + 1e-05)
    normed = varied * inverse
    if own_out:
        for g in range(4):
            own_out[0][32 * g : 32 * g + 32, :] = normed[128 * g : 128 * g + 32]
            own_out[1][32 * g : 32 * g + 32, :] = inverse[128 * g : 128 * g + 32]
    normal = jnp.where(present, normed * gain + offset, 0.0).astype(BF)
    rhs_out[:, 0:128] = normal
    rhs_out[:, 128:256] = normed.astype(BF)
    here = jnp.where(present, 1.0, 0.0)
    lane = lax.broadcasted_iota(jnp.int32, (128, 128), 1)
    found = jnp.zeros((128, 128), F32)
    for g in range(4):
        found = jnp.where(lane % 32 // 2 == 4 * a + g, here[128 * g : 128 * g + 128], found)
    found_out[...] = found
    for h in range(2):
        masked = jnp.concatenate(
            [normal[128 * g : 128 * g + 128] for g in (2 * h, 2 * h + 1)], axis=1
        )
        at = slice(128 * h, 128 * h + 128)
        left_out[:, at] = mm_nt(masked, back_ref[:128, :]).astype(BF)
        both = mm_nt(back_ref[...], masked)
        turn_scr[at, :] = both[128:]
        for k in range(2):
            leftt_out[64 * h + 32 * k : 64 * h + 32 * k + 32, :] = jnp.concatenate(
                [both[32 * k : 32 * k + 32], both[32 * k + 64 : 32 * k + 96]], axis=1
            ).astype(BF)

    for e in range(32):
        rightt_out[e] = turn_scr[pl.ds(e, 8, stride=32), :]

    pair = pair_out[...].reshape(256, 128).astype(BF)
    for n in range(2):
        pairs = jnp.concatenate(
            [diagonal_pair(pair[64 * p : 64 * p + 64]) for p in (2 * n, 2 * n + 1)], axis=0
        )
        grad = mm_nt(final_ref[...], pairs).astype(BF)
        for p in range(2):
            for q in range(8):
                rows = 64 * (2 * n + p)
                block = grad[64 * q : 64 * q + 64, 128 * p : 128 * p + 128]
                even, odd = interleave(block[:32], block[32:])
                grad_out[rows : rows + 32, 128 * q : 128 * q + 128] = even
                grad_out[rows + 32 : rows + 64, 128 * q : 128 * q + 128] = odd


def own_kernel(n_col, place_ref, front_ref, rear_ref, norm_ref, back_ref, final_ref, *rest):
    stage_kernel(n_col, 0, place_ref, (front_ref, rear_ref), norm_ref, back_ref, final_ref, *rest)


def pair_kernel(n_col, place_ref, core_ref, front_ref, rear_ref, norm_ref, back_ref, final_ref, *rest):
    common = (norm_ref, back_ref, final_ref)
    stage_kernel(n_col, 1, place_ref, (core_ref,), *common, *rest[:7], rest[14])
    stage_kernel(n_col, 2, place_ref, (front_ref, rear_ref), *common, *rest[7:14], rest[15])


def part_kernel(n_row, n_col, place_ref, front_ref, rear_ref, *refs):
    stages = [refs[7 * a : 7 * a + 7] for a in range(n_row - 1)]
    (
        normed_ref, inverse_ref, norm_ref, back_ref, final_ref, first_ref,
        emb_out, final_hbm_out, first_out, second_out, gain_out, offset_out, bias_out,
        right_scr, scaled_scr, grad_scr, outer_scr, wide_scr, all_scr,
        final_out, out_sem, turn_scr,
    ) = refs[7 * (n_row - 1) : -7]
    stages.append(refs[-7:])
    stage_kernel(
        n_col, n_row - 1, place_ref, (front_ref, rear_ref),
        norm_ref, back_ref, final_ref, *stages[-1], turn_scr,
    )
    gain = norm_ref[0:1, :]
    averager = averager_of()
    lane = lax.broadcasted_iota(jnp.int32, (128, 128), 1)

    found = sum(stage[6][...] for stage in stages)
    turned = pltpu.roll(found, 64, 1)
    mask = jnp.where((lane % 2 == 0) == (lane < 64), found, turned)
    mask_t = mask.T

    for e in range(32):
        right_scr[32 * e : 32 * e + 32, :] = jnp.concatenate(
            [stage[3][e] for stage in stages], axis=0
        ).astype(BF)

    mask_bf = mask.astype(BF)
    share = (1.0 / (mm_tn(mask_bf, mask_bf)[0:32] + 0.001)).astype(BF)
    for i in range(32):
        a, at = i // 8, 32 * (i % 8)
        for q in range(8):
            grad_scr[32 * i : 32 * i + 32, 128 * q : 128 * q + 128] = (
                stages[a][4][at : at + 32, 128 * q : 128 * q + 128] * share[i : i + 1]
            )
    left = jnp.concatenate([stage[1][...] for stage in stages], axis=1)
    right_grad = mm(left, grad_scr[...])
    left_grad = mm(grad_scr[...], right_scr[...])

    turn = spread(
        256, 256, lambda r, c: jnp.where((r // 8 == c % 32) & (r % 8 == c // 32), 1.0, 0.0)
    ).astype(BF)
    mask_two = jnp.concatenate([mask, mask], axis=1)
    right_in = [
        mm_nt(turn, (right_grad[:, 256 * q : 256 * q + 256] * mask_two).astype(BF))
        for q in range(4)
    ]
    for t in range(32):
        at = slice(128 * (t // 2), 128 * (t // 2) + 128)
        row = 32 * (t % 2)
        all_scr[row : row + 32, at] = (
            left_grad[32 * t : 32 * t + 32] * mask_t[t : t + 1]
        ).astype(BF)
        all_scr[row + 64 : row + 96, at] = jnp.concatenate(
            [part[8 * t : 8 * t + 8] for part in right_in], axis=0
        ).astype(BF)

    total = mm(
        all_scr[...], jnp.concatenate([stage[0][...] for stage in stages], axis=0)
    )
    sums = all_scr[:, 0:128].astype(F32)
    for g in range(1, 16):
        sums = sums + all_scr[:, 128 * g : 128 * g + 128].astype(F32)

    def fold(block):
        return block[0:32, 0:64] + block[32:64, 64:128]

    first_out[...] = fold(total[0:64, 0:128])
    second_out[...] = fold(total[64:128, 0:128])
    sums = jnp.sum(sums, axis=1, keepdims=True)
    left_sum = sums[0:32] + sums[32:64]
    right_sum = sums[64:96] + sums[96:128]
    first, second = first_ref[0:32, :], first_ref[32:64, :]
    gain_out[...] = jnp.sum(
        first * fold(total[0:64, 128:256]) + second * fold(total[64:128, 128:256]),
        axis=0, keepdims=True,
    )
    offset_out[...] = jnp.sum(first * left_sum + second * right_sum, axis=0, keepdims=True)

    d_hat = []
    for h in range(2):
        sides = [
            jnp.concatenate(
                [all_scr[row : row + 64, 128 * g : 128 * g + 128] for g in (2 * h, 2 * h + 1)], axis=0
            )
            for row in (0, 64)
        ]
        d_normal = mm_tn(jnp.concatenate(sides, axis=0), back_ref[...])
        d_hat += [d_normal[0:32, 0:128] * gain, d_normal[0:32, 128:256] * gain]
    d_hat = jnp.concatenate(d_hat, axis=0)
    normed = normed_ref[...]
    means = mm(jnp.concatenate([d_hat, d_hat * normed], axis=0).astype(BF), averager)
    result = inverse_ref[...] * (d_hat - means[:128] - normed * means[128:])
    for g in range(4):
        emb_out[:, 2 * g, :] = result[32 * g : 32 * g + 32, 0:64]
        emb_out[:, 2 * g + 1, :] = result[32 * g : 32 * g + 32, 64:128]
    bias = jnp.zeros((1, 128), F32)
    ones = jnp.ones((128, 128), BF)
    for p in range(8):
        both_on = jnp.concatenate(
            [mask_t[0:32] * mask_t[i : i + 1] for i in range(4 * p, 4 * p + 4)], axis=0
        ).astype(BF)
        counts = mm(both_on, ones)
        pair = stages[p // 2][5][4 * (p % 2) : 4 * (p % 2) + 4]
        scaled = pair.reshape(128, 128) / (counts + 0.001)
        bias = bias + jnp.sum(scaled, axis=0, keepdims=True)
        scaled_scr[128 * p : 128 * p + 128, :] = scaled.astype(BF)
    bias_out[...] = bias

    left_t = jnp.concatenate([stage[2][...] for stage in stages], axis=0)
    for n in range(8):
        rights = jnp.concatenate(
            [diagonal_pair(right_scr[64 * p : 64 * p + 64, :]) for p in (2 * n, 2 * n + 1)], axis=0
        )
        outer = mm_nt(left_t, rights).astype(BF)
        for p in range(2):
            for q in range(8):
                rows = 64 * (2 * n + p)
                block = outer[64 * q : 64 * q + 64, 128 * p : 128 * p + 128]
                even, odd = interleave(block[:32], block[32:])
                outer_scr[rows : rows + 32, 128 * q : 128 * q + 128] = even
                outer_scr[rows + 32 : rows + 64, 128 * q : 128 * q + 128] = odd
    wide_scr[...] = mm(outer_scr[...], scaled_scr[...])
    sends = []
    for h in range(4):
        for c in range(8 * h, 8 * h + 8):
            final_out[32 * c : 32 * c + 32, :] = wide_scr[pl.ds(c, 32, stride=32), :]
        at = pl.ds(256 * h, 256)
        sends.append(
            pltpu.make_async_copy(final_out.at[at], final_hbm_out.at[at], out_sem.at[h])
        )
        sends[-1].start()
    for send in sends:
        send.wait()


def vmem(count):
    return [pl.BlockSpec(memory_space=pltpu.VMEM)] * count


LIMIT = pltpu.CompilerParams(vmem_limit_bytes=32 * 1024 * 1024)


def gathered_body(
    n_row,
    n_col,
    homolog_embedding,
    presence_indicator,
    coupling_change_derivative,
    standardizer_scale,
    standardizer_shift,
    first_projection_matrix,
    second_projection_matrix,
    final_projection_matrix,
):
    shards, tokens, features = homolog_embedding.shape
    width = first_projection_matrix.shape[1]
    first_t, second_t = first_projection_matrix.T, second_projection_matrix.T
    shape = lambda *dims: jax.ShapeDtypeStruct(dims, F32)
    held = lambda *dims: pltpu.VMEM(dims, F32)
    held_bf = lambda *dims: pltpu.VMEM(dims, BF)
    hbm = pl.BlockSpec(memory_space=pltpu.HBM)
    place = lax.bitwise_xor(lax.axis_index("row"), lax.axis_index("col"))
    place = place.astype(jnp.int32).reshape(1)
    packed = pl.pallas_call(
        pack_kernel,
        out_shape=held_bf(192, 128),
        in_specs=vmem(3),
        out_specs=vmem(1)[0],
        scratch_shapes=[pltpu.VMEM((256, 64), F32)],
    )(homolog_embedding, presence_indicator.T, coupling_change_derivative)
    def over(axis, size, step, array):
        return lax.ppermute(array, axis, [(k, k ^ step) for k in range(size)])

    far = over("col", n_col, 2, packed)
    near = over("col", n_col, 1, packed)
    last = over("col", n_col, 3, packed)
    front = jnp.stack([packed, far])
    chip_front = over("row", n_row, 2, front)
    rear = jnp.stack([near, last])
    chip_rear = over("row", n_row, 2, rear)
    front, final_projection_matrix = lax.optimization_barrier((front, final_projection_matrix))
    weights = pl.pallas_call(
        weights_kernel,
        out_shape=(
            held(8, 128), held_bf(256, 256), held_bf(width * width // 2, 256), held(2 * width, features),
        ),
        in_specs=[hbm] * 5,
        out_specs=tuple(vmem(4)),
        scratch_shapes=[
            pltpu.VMEM((1, features), F32),
            pltpu.VMEM((1, features), F32),
            pltpu.VMEM((width, features), BF),
            pltpu.VMEM((width, features), BF),
            pltpu.VMEM((width * width, 128), BF),
            pltpu.VMEM((width * width, 128), F32),
            pltpu.SemaphoreType.DMA((5,)),
        ],
        compiler_params=LIMIT,
    )(
        *[
            pltpu.with_memory_space_constraint(x, pltpu.HBM)
            for x in (
                standardizer_scale.reshape(1, features),
                standardizer_shift.reshape(1, features),
                first_t,
                second_t,
                final_projection_matrix,
            )
        ]
    )
    norm, back, final_turned, first = weights
    own = jnp.concatenate([front, rear])
    own, chip_front, norm = lax.optimization_barrier((own, chip_front, norm))
    core = over("row", n_row, 1, own)
    stage_outs = [
        held_bf(512, 256), held_bf(128, 256), held_bf(128, 256), held(width, 8, 128),
        held_bf(256, 1024), held(8, 32, 128), held(128, 128),
    ]
    scalar = pl.BlockSpec(memory_space=pltpu.SMEM)

    def stages_of(kernel, sets, outs, flops):
        return pl.pallas_call(
            functools.partial(kernel, n_col),
            out_shape=tuple(outs),
            in_specs=[scalar] + vmem(len(sets) + 3),
            out_specs=tuple(vmem(len(outs))),
            scratch_shapes=[pltpu.VMEM((256, 128), F32)] * (len(outs) // 7),
            compiler_params=LIMIT,
            cost_estimate=pl.CostEstimate(
                flops=flops, bytes_accessed=flops // 256, transcendentals=0
            ),
        )(place, *sets, norm, back, final_turned)

    both_front = over("row", n_row, 1, chip_front)
    own_stage = stages_of(own_kernel, (front, rear), stage_outs + [held(128, 128)] * 2, 1_000_000_000)
    chip_rear, own_stage = lax.optimization_barrier((chip_rear, own_stage))
    both_rear = over("row", n_row, 1, chip_rear)
    pair_stages = stages_of(pair_kernel, (core, chip_front, chip_rear), stage_outs * 2, 1000000)
    stages = [own_stage[:7], pair_stages]
    outs = pl.pallas_call(
        functools.partial(part_kernel, n_row, n_col),
        out_shape=(
            shape(shards, tokens, features),
            shape(width * width, 128),
            shape(width, features),
            shape(width, features),
            shape(1, features),
            shape(1, features),
            shape(1, 128),
        ),
        in_specs=[scalar] + vmem(7 * (n_row - 1) + 8),
        out_specs=(*vmem(1), hbm, *vmem(5)),
        scratch_shapes=[
            pltpu.VMEM((1024, 128), BF),
            pltpu.VMEM((1024, 128), BF),
            pltpu.VMEM((1024, 1024), BF),
            pltpu.VMEM((1024, 1024), BF),
            pltpu.VMEM((1024, 128), F32),
            pltpu.VMEM((128, 2048), BF),
            pltpu.VMEM((1024, 128), F32),
            pltpu.SemaphoreType.DMA((4,)),
            pltpu.VMEM((256, 128), F32),
            *stage_outs,
        ],
        compiler_params=LIMIT,
    )(place, both_front, both_rear, *[x for s in stages for x in s], *own_stage[7:], norm, back, final_turned, first)
    emb, final, first, second, gain, offset, bias = outs
    return emb, final, first.T, second.T, gain.reshape(-1), offset.reshape(-1), bias.reshape(-1)


def body(n_row, n_col, *arguments):
    msa, _, pair = arguments[:3]
    width = arguments[5].shape[1]
    fits = (
        n_row == 4
        and n_col == 4
        and msa.shape == (32, 8, 64)
        and pair.shape == (8, 8, 128)
        and width == 32
    )
    if fits:
        return gathered_body(n_row, n_col, *arguments)
    return sharded_body(*arguments)


def solution(mesh):
    placed = (
        P(("grp", "col"), "row", None),
        P(("grp", "col"), "row"),
        P(("grp", "row"), "col", None),
        P(),
        P(),
        P(),
        P(),
        P(),
    )
    return jax.shard_map(
        functools.partial(body, mesh.shape["row"], mesh.shape["col"]),
        mesh=mesh,
        in_specs=placed,
        out_specs=(
            P(("grp", "col"), "row", None),
            P("grp", None),
            P("grp", None),
            P("grp", None),
            P("grp"),
            P("grp"),
            P("grp"),
        ),
        check_vma=False,
    )
```

```python
import functools
from itertools import zip_longest

import jax
import jax.numpy as jnp
from jax import lax
from jax.experimental import pallas as pl
from jax.experimental.pallas import tpu as pltpu
from jax.sharding import PartitionSpec as P

TOKB = 2


def standardizer_parts(homolog_embedding, standardizer_scale, standardizer_shift):
    incoming_entries = homolog_embedding.astype(jnp.float32)
    center = jnp.mean(incoming_entries, axis=-1, keepdims=True)
    varied = incoming_entries - center
    variance = jnp.mean(varied * varied, axis=-1, keepdims=True)
    reciprocal_spread = lax.rsqrt(variance + 1e-05)
    standardized_entries = varied * reciprocal_spread
    standardized_bfloat = (standardized_entries * standardizer_scale + standardizer_shift).astype(
        jnp.bfloat16
    )
    return (standardized_entries, reciprocal_spread, standardized_bfloat)


def sharded_body(
    homolog_embedding,
    presence_indicator,
    coupling_change_derivative,
    standardizer_scale,
    standardizer_shift,
    first_projection_matrix,
    second_projection_matrix,
    final_projection_matrix,
):
    shard_homolog_number, residue_line_number, feature_number = homolog_embedding.shape
    tok_cols = coupling_change_derivative.shape[1]
    width = first_projection_matrix.shape[1]
    standardized_entries, reciprocal_spread, standardized_bfloat = standardizer_parts(
        homolog_embedding, standardizer_scale, standardizer_shift
    )
    mask_single_precision = presence_indicator.astype(jnp.float32)
    mask_half_precision = presence_indicator.astype(jnp.bfloat16)
    left = (
        jnp.einsum(
            "sic,cp->sip",
            standardized_bfloat,
            first_projection_matrix,
            preferred_element_type=jnp.float32,
        )
        * mask_single_precision[..., None]
    ).astype(jnp.bfloat16)
    right = (
        jnp.einsum(
            "sic,cp->sip",
            standardized_bfloat,
            second_projection_matrix,
            preferred_element_type=jnp.float32,
        )
        * mask_single_precision[..., None]
    ).astype(jnp.bfloat16)
    left_flat = left.reshape(shard_homolog_number, residue_line_number * width)
    right_flat = right.reshape(shard_homolog_number, residue_line_number * width)
    left_all, mask_left = (
        lax.all_gather(left_flat, "col", axis=0, tiled=True),
        lax.all_gather(mask_half_precision, "col", axis=0, tiled=True),
    )
    right_wide, mask_wide = (
        lax.all_gather(right_flat, "row", axis=1, tiled=True),
        lax.all_gather(mask_half_precision, "row", axis=1, tiled=True),
    )
    right_all, mask_right = (
        lax.all_to_all(right_wide, "col", split_axis=1, concat_axis=0, tiled=True),
        lax.all_to_all(mask_wide, "col", split_axis=1, concat_axis=0, tiled=True),
    )
    seq_total = left_all.shape[0]
    right_three = right_all.reshape(seq_total, tok_cols, width)
    counts = jnp.einsum("si,sj->ij", mask_left, mask_right, preferred_element_type=jnp.float32)
    scaled = coupling_change_derivative.astype(jnp.float32) / (counts + 0.001)[..., None]
    bias_part = jnp.sum(scaled, axis=(0, 1))
    scaled_bf = scaled.astype(jnp.bfloat16)
    block_rows = residue_line_number // TOKB
    right_acc = jnp.zeros((seq_total, tok_cols, width), jnp.float32)
    wout_acc = jnp.zeros(final_projection_matrix.shape, jnp.float32)
    left_pieces = []
    for block_index in range(TOKB):
        first = block_index * block_rows
        rows_bf = scaled_bf[first : first + block_rows]
        outer_grad = jnp.einsum(
            "ijz,fz->ijf", rows_bf, final_projection_matrix, preferred_element_type=jnp.float32
        ).astype(jnp.bfloat16)
        outer_grad = outer_grad.reshape(block_rows, tok_cols, width, width)
        left_block = left_all[:, first * width : (first + block_rows) * width].reshape(
            seq_total, block_rows, width
        )
        first_factor_derivative = jnp.einsum(
            "ijce,sje->sic", outer_grad, right_three, preferred_element_type=jnp.float32
        )
        right_acc = right_acc + jnp.einsum(
            "ijce,sic->sje", outer_grad, left_block, preferred_element_type=jnp.float32
        )
        outer = jnp.einsum(
            "sic,sje->ijce", left_block, right_three, preferred_element_type=jnp.float32
        ).astype(jnp.bfloat16)
        outer = outer.reshape(block_rows, tok_cols, width * width)
        wout_acc = wout_acc + jnp.einsum(
            "ijf,ijz->fz", outer, rows_bf, preferred_element_type=jnp.float32
        )
        first_factor_derivative = first_factor_derivative.reshape(seq_total, block_rows * width)
        left_pieces.append(first_factor_derivative)
    left_terms = jnp.concatenate(left_pieces, axis=1)
    left_own = lax.psum_scatter(left_terms, "col", scatter_dimension=0, tiled=True)
    right_spread = lax.all_to_all(
        right_acc.reshape(seq_total, tok_cols * width),
        "col",
        split_axis=0,
        concat_axis=1,
        tiled=True,
    )
    right_own = lax.psum_scatter(right_spread, "row", scatter_dimension=1, tiled=True)
    left_in = (
        left_own.reshape(shard_homolog_number, residue_line_number, width)
        * mask_single_precision[..., None]
    ).astype(jnp.bfloat16)
    right_in = (
        right_own.reshape(shard_homolog_number, residue_line_number, width)
        * mask_single_precision[..., None]
    ).astype(jnp.bfloat16)
    left_part = jnp.einsum(
        "sic,sip->cp", standardized_bfloat, left_in, preferred_element_type=jnp.float32
    )
    right_part = jnp.einsum(
        "sic,sip->cp", standardized_bfloat, right_in, preferred_element_type=jnp.float32
    )
    d_normal = jnp.einsum(
        "sip,cp->sic", left_in, first_projection_matrix, preferred_element_type=jnp.float32
    ) + jnp.einsum(
        "sip,cp->sic", right_in, second_projection_matrix, preferred_element_type=jnp.float32
    )
    gain_part = jnp.sum(d_normal * standardized_entries, axis=(0, 1))
    beta_part = jnp.sum(d_normal, axis=(0, 1))
    standardized_derivative = d_normal * standardizer_scale
    embedding_derivative = reciprocal_spread * (
        standardized_derivative
        - jnp.mean(standardized_derivative, axis=-1, keepdims=True)
        - standardized_entries
        * jnp.mean(standardized_derivative * standardized_entries, axis=-1, keepdims=True)
    )
    (
        final_matrix_derivative,
        first_matrix_derivative,
        second_matrix_derivative,
        scale_factor_derivative,
        shift_term_derivative,
        shift_derivative,
    ) = lax.psum((wout_acc, left_part, right_part, gain_part, beta_part, bias_part), ("row", "col"))
    return (
        embedding_derivative,
        final_matrix_derivative,
        first_matrix_derivative,
        second_matrix_derivative,
        scale_factor_derivative,
        shift_term_derivative,
        shift_derivative,
    )


BF = jnp.bfloat16
F32 = jnp.float32


def spread(rows, cols, rule):
    r = lax.broadcasted_iota(jnp.int32, (rows, cols), 0)
    c = lax.broadcasted_iota(jnp.int32, (rows, cols), 1)
    return rule(r, c)


def mm(a, b):
    return jnp.dot(a, b, preferred_element_type=F32)


def mm_nt(a, b):
    return lax.dot_general(a, b, (((1,), (1,)), ((), ())), preferred_element_type=F32)


def mm_tn(a, b):
    return lax.dot_general(a, b, (((0,), (0,)), ((), ())), preferred_element_type=F32)


def interleave(first, second):
    odd = lax.broadcasted_iota(jnp.int16, (32, 128), 1) & 32 != 0
    return (
        jnp.where(odd, pltpu.roll(second, 32, 1), first),
        jnp.where(odd, second, pltpu.roll(first, 96, 1)),
    )


def diagonal_pair(block):
    zero = jnp.zeros_like(block)
    return jnp.concatenate(
        [jnp.concatenate([block, zero], axis=1), jnp.concatenate([zero, block], axis=1)], axis=0
    )


ABSENT = 1024.0


def pack_kernel(msa_ref, mask_ref, pair_ref, out_ref):
    msa = msa_ref[...].astype(F32)
    pick = spread(8, 512, lambda r, c: jnp.where(c // 64 == r, 1.0, 0.0)).astype(BF)
    present = mm_tn(mask_ref[...].astype(F32).astype(BF), pick) > 0.5
    for g in range(4):
        rows = jnp.concatenate([msa[:, 2 * g, :], msa[:, 2 * g + 1, :]], axis=1)
        out_ref[32 * g : 32 * g + 32, :] = jnp.where(
            present[:, 128 * g : 128 * g + 128], rows, ABSENT
        ).astype(BF)
    out_ref[128:192, :] = pair_ref[...].astype(F32).reshape(64, 128).astype(BF)


def weights_kernel(*refs):
    sources, (norm_out, back_out, final_out, first_out) = refs[:5], refs[5:9]
    held, scr, sems = refs[9:14], refs[14], refs[15]
    copies = [pltpu.make_async_copy(sources[k], held[k], sems.at[k]) for k in range(5)]
    for copy in copies:
        copy.start()
    for copy in copies:
        copy.wait()
    gain_ref, offset_ref, first_ref, second_ref, final_ref = held
    norm_out[...] = jnp.concatenate(
        [
            jnp.concatenate([ref[...]] * 2, axis=1)
            for ref in (gain_ref, offset_ref, gain_ref, offset_ref) * 2
        ],
        axis=0,
    )
    for k, ref in enumerate((first_ref, second_ref)):
        narrow = ref[...].astype(F32)
        first_out[32 * k : 32 * k + 32, :] = narrow
        wide = jnp.concatenate([narrow] * 4, axis=1)
        wide = jnp.concatenate([wide] * 4, axis=0)
        own = spread(128, 256, lambda r, c: r // 32 == c // 64)
        back_out[128 * k : 128 * k + 128, :] = jnp.where(own, wide, 0.0).astype(BF)
    scr[...] = final_ref[...].astype(F32)
    for k in range(16):
        e = 4 * (k // 2) + k % 2
        final_out[32 * k : 32 * k + 32, :] = jnp.concatenate(
            [scr[pl.ds(e, 32, stride=32), :], scr[pl.ds(e + 2, 32, stride=32), :]], axis=1
        ).astype(BF)


def averager_of():
    return spread(128, 128, lambda r, c: jnp.where(r // 64 == c // 64, 1.0 / 64, 0.0)).astype(BF)


ORDER = (0, 2, 1, 3)


def stage_steps(
    n_col, a, place_ref, set_refs, norm_ref, back_ref, final_ref,
    rhs_out, left_out, leftt_out, rightt_out, grad_out, pair_out, found_out, *rest
):
    *own_out, turn_scr = rest
    blocks = [ref.at[k] for ref in set_refs for k in range(ref.shape[0])]

    gain = norm_ref[0:1, :]
    offset = norm_ref[1:2, :]
    averager = averager_of()
    x = jnp.concatenate(
        [blocks[b][32 * g : 32 * g + 32, :] for g in range(4) for b in range(n_col)], axis=0
    )
    mean = mm(x, averager)
    present = mean < ABSENT / 2
    here = jnp.where(present, 1.0, 0.0)
    lane = lax.broadcasted_iota(jnp.int32, (128, 128), 1)
    found = jnp.zeros((128, 128), F32)
    for g in range(4):
        found = jnp.where(lane % 32 // 2 == 4 * a + g, here[128 * g : 128 * g + 128], found)
    found_out[...] = found
    for b in range(n_col):
        at = pl.multiple_of(lax.bitwise_xor(place_ref[0], ORDER[b]) * 8, 8)
        pair_out[:, pl.ds(at, 8), :] = blocks[b][128:192, :].astype(F32).reshape(8, 8, 128)
    yield
    varied = x.astype(F32) - mean
    inverse = lax.rsqrt(mm((varied * varied).astype(BF), averager) + 1e-05)
    normed = varied * inverse
    if own_out:
        for g in range(4):
            own_out[0][32 * g : 32 * g + 32, :] = normed[128 * g : 128 * g + 32]
            own_out[1][32 * g : 32 * g + 32, :] = inverse[128 * g : 128 * g + 32]
    yield

    def grad_piece(n):
        pair = pair_out[4 * n : 4 * n + 4].reshape(128, 128).astype(BF)
        pairs = jnp.concatenate([diagonal_pair(pair[:64]), diagonal_pair(pair[64:])], axis=0)
        grad = mm_nt(final_ref[...], pairs).astype(BF)
        for p in range(2):
            for q in range(8):
                rows = 64 * (2 * n + p)
                block = grad[64 * q : 64 * q + 64, 128 * p : 128 * p + 128]
                even, odd = interleave(block[:32], block[32:])
                grad_out[rows : rows + 32, 128 * q : 128 * q + 128] = even
                grad_out[rows + 32 : rows + 64, 128 * q : 128 * q + 128] = odd

    grad_piece(0)
    yield

    normal = jnp.where(present, normed * gain + offset, 0.0).astype(BF)
    rhs_out[:, 0:128] = normal
    rhs_out[:, 128:256] = normed.astype(BF)
    for h in range(2):
        masked = jnp.concatenate(
            [normal[128 * g : 128 * g + 128] for g in (2 * h, 2 * h + 1)], axis=1
        )
        at = slice(128 * h, 128 * h + 128)
        left_out[:, at] = mm_nt(masked, back_ref[:128, :]).astype(BF)
        both = mm_nt(back_ref[...], masked)
        turn_scr[at, :] = both[128:]
        for k in range(2):
            leftt_out[64 * h + 32 * k : 64 * h + 32 * k + 32, :] = jnp.concatenate(
                [both[32 * k : 32 * k + 32], both[32 * k + 64 : 32 * k + 96]], axis=1
            ).astype(BF)
    yield
    grad_piece(1)
    yield
    for e in range(32):
        rightt_out[e] = turn_scr[pl.ds(e, 8, stride=32), :]


def stage_kernel(*arguments):
    for _ in stage_steps(*arguments):
        pass


def own_kernel(n_col, place_ref, front_ref, rear_ref, norm_ref, back_ref, final_ref, *rest):
    stage_kernel(n_col, 0, place_ref, (front_ref, rear_ref), norm_ref, back_ref, final_ref, *rest)


def pair_kernel(n_col, place_ref, core_ref, front_ref, rear_ref, norm_ref, back_ref, final_ref, *rest):
    common = (norm_ref, back_ref, final_ref)
    both = (
        stage_steps(n_col, 1, place_ref, (core_ref,), *common, *rest[:7], rest[14]),
        stage_steps(n_col, 2, place_ref, (front_ref, rear_ref), *common, *rest[7:14], rest[15]),
    )
    for _ in zip_longest(*both):
        pass


def part_kernel(n_row, n_col, place_ref, front_ref, rear_ref, *refs):
    stages = [refs[7 * a : 7 * a + 7] for a in range(n_row - 1)]
    (
        normed_ref, inverse_ref, norm_ref, back_ref, final_ref, first_ref,
        emb_out, final_hbm_out, first_out, second_out, gain_out, offset_out, bias_out,
        right_scr, scaled_scr, grad_scr, outer_scr, wide_scr, all_scr,
        final_out, out_sem, turn_scr,
    ) = refs[7 * (n_row - 1) : -7]
    stages.append(refs[-7:])
    last = stage_steps(
        n_col, n_row - 1, place_ref, (front_ref, rear_ref),
        norm_ref, back_ref, final_ref, *stages[-1], turn_scr,
    )
    next(last)
    gain = norm_ref[0:1, :]
    averager = averager_of()
    lane = lax.broadcasted_iota(jnp.int32, (128, 128), 1)

    found = sum(stage[6][...] for stage in stages)
    turned = pltpu.roll(found, 64, 1)
    mask = jnp.where((lane % 2 == 0) == (lane < 64), found, turned)
    mask_t = mask.T
    mask_bf = mask.astype(BF)
    share = (1.0 / (mm_tn(mask_bf, mask_bf)[0:32] + 0.001)).astype(BF)

    def scale(a):
        for i in range(8 * a, 8 * a + 8):
            at = 32 * (i % 8)
            for q in range(8):
                grad_scr[32 * i : 32 * i + 32, 128 * q : 128 * q + 128] = (
                    stages[a][4][at : at + 32, 128 * q : 128 * q + 128] * share[i : i + 1]
                )

    ones = jnp.ones((128, 128), BF)

    def scaled_piece(p):
        both_on = jnp.concatenate(
            [mask_t[0:32] * mask_t[i : i + 1] for i in range(4 * p, 4 * p + 4)], axis=0
        ).astype(BF)
        counts = mm(both_on, ones)
        pair = stages[p // 2][5][4 * (p % 2) : 4 * (p % 2) + 4]
        scaled = pair.reshape(128, 128) / (counts + 0.001)
        scaled_scr[128 * p : 128 * p + 128, :] = scaled.astype(BF)
        return jnp.sum(scaled, axis=0, keepdims=True)

    next(last)
    bias = scaled_piece(0)
    scale(0)
    next(last)
    bias = bias + scaled_piece(1)
    scale(1)
    next(last)
    bias = bias + scaled_piece(2)
    scale(2)
    next(last)
    bias = bias + scaled_piece(3)
    for _ in last:
        pass
    scale(3)

    for e in range(32):
        right_scr[32 * e : 32 * e + 32, :] = jnp.concatenate(
            [stage[3][e] for stage in stages], axis=0
        ).astype(BF)

    left = jnp.concatenate([stage[1][...] for stage in stages], axis=1)
    right_grad = mm(left, grad_scr[...])
    bias = bias + scaled_piece(4) + scaled_piece(5)
    left_grad = mm(grad_scr[...], right_scr[...])
    bias = bias + scaled_piece(6) + scaled_piece(7)
    bias_out[...] = bias

    def finish():
        turn = spread(
            256, 256, lambda r, c: jnp.where((r // 8 == c % 32) & (r % 8 == c // 32), 1.0, 0.0)
        ).astype(BF)
        mask_two = jnp.concatenate([mask, mask], axis=1)
        right_in = []
        for q in range(4):
            right_in.append(
                mm_nt(turn, (right_grad[:, 256 * q : 256 * q + 256] * mask_two).astype(BF))
            )
            if q % 2:
                yield
        for t in range(32):
            at = slice(128 * (t // 2), 128 * (t // 2) + 128)
            row = 32 * (t % 2)
            all_scr[row : row + 32, at] = (
                left_grad[32 * t : 32 * t + 32] * mask_t[t : t + 1]
            ).astype(BF)
            all_scr[row + 64 : row + 96, at] = jnp.concatenate(
                [part[8 * t : 8 * t + 8] for part in right_in], axis=0
            ).astype(BF)
            if t % 16 == 15:
                yield

        d_hat = []
        for h in range(2):
            sides = [
                jnp.concatenate(
                    [all_scr[row : row + 64, 128 * g : 128 * g + 128] for g in (2 * h, 2 * h + 1)],
                    axis=0,
                )
                for row in (0, 64)
            ]
            d_normal = mm_tn(jnp.concatenate(sides, axis=0), back_ref[...])
            d_hat += [d_normal[0:32, 0:128] * gain, d_normal[0:32, 128:256] * gain]
        d_hat = jnp.concatenate(d_hat, axis=0)
        yield
        normed = normed_ref[...]
        means = mm(jnp.concatenate([d_hat, d_hat * normed], axis=0).astype(BF), averager)
        yield
        result = inverse_ref[...] * (d_hat - means[:128] - normed * means[128:])
        for g in range(4):
            emb_out[:, 2 * g, :] = result[32 * g : 32 * g + 32, 0:64]
            emb_out[:, 2 * g + 1, :] = result[32 * g : 32 * g + 32, 64:128]

    finishing = finish()
    left_t = jnp.concatenate([stage[2][...] for stage in stages], axis=0)
    for n in range(8):
        rights = jnp.concatenate(
            [diagonal_pair(right_scr[64 * p : 64 * p + 64, :]) for p in (2 * n, 2 * n + 1)], axis=0
        )
        outer = mm_nt(left_t, rights).astype(BF)
        next(finishing, None)
        for p in range(2):
            for q in range(8):
                rows = 64 * (2 * n + p)
                block = outer[64 * q : 64 * q + 64, 128 * p : 128 * p + 128]
                even, odd = interleave(block[:32], block[32:])
                outer_scr[rows : rows + 32, 128 * q : 128 * q + 128] = even
                outer_scr[rows + 32 : rows + 64, 128 * q : 128 * q + 128] = odd
    for _ in finishing:
        pass
    wide_scr[...] = mm(outer_scr[...], scaled_scr[...])
    for c in range(32):
        final_out[32 * c : 32 * c + 32, :] = wide_scr[pl.ds(c, 32, stride=32), :]
    final_send = pltpu.make_async_copy(final_out, final_hbm_out, out_sem)
    final_send.start()

    total = mm(
        all_scr[...], jnp.concatenate([stage[0][...] for stage in stages], axis=0)
    )
    sums = all_scr[:, 0:128].astype(F32)
    for g in range(1, 16):
        sums = sums + all_scr[:, 128 * g : 128 * g + 128].astype(F32)

    def fold(block):
        return block[0:32, 0:64] + block[32:64, 64:128]

    first_out[...] = fold(total[0:64, 0:128])
    second_out[...] = fold(total[64:128, 0:128])
    sums = jnp.sum(sums, axis=1, keepdims=True)
    left_sum = sums[0:32] + sums[32:64]
    right_sum = sums[64:96] + sums[96:128]
    first, second = first_ref[0:32, :], first_ref[32:64, :]
    gain_out[...] = jnp.sum(
        first * fold(total[0:64, 128:256]) + second * fold(total[64:128, 128:256]),
        axis=0, keepdims=True,
    )
    offset_out[...] = jnp.sum(first * left_sum + second * right_sum, axis=0, keepdims=True)

    final_send.wait()


def vmem(count):
    return [pl.BlockSpec(memory_space=pltpu.VMEM)] * count


LIMIT = pltpu.CompilerParams(vmem_limit_bytes=32 * 1024 * 1024)


def gathered_body(
    n_row,
    n_col,
    homolog_embedding,
    presence_indicator,
    coupling_change_derivative,
    standardizer_scale,
    standardizer_shift,
    first_projection_matrix,
    second_projection_matrix,
    final_projection_matrix,
):
    shards, tokens, features = homolog_embedding.shape
    width = first_projection_matrix.shape[1]
    first_t, second_t = first_projection_matrix.T, second_projection_matrix.T
    shape = lambda *dims: jax.ShapeDtypeStruct(dims, F32)
    held = lambda *dims: pltpu.VMEM(dims, F32)
    held_bf = lambda *dims: pltpu.VMEM(dims, BF)
    hbm = pl.BlockSpec(memory_space=pltpu.HBM)
    place = lax.bitwise_xor(lax.axis_index("row"), lax.axis_index("col"))
    place = place.astype(jnp.int32).reshape(1)
    packed = pl.pallas_call(
        pack_kernel,
        out_shape=held_bf(192, 128),
        in_specs=vmem(3),
        out_specs=vmem(1)[0],
    )(homolog_embedding, presence_indicator.T, coupling_change_derivative)
    def over(axis, size, step, array):
        return lax.ppermute(array, axis, [(k, k ^ step) for k in range(size)])

    far = over("col", n_col, 2, packed)
    near = over("col", n_col, 1, packed)
    last = over("col", n_col, 3, packed)
    front = jnp.stack([packed, far])
    chip_front = over("row", n_row, 2, front)
    rear = jnp.stack([near, last])
    chip_rear = over("row", n_row, 2, rear)
    front, final_projection_matrix = lax.optimization_barrier((front, final_projection_matrix))
    weights = pl.pallas_call(
        weights_kernel,
        out_shape=(
            held(8, 128), held_bf(256, 256), held_bf(width * width // 2, 256), held(2 * width, features),
        ),
        in_specs=[hbm] * 5,
        out_specs=tuple(vmem(4)),
        scratch_shapes=[
            pltpu.VMEM((1, features), F32),
            pltpu.VMEM((1, features), F32),
            pltpu.VMEM((width, features), BF),
            pltpu.VMEM((width, features), BF),
            pltpu.VMEM((width * width, 128), BF),
            pltpu.VMEM((width * width, 128), F32),
            pltpu.SemaphoreType.DMA((5,)),
        ],
        compiler_params=LIMIT,
    )(
        *[
            pltpu.with_memory_space_constraint(x, pltpu.HBM)
            for x in (
                standardizer_scale.reshape(1, features),
                standardizer_shift.reshape(1, features),
                first_t,
                second_t,
                final_projection_matrix,
            )
        ]
    )
    norm, back, final_turned, first = weights
    own = jnp.concatenate([front, rear])
    own, chip_front, norm = lax.optimization_barrier((own, chip_front, norm))
    core = over("row", n_row, 1, own)
    stage_outs = [
        held_bf(512, 256), held_bf(128, 256), held_bf(128, 256), held(width, 8, 128),
        held_bf(256, 1024), held(8, 32, 128), held(128, 128),
    ]
    scalar = pl.BlockSpec(memory_space=pltpu.SMEM)

    def stages_of(kernel, sets, outs, flops):
        return pl.pallas_call(
            functools.partial(kernel, n_col),
            out_shape=tuple(outs),
            in_specs=[scalar] + vmem(len(sets) + 3),
            out_specs=tuple(vmem(len(outs))),
            scratch_shapes=[pltpu.VMEM((256, 128), F32)] * (len(outs) // 7),
            compiler_params=LIMIT,
            cost_estimate=pl.CostEstimate(
                flops=flops, bytes_accessed=flops // 256, transcendentals=0
            ),
        )(place, *sets, norm, back, final_turned)

    both_front = over("row", n_row, 1, chip_front)
    own_stage = stages_of(own_kernel, (front, rear), stage_outs + [held(128, 128)] * 2, 1_000_000_000)
    chip_rear, own_stage = lax.optimization_barrier((chip_rear, own_stage))
    both_rear = over("row", n_row, 1, chip_rear)
    pair_stages = stages_of(pair_kernel, (core, chip_front, chip_rear), stage_outs * 2, 1000000)
    stages = [own_stage[:7], pair_stages]
    outs = pl.pallas_call(
        functools.partial(part_kernel, n_row, n_col),
        out_shape=(
            shape(shards, tokens, features),
            shape(width * width, 128),
            shape(width, features),
            shape(width, features),
            shape(1, features),
            shape(1, features),
            shape(1, 128),
        ),
        in_specs=[scalar] + vmem(7 * (n_row - 1) + 8),
        out_specs=(*vmem(1), hbm, *vmem(5)),
        scratch_shapes=[
            pltpu.VMEM((1024, 128), BF),
            pltpu.VMEM((1024, 128), BF),
            pltpu.VMEM((1024, 1024), BF),
            pltpu.VMEM((1024, 1024), BF),
            pltpu.VMEM((1024, 128), F32),
            pltpu.VMEM((128, 2048), BF),
            pltpu.VMEM((1024, 128), F32),
            pltpu.SemaphoreType.DMA,
            pltpu.VMEM((256, 128), F32),
            *stage_outs,
        ],
        compiler_params=LIMIT,
    )(place, both_front, both_rear, *[x for s in stages for x in s], *own_stage[7:], norm, back, final_turned, first)
    emb, final, first, second, gain, offset, bias = outs
    return emb, final, first.T, second.T, gain.reshape(-1), offset.reshape(-1), bias.reshape(-1)


def body(n_row, n_col, *arguments):
    msa, _, pair = arguments[:3]
    width = arguments[5].shape[1]
    fits = (
        n_row == 4
        and n_col == 4
        and msa.shape == (32, 8, 64)
        and pair.shape == (8, 8, 128)
        and width == 32
    )
    if fits:
        return gathered_body(n_row, n_col, *arguments)
    return sharded_body(*arguments)


def solution(mesh):
    placed = (
        P(("grp", "col"), "row", None),
        P(("grp", "col"), "row"),
        P(("grp", "row"), "col", None),
        P(),
        P(),
        P(),
        P(),
        P(),
    )
    return jax.shard_map(
        functools.partial(body, mesh.shape["row"], mesh.shape["col"]),
        mesh=mesh,
        in_specs=placed,
        out_specs=(
            P(("grp", "col"), "row", None),
            P("grp", None),
            P("grp", None),
            P("grp", None),
            P("grp"),
            P("grp"),
            P("grp"),
        ),
        check_vma=False,
    )
```

```python
import functools
from itertools import zip_longest

import jax
import jax.numpy as jnp
from jax import lax
from jax.experimental import pallas as pl
from jax.experimental.pallas import tpu as pltpu
from jax.sharding import PartitionSpec as P

TOKB = 2


def standardizer_parts(homolog_embedding, standardizer_scale, standardizer_shift):
    incoming_entries = homolog_embedding.astype(jnp.float32)
    center = jnp.mean(incoming_entries, axis=-1, keepdims=True)
    varied = incoming_entries - center
    variance = jnp.mean(varied * varied, axis=-1, keepdims=True)
    reciprocal_spread = lax.rsqrt(variance + 1e-05)
    standardized_entries = varied * reciprocal_spread
    standardized_bfloat = (standardized_entries * standardizer_scale + standardizer_shift).astype(
        jnp.bfloat16
    )
    return (standardized_entries, reciprocal_spread, standardized_bfloat)


def sharded_body(
    homolog_embedding,
    presence_indicator,
    coupling_change_derivative,
    standardizer_scale,
    standardizer_shift,
    first_projection_matrix,
    second_projection_matrix,
    final_projection_matrix,
):
    shard_homolog_number, residue_line_number, feature_number = homolog_embedding.shape
    tok_cols = coupling_change_derivative.shape[1]
    width = first_projection_matrix.shape[1]
    standardized_entries, reciprocal_spread, standardized_bfloat = standardizer_parts(
        homolog_embedding, standardizer_scale, standardizer_shift
    )
    mask_single_precision = presence_indicator.astype(jnp.float32)
    mask_half_precision = presence_indicator.astype(jnp.bfloat16)
    left = (
        jnp.einsum(
            "sic,cp->sip",
            standardized_bfloat,
            first_projection_matrix,
            preferred_element_type=jnp.float32,
        )
        * mask_single_precision[..., None]
    ).astype(jnp.bfloat16)
    right = (
        jnp.einsum(
            "sic,cp->sip",
            standardized_bfloat,
            second_projection_matrix,
            preferred_element_type=jnp.float32,
        )
        * mask_single_precision[..., None]
    ).astype(jnp.bfloat16)
    left_flat = left.reshape(shard_homolog_number, residue_line_number * width)
    right_flat = right.reshape(shard_homolog_number, residue_line_number * width)
    left_all, mask_left = (
        lax.all_gather(left_flat, "col", axis=0, tiled=True),
        lax.all_gather(mask_half_precision, "col", axis=0, tiled=True),
    )
    right_wide, mask_wide = (
        lax.all_gather(right_flat, "row", axis=1, tiled=True),
        lax.all_gather(mask_half_precision, "row", axis=1, tiled=True),
    )
    right_all, mask_right = (
        lax.all_to_all(right_wide, "col", split_axis=1, concat_axis=0, tiled=True),
        lax.all_to_all(mask_wide, "col", split_axis=1, concat_axis=0, tiled=True),
    )
    seq_total = left_all.shape[0]
    right_three = right_all.reshape(seq_total, tok_cols, width)
    counts = jnp.einsum("si,sj->ij", mask_left, mask_right, preferred_element_type=jnp.float32)
    scaled = coupling_change_derivative.astype(jnp.float32) / (counts + 0.001)[..., None]
    bias_part = jnp.sum(scaled, axis=(0, 1))
    scaled_bf = scaled.astype(jnp.bfloat16)
    block_rows = residue_line_number // TOKB
    right_acc = jnp.zeros((seq_total, tok_cols, width), jnp.float32)
    wout_acc = jnp.zeros(final_projection_matrix.shape, jnp.float32)
    left_pieces = []
    for block_index in range(TOKB):
        first = block_index * block_rows
        rows_bf = scaled_bf[first : first + block_rows]
        outer_grad = jnp.einsum(
            "ijz,fz->ijf", rows_bf, final_projection_matrix, preferred_element_type=jnp.float32
        ).astype(jnp.bfloat16)
        outer_grad = outer_grad.reshape(block_rows, tok_cols, width, width)
        left_block = left_all[:, first * width : (first + block_rows) * width].reshape(
            seq_total, block_rows, width
        )
        first_factor_derivative = jnp.einsum(
            "ijce,sje->sic", outer_grad, right_three, preferred_element_type=jnp.float32
        )
        right_acc = right_acc + jnp.einsum(
            "ijce,sic->sje", outer_grad, left_block, preferred_element_type=jnp.float32
        )
        outer = jnp.einsum(
            "sic,sje->ijce", left_block, right_three, preferred_element_type=jnp.float32
        ).astype(jnp.bfloat16)
        outer = outer.reshape(block_rows, tok_cols, width * width)
        wout_acc = wout_acc + jnp.einsum(
            "ijf,ijz->fz", outer, rows_bf, preferred_element_type=jnp.float32
        )
        first_factor_derivative = first_factor_derivative.reshape(seq_total, block_rows * width)
        left_pieces.append(first_factor_derivative)
    left_terms = jnp.concatenate(left_pieces, axis=1)
    left_own = lax.psum_scatter(left_terms, "col", scatter_dimension=0, tiled=True)
    right_spread = lax.all_to_all(
        right_acc.reshape(seq_total, tok_cols * width),
        "col",
        split_axis=0,
        concat_axis=1,
        tiled=True,
    )
    right_own = lax.psum_scatter(right_spread, "row", scatter_dimension=1, tiled=True)
    left_in = (
        left_own.reshape(shard_homolog_number, residue_line_number, width)
        * mask_single_precision[..., None]
    ).astype(jnp.bfloat16)
    right_in = (
        right_own.reshape(shard_homolog_number, residue_line_number, width)
        * mask_single_precision[..., None]
    ).astype(jnp.bfloat16)
    left_part = jnp.einsum(
        "sic,sip->cp", standardized_bfloat, left_in, preferred_element_type=jnp.float32
    )
    right_part = jnp.einsum(
        "sic,sip->cp", standardized_bfloat, right_in, preferred_element_type=jnp.float32
    )
    d_normal = jnp.einsum(
        "sip,cp->sic", left_in, first_projection_matrix, preferred_element_type=jnp.float32
    ) + jnp.einsum(
        "sip,cp->sic", right_in, second_projection_matrix, preferred_element_type=jnp.float32
    )
    gain_part = jnp.sum(d_normal * standardized_entries, axis=(0, 1))
    beta_part = jnp.sum(d_normal, axis=(0, 1))
    standardized_derivative = d_normal * standardizer_scale
    embedding_derivative = reciprocal_spread * (
        standardized_derivative
        - jnp.mean(standardized_derivative, axis=-1, keepdims=True)
        - standardized_entries
        * jnp.mean(standardized_derivative * standardized_entries, axis=-1, keepdims=True)
    )
    (
        final_matrix_derivative,
        first_matrix_derivative,
        second_matrix_derivative,
        scale_factor_derivative,
        shift_term_derivative,
        shift_derivative,
    ) = lax.psum((wout_acc, left_part, right_part, gain_part, beta_part, bias_part), ("row", "col"))
    return (
        embedding_derivative,
        final_matrix_derivative,
        first_matrix_derivative,
        second_matrix_derivative,
        scale_factor_derivative,
        shift_term_derivative,
        shift_derivative,
    )


BF = jnp.bfloat16
F32 = jnp.float32


def spread(rows, cols, rule):
    r = lax.broadcasted_iota(jnp.int32, (rows, cols), 0)
    c = lax.broadcasted_iota(jnp.int32, (rows, cols), 1)
    return rule(r, c)


def mm(a, b):
    return jnp.dot(a, b, preferred_element_type=F32)


def mm_nt(a, b):
    return lax.dot_general(a, b, (((1,), (1,)), ((), ())), preferred_element_type=F32)


def mm_tn(a, b):
    return lax.dot_general(a, b, (((0,), (0,)), ((), ())), preferred_element_type=F32)


def interleave(first, second):
    odd = lax.broadcasted_iota(jnp.int16, (32, 128), 1) & 32 != 0
    return (
        jnp.where(odd, pltpu.roll(second, 32, 1), first),
        jnp.where(odd, second, pltpu.roll(first, 96, 1)),
    )


def diagonal_pair(block):
    zero = jnp.zeros_like(block)
    return jnp.concatenate(
        [jnp.concatenate([block, zero], axis=1), jnp.concatenate([zero, block], axis=1)], axis=0
    )


ABSENT = 1024.0


def pack_kernel(msa_ref, mask_ref, pair_ref, out_ref):
    msa = msa_ref[...].astype(F32)
    pick = spread(8, 512, lambda r, c: jnp.where(c // 64 == r, 1.0, 0.0)).astype(BF)
    present = mm_tn(mask_ref[...].astype(F32).astype(BF), pick) > 0.5
    for g in range(4):
        rows = jnp.concatenate([msa[:, 2 * g, :], msa[:, 2 * g + 1, :]], axis=1)
        out_ref[32 * g : 32 * g + 32, :] = jnp.where(
            present[:, 128 * g : 128 * g + 128], rows, ABSENT
        ).astype(BF)
    out_ref[128:192, :] = pair_ref[...].astype(F32).reshape(64, 128).astype(BF)


def weights_kernel(*refs):
    sources, (norm_out, back_out, final_out, first_out) = refs[:5], refs[5:9]
    held, scr, sems = refs[9:14], refs[14], refs[15]
    copies = [pltpu.make_async_copy(sources[k], held[k], sems.at[k]) for k in range(5)]
    for copy in copies:
        copy.start()
    for copy in copies:
        copy.wait()
    gain_ref, offset_ref, first_ref, second_ref, final_ref = held
    norm_out[...] = jnp.concatenate(
        [
            jnp.concatenate([ref[...]] * 2, axis=1)
            for ref in (gain_ref, offset_ref, gain_ref, offset_ref) * 2
        ],
        axis=0,
    )
    for k, ref in enumerate((first_ref, second_ref)):
        narrow = ref[...].astype(F32)
        first_out[32 * k : 32 * k + 32, :] = narrow
        wide = jnp.concatenate([narrow] * 4, axis=1)
        wide = jnp.concatenate([wide] * 4, axis=0)
        own = spread(128, 256, lambda r, c: r // 32 == c // 64)
        back_out[128 * k : 128 * k + 128, :] = jnp.where(own, wide, 0.0).astype(BF)
    scr[...] = final_ref[...].astype(F32)
    for k in range(16):
        e = 4 * (k // 2) + k % 2
        final_out[32 * k : 32 * k + 32, :] = jnp.concatenate(
            [scr[pl.ds(e, 32, stride=32), :], scr[pl.ds(e + 2, 32, stride=32), :]], axis=1
        ).astype(BF)


def averager_of():
    return spread(128, 128, lambda r, c: jnp.where(r // 64 == c // 64, 1.0 / 64, 0.0)).astype(BF)


ORDER = (0, 2, 1, 3)


def stage_steps(
    n_col, a, place_ref, set_refs, norm_ref, back_ref, final_ref,
    rhs_out, left_out, leftt_out, rightt_out, grad_out, pair_out, found_out, *rest
):
    *own_out, turn_scr = rest
    blocks = [ref.at[k] for ref in set_refs for k in range(ref.shape[0])]

    gain = norm_ref[0:1, :]
    offset = norm_ref[1:2, :]
    averager = averager_of()
    x = jnp.concatenate(
        [blocks[b][32 * g : 32 * g + 32, :] for g in range(4) for b in range(n_col)], axis=0
    )
    mean = mm(x, averager)
    present = mean < ABSENT / 2
    here = jnp.where(present, 1.0, 0.0)
    lane = lax.broadcasted_iota(jnp.int32, (128, 128), 1)
    found = jnp.zeros((128, 128), F32)
    for g in range(4):
        found = jnp.where(lane % 32 // 2 == 4 * a + g, here[128 * g : 128 * g + 128], found)
    found_out[...] = found
    for b in range(n_col):
        at = pl.multiple_of(lax.bitwise_xor(place_ref[0], ORDER[b]) * 8, 8)
        pair_out[:, pl.ds(at, 8), :] = blocks[b][128:192, :].astype(F32).reshape(8, 8, 128)
    yield
    varied = x.astype(F32) - mean
    inverse = lax.rsqrt(mm((varied * varied).astype(BF), averager) + 1e-05)
    normed = varied * inverse
    if own_out:
        for g in range(4):
            own_out[0][32 * g : 32 * g + 32, :] = normed[128 * g : 128 * g + 32]
            own_out[1][32 * g : 32 * g + 32, :] = inverse[128 * g : 128 * g + 32]
    yield

    def grad_piece(n):
        pair = pair_out[4 * n : 4 * n + 4].reshape(128, 128).astype(BF)
        pairs = jnp.concatenate([diagonal_pair(pair[:64]), diagonal_pair(pair[64:])], axis=0)
        grad = mm_nt(final_ref[...], pairs).astype(BF)
        for p in range(2):
            for q in range(8):
                rows = 64 * (2 * n + p)
                block = grad[64 * q : 64 * q + 64, 128 * p : 128 * p + 128]
                even, odd = interleave(block[:32], block[32:])
                grad_out[rows : rows + 32, 128 * q : 128 * q + 128] = even
                grad_out[rows + 32 : rows + 64, 128 * q : 128 * q + 128] = odd

    grad_piece(0)
    yield

    normal = jnp.where(present, normed * gain + offset, 0.0).astype(BF)
    rhs_out[:, 0:128] = normal
    rhs_out[:, 128:256] = normed.astype(BF)
    for h in range(2):
        masked = jnp.concatenate(
            [normal[128 * g : 128 * g + 128] for g in (2 * h, 2 * h + 1)], axis=1
        )
        at = slice(128 * h, 128 * h + 128)
        left_out[:, at] = mm_nt(masked, back_ref[:128, :]).astype(BF)
        both = mm_nt(back_ref[...], masked)
        turn_scr[at, :] = both[128:]
        for k in range(2):
            leftt_out[64 * h + 32 * k : 64 * h + 32 * k + 32, :] = jnp.concatenate(
                [both[32 * k : 32 * k + 32], both[32 * k + 64 : 32 * k + 96]], axis=1
            ).astype(BF)
    yield
    grad_piece(1)
    yield
    for e in range(32):
        rightt_out[e] = turn_scr[pl.ds(e, 8, stride=32), :]


def stage_kernel(*arguments):
    for _ in stage_steps(*arguments):
        pass


def own_kernel(n_col, place_ref, front_ref, rear_ref, norm_ref, back_ref, final_ref, *rest):
    stage_kernel(n_col, 0, place_ref, (front_ref, rear_ref), norm_ref, back_ref, final_ref, *rest)


def pair_kernel(n_col, place_ref, core_ref, front_ref, rear_ref, norm_ref, back_ref, final_ref, *rest):
    common = (norm_ref, back_ref, final_ref)
    both = (
        stage_steps(n_col, 1, place_ref, (core_ref,), *common, *rest[:7], rest[14]),
        stage_steps(n_col, 2, place_ref, (front_ref, rear_ref), *common, *rest[7:14], rest[15]),
    )
    for _ in zip_longest(*both):
        pass


def part_kernel(n_row, n_col, place_ref, front_ref, rear_ref, *refs):
    stages = [refs[7 * a : 7 * a + 7] for a in range(n_row - 1)]
    (
        normed_ref, inverse_ref, norm_ref, back_ref, final_ref, first_ref,
        emb_out, final_hbm_out, first_out, second_out, gain_out, offset_out, bias_out,
        right_scr, scaled_scr, grad_scr, outer_scr, wide_scr, all_scr,
        final_out, out_sem, turn_scr,
    ) = refs[7 * (n_row - 1) : -7]
    stages.append(refs[-7:])
    last = stage_steps(
        n_col, n_row - 1, place_ref, (front_ref, rear_ref),
        norm_ref, back_ref, final_ref, *stages[-1], turn_scr,
    )
    next(last)
    gain = norm_ref[0:1, :]
    averager = averager_of()
    lane = lax.broadcasted_iota(jnp.int32, (128, 128), 1)

    found = sum(stage[6][...] for stage in stages)
    turned = pltpu.roll(found, 64, 1)
    mask = jnp.where((lane % 2 == 0) == (lane < 64), found, turned)
    mask_t = mask.T

    mask_bf = mask.astype(BF)
    share = (1.0 / (mm_tn(mask_bf, mask_bf)[0:32] + 0.001)).astype(BF)
    for a in range(n_row):
        if a < n_row - 1:
            next(last)
        else:
            for _ in last:
                pass
        for i in range(8 * a, 8 * a + 8):
            at = 32 * (i % 8)
            for q in range(8):
                grad_scr[32 * i : 32 * i + 32, 128 * q : 128 * q + 128] = (
                    stages[a][4][at : at + 32, 128 * q : 128 * q + 128] * share[i : i + 1]
                )

    for e in range(32):
        right_scr[32 * e : 32 * e + 32, :] = jnp.concatenate(
            [stage[3][e] for stage in stages], axis=0
        ).astype(BF)

    left = jnp.concatenate([stage[1][...] for stage in stages], axis=1)
    right_grad = mm(left, grad_scr[...])
    left_grad = mm(grad_scr[...], right_scr[...])

    turn = spread(
        256, 256, lambda r, c: jnp.where((r // 8 == c % 32) & (r % 8 == c // 32), 1.0, 0.0)
    ).astype(BF)
    mask_two = jnp.concatenate([mask, mask], axis=1)
    right_in = [
        mm_nt(turn, (right_grad[:, 256 * q : 256 * q + 256] * mask_two).astype(BF))
        for q in range(4)
    ]
    for t in range(32):
        at = slice(128 * (t // 2), 128 * (t // 2) + 128)
        row = 32 * (t % 2)
        all_scr[row : row + 32, at] = (
            left_grad[32 * t : 32 * t + 32] * mask_t[t : t + 1]
        ).astype(BF)
        all_scr[row + 64 : row + 96, at] = jnp.concatenate(
            [part[8 * t : 8 * t + 8] for part in right_in], axis=0
        ).astype(BF)

    bias = jnp.zeros((1, 128), F32)
    ones = jnp.ones((128, 128), BF)
    for p in range(8):
        both_on = jnp.concatenate(
            [mask_t[0:32] * mask_t[i : i + 1] for i in range(4 * p, 4 * p + 4)], axis=0
        ).astype(BF)
        counts = mm(both_on, ones)
        pair = stages[p // 2][5][4 * (p % 2) : 4 * (p % 2) + 4]
        scaled = pair.reshape(128, 128) / (counts + 0.001)
        bias = bias + jnp.sum(scaled, axis=0, keepdims=True)
        scaled_scr[128 * p : 128 * p + 128, :] = scaled.astype(BF)
    bias_out[...] = bias

    left_t = jnp.concatenate([stage[2][...] for stage in stages], axis=0)
    for n in range(8):
        rights = jnp.concatenate(
            [diagonal_pair(right_scr[64 * p : 64 * p + 64, :]) for p in (2 * n, 2 * n + 1)], axis=0
        )
        outer = mm_nt(left_t, rights).astype(BF)
        for p in range(2):
            for q in range(8):
                rows = 64 * (2 * n + p)
                block = outer[64 * q : 64 * q + 64, 128 * p : 128 * p + 128]
                even, odd = interleave(block[:32], block[32:])
                outer_scr[rows : rows + 32, 128 * q : 128 * q + 128] = even
                outer_scr[rows + 32 : rows + 64, 128 * q : 128 * q + 128] = odd
    wide_scr[...] = mm(outer_scr[...], scaled_scr[...])
    for c in range(32):
        final_out[32 * c : 32 * c + 32, :] = wide_scr[pl.ds(c, 32, stride=32), :]
    final_send = pltpu.make_async_copy(final_out, final_hbm_out, out_sem)
    final_send.start()

    total = mm(
        all_scr[...], jnp.concatenate([stage[0][...] for stage in stages], axis=0)
    )
    sums = all_scr[:, 0:128].astype(F32)
    for g in range(1, 16):
        sums = sums + all_scr[:, 128 * g : 128 * g + 128].astype(F32)

    def fold(block):
        return block[0:32, 0:64] + block[32:64, 64:128]

    first_out[...] = fold(total[0:64, 0:128])
    second_out[...] = fold(total[64:128, 0:128])
    sums = jnp.sum(sums, axis=1, keepdims=True)
    left_sum = sums[0:32] + sums[32:64]
    right_sum = sums[64:96] + sums[96:128]
    first, second = first_ref[0:32, :], first_ref[32:64, :]
    gain_out[...] = jnp.sum(
        first * fold(total[0:64, 128:256]) + second * fold(total[64:128, 128:256]),
        axis=0, keepdims=True,
    )
    offset_out[...] = jnp.sum(first * left_sum + second * right_sum, axis=0, keepdims=True)

    d_hat = []
    for h in range(2):
        sides = [
            jnp.concatenate(
                [all_scr[row : row + 64, 128 * g : 128 * g + 128] for g in (2 * h, 2 * h + 1)], axis=0
            )
            for row in (0, 64)
        ]
        d_normal = mm_tn(jnp.concatenate(sides, axis=0), back_ref[...])
        d_hat += [d_normal[0:32, 0:128] * gain, d_normal[0:32, 128:256] * gain]
    d_hat = jnp.concatenate(d_hat, axis=0)
    normed = normed_ref[...]
    means = mm(jnp.concatenate([d_hat, d_hat * normed], axis=0).astype(BF), averager)
    result = inverse_ref[...] * (d_hat - means[:128] - normed * means[128:])
    for g in range(4):
        emb_out[:, 2 * g, :] = result[32 * g : 32 * g + 32, 0:64]
        emb_out[:, 2 * g + 1, :] = result[32 * g : 32 * g + 32, 64:128]
    final_send.wait()


def vmem(count):
    return [pl.BlockSpec(memory_space=pltpu.VMEM)] * count


LIMIT = pltpu.CompilerParams(vmem_limit_bytes=32 * 1024 * 1024)


def gathered_body(
    n_row,
    n_col,
    homolog_embedding,
    presence_indicator,
    coupling_change_derivative,
    standardizer_scale,
    standardizer_shift,
    first_projection_matrix,
    second_projection_matrix,
    final_projection_matrix,
):
    shards, tokens, features = homolog_embedding.shape
    width = first_projection_matrix.shape[1]
    first_t, second_t = first_projection_matrix.T, second_projection_matrix.T
    shape = lambda *dims: jax.ShapeDtypeStruct(dims, F32)
    held = lambda *dims: pltpu.VMEM(dims, F32)
    held_bf = lambda *dims: pltpu.VMEM(dims, BF)
    hbm = pl.BlockSpec(memory_space=pltpu.HBM)
    place = lax.bitwise_xor(lax.axis_index("row"), lax.axis_index("col"))
    place = place.astype(jnp.int32).reshape(1)
    packed = pl.pallas_call(
        pack_kernel,
        out_shape=held_bf(192, 128),
        in_specs=vmem(3),
        out_specs=vmem(1)[0],
    )(homolog_embedding, presence_indicator.T, coupling_change_derivative)
    def over(axis, size, step, array):
        return lax.ppermute(array, axis, [(k, k ^ step) for k in range(size)])

    far = over("col", n_col, 2, packed)
    near = over("col", n_col, 1, packed)
    last = over("col", n_col, 3, packed)
    front = jnp.stack([packed, far])
    chip_front = over("row", n_row, 2, front)
    rear = jnp.stack([near, last])
    chip_rear = over("row", n_row, 2, rear)
    front, final_projection_matrix = lax.optimization_barrier((front, final_projection_matrix))
    weights = pl.pallas_call(
        weights_kernel,
        out_shape=(
            held(8, 128), held_bf(256, 256), held_bf(width * width // 2, 256), held(2 * width, features),
        ),
        in_specs=[hbm] * 5,
        out_specs=tuple(vmem(4)),
        scratch_shapes=[
            pltpu.VMEM((1, features), F32),
            pltpu.VMEM((1, features), F32),
            pltpu.VMEM((width, features), BF),
            pltpu.VMEM((width, features), BF),
            pltpu.VMEM((width * width, 128), BF),
            pltpu.VMEM((width * width, 128), F32),
            pltpu.SemaphoreType.DMA((5,)),
        ],
        compiler_params=LIMIT,
    )(
        *[
            pltpu.with_memory_space_constraint(x, pltpu.HBM)
            for x in (
                standardizer_scale.reshape(1, features),
                standardizer_shift.reshape(1, features),
                first_t,
                second_t,
                final_projection_matrix,
            )
        ]
    )
    norm, back, final_turned, first = weights
    own = jnp.concatenate([front, rear])
    own, chip_front, norm = lax.optimization_barrier((own, chip_front, norm))
    core = over("row", n_row, 1, own)
    stage_outs = [
        held_bf(512, 256), held_bf(128, 256), held_bf(128, 256), held(width, 8, 128),
        held_bf(256, 1024), held(8, 32, 128), held(128, 128),
    ]
    scalar = pl.BlockSpec(memory_space=pltpu.SMEM)

    def stages_of(kernel, sets, outs, flops):
        return pl.pallas_call(
            functools.partial(kernel, n_col),
            out_shape=tuple(outs),
            in_specs=[scalar] + vmem(len(sets) + 3),
            out_specs=tuple(vmem(len(outs))),
            scratch_shapes=[pltpu.VMEM((256, 128), F32)] * (len(outs) // 7),
            compiler_params=LIMIT,
            cost_estimate=pl.CostEstimate(
                flops=flops, bytes_accessed=flops // 256, transcendentals=0
            ),
        )(place, *sets, norm, back, final_turned)

    both_front = over("row", n_row, 1, chip_front)
    own_stage = stages_of(own_kernel, (front, rear), stage_outs + [held(128, 128)] * 2, 1_000_000_000)
    chip_rear, own_stage = lax.optimization_barrier((chip_rear, own_stage))
    both_rear = over("row", n_row, 1, chip_rear)
    pair_stages = stages_of(pair_kernel, (core, chip_front, chip_rear), stage_outs * 2, 1000000)
    stages = [own_stage[:7], pair_stages]
    outs = pl.pallas_call(
        functools.partial(part_kernel, n_row, n_col),
        out_shape=(
            shape(shards, tokens, features),
            shape(width * width, 128),
            shape(width, features),
            shape(width, features),
            shape(1, features),
            shape(1, features),
            shape(1, 128),
        ),
        in_specs=[scalar] + vmem(7 * (n_row - 1) + 8),
        out_specs=(*vmem(1), hbm, *vmem(5)),
        scratch_shapes=[
            pltpu.VMEM((1024, 128), BF),
            pltpu.VMEM((1024, 128), BF),
            pltpu.VMEM((1024, 1024), BF),
            pltpu.VMEM((1024, 1024), BF),
            pltpu.VMEM((1024, 128), F32),
            pltpu.VMEM((128, 2048), BF),
            pltpu.VMEM((1024, 128), F32),
            pltpu.SemaphoreType.DMA,
            pltpu.VMEM((256, 128), F32),
            *stage_outs,
        ],
        compiler_params=LIMIT,
    )(place, both_front, both_rear, *[x for s in stages for x in s], *own_stage[7:], norm, back, final_turned, first)
    emb, final, first, second, gain, offset, bias = outs
    return emb, final, first.T, second.T, gain.reshape(-1), offset.reshape(-1), bias.reshape(-1)


def body(n_row, n_col, *arguments):
    msa, _, pair = arguments[:3]
    width = arguments[5].shape[1]
    fits = (
        n_row == 4
        and n_col == 4
        and msa.shape == (32, 8, 64)
        and pair.shape == (8, 8, 128)
        and width == 32
    )
    if fits:
        return gathered_body(n_row, n_col, *arguments)
    return sharded_body(*arguments)


def solution(mesh):
    placed = (
        P(("grp", "col"), "row", None),
        P(("grp", "col"), "row"),
        P(("grp", "row"), "col", None),
        P(),
        P(),
        P(),
        P(),
        P(),
    )
    return jax.shard_map(
        functools.partial(body, mesh.shape["row"], mesh.shape["col"]),
        mesh=mesh,
        in_specs=placed,
        out_specs=(
            P(("grp", "col"), "row", None),
            P("grp", None),
            P("grp", None),
            P("grp", None),
            P("grp"),
            P("grp"),
            P("grp"),
        ),
        check_vma=False,
    )
```

```python
import functools
from itertools import zip_longest

import jax
import jax.numpy as jnp
from jax import lax
from jax.experimental import pallas as pl
from jax.experimental.pallas import tpu as pltpu
from jax.sharding import PartitionSpec as P

TOKB = 2


def standardizer_parts(homolog_embedding, standardizer_scale, standardizer_shift):
    incoming_entries = homolog_embedding.astype(jnp.float32)
    center = jnp.mean(incoming_entries, axis=-1, keepdims=True)
    varied = incoming_entries - center
    variance = jnp.mean(varied * varied, axis=-1, keepdims=True)
    reciprocal_spread = lax.rsqrt(variance + 1e-05)
    standardized_entries = varied * reciprocal_spread
    standardized_bfloat = (standardized_entries * standardizer_scale + standardizer_shift).astype(
        jnp.bfloat16
    )
    return (standardized_entries, reciprocal_spread, standardized_bfloat)


def sharded_body(
    homolog_embedding,
    presence_indicator,
    coupling_change_derivative,
    standardizer_scale,
    standardizer_shift,
    first_projection_matrix,
    second_projection_matrix,
    final_projection_matrix,
):
    shard_homolog_number, residue_line_number, feature_number = homolog_embedding.shape
    tok_cols = coupling_change_derivative.shape[1]
    width = first_projection_matrix.shape[1]
    standardized_entries, reciprocal_spread, standardized_bfloat = standardizer_parts(
        homolog_embedding, standardizer_scale, standardizer_shift
    )
    mask_single_precision = presence_indicator.astype(jnp.float32)
    mask_half_precision = presence_indicator.astype(jnp.bfloat16)
    left = (
        jnp.einsum(
            "sic,cp->sip",
            standardized_bfloat,
            first_projection_matrix,
            preferred_element_type=jnp.float32,
        )
        * mask_single_precision[..., None]
    ).astype(jnp.bfloat16)
    right = (
        jnp.einsum(
            "sic,cp->sip",
            standardized_bfloat,
            second_projection_matrix,
            preferred_element_type=jnp.float32,
        )
        * mask_single_precision[..., None]
    ).astype(jnp.bfloat16)
    left_flat = left.reshape(shard_homolog_number, residue_line_number * width)
    right_flat = right.reshape(shard_homolog_number, residue_line_number * width)
    left_all, mask_left = (
        lax.all_gather(left_flat, "col", axis=0, tiled=True),
        lax.all_gather(mask_half_precision, "col", axis=0, tiled=True),
    )
    right_wide, mask_wide = (
        lax.all_gather(right_flat, "row", axis=1, tiled=True),
        lax.all_gather(mask_half_precision, "row", axis=1, tiled=True),
    )
    right_all, mask_right = (
        lax.all_to_all(right_wide, "col", split_axis=1, concat_axis=0, tiled=True),
        lax.all_to_all(mask_wide, "col", split_axis=1, concat_axis=0, tiled=True),
    )
    seq_total = left_all.shape[0]
    right_three = right_all.reshape(seq_total, tok_cols, width)
    counts = jnp.einsum("si,sj->ij", mask_left, mask_right, preferred_element_type=jnp.float32)
    scaled = coupling_change_derivative.astype(jnp.float32) / (counts + 0.001)[..., None]
    bias_part = jnp.sum(scaled, axis=(0, 1))
    scaled_bf = scaled.astype(jnp.bfloat16)
    block_rows = residue_line_number // TOKB
    right_acc = jnp.zeros((seq_total, tok_cols, width), jnp.float32)
    wout_acc = jnp.zeros(final_projection_matrix.shape, jnp.float32)
    left_pieces = []
    for block_index in range(TOKB):
        first = block_index * block_rows
        rows_bf = scaled_bf[first : first + block_rows]
        outer_grad = jnp.einsum(
            "ijz,fz->ijf", rows_bf, final_projection_matrix, preferred_element_type=jnp.float32
        ).astype(jnp.bfloat16)
        outer_grad = outer_grad.reshape(block_rows, tok_cols, width, width)
        left_block = left_all[:, first * width : (first + block_rows) * width].reshape(
            seq_total, block_rows, width
        )
        first_factor_derivative = jnp.einsum(
            "ijce,sje->sic", outer_grad, right_three, preferred_element_type=jnp.float32
        )
        right_acc = right_acc + jnp.einsum(
            "ijce,sic->sje", outer_grad, left_block, preferred_element_type=jnp.float32
        )
        outer = jnp.einsum(
            "sic,sje->ijce", left_block, right_three, preferred_element_type=jnp.float32
        ).astype(jnp.bfloat16)
        outer = outer.reshape(block_rows, tok_cols, width * width)
        wout_acc = wout_acc + jnp.einsum(
            "ijf,ijz->fz", outer, rows_bf, preferred_element_type=jnp.float32
        )
        first_factor_derivative = first_factor_derivative.reshape(seq_total, block_rows * width)
        left_pieces.append(first_factor_derivative)
    left_terms = jnp.concatenate(left_pieces, axis=1)
    left_own = lax.psum_scatter(left_terms, "col", scatter_dimension=0, tiled=True)
    right_spread = lax.all_to_all(
        right_acc.reshape(seq_total, tok_cols * width),
        "col",
        split_axis=0,
        concat_axis=1,
        tiled=True,
    )
    right_own = lax.psum_scatter(right_spread, "row", scatter_dimension=1, tiled=True)
    left_in = (
        left_own.reshape(shard_homolog_number, residue_line_number, width)
        * mask_single_precision[..., None]
    ).astype(jnp.bfloat16)
    right_in = (
        right_own.reshape(shard_homolog_number, residue_line_number, width)
        * mask_single_precision[..., None]
    ).astype(jnp.bfloat16)
    left_part = jnp.einsum(
        "sic,sip->cp", standardized_bfloat, left_in, preferred_element_type=jnp.float32
    )
    right_part = jnp.einsum(
        "sic,sip->cp", standardized_bfloat, right_in, preferred_element_type=jnp.float32
    )
    d_normal = jnp.einsum(
        "sip,cp->sic", left_in, first_projection_matrix, preferred_element_type=jnp.float32
    ) + jnp.einsum(
        "sip,cp->sic", right_in, second_projection_matrix, preferred_element_type=jnp.float32
    )
    gain_part = jnp.sum(d_normal * standardized_entries, axis=(0, 1))
    beta_part = jnp.sum(d_normal, axis=(0, 1))
    standardized_derivative = d_normal * standardizer_scale
    embedding_derivative = reciprocal_spread * (
        standardized_derivative
        - jnp.mean(standardized_derivative, axis=-1, keepdims=True)
        - standardized_entries
        * jnp.mean(standardized_derivative * standardized_entries, axis=-1, keepdims=True)
    )
    (
        final_matrix_derivative,
        first_matrix_derivative,
        second_matrix_derivative,
        scale_factor_derivative,
        shift_term_derivative,
        shift_derivative,
    ) = lax.psum((wout_acc, left_part, right_part, gain_part, beta_part, bias_part), ("row", "col"))
    return (
        embedding_derivative,
        final_matrix_derivative,
        first_matrix_derivative,
        second_matrix_derivative,
        scale_factor_derivative,
        shift_term_derivative,
        shift_derivative,
    )


BF = jnp.bfloat16
F32 = jnp.float32


def spread(rows, cols, rule):
    r = lax.broadcasted_iota(jnp.int32, (rows, cols), 0)
    c = lax.broadcasted_iota(jnp.int32, (rows, cols), 1)
    return rule(r, c)


def mm(a, b):
    return jnp.dot(a, b, preferred_element_type=F32)


def mm_nt(a, b):
    return lax.dot_general(a, b, (((1,), (1,)), ((), ())), preferred_element_type=F32)


def mm_tn(a, b):
    return lax.dot_general(a, b, (((0,), (0,)), ((), ())), preferred_element_type=F32)


def interleave(first, second):
    odd = lax.broadcasted_iota(jnp.int16, (32, 128), 1) & 32 != 0
    return (
        jnp.where(odd, pltpu.roll(second, 32, 1), first),
        jnp.where(odd, second, pltpu.roll(first, 96, 1)),
    )


def diagonal_pair(block):
    zero = jnp.zeros_like(block)
    return jnp.concatenate(
        [jnp.concatenate([block, zero], axis=1), jnp.concatenate([zero, block], axis=1)], axis=0
    )


ABSENT = 1024.0


def pack_kernel(msa_ref, mask_ref, pair_ref, out_ref):
    msa = msa_ref[...].astype(F32)
    pick = spread(8, 512, lambda r, c: jnp.where(c // 64 == r, 1.0, 0.0)).astype(BF)
    present = mm_tn(mask_ref[...].astype(F32).astype(BF), pick) > 0.5
    for g in range(4):
        rows = jnp.concatenate([msa[:, 2 * g, :], msa[:, 2 * g + 1, :]], axis=1)
        out_ref[32 * g : 32 * g + 32, :] = jnp.where(
            present[:, 128 * g : 128 * g + 128], rows, ABSENT
        ).astype(BF)
    out_ref[128:192, :] = pair_ref[...].astype(F32).reshape(64, 128).astype(BF)


def weights_kernel(*refs):
    sources, (norm_out, back_out, final_out, first_out) = refs[:5], refs[5:9]
    held, scr, sems = refs[9:14], refs[14], refs[15]
    copies = [pltpu.make_async_copy(sources[k], held[k], sems.at[k]) for k in range(5)]
    for copy in copies:
        copy.start()
    for copy in copies:
        copy.wait()
    gain_ref, offset_ref, first_ref, second_ref, final_ref = held
    norm_out[...] = jnp.concatenate(
        [
            jnp.concatenate([ref[...]] * 2, axis=1)
            for ref in (gain_ref, offset_ref, gain_ref, offset_ref) * 2
        ],
        axis=0,
    )
    for k, ref in enumerate((first_ref, second_ref)):
        narrow = ref[...].astype(F32)
        first_out[32 * k : 32 * k + 32, :] = narrow
        wide = jnp.concatenate([narrow] * 4, axis=1)
        wide = jnp.concatenate([wide] * 4, axis=0)
        own = spread(128, 256, lambda r, c: r // 32 == c // 64)
        back_out[128 * k : 128 * k + 128, :] = jnp.where(own, wide, 0.0).astype(BF)
    scr[...] = final_ref[...].astype(F32)
    for k in range(16):
        e = 4 * (k // 2) + k % 2
        final_out[32 * k : 32 * k + 32, :] = jnp.concatenate(
            [scr[pl.ds(e, 32, stride=32), :], scr[pl.ds(e + 2, 32, stride=32), :]], axis=1
        ).astype(BF)


def averager_of():
    return spread(128, 128, lambda r, c: jnp.where(r // 64 == c // 64, 1.0 / 64, 0.0)).astype(BF)


ORDER = (0, 2, 1, 3)


def stage_steps(
    n_col, a, last, place_ref, set_refs, norm_ref, back_ref, final_ref,
    rhs_out, left_out, leftt_out, rightt_out, grad_out, pair_out, found_out, *rest
):
    *own_out, turn_scr = rest
    blocks = [ref.at[k] for ref in set_refs for k in range(ref.shape[0])]

    gain = norm_ref[0:1, :]
    offset = norm_ref[1:2, :]
    averager = averager_of()
    x = jnp.concatenate(
        [blocks[b][32 * g : 32 * g + 32, :] for g in range(4) for b in range(n_col)], axis=0
    )
    mean = mm(x, averager)
    present = mean < ABSENT / 2
    here = jnp.where(present, 1.0, 0.0)
    lane = lax.broadcasted_iota(jnp.int32, (128, 128), 1)
    found = jnp.zeros((128, 128), F32)
    for g in range(4):
        found = jnp.where(lane % 32 // 2 == 4 * a + g, here[128 * g : 128 * g + 128], found)
    found_out[...] = found
    for b in range(n_col):
        at = pl.multiple_of(lax.bitwise_xor(place_ref[0], ORDER[b]) * 8, 8)
        pair_out[:, pl.ds(at, 8), :] = blocks[b][128:192, :].astype(F32).reshape(8, 8, 128)
    yield
    varied = x.astype(F32) - mean
    inverse = lax.rsqrt(mm((varied * varied).astype(BF), averager) + 1e-05)
    normed = varied * inverse
    if own_out:
        for g in range(4):
            own_out[0][32 * g : 32 * g + 32, :] = normed[128 * g : 128 * g + 32]
            own_out[1][32 * g : 32 * g + 32, :] = inverse[128 * g : 128 * g + 32]
    yield

    def grad_piece(n):
        pair = pair_out[4 * n : 4 * n + 4].reshape(128, 128).astype(BF)
        pairs = jnp.concatenate([diagonal_pair(pair[:64]), diagonal_pair(pair[64:])], axis=0)
        grad = mm_nt(final_ref[...], pairs).astype(BF)
        for p in range(2):
            for q in range(8):
                rows = 64 * (2 * n + p)
                block = grad[64 * q : 64 * q + 64, 128 * p : 128 * p + 128]
                even, odd = interleave(block[:32], block[32:])
                grad_out[rows : rows + 32, 128 * q : 128 * q + 128] = even
                grad_out[rows + 32 : rows + 64, 128 * q : 128 * q + 128] = odd

    if not last:
        grad_piece(0)
    yield

    normal = jnp.where(present, normed * gain + offset, 0.0).astype(BF)
    rhs_out[:, 0:128] = normal
    rhs_out[:, 128:256] = normed.astype(BF)
    for h in range(2):
        masked = jnp.concatenate(
            [normal[128 * g : 128 * g + 128] for g in (2 * h, 2 * h + 1)], axis=1
        )
        at = slice(128 * h, 128 * h + 128)
        left_out[:, at] = mm_nt(masked, back_ref[:128, :]).astype(BF)
        both = mm_nt(back_ref[...], masked)
        turn_scr[at, :] = both[128:]
        for k in range(2):
            leftt_out[64 * h + 32 * k : 64 * h + 32 * k + 32, :] = jnp.concatenate(
                [both[32 * k : 32 * k + 32], both[32 * k + 64 : 32 * k + 96]], axis=1
            ).astype(BF)
    yield
    if not last:
        grad_piece(1)
    yield
    for e in range(32):
        rightt_out[e] = turn_scr[pl.ds(e, 8, stride=32), :]
    if last:
        grad_piece(0)
        grad_piece(1)


def stage_kernel(*arguments):
    for _ in stage_steps(*arguments):
        pass


def own_kernel(n_col, place_ref, front_ref, rear_ref, norm_ref, back_ref, final_ref, *rest):
    stage_kernel(n_col, 0, False, place_ref, (front_ref, rear_ref), norm_ref, back_ref, final_ref, *rest)


def pair_kernel(n_col, place_ref, core_ref, front_ref, rear_ref, norm_ref, back_ref, final_ref, *rest):
    common = (norm_ref, back_ref, final_ref)
    both = (
        stage_steps(n_col, 1, False, place_ref, (core_ref,), *common, *rest[:7], rest[14]),
        stage_steps(n_col, 2, False, place_ref, (front_ref, rear_ref), *common, *rest[7:14], rest[15]),
    )
    for _ in zip_longest(*both):
        pass


def part_kernel(n_row, n_col, place_ref, front_ref, rear_ref, *refs):
    stages = [refs[7 * a : 7 * a + 7] for a in range(n_row - 1)]
    (
        normed_ref, inverse_ref, norm_ref, back_ref, final_ref, first_ref,
        emb_out, final_hbm_out, first_out, second_out, gain_out, offset_out, bias_out,
        right_scr, scaled_scr, grad_scr, outer_scr, wide_scr, all_scr,
        final_out, out_sem, turn_scr,
    ) = refs[7 * (n_row - 1) : -7]
    stages.append(refs[-7:])
    stage_kernel(
        n_col, n_row - 1, True, place_ref, (front_ref, rear_ref),
        norm_ref, back_ref, final_ref, *stages[-1], turn_scr,
    )
    gain = norm_ref[0:1, :]
    averager = averager_of()
    lane = lax.broadcasted_iota(jnp.int32, (128, 128), 1)

    found = sum(stage[6][...] for stage in stages)
    turned = pltpu.roll(found, 64, 1)
    mask = jnp.where((lane % 2 == 0) == (lane < 64), found, turned)
    mask_t = mask.T

    for e in range(32):
        right_scr[32 * e : 32 * e + 32, :] = jnp.concatenate(
            [stage[3][e] for stage in stages], axis=0
        ).astype(BF)

    mask_bf = mask.astype(BF)
    share = (1.0 / (mm_tn(mask_bf, mask_bf)[0:32] + 0.001)).astype(BF)
    for i in range(32):
        a, at = i // 8, 32 * (i % 8)
        for q in range(8):
            grad_scr[32 * i : 32 * i + 32, 128 * q : 128 * q + 128] = (
                stages[a][4][at : at + 32, 128 * q : 128 * q + 128] * share[i : i + 1]
            )
    left = jnp.concatenate([stage[1][...] for stage in stages], axis=1)
    right_grad = mm(left, grad_scr[...])
    left_grad = mm(grad_scr[...], right_scr[...])

    turn = spread(
        256, 256, lambda r, c: jnp.where((r // 8 == c % 32) & (r % 8 == c // 32), 1.0, 0.0)
    ).astype(BF)
    mask_two = jnp.concatenate([mask, mask], axis=1)
    right_in = [
        mm_nt(turn, (right_grad[:, 256 * q : 256 * q + 256] * mask_two).astype(BF))
        for q in range(4)
    ]
    for t in range(32):
        at = slice(128 * (t // 2), 128 * (t // 2) + 128)
        row = 32 * (t % 2)
        all_scr[row : row + 32, at] = (
            left_grad[32 * t : 32 * t + 32] * mask_t[t : t + 1]
        ).astype(BF)
        all_scr[row + 64 : row + 96, at] = jnp.concatenate(
            [part[8 * t : 8 * t + 8] for part in right_in], axis=0
        ).astype(BF)

    bias = jnp.zeros((1, 128), F32)
    ones = jnp.ones((128, 128), BF)
    for p in range(8):
        both_on = jnp.concatenate(
            [mask_t[0:32] * mask_t[i : i + 1] for i in range(4 * p, 4 * p + 4)], axis=0
        ).astype(BF)
        counts = mm(both_on, ones)
        pair = stages[p // 2][5][4 * (p % 2) : 4 * (p % 2) + 4]
        scaled = pair.reshape(128, 128) / (counts + 0.001)
        bias = bias + jnp.sum(scaled, axis=0, keepdims=True)
        scaled_scr[128 * p : 128 * p + 128, :] = scaled.astype(BF)
    bias_out[...] = bias

    left_t = jnp.concatenate([stage[2][...] for stage in stages], axis=0)
    for n in range(8):
        rights = jnp.concatenate(
            [diagonal_pair(right_scr[64 * p : 64 * p + 64, :]) for p in (2 * n, 2 * n + 1)], axis=0
        )
        outer = mm_nt(left_t, rights).astype(BF)
        for p in range(2):
            for q in range(8):
                rows = 64 * (2 * n + p)
                block = outer[64 * q : 64 * q + 64, 128 * p : 128 * p + 128]
                even, odd = interleave(block[:32], block[32:])
                outer_scr[rows : rows + 32, 128 * q : 128 * q + 128] = even
                outer_scr[rows + 32 : rows + 64, 128 * q : 128 * q + 128] = odd
    wide_scr[...] = mm(outer_scr[...], scaled_scr[...])
    for c in range(32):
        final_out[32 * c : 32 * c + 32, :] = wide_scr[pl.ds(c, 32, stride=32), :]
    final_send = pltpu.make_async_copy(final_out, final_hbm_out, out_sem)
    final_send.start()

    total = mm(
        all_scr[...], jnp.concatenate([stage[0][...] for stage in stages], axis=0)
    )
    sums = all_scr[:, 0:128].astype(F32)
    for g in range(1, 16):
        sums = sums + all_scr[:, 128 * g : 128 * g + 128].astype(F32)

    def fold(block):
        return block[0:32, 0:64] + block[32:64, 64:128]

    first_out[...] = fold(total[0:64, 0:128])
    second_out[...] = fold(total[64:128, 0:128])
    sums = jnp.sum(sums, axis=1, keepdims=True)
    left_sum = sums[0:32] + sums[32:64]
    right_sum = sums[64:96] + sums[96:128]
    first, second = first_ref[0:32, :], first_ref[32:64, :]
    gain_out[...] = jnp.sum(
        first * fold(total[0:64, 128:256]) + second * fold(total[64:128, 128:256]),
        axis=0, keepdims=True,
    )
    offset_out[...] = jnp.sum(first * left_sum + second * right_sum, axis=0, keepdims=True)

    d_hat = []
    for h in range(2):
        sides = [
            jnp.concatenate(
                [all_scr[row : row + 64, 128 * g : 128 * g + 128] for g in (2 * h, 2 * h + 1)], axis=0
            )
            for row in (0, 64)
        ]
        d_normal = mm_tn(jnp.concatenate(sides, axis=0), back_ref[...])
        d_hat += [d_normal[0:32, 0:128] * gain, d_normal[0:32, 128:256] * gain]
    d_hat = jnp.concatenate(d_hat, axis=0)
    normed = normed_ref[...]
    means = mm(jnp.concatenate([d_hat, d_hat * normed], axis=0).astype(BF), averager)
    result = inverse_ref[...] * (d_hat - means[:128] - normed * means[128:])
    for g in range(4):
        emb_out[:, 2 * g, :] = result[32 * g : 32 * g + 32, 0:64]
        emb_out[:, 2 * g + 1, :] = result[32 * g : 32 * g + 32, 64:128]
    final_send.wait()


def vmem(count):
    return [pl.BlockSpec(memory_space=pltpu.VMEM)] * count


LIMIT = pltpu.CompilerParams(vmem_limit_bytes=32 * 1024 * 1024)


def gathered_body(
    n_row,
    n_col,
    homolog_embedding,
    presence_indicator,
    coupling_change_derivative,
    standardizer_scale,
    standardizer_shift,
    first_projection_matrix,
    second_projection_matrix,
    final_projection_matrix,
):
    shards, tokens, features = homolog_embedding.shape
    width = first_projection_matrix.shape[1]
    first_t, second_t = first_projection_matrix.T, second_projection_matrix.T
    shape = lambda *dims: jax.ShapeDtypeStruct(dims, F32)
    held = lambda *dims: pltpu.VMEM(dims, F32)
    held_bf = lambda *dims: pltpu.VMEM(dims, BF)
    hbm = pl.BlockSpec(memory_space=pltpu.HBM)
    place = lax.bitwise_xor(lax.axis_index("row"), lax.axis_index("col"))
    place = place.astype(jnp.int32).reshape(1)
    packed = pl.pallas_call(
        pack_kernel,
        out_shape=held_bf(192, 128),
        in_specs=vmem(3),
        out_specs=vmem(1)[0],
    )(homolog_embedding, presence_indicator.T, coupling_change_derivative)
    def over(axis, size, step, array):
        return lax.ppermute(array, axis, [(k, k ^ step) for k in range(size)])

    far = over("col", n_col, 2, packed)
    near = over("col", n_col, 1, packed)
    last = over("col", n_col, 3, packed)
    front = jnp.stack([packed, far])
    chip_front = over("row", n_row, 2, front)
    rear = jnp.stack([near, last])
    chip_rear = over("row", n_row, 2, rear)
    front, final_projection_matrix = lax.optimization_barrier((front, final_projection_matrix))
    weights = pl.pallas_call(
        weights_kernel,
        out_shape=(
            held(8, 128), held_bf(256, 256), held_bf(width * width // 2, 256), held(2 * width, features),
        ),
        in_specs=[hbm] * 5,
        out_specs=tuple(vmem(4)),
        scratch_shapes=[
            pltpu.VMEM((1, features), F32),
            pltpu.VMEM((1, features), F32),
            pltpu.VMEM((width, features), BF),
            pltpu.VMEM((width, features), BF),
            pltpu.VMEM((width * width, 128), BF),
            pltpu.VMEM((width * width, 128), F32),
            pltpu.SemaphoreType.DMA((5,)),
        ],
        compiler_params=LIMIT,
    )(
        *[
            pltpu.with_memory_space_constraint(x, pltpu.HBM)
            for x in (
                standardizer_scale.reshape(1, features),
                standardizer_shift.reshape(1, features),
                first_t,
                second_t,
                final_projection_matrix,
            )
        ]
    )
    norm, back, final_turned, first = weights
    own = jnp.concatenate([front, rear])
    own, chip_front, norm = lax.optimization_barrier((own, chip_front, norm))
    core = over("row", n_row, 1, own)
    stage_outs = [
        held_bf(512, 256), held_bf(128, 256), held_bf(128, 256), held(width, 8, 128),
        held_bf(256, 1024), held(8, 32, 128), held(128, 128),
    ]
    scalar = pl.BlockSpec(memory_space=pltpu.SMEM)

    def stages_of(kernel, sets, outs, flops):
        return pl.pallas_call(
            functools.partial(kernel, n_col),
            out_shape=tuple(outs),
            in_specs=[scalar] + vmem(len(sets) + 3),
            out_specs=tuple(vmem(len(outs))),
            scratch_shapes=[pltpu.VMEM((256, 128), F32)] * (len(outs) // 7),
            compiler_params=LIMIT,
            cost_estimate=pl.CostEstimate(
                flops=flops, bytes_accessed=flops // 256, transcendentals=0
            ),
        )(place, *sets, norm, back, final_turned)

    both_front = over("row", n_row, 1, chip_front)
    own_stage = stages_of(own_kernel, (front, rear), stage_outs + [held(128, 128)] * 2, 1_000_000_000)
    chip_rear, own_stage = lax.optimization_barrier((chip_rear, own_stage))
    both_rear = over("row", n_row, 1, chip_rear)
    pair_stages = stages_of(pair_kernel, (core, chip_front, chip_rear), stage_outs * 2, 1000000)
    stages = [own_stage[:7], pair_stages]
    outs = pl.pallas_call(
        functools.partial(part_kernel, n_row, n_col),
        out_shape=(
            shape(shards, tokens, features),
            shape(width * width, 128),
            shape(width, features),
            shape(width, features),
            shape(1, features),
            shape(1, features),
            shape(1, 128),
        ),
        in_specs=[scalar] + vmem(7 * (n_row - 1) + 8),
        out_specs=(*vmem(1), hbm, *vmem(5)),
        scratch_shapes=[
            pltpu.VMEM((1024, 128), BF),
            pltpu.VMEM((1024, 128), BF),
            pltpu.VMEM((1024, 1024), BF),
            pltpu.VMEM((1024, 1024), BF),
            pltpu.VMEM((1024, 128), F32),
            pltpu.VMEM((128, 2048), BF),
            pltpu.VMEM((1024, 128), F32),
            pltpu.SemaphoreType.DMA,
            pltpu.VMEM((256, 128), F32),
            *stage_outs,
        ],
        compiler_params=LIMIT,
    )(place, both_front, both_rear, *[x for s in stages for x in s], *own_stage[7:], norm, back, final_turned, first)
    emb, final, first, second, gain, offset, bias = outs
    return emb, final, first.T, second.T, gain.reshape(-1), offset.reshape(-1), bias.reshape(-1)


def body(n_row, n_col, *arguments):
    msa, _, pair = arguments[:3]
    width = arguments[5].shape[1]
    fits = (
        n_row == 4
        and n_col == 4
        and msa.shape == (32, 8, 64)
        and pair.shape == (8, 8, 128)
        and width == 32
    )
    if fits:
        return gathered_body(n_row, n_col, *arguments)
    return sharded_body(*arguments)


def solution(mesh):
    placed = (
        P(("grp", "col"), "row", None),
        P(("grp", "col"), "row"),
        P(("grp", "row"), "col", None),
        P(),
        P(),
        P(),
        P(),
        P(),
    )
    return jax.shard_map(
        functools.partial(body, mesh.shape["row"], mesh.shape["col"]),
        mesh=mesh,
        in_specs=placed,
        out_specs=(
            P(("grp", "col"), "row", None),
            P("grp", None),
            P("grp", None),
            P("grp", None),
            P("grp"),
            P("grp"),
            P("grp"),
        ),
        check_vma=False,
    )
```

```python
import functools
from itertools import zip_longest

import jax
import jax.numpy as jnp
from jax import lax
from jax.experimental import pallas as pl
from jax.experimental.pallas import tpu as pltpu
from jax.sharding import PartitionSpec as P

TOKB = 2


def standardizer_parts(homolog_embedding, standardizer_scale, standardizer_shift):
    incoming_entries = homolog_embedding.astype(jnp.float32)
    center = jnp.mean(incoming_entries, axis=-1, keepdims=True)
    varied = incoming_entries - center
    variance = jnp.mean(varied * varied, axis=-1, keepdims=True)
    reciprocal_spread = lax.rsqrt(variance + 1e-05)
    standardized_entries = varied * reciprocal_spread
    standardized_bfloat = (standardized_entries * standardizer_scale + standardizer_shift).astype(
        jnp.bfloat16
    )
    return (standardized_entries, reciprocal_spread, standardized_bfloat)


def sharded_body(
    homolog_embedding,
    presence_indicator,
    coupling_change_derivative,
    standardizer_scale,
    standardizer_shift,
    first_projection_matrix,
    second_projection_matrix,
    final_projection_matrix,
):
    shard_homolog_number, residue_line_number, feature_number = homolog_embedding.shape
    tok_cols = coupling_change_derivative.shape[1]
    width = first_projection_matrix.shape[1]
    standardized_entries, reciprocal_spread, standardized_bfloat = standardizer_parts(
        homolog_embedding, standardizer_scale, standardizer_shift
    )
    mask_single_precision = presence_indicator.astype(jnp.float32)
    mask_half_precision = presence_indicator.astype(jnp.bfloat16)
    left = (
        jnp.einsum(
            "sic,cp->sip",
            standardized_bfloat,
            first_projection_matrix,
            preferred_element_type=jnp.float32,
        )
        * mask_single_precision[..., None]
    ).astype(jnp.bfloat16)
    right = (
        jnp.einsum(
            "sic,cp->sip",
            standardized_bfloat,
            second_projection_matrix,
            preferred_element_type=jnp.float32,
        )
        * mask_single_precision[..., None]
    ).astype(jnp.bfloat16)
    left_flat = left.reshape(shard_homolog_number, residue_line_number * width)
    right_flat = right.reshape(shard_homolog_number, residue_line_number * width)
    left_all, mask_left = (
        lax.all_gather(left_flat, "col", axis=0, tiled=True),
        lax.all_gather(mask_half_precision, "col", axis=0, tiled=True),
    )
    right_wide, mask_wide = (
        lax.all_gather(right_flat, "row", axis=1, tiled=True),
        lax.all_gather(mask_half_precision, "row", axis=1, tiled=True),
    )
    right_all, mask_right = (
        lax.all_to_all(right_wide, "col", split_axis=1, concat_axis=0, tiled=True),
        lax.all_to_all(mask_wide, "col", split_axis=1, concat_axis=0, tiled=True),
    )
    seq_total = left_all.shape[0]
    right_three = right_all.reshape(seq_total, tok_cols, width)
    counts = jnp.einsum("si,sj->ij", mask_left, mask_right, preferred_element_type=jnp.float32)
    scaled = coupling_change_derivative.astype(jnp.float32) / (counts + 0.001)[..., None]
    bias_part = jnp.sum(scaled, axis=(0, 1))
    scaled_bf = scaled.astype(jnp.bfloat16)
    block_rows = residue_line_number // TOKB
    right_acc = jnp.zeros((seq_total, tok_cols, width), jnp.float32)
    wout_acc = jnp.zeros(final_projection_matrix.shape, jnp.float32)
    left_pieces = []
    for block_index in range(TOKB):
        first = block_index * block_rows
        rows_bf = scaled_bf[first : first + block_rows]
        outer_grad = jnp.einsum(
            "ijz,fz->ijf", rows_bf, final_projection_matrix, preferred_element_type=jnp.float32
        ).astype(jnp.bfloat16)
        outer_grad = outer_grad.reshape(block_rows, tok_cols, width, width)
        left_block = left_all[:, first * width : (first + block_rows) * width].reshape(
            seq_total, block_rows, width
        )
        first_factor_derivative = jnp.einsum(
            "ijce,sje->sic", outer_grad, right_three, preferred_element_type=jnp.float32
        )
        right_acc = right_acc + jnp.einsum(
            "ijce,sic->sje", outer_grad, left_block, preferred_element_type=jnp.float32
        )
        outer = jnp.einsum(
            "sic,sje->ijce", left_block, right_three, preferred_element_type=jnp.float32
        ).astype(jnp.bfloat16)
        outer = outer.reshape(block_rows, tok_cols, width * width)
        wout_acc = wout_acc + jnp.einsum(
            "ijf,ijz->fz", outer, rows_bf, preferred_element_type=jnp.float32
        )
        first_factor_derivative = first_factor_derivative.reshape(seq_total, block_rows * width)
        left_pieces.append(first_factor_derivative)
    left_terms = jnp.concatenate(left_pieces, axis=1)
    left_own = lax.psum_scatter(left_terms, "col", scatter_dimension=0, tiled=True)
    right_spread = lax.all_to_all(
        right_acc.reshape(seq_total, tok_cols * width),
        "col",
        split_axis=0,
        concat_axis=1,
        tiled=True,
    )
    right_own = lax.psum_scatter(right_spread, "row", scatter_dimension=1, tiled=True)
    left_in = (
        left_own.reshape(shard_homolog_number, residue_line_number, width)
        * mask_single_precision[..., None]
    ).astype(jnp.bfloat16)
    right_in = (
        right_own.reshape(shard_homolog_number, residue_line_number, width)
        * mask_single_precision[..., None]
    ).astype(jnp.bfloat16)
    left_part = jnp.einsum(
        "sic,sip->cp", standardized_bfloat, left_in, preferred_element_type=jnp.float32
    )
    right_part = jnp.einsum(
        "sic,sip->cp", standardized_bfloat, right_in, preferred_element_type=jnp.float32
    )
    d_normal = jnp.einsum(
        "sip,cp->sic", left_in, first_projection_matrix, preferred_element_type=jnp.float32
    ) + jnp.einsum(
        "sip,cp->sic", right_in, second_projection_matrix, preferred_element_type=jnp.float32
    )
    gain_part = jnp.sum(d_normal * standardized_entries, axis=(0, 1))
    beta_part = jnp.sum(d_normal, axis=(0, 1))
    standardized_derivative = d_normal * standardizer_scale
    embedding_derivative = reciprocal_spread * (
        standardized_derivative
        - jnp.mean(standardized_derivative, axis=-1, keepdims=True)
        - standardized_entries
        * jnp.mean(standardized_derivative * standardized_entries, axis=-1, keepdims=True)
    )
    (
        final_matrix_derivative,
        first_matrix_derivative,
        second_matrix_derivative,
        scale_factor_derivative,
        shift_term_derivative,
        shift_derivative,
    ) = lax.psum((wout_acc, left_part, right_part, gain_part, beta_part, bias_part), ("row", "col"))
    return (
        embedding_derivative,
        final_matrix_derivative,
        first_matrix_derivative,
        second_matrix_derivative,
        scale_factor_derivative,
        shift_term_derivative,
        shift_derivative,
    )


BF = jnp.bfloat16
F32 = jnp.float32


def spread(rows, cols, rule):
    r = lax.broadcasted_iota(jnp.int32, (rows, cols), 0)
    c = lax.broadcasted_iota(jnp.int32, (rows, cols), 1)
    return rule(r, c)


def mm(a, b):
    return jnp.dot(a, b, preferred_element_type=F32)


def mm_nt(a, b):
    return lax.dot_general(a, b, (((1,), (1,)), ((), ())), preferred_element_type=F32)


def mm_tn(a, b):
    return lax.dot_general(a, b, (((0,), (0,)), ((), ())), preferred_element_type=F32)


def interleave(first, second):
    odd = lax.broadcasted_iota(jnp.int16, (32, 128), 1) & 32 != 0
    return (
        jnp.where(odd, pltpu.roll(second, 32, 1), first),
        jnp.where(odd, second, pltpu.roll(first, 96, 1)),
    )


def diagonal_pair(block):
    zero = jnp.zeros_like(block)
    return jnp.concatenate(
        [jnp.concatenate([block, zero], axis=1), jnp.concatenate([zero, block], axis=1)], axis=0
    )


ABSENT = 1024.0


def pack_kernel(msa_ref, mask_ref, pair_ref, out_ref):
    msa = msa_ref[...].astype(F32)
    pick = spread(8, 512, lambda r, c: jnp.where(c // 64 == r, 1.0, 0.0)).astype(BF)
    present = mm_tn(mask_ref[...].astype(F32).astype(BF), pick) > 0.5
    for g in range(4):
        rows = jnp.concatenate([msa[:, 2 * g, :], msa[:, 2 * g + 1, :]], axis=1)
        out_ref[32 * g : 32 * g + 32, :] = jnp.where(
            present[:, 128 * g : 128 * g + 128], rows, ABSENT
        ).astype(BF)
    out_ref[128:192, :] = pair_ref[...].astype(F32).reshape(64, 128).astype(BF)


def weights_kernel(*refs):
    sources, (norm_out, back_out, final_out, first_out) = refs[:5], refs[5:9]
    held, scr, sems = refs[9:14], refs[14], refs[15]
    copies = [pltpu.make_async_copy(sources[k], held[k], sems.at[k]) for k in range(5)]
    for copy in copies:
        copy.start()
    for copy in copies:
        copy.wait()
    gain_ref, offset_ref, first_ref, second_ref, final_ref = held
    norm_out[...] = jnp.concatenate(
        [
            jnp.concatenate([ref[...]] * 2, axis=1)
            for ref in (gain_ref, offset_ref, gain_ref, offset_ref) * 2
        ],
        axis=0,
    )
    for k, ref in enumerate((first_ref, second_ref)):
        narrow = ref[...].astype(F32)
        first_out[32 * k : 32 * k + 32, :] = narrow
        wide = jnp.concatenate([narrow] * 4, axis=1)
        wide = jnp.concatenate([wide] * 4, axis=0)
        own = spread(128, 256, lambda r, c: r // 32 == c // 64)
        back_out[128 * k : 128 * k + 128, :] = jnp.where(own, wide, 0.0).astype(BF)
    scr[...] = final_ref[...].astype(F32)
    for k in range(16):
        e = 4 * (k // 2) + k % 2
        final_out[32 * k : 32 * k + 32, :] = jnp.concatenate(
            [scr[pl.ds(e, 32, stride=32), :], scr[pl.ds(e + 2, 32, stride=32), :]], axis=1
        ).astype(BF)


def averager_of():
    return spread(128, 128, lambda r, c: jnp.where(r // 64 == c // 64, 1.0 / 64, 0.0)).astype(BF)


ORDER = (0, 2, 1, 3)


def stage_steps(
    n_col, a, last, place_ref, set_refs, norm_ref, back_ref, final_ref,
    rhs_out, left_out, leftt_out, rightt_out, grad_out, pair_out, found_out, *rest
):
    *own_out, turn_scr = rest
    blocks = [ref.at[k] for ref in set_refs for k in range(ref.shape[0])]

    gain = norm_ref[0:1, :]
    offset = norm_ref[1:2, :]
    averager = averager_of()
    x = jnp.concatenate(
        [blocks[b][32 * g : 32 * g + 32, :] for g in range(4) for b in range(n_col)], axis=0
    )
    mean = mm(x, averager)
    present = mean < ABSENT / 2
    here = jnp.where(present, 1.0, 0.0)
    lane = lax.broadcasted_iota(jnp.int32, (128, 128), 1)
    found = jnp.zeros((128, 128), F32)
    for g in range(4):
        found = jnp.where(lane % 32 // 2 == 4 * a + g, here[128 * g : 128 * g + 128], found)
    found_out[...] = found
    for b in range(n_col):
        at = pl.multiple_of(lax.bitwise_xor(place_ref[0], ORDER[b]) * 8, 8)
        pair_out[:, pl.ds(at, 8), :] = blocks[b][128:192, :].astype(F32).reshape(8, 8, 128)
    yield
    varied = x.astype(F32) - mean
    inverse = lax.rsqrt(mm((varied * varied).astype(BF), averager) + 1e-05)
    normed = varied * inverse
    if own_out:
        for g in range(4):
            own_out[0][32 * g : 32 * g + 32, :] = normed[128 * g : 128 * g + 32]
            own_out[1][32 * g : 32 * g + 32, :] = inverse[128 * g : 128 * g + 32]
    yield

    def grad_piece(n):
        pair = pair_out[4 * n : 4 * n + 4].reshape(128, 128).astype(BF)
        pairs = jnp.concatenate([diagonal_pair(pair[:64]), diagonal_pair(pair[64:])], axis=0)
        grad = mm_nt(final_ref[...], pairs).astype(BF)
        for p in range(2):
            for q in range(8):
                rows = 64 * (2 * n + p)
                block = grad[64 * q : 64 * q + 64, 128 * p : 128 * p + 128]
                even, odd = interleave(block[:32], block[32:])
                grad_out[rows : rows + 32, 128 * q : 128 * q + 128] = even
                grad_out[rows + 32 : rows + 64, 128 * q : 128 * q + 128] = odd

    if not last:
        grad_piece(0)
    yield

    normal = jnp.where(present, normed * gain + offset, 0.0).astype(BF)
    rhs_out[:, 0:128] = normal
    rhs_out[:, 128:256] = normed.astype(BF)
    masked = jnp.concatenate(
        [
            jnp.concatenate([normal[128 * g : 128 * g + 128] for g in (2 * h, 2 * h + 1)], axis=1)
            for h in range(2)
        ],
        axis=0,
    )
    lefts = mm_nt(masked, back_ref[:128, :]).astype(BF)
    sides = mm_nt(back_ref[...], masked)
    for h in range(2):
        at = slice(128 * h, 128 * h + 128)
        left_out[:, at] = lefts[at]
        both = sides[:, at]
        turn_scr[at, :] = both[128:]
        for k in range(2):
            leftt_out[64 * h + 32 * k : 64 * h + 32 * k + 32, :] = jnp.concatenate(
                [both[32 * k : 32 * k + 32], both[32 * k + 64 : 32 * k + 96]], axis=1
            ).astype(BF)
    yield
    if not last:
        grad_piece(1)
    yield
    for e in range(32):
        rightt_out[e] = turn_scr[pl.ds(e, 8, stride=32), :]
    if last:
        grad_piece(0)
        grad_piece(1)


def stage_kernel(*arguments):
    for _ in stage_steps(*arguments):
        pass


def own_kernel(n_col, place_ref, front_ref, rear_ref, norm_ref, back_ref, final_ref, *rest):
    stage_kernel(n_col, 0, False, place_ref, (front_ref, rear_ref), norm_ref, back_ref, final_ref, *rest)


def pair_kernel(n_col, place_ref, core_ref, front_ref, rear_ref, norm_ref, back_ref, final_ref, *rest):
    common = (norm_ref, back_ref, final_ref)
    both = (
        stage_steps(n_col, 1, False, place_ref, (core_ref,), *common, *rest[:7], rest[14]),
        stage_steps(n_col, 2, False, place_ref, (front_ref, rear_ref), *common, *rest[7:14], rest[15]),
    )
    for _ in zip_longest(*both):
        pass


def part_kernel(n_row, n_col, place_ref, front_ref, rear_ref, *refs):
    stages = [refs[7 * a : 7 * a + 7] for a in range(n_row - 1)]
    (
        normed_ref, inverse_ref, norm_ref, back_ref, final_ref, first_ref,
        emb_out, final_hbm_out, first_out, second_out, gain_out, offset_out, bias_out,
        right_scr, scaled_scr, grad_scr, outer_scr, wide_scr, all_scr,
        final_out, out_sem, turn_scr,
    ) = refs[7 * (n_row - 1) : -7]
    stages.append(refs[-7:])
    stage_kernel(
        n_col, n_row - 1, True, place_ref, (front_ref, rear_ref),
        norm_ref, back_ref, final_ref, *stages[-1], turn_scr,
    )
    gain = norm_ref[0:1, :]
    averager = averager_of()
    lane = lax.broadcasted_iota(jnp.int32, (128, 128), 1)

    found = sum(stage[6][...] for stage in stages)
    turned = pltpu.roll(found, 64, 1)
    mask = jnp.where((lane % 2 == 0) == (lane < 64), found, turned)
    mask_t = mask.T

    for e in range(32):
        right_scr[32 * e : 32 * e + 32, :] = jnp.concatenate(
            [stage[3][e] for stage in stages], axis=0
        ).astype(BF)

    mask_bf = mask.astype(BF)
    share = (1.0 / (mm_tn(mask_bf, mask_bf)[0:32] + 0.001)).astype(BF)
    for i in range(32):
        a, at = i // 8, 32 * (i % 8)
        for q in range(8):
            grad_scr[32 * i : 32 * i + 32, 128 * q : 128 * q + 128] = (
                stages[a][4][at : at + 32, 128 * q : 128 * q + 128] * share[i : i + 1]
            )
    left = jnp.concatenate([stage[1][...] for stage in stages], axis=1)
    right_grad = mm(left, grad_scr[...])
    left_grad = mm(grad_scr[...], right_scr[...])

    turn = spread(
        256, 256, lambda r, c: jnp.where((r // 8 == c % 32) & (r % 8 == c // 32), 1.0, 0.0)
    ).astype(BF)
    mask_two = jnp.concatenate([mask, mask], axis=1)
    right_in = [
        mm_nt(turn, (right_grad[:, 256 * q : 256 * q + 256] * mask_two).astype(BF))
        for q in range(4)
    ]
    for t in range(32):
        at = slice(128 * (t // 2), 128 * (t // 2) + 128)
        row = 32 * (t % 2)
        all_scr[row : row + 32, at] = (
            left_grad[32 * t : 32 * t + 32] * mask_t[t : t + 1]
        ).astype(BF)
        all_scr[row + 64 : row + 96, at] = jnp.concatenate(
            [part[8 * t : 8 * t + 8] for part in right_in], axis=0
        ).astype(BF)

    both_on = jnp.concatenate(
        [mask_t[0:32] * mask_t[i : i + 1] for i in range(32)], axis=0
    ).astype(BF)
    counts = mm(both_on, jnp.ones((128, 128), BF))
    pair = jnp.concatenate([stage[5][...].reshape(256, 128) for stage in stages], axis=0)
    scaled = pair / (counts + 0.001)
    scaled_scr[...] = scaled.astype(BF)
    bias_out[...] = jnp.sum(scaled, axis=0, keepdims=True)

    left_t = jnp.concatenate([stage[2][...] for stage in stages], axis=0)
    for n in range(8):
        rights = jnp.concatenate(
            [diagonal_pair(right_scr[64 * p : 64 * p + 64, :]) for p in (2 * n, 2 * n + 1)], axis=0
        )
        outer = mm_nt(left_t, rights).astype(BF)
        for p in range(2):
            for q in range(8):
                rows = 64 * (2 * n + p)
                block = outer[64 * q : 64 * q + 64, 128 * p : 128 * p + 128]
                even, odd = interleave(block[:32], block[32:])
                outer_scr[rows : rows + 32, 128 * q : 128 * q + 128] = even
                outer_scr[rows + 32 : rows + 64, 128 * q : 128 * q + 128] = odd
    wide_scr[...] = mm(outer_scr[...], scaled_scr[...])
    for c in range(32):
        final_out[32 * c : 32 * c + 32, :] = wide_scr[pl.ds(c, 32, stride=32), :]
    final_send = pltpu.make_async_copy(final_out, final_hbm_out, out_sem)
    final_send.start()

    total = mm(
        all_scr[...], jnp.concatenate([stage[0][...] for stage in stages], axis=0)
    )
    sums = all_scr[:, 0:128].astype(F32)
    for g in range(1, 16):
        sums = sums + all_scr[:, 128 * g : 128 * g + 128].astype(F32)

    def fold(block):
        return block[0:32, 0:64] + block[32:64, 64:128]

    first_out[...] = fold(total[0:64, 0:128])
    second_out[...] = fold(total[64:128, 0:128])
    sums = jnp.sum(sums, axis=1, keepdims=True)
    left_sum = sums[0:32] + sums[32:64]
    right_sum = sums[64:96] + sums[96:128]
    first, second = first_ref[0:32, :], first_ref[32:64, :]
    gain_out[...] = jnp.sum(
        first * fold(total[0:64, 128:256]) + second * fold(total[64:128, 128:256]),
        axis=0, keepdims=True,
    )
    offset_out[...] = jnp.sum(first * left_sum + second * right_sum, axis=0, keepdims=True)

    grads = jnp.concatenate(
        [
            jnp.concatenate(
                [
                    all_scr[row : row + 64, 128 * g : 128 * g + 128]
                    for row in (0, 64)
                    for g in (2 * h, 2 * h + 1)
                ],
                axis=0,
            )
            for h in range(2)
        ],
        axis=1,
    )
    d_normal = mm_tn(grads, back_ref[...])
    d_hat = jnp.concatenate(
        [
            d_normal[128 * h : 128 * h + 32, 128 * half : 128 * half + 128] * gain
            for h in range(2)
            for half in range(2)
        ],
        axis=0,
    )
    normed = normed_ref[...]
    means = mm(jnp.concatenate([d_hat, d_hat * normed], axis=0).astype(BF), averager)
    result = inverse_ref[...] * (d_hat - means[:128] - normed * means[128:])
    for g in range(4):
        emb_out[:, 2 * g, :] = result[32 * g : 32 * g + 32, 0:64]
        emb_out[:, 2 * g + 1, :] = result[32 * g : 32 * g + 32, 64:128]
    final_send.wait()


def vmem(count):
    return [pl.BlockSpec(memory_space=pltpu.VMEM)] * count


LIMIT = pltpu.CompilerParams(vmem_limit_bytes=32 * 1024 * 1024)


def gathered_body(
    n_row,
    n_col,
    homolog_embedding,
    presence_indicator,
    coupling_change_derivative,
    standardizer_scale,
    standardizer_shift,
    first_projection_matrix,
    second_projection_matrix,
    final_projection_matrix,
):
    shards, tokens, features = homolog_embedding.shape
    width = first_projection_matrix.shape[1]
    first_t, second_t = first_projection_matrix.T, second_projection_matrix.T
    shape = lambda *dims: jax.ShapeDtypeStruct(dims, F32)
    held = lambda *dims: pltpu.VMEM(dims, F32)
    held_bf = lambda *dims: pltpu.VMEM(dims, BF)
    hbm = pl.BlockSpec(memory_space=pltpu.HBM)
    place = lax.bitwise_xor(lax.axis_index("row"), lax.axis_index("col"))
    place = place.astype(jnp.int32).reshape(1)
    packed = pl.pallas_call(
        pack_kernel,
        out_shape=held_bf(192, 128),
        in_specs=vmem(3),
        out_specs=vmem(1)[0],
    )(homolog_embedding, presence_indicator.T, coupling_change_derivative)
    def over(axis, size, step, array):
        return lax.ppermute(array, axis, [(k, k ^ step) for k in range(size)])

    far = over("col", n_col, 2, packed)
    near = over("col", n_col, 1, packed)
    last = over("col", n_col, 3, packed)
    front = jnp.stack([packed, far])
    chip_front = over("row", n_row, 2, front)
    rear = jnp.stack([near, last])
    chip_rear = over("row", n_row, 2, rear)
    front, final_projection_matrix = lax.optimization_barrier((front, final_projection_matrix))
    weights = pl.pallas_call(
        weights_kernel,
        out_shape=(
            held(8, 128), held_bf(256, 256), held_bf(width * width // 2, 256), held(2 * width, features),
        ),
        in_specs=[hbm] * 5,
        out_specs=tuple(vmem(4)),
        scratch_shapes=[
            pltpu.VMEM((1, features), F32),
            pltpu.VMEM((1, features), F32),
            pltpu.VMEM((width, features), BF),
            pltpu.VMEM((width, features), BF),
            pltpu.VMEM((width * width, 128), BF),
            pltpu.VMEM((width * width, 128), F32),
            pltpu.SemaphoreType.DMA((5,)),
        ],
        compiler_params=LIMIT,
    )(
        *[
            pltpu.with_memory_space_constraint(x, pltpu.HBM)
            for x in (
                standardizer_scale.reshape(1, features),
                standardizer_shift.reshape(1, features),
                first_t,
                second_t,
                final_projection_matrix,
            )
        ]
    )
    norm, back, final_turned, first = weights
    own = jnp.concatenate([front, rear])
    own, chip_front, norm = lax.optimization_barrier((own, chip_front, norm))
    core = over("row", n_row, 1, own)
    stage_outs = [
        held_bf(512, 256), held_bf(128, 256), held_bf(128, 256), held(width, 8, 128),
        held_bf(256, 1024), held(8, 32, 128), held(128, 128),
    ]
    scalar = pl.BlockSpec(memory_space=pltpu.SMEM)

    def stages_of(kernel, sets, outs, flops):
        return pl.pallas_call(
            functools.partial(kernel, n_col),
            out_shape=tuple(outs),
            in_specs=[scalar] + vmem(len(sets) + 3),
            out_specs=tuple(vmem(len(outs))),
            scratch_shapes=[pltpu.VMEM((256, 128), F32)] * (len(outs) // 7),
            compiler_params=LIMIT,
            cost_estimate=pl.CostEstimate(
                flops=flops, bytes_accessed=flops // 256, transcendentals=0
            ),
        )(place, *sets, norm, back, final_turned)

    both_front = over("row", n_row, 1, chip_front)
    own_stage = stages_of(own_kernel, (front, rear), stage_outs + [held(128, 128)] * 2, 1_000_000_000)
    chip_rear, own_stage = lax.optimization_barrier((chip_rear, own_stage))
    both_rear = over("row", n_row, 1, chip_rear)
    pair_stages = stages_of(pair_kernel, (core, chip_front, chip_rear), stage_outs * 2, 1000000)
    stages = [own_stage[:7], pair_stages]
    outs = pl.pallas_call(
        functools.partial(part_kernel, n_row, n_col),
        out_shape=(
            shape(shards, tokens, features),
            shape(width * width, 128),
            shape(width, features),
            shape(width, features),
            shape(1, features),
            shape(1, features),
            shape(1, 128),
        ),
        in_specs=[scalar] + vmem(7 * (n_row - 1) + 8),
        out_specs=(*vmem(1), hbm, *vmem(5)),
        scratch_shapes=[
            pltpu.VMEM((1024, 128), BF),
            pltpu.VMEM((1024, 128), BF),
            pltpu.VMEM((1024, 1024), BF),
            pltpu.VMEM((1024, 1024), BF),
            pltpu.VMEM((1024, 128), F32),
            pltpu.VMEM((128, 2048), BF),
            pltpu.VMEM((1024, 128), F32),
            pltpu.SemaphoreType.DMA,
            pltpu.VMEM((256, 128), F32),
            *stage_outs,
        ],
        compiler_params=LIMIT,
    )(place, both_front, both_rear, *[x for s in stages for x in s], *own_stage[7:], norm, back, final_turned, first)
    emb, final, first, second, gain, offset, bias = outs
    return emb, final, first.T, second.T, gain.reshape(-1), offset.reshape(-1), bias.reshape(-1)


def body(n_row, n_col, *arguments):
    msa, _, pair = arguments[:3]
    width = arguments[5].shape[1]
    fits = (
        n_row == 4
        and n_col == 4
        and msa.shape == (32, 8, 64)
        and pair.shape == (8, 8, 128)
        and width == 32
    )
    if fits:
        return gathered_body(n_row, n_col, *arguments)
    return sharded_body(*arguments)


def solution(mesh):
    placed = (
        P(("grp", "col"), "row", None),
        P(("grp", "col"), "row"),
        P(("grp", "row"), "col", None),
        P(),
        P(),
        P(),
        P(),
        P(),
    )
    return jax.shard_map(
        functools.partial(body, mesh.shape["row"], mesh.shape["col"]),
        mesh=mesh,
        in_specs=placed,
        out_specs=(
            P(("grp", "col"), "row", None),
            P("grp", None),
            P("grp", None),
            P("grp", None),
            P("grp"),
            P("grp"),
            P("grp"),
        ),
        check_vma=False,
    )
```

```python
import functools
from itertools import zip_longest

import jax
import jax.numpy as jnp
from jax import lax
from jax.experimental import pallas as pl
from jax.experimental.pallas import tpu as pltpu
from jax.sharding import PartitionSpec as P

TOKB = 2


def standardizer_parts(homolog_embedding, standardizer_scale, standardizer_shift):
    incoming_entries = homolog_embedding.astype(jnp.float32)
    center = jnp.mean(incoming_entries, axis=-1, keepdims=True)
    varied = incoming_entries - center
    variance = jnp.mean(varied * varied, axis=-1, keepdims=True)
    reciprocal_spread = lax.rsqrt(variance + 1e-05)
    standardized_entries = varied * reciprocal_spread
    standardized_bfloat = (standardized_entries * standardizer_scale + standardizer_shift).astype(
        jnp.bfloat16
    )
    return (standardized_entries, reciprocal_spread, standardized_bfloat)


def sharded_body(
    homolog_embedding,
    presence_indicator,
    coupling_change_derivative,
    standardizer_scale,
    standardizer_shift,
    first_projection_matrix,
    second_projection_matrix,
    final_projection_matrix,
):
    shard_homolog_number, residue_line_number, feature_number = homolog_embedding.shape
    tok_cols = coupling_change_derivative.shape[1]
    width = first_projection_matrix.shape[1]
    standardized_entries, reciprocal_spread, standardized_bfloat = standardizer_parts(
        homolog_embedding, standardizer_scale, standardizer_shift
    )
    mask_single_precision = presence_indicator.astype(jnp.float32)
    mask_half_precision = presence_indicator.astype(jnp.bfloat16)
    left = (
        jnp.einsum(
            "sic,cp->sip",
            standardized_bfloat,
            first_projection_matrix,
            preferred_element_type=jnp.float32,
        )
        * mask_single_precision[..., None]
    ).astype(jnp.bfloat16)
    right = (
        jnp.einsum(
            "sic,cp->sip",
            standardized_bfloat,
            second_projection_matrix,
            preferred_element_type=jnp.float32,
        )
        * mask_single_precision[..., None]
    ).astype(jnp.bfloat16)
    left_flat = left.reshape(shard_homolog_number, residue_line_number * width)
    right_flat = right.reshape(shard_homolog_number, residue_line_number * width)
    left_all, mask_left = (
        lax.all_gather(left_flat, "col", axis=0, tiled=True),
        lax.all_gather(mask_half_precision, "col", axis=0, tiled=True),
    )
    right_wide, mask_wide = (
        lax.all_gather(right_flat, "row", axis=1, tiled=True),
        lax.all_gather(mask_half_precision, "row", axis=1, tiled=True),
    )
    right_all, mask_right = (
        lax.all_to_all(right_wide, "col", split_axis=1, concat_axis=0, tiled=True),
        lax.all_to_all(mask_wide, "col", split_axis=1, concat_axis=0, tiled=True),
    )
    seq_total = left_all.shape[0]
    right_three = right_all.reshape(seq_total, tok_cols, width)
    counts = jnp.einsum("si,sj->ij", mask_left, mask_right, preferred_element_type=jnp.float32)
    scaled = coupling_change_derivative.astype(jnp.float32) / (counts + 0.001)[..., None]
    bias_part = jnp.sum(scaled, axis=(0, 1))
    scaled_bf = scaled.astype(jnp.bfloat16)
    block_rows = residue_line_number // TOKB
    right_acc = jnp.zeros((seq_total, tok_cols, width), jnp.float32)
    wout_acc = jnp.zeros(final_projection_matrix.shape, jnp.float32)
    left_pieces = []
    for block_index in range(TOKB):
        first = block_index * block_rows
        rows_bf = scaled_bf[first : first + block_rows]
        outer_grad = jnp.einsum(
            "ijz,fz->ijf", rows_bf, final_projection_matrix, preferred_element_type=jnp.float32
        ).astype(jnp.bfloat16)
        outer_grad = outer_grad.reshape(block_rows, tok_cols, width, width)
        left_block = left_all[:, first * width : (first + block_rows) * width].reshape(
            seq_total, block_rows, width
        )
        first_factor_derivative = jnp.einsum(
            "ijce,sje->sic", outer_grad, right_three, preferred_element_type=jnp.float32
        )
        right_acc = right_acc + jnp.einsum(
            "ijce,sic->sje", outer_grad, left_block, preferred_element_type=jnp.float32
        )
        outer = jnp.einsum(
            "sic,sje->ijce", left_block, right_three, preferred_element_type=jnp.float32
        ).astype(jnp.bfloat16)
        outer = outer.reshape(block_rows, tok_cols, width * width)
        wout_acc = wout_acc + jnp.einsum(
            "ijf,ijz->fz", outer, rows_bf, preferred_element_type=jnp.float32
        )
        first_factor_derivative = first_factor_derivative.reshape(seq_total, block_rows * width)
        left_pieces.append(first_factor_derivative)
    left_terms = jnp.concatenate(left_pieces, axis=1)
    left_own = lax.psum_scatter(left_terms, "col", scatter_dimension=0, tiled=True)
    right_spread = lax.all_to_all(
        right_acc.reshape(seq_total, tok_cols * width),
        "col",
        split_axis=0,
        concat_axis=1,
        tiled=True,
    )
    right_own = lax.psum_scatter(right_spread, "row", scatter_dimension=1, tiled=True)
    left_in = (
        left_own.reshape(shard_homolog_number, residue_line_number, width)
        * mask_single_precision[..., None]
    ).astype(jnp.bfloat16)
    right_in = (
        right_own.reshape(shard_homolog_number, residue_line_number, width)
        * mask_single_precision[..., None]
    ).astype(jnp.bfloat16)
    left_part = jnp.einsum(
        "sic,sip->cp", standardized_bfloat, left_in, preferred_element_type=jnp.float32
    )
    right_part = jnp.einsum(
        "sic,sip->cp", standardized_bfloat, right_in, preferred_element_type=jnp.float32
    )
    d_normal = jnp.einsum(
        "sip,cp->sic", left_in, first_projection_matrix, preferred_element_type=jnp.float32
    ) + jnp.einsum(
        "sip,cp->sic", right_in, second_projection_matrix, preferred_element_type=jnp.float32
    )
    gain_part = jnp.sum(d_normal * standardized_entries, axis=(0, 1))
    beta_part = jnp.sum(d_normal, axis=(0, 1))
    standardized_derivative = d_normal * standardizer_scale
    embedding_derivative = reciprocal_spread * (
        standardized_derivative
        - jnp.mean(standardized_derivative, axis=-1, keepdims=True)
        - standardized_entries
        * jnp.mean(standardized_derivative * standardized_entries, axis=-1, keepdims=True)
    )
    (
        final_matrix_derivative,
        first_matrix_derivative,
        second_matrix_derivative,
        scale_factor_derivative,
        shift_term_derivative,
        shift_derivative,
    ) = lax.psum((wout_acc, left_part, right_part, gain_part, beta_part, bias_part), ("row", "col"))
    return (
        embedding_derivative,
        final_matrix_derivative,
        first_matrix_derivative,
        second_matrix_derivative,
        scale_factor_derivative,
        shift_term_derivative,
        shift_derivative,
    )


BF = jnp.bfloat16
F32 = jnp.float32


def spread(rows, cols, rule):
    r = lax.broadcasted_iota(jnp.int32, (rows, cols), 0)
    c = lax.broadcasted_iota(jnp.int32, (rows, cols), 1)
    return rule(r, c)


def mm(a, b):
    return jnp.dot(a, b, preferred_element_type=F32)


def mm_nt(a, b):
    return lax.dot_general(a, b, (((1,), (1,)), ((), ())), preferred_element_type=F32)


def mm_tn(a, b):
    return lax.dot_general(a, b, (((0,), (0,)), ((), ())), preferred_element_type=F32)


def interleave(first, second):
    odd = lax.broadcasted_iota(jnp.int16, (32, 128), 1) & 32 != 0
    return (
        jnp.where(odd, pltpu.roll(second, 32, 1), first),
        jnp.where(odd, second, pltpu.roll(first, 96, 1)),
    )


def diagonal_pair(block):
    zero = jnp.zeros_like(block)
    return jnp.concatenate(
        [jnp.concatenate([block, zero], axis=1), jnp.concatenate([zero, block], axis=1)], axis=0
    )


ABSENT = 1024.0


def pack_kernel(msa_ref, mask_ref, pair_ref, out_ref):
    msa = msa_ref[...].astype(F32)
    pick = spread(8, 512, lambda r, c: jnp.where(c // 64 == r, 1.0, 0.0)).astype(BF)
    present = mm_tn(mask_ref[...].astype(F32).astype(BF), pick) > 0.5
    for g in range(4):
        rows = jnp.concatenate([msa[:, 2 * g, :], msa[:, 2 * g + 1, :]], axis=1)
        out_ref[32 * g : 32 * g + 32, :] = jnp.where(
            present[:, 128 * g : 128 * g + 128], rows, ABSENT
        ).astype(BF)
    out_ref[128:192, :] = pair_ref[...].astype(F32).reshape(64, 128).astype(BF)


def weights_kernel(*refs):
    sources, (norm_out, back_out, final_out, first_out) = refs[:5], refs[5:9]
    held, scr, sems = refs[9:14], refs[14], refs[15]
    copies = [pltpu.make_async_copy(sources[k], held[k], sems.at[k]) for k in range(5)]
    for copy in copies:
        copy.start()
    for copy in copies:
        copy.wait()
    gain_ref, offset_ref, first_ref, second_ref, final_ref = held
    norm_out[...] = jnp.concatenate(
        [
            jnp.concatenate([ref[...]] * 2, axis=1)
            for ref in (gain_ref, offset_ref, gain_ref, offset_ref) * 2
        ],
        axis=0,
    )
    for k, ref in enumerate((first_ref, second_ref)):
        narrow = ref[...].astype(F32)
        first_out[32 * k : 32 * k + 32, :] = narrow
        wide = jnp.concatenate([narrow] * 4, axis=1)
        wide = jnp.concatenate([wide] * 4, axis=0)
        own = spread(128, 256, lambda r, c: r // 32 == c // 64)
        back_out[128 * k : 128 * k + 128, :] = jnp.where(own, wide, 0.0).astype(BF)
    scr[...] = final_ref[...].astype(F32)
    for k in range(16):
        e = 4 * (k // 2) + k % 2
        final_out[32 * k : 32 * k + 32, :] = jnp.concatenate(
            [scr[pl.ds(e, 32, stride=32), :], scr[pl.ds(e + 2, 32, stride=32), :]], axis=1
        ).astype(BF)


def averager_of():
    return spread(128, 128, lambda r, c: jnp.where(r // 64 == c // 64, 1.0 / 64, 0.0)).astype(BF)


ORDER = (0, 2, 1, 3)


def stage_steps(
    n_col, a, last, place_ref, set_refs, norm_ref, back_ref, final_ref,
    rhs_out, left_out, leftt_out, rightt_out, grad_out, pair_out, found_out, *rest
):
    *own_out, turn_scr = rest
    blocks = [ref.at[k] for ref in set_refs for k in range(ref.shape[0])]

    gain = norm_ref[0:1, :]
    offset = norm_ref[1:2, :]
    averager = averager_of()
    x = jnp.concatenate(
        [blocks[b][32 * g : 32 * g + 32, :] for g in range(4) for b in range(n_col)], axis=0
    )
    mean = mm(x, averager)
    present = mean < ABSENT / 2
    here = jnp.where(present, 1.0, 0.0)
    lane = lax.broadcasted_iota(jnp.int32, (128, 128), 1)
    found = jnp.zeros((128, 128), F32)
    for g in range(4):
        found = jnp.where(lane % 32 // 2 == 4 * a + g, here[128 * g : 128 * g + 128], found)
    found_out[...] = found
    for b in range(n_col):
        at = pl.multiple_of(lax.bitwise_xor(place_ref[0], ORDER[b]) * 8, 8)
        pair_out[:, pl.ds(at, 8), :] = blocks[b][128:192, :].astype(F32).reshape(8, 8, 128)
    yield
    varied = x.astype(F32) - mean
    inverse = lax.rsqrt(mm((varied * varied).astype(BF), averager) + 1e-05)
    normed = varied * inverse
    if own_out:
        for g in range(4):
            own_out[0][32 * g : 32 * g + 32, :] = normed[128 * g : 128 * g + 32]
            own_out[1][32 * g : 32 * g + 32, :] = inverse[128 * g : 128 * g + 32]
    yield

    def grad_piece(n):
        pair = pair_out[4 * n : 4 * n + 4].reshape(128, 128).astype(BF)
        pairs = jnp.concatenate([diagonal_pair(pair[:64]), diagonal_pair(pair[64:])], axis=0)
        grad = mm_nt(final_ref[...], pairs).astype(BF)
        for p in range(2):
            for q in range(8):
                rows = 64 * (2 * n + p)
                block = grad[64 * q : 64 * q + 64, 128 * p : 128 * p + 128]
                even, odd = interleave(block[:32], block[32:])
                grad_out[rows : rows + 32, 128 * q : 128 * q + 128] = even
                grad_out[rows + 32 : rows + 64, 128 * q : 128 * q + 128] = odd

    if not last:
        grad_piece(0)
    yield

    normal = jnp.where(present, normed * gain + offset, 0.0).astype(BF)
    rhs_out[:, 0:128] = normal
    rhs_out[:, 128:256] = normed.astype(BF)
    masked = jnp.concatenate(
        [
            jnp.concatenate([normal[128 * g : 128 * g + 128] for g in (2 * h, 2 * h + 1)], axis=1)
            for h in range(2)
        ],
        axis=0,
    )
    lefts = mm_nt(masked, back_ref[:128, :]).astype(BF)
    sides = mm_nt(back_ref[...], masked)
    for h in range(2):
        at = slice(128 * h, 128 * h + 128)
        left_out[:, at] = lefts[at]
        both = sides[:, at]
        turn_scr[at, :] = both[128:]
        for k in range(2):
            leftt_out[64 * h + 32 * k : 64 * h + 32 * k + 32, :] = jnp.concatenate(
                [both[32 * k : 32 * k + 32], both[32 * k + 64 : 32 * k + 96]], axis=1
            ).astype(BF)
    yield
    if not last:
        grad_piece(1)
    yield
    for e in range(32):
        rightt_out[e] = turn_scr[pl.ds(e, 8, stride=32), :]
    if last:
        grad_piece(0)
        grad_piece(1)


def stage_kernel(*arguments):
    for _ in stage_steps(*arguments):
        pass


def own_kernel(n_col, place_ref, front_ref, rear_ref, norm_ref, back_ref, final_ref, *rest):
    stage_kernel(n_col, 0, False, place_ref, (front_ref, rear_ref), norm_ref, back_ref, final_ref, *rest)


def pair_kernel(n_col, place_ref, core_ref, front_ref, rear_ref, norm_ref, back_ref, final_ref, *rest):
    common = (norm_ref, back_ref, final_ref)
    both = (
        stage_steps(n_col, 1, False, place_ref, (core_ref,), *common, *rest[:7], rest[14]),
        stage_steps(n_col, 2, False, place_ref, (front_ref, rear_ref), *common, *rest[7:14], rest[15]),
    )
    for _ in zip_longest(*both):
        pass


def part_kernel(n_row, n_col, place_ref, front_ref, rear_ref, *refs):
    stages = [refs[7 * a : 7 * a + 7] for a in range(n_row - 1)]
    (
        normed_ref, inverse_ref, norm_ref, back_ref, final_ref, first_ref,
        emb_out, final_hbm_out, first_out, second_out, gain_out, offset_out, bias_out,
        right_scr, scaled_scr, grad_scr, outer_scr, wide_scr, all_scr,
        final_out, out_sem, turn_scr,
    ) = refs[7 * (n_row - 1) : -7]
    stages.append(refs[-7:])
    stage_kernel(
        n_col, n_row - 1, True, place_ref, (front_ref, rear_ref),
        norm_ref, back_ref, final_ref, *stages[-1], turn_scr,
    )
    gain = norm_ref[0:1, :]
    averager = averager_of()
    lane = lax.broadcasted_iota(jnp.int32, (128, 128), 1)

    found = sum(stage[6][...] for stage in stages)
    turned = pltpu.roll(found, 64, 1)
    mask = jnp.where((lane % 2 == 0) == (lane < 64), found, turned)
    mask_t = mask.T

    for e in range(32):
        right_scr[32 * e : 32 * e + 32, :] = jnp.concatenate(
            [stage[3][e] for stage in stages], axis=0
        ).astype(BF)

    mask_bf = mask.astype(BF)
    share = (1.0 / (mm_tn(mask_bf, mask_bf)[0:32] + 0.001)).astype(BF)
    for i in range(32):
        a, at = i // 8, 32 * (i % 8)
        for q in range(8):
            grad_scr[32 * i : 32 * i + 32, 128 * q : 128 * q + 128] = (
                stages[a][4][at : at + 32, 128 * q : 128 * q + 128] * share[i : i + 1]
            )
    left = jnp.concatenate([stage[1][...] for stage in stages], axis=1)
    right_grad = mm(left, grad_scr[...])
    left_grad = mm(grad_scr[...], right_scr[...])

    turn = spread(
        256, 256, lambda r, c: jnp.where((r // 8 == c % 32) & (r % 8 == c // 32), 1.0, 0.0)
    ).astype(BF)
    mask_two = jnp.concatenate([mask, mask], axis=1)
    right_in = [
        mm_nt(turn, (right_grad[:, 256 * q : 256 * q + 256] * mask_two).astype(BF))
        for q in range(4)
    ]
    for t in range(32):
        at = slice(128 * (t // 2), 128 * (t // 2) + 128)
        row = 32 * (t % 2)
        all_scr[row : row + 32, at] = (
            left_grad[32 * t : 32 * t + 32] * mask_t[t : t + 1]
        ).astype(BF)
        all_scr[row + 64 : row + 96, at] = jnp.concatenate(
            [part[8 * t : 8 * t + 8] for part in right_in], axis=0
        ).astype(BF)

    bias = jnp.zeros((1, 128), F32)
    ones = jnp.ones((128, 128), BF)
    for p in range(8):
        both_on = jnp.concatenate(
            [mask_t[0:32] * mask_t[i : i + 1] for i in range(4 * p, 4 * p + 4)], axis=0
        ).astype(BF)
        counts = mm(both_on, ones)
        pair = stages[p // 2][5][4 * (p % 2) : 4 * (p % 2) + 4]
        scaled = pair.reshape(128, 128) / (counts + 0.001)
        bias = bias + jnp.sum(scaled, axis=0, keepdims=True)
        scaled_scr[128 * p : 128 * p + 128, :] = scaled.astype(BF)
    bias_out[...] = bias

    left_t = jnp.concatenate([stage[2][...] for stage in stages], axis=0)
    for n in range(8):
        rights = jnp.concatenate(
            [diagonal_pair(right_scr[64 * p : 64 * p + 64, :]) for p in (2 * n, 2 * n + 1)], axis=0
        )
        outer = mm_nt(left_t, rights).astype(BF)
        for p in range(2):
            for q in range(8):
                rows = 64 * (2 * n + p)
                block = outer[64 * q : 64 * q + 64, 128 * p : 128 * p + 128]
                even, odd = interleave(block[:32], block[32:])
                outer_scr[rows : rows + 32, 128 * q : 128 * q + 128] = even
                outer_scr[rows + 32 : rows + 64, 128 * q : 128 * q + 128] = odd
    wide_scr[...] = mm(outer_scr[...], scaled_scr[...])
    for c in range(32):
        final_out[32 * c : 32 * c + 32, :] = wide_scr[pl.ds(c, 32, stride=32), :]
    final_send = pltpu.make_async_copy(final_out, final_hbm_out, out_sem)
    final_send.start()

    total = mm(
        all_scr[...], jnp.concatenate([stage[0][...] for stage in stages], axis=0)
    )
    sums = all_scr[:, 0:128].astype(F32)
    for g in range(1, 16):
        sums = sums + all_scr[:, 128 * g : 128 * g + 128].astype(F32)

    def fold(block):
        return block[0:32, 0:64] + block[32:64, 64:128]

    first_out[...] = fold(total[0:64, 0:128])
    second_out[...] = fold(total[64:128, 0:128])
    sums = jnp.sum(sums, axis=1, keepdims=True)
    left_sum = sums[0:32] + sums[32:64]
    right_sum = sums[64:96] + sums[96:128]
    first, second = first_ref[0:32, :], first_ref[32:64, :]
    gain_out[...] = jnp.sum(
        first * fold(total[0:64, 128:256]) + second * fold(total[64:128, 128:256]),
        axis=0, keepdims=True,
    )
    offset_out[...] = jnp.sum(first * left_sum + second * right_sum, axis=0, keepdims=True)

    grads = jnp.concatenate(
        [
            jnp.concatenate(
                [
                    all_scr[row : row + 64, 128 * g : 128 * g + 128]
                    for row in (0, 64)
                    for g in (2 * h, 2 * h + 1)
                ],
                axis=0,
            )
            for h in range(2)
        ],
        axis=1,
    )
    d_normal = mm_tn(grads, back_ref[...])
    d_hat = jnp.concatenate(
        [
            d_normal[128 * h : 128 * h + 32, 128 * half : 128 * half + 128] * gain
            for h in range(2)
            for half in range(2)
        ],
        axis=0,
    )
    normed = normed_ref[...]
    means = mm(jnp.concatenate([d_hat, d_hat * normed], axis=0).astype(BF), averager)
    result = inverse_ref[...] * (d_hat - means[:128] - normed * means[128:])
    for g in range(4):
        emb_out[:, 2 * g, :] = result[32 * g : 32 * g + 32, 0:64]
        emb_out[:, 2 * g + 1, :] = result[32 * g : 32 * g + 32, 64:128]
    final_send.wait()


def vmem(count):
    return [pl.BlockSpec(memory_space=pltpu.VMEM)] * count


LIMIT = pltpu.CompilerParams(vmem_limit_bytes=32 * 1024 * 1024)


def gathered_body(
    n_row,
    n_col,
    homolog_embedding,
    presence_indicator,
    coupling_change_derivative,
    standardizer_scale,
    standardizer_shift,
    first_projection_matrix,
    second_projection_matrix,
    final_projection_matrix,
):
    shards, tokens, features = homolog_embedding.shape
    width = first_projection_matrix.shape[1]
    first_t, second_t = first_projection_matrix.T, second_projection_matrix.T
    shape = lambda *dims: jax.ShapeDtypeStruct(dims, F32)
    held = lambda *dims: pltpu.VMEM(dims, F32)
    held_bf = lambda *dims: pltpu.VMEM(dims, BF)
    hbm = pl.BlockSpec(memory_space=pltpu.HBM)
    place = lax.bitwise_xor(lax.axis_index("row"), lax.axis_index("col"))
    place = place.astype(jnp.int32).reshape(1)
    packed = pl.pallas_call(
        pack_kernel,
        out_shape=held_bf(192, 128),
        in_specs=vmem(3),
        out_specs=vmem(1)[0],
    )(homolog_embedding, presence_indicator.T, coupling_change_derivative)
    def over(axis, size, step, array):
        return lax.ppermute(array, axis, [(k, k ^ step) for k in range(size)])

    far = over("col", n_col, 2, packed)
    near = over("col", n_col, 1, packed)
    last = over("col", n_col, 3, packed)
    front = jnp.stack([packed, far])
    chip_front = over("row", n_row, 2, front)
    rear = jnp.stack([near, last])
    chip_rear = over("row", n_row, 2, rear)
    front, final_projection_matrix = lax.optimization_barrier((front, final_projection_matrix))
    weights = pl.pallas_call(
        weights_kernel,
        out_shape=(
            held(8, 128), held_bf(256, 256), held_bf(width * width // 2, 256), held(2 * width, features),
        ),
        in_specs=[hbm] * 5,
        out_specs=tuple(vmem(4)),
        scratch_shapes=[
            pltpu.VMEM((1, features), F32),
            pltpu.VMEM((1, features), F32),
            pltpu.VMEM((width, features), BF),
            pltpu.VMEM((width, features), BF),
            pltpu.VMEM((width * width, 128), BF),
            pltpu.VMEM((width * width, 128), F32),
            pltpu.SemaphoreType.DMA((5,)),
        ],
        compiler_params=LIMIT,
    )(
        *[
            pltpu.with_memory_space_constraint(x, pltpu.HBM)
            for x in (
                standardizer_scale.reshape(1, features),
                standardizer_shift.reshape(1, features),
                first_t,
                second_t,
                final_projection_matrix,
            )
        ]
    )
    norm, back, final_turned, first = weights
    own = jnp.concatenate([front, rear])
    own, chip_front, norm = lax.optimization_barrier((own, chip_front, norm))
    core = over("row", n_row, 1, own)
    stage_outs = [
        held_bf(512, 256), held_bf(128, 256), held_bf(128, 256), held(width, 8, 128),
        held_bf(256, 1024), held(8, 32, 128), held(128, 128),
    ]
    scalar = pl.BlockSpec(memory_space=pltpu.SMEM)

    def stages_of(kernel, sets, outs, flops):
        return pl.pallas_call(
            functools.partial(kernel, n_col),
            out_shape=tuple(outs),
            in_specs=[scalar] + vmem(len(sets) + 3),
            out_specs=tuple(vmem(len(outs))),
            scratch_shapes=[pltpu.VMEM((256, 128), F32)] * (len(outs) // 7),
            compiler_params=LIMIT,
            cost_estimate=pl.CostEstimate(
                flops=flops, bytes_accessed=flops // 256, transcendentals=0
            ),
        )(place, *sets, norm, back, final_turned)

    both_front = over("row", n_row, 1, chip_front)
    own_stage = stages_of(own_kernel, (front, rear), stage_outs + [held(128, 128)] * 2, 1_000_000_000)
    chip_rear, own_stage = lax.optimization_barrier((chip_rear, own_stage))
    both_rear = over("row", n_row, 1, chip_rear)
    pair_stages = stages_of(pair_kernel, (core, chip_front, chip_rear), stage_outs * 2, 1000000)
    stages = [own_stage[:7], pair_stages]
    outs = pl.pallas_call(
        functools.partial(part_kernel, n_row, n_col),
        out_shape=(
            shape(shards, tokens, features),
            shape(width * width, 128),
            shape(width, features),
            shape(width, features),
            shape(1, features),
            shape(1, features),
            shape(1, 128),
        ),
        in_specs=[scalar] + vmem(7 * (n_row - 1) + 8),
        out_specs=(*vmem(1), hbm, *vmem(5)),
        scratch_shapes=[
            pltpu.VMEM((1024, 128), BF),
            pltpu.VMEM((1024, 128), BF),
            pltpu.VMEM((1024, 1024), BF),
            pltpu.VMEM((1024, 1024), BF),
            pltpu.VMEM((1024, 128), F32),
            pltpu.VMEM((128, 2048), BF),
            pltpu.VMEM((1024, 128), F32),
            pltpu.SemaphoreType.DMA,
            pltpu.VMEM((256, 128), F32),
            *stage_outs,
        ],
        compiler_params=LIMIT,
    )(place, both_front, both_rear, *[x for s in stages for x in s], *own_stage[7:], norm, back, final_turned, first)
    emb, final, first, second, gain, offset, bias = outs
    return emb, final, first.T, second.T, gain.reshape(-1), offset.reshape(-1), bias.reshape(-1)


def body(n_row, n_col, *arguments):
    msa, _, pair = arguments[:3]
    width = arguments[5].shape[1]
    fits = (
        n_row == 4
        and n_col == 4
        and msa.shape == (32, 8, 64)
        and pair.shape == (8, 8, 128)
        and width == 32
    )
    if fits:
        return gathered_body(n_row, n_col, *arguments)
    return sharded_body(*arguments)


def solution(mesh):
    placed = (
        P(("grp", "col"), "row", None),
        P(("grp", "col"), "row"),
        P(("grp", "row"), "col", None),
        P(),
        P(),
        P(),
        P(),
        P(),
    )
    return jax.shard_map(
        functools.partial(body, mesh.shape["row"], mesh.shape["col"]),
        mesh=mesh,
        in_specs=placed,
        out_specs=(
            P(("grp", "col"), "row", None),
            P("grp", None),
            P("grp", None),
            P("grp", None),
            P("grp"),
            P("grp"),
            P("grp"),
        ),
        check_vma=False,
    )
```

```python
import functools
from itertools import zip_longest

import jax
import jax.numpy as jnp
from jax import lax
from jax.experimental import pallas as pl
from jax.experimental.pallas import tpu as pltpu
from jax.sharding import PartitionSpec as P

TOKB = 2


def standardizer_parts(homolog_embedding, standardizer_scale, standardizer_shift):
    incoming_entries = homolog_embedding.astype(jnp.float32)
    center = jnp.mean(incoming_entries, axis=-1, keepdims=True)
    varied = incoming_entries - center
    variance = jnp.mean(varied * varied, axis=-1, keepdims=True)
    reciprocal_spread = lax.rsqrt(variance + 1e-05)
    standardized_entries = varied * reciprocal_spread
    standardized_bfloat = (standardized_entries * standardizer_scale + standardizer_shift).astype(
        jnp.bfloat16
    )
    return (standardized_entries, reciprocal_spread, standardized_bfloat)


def sharded_body(
    homolog_embedding,
    presence_indicator,
    coupling_change_derivative,
    standardizer_scale,
    standardizer_shift,
    first_projection_matrix,
    second_projection_matrix,
    final_projection_matrix,
):
    shard_homolog_number, residue_line_number, feature_number = homolog_embedding.shape
    tok_cols = coupling_change_derivative.shape[1]
    width = first_projection_matrix.shape[1]
    standardized_entries, reciprocal_spread, standardized_bfloat = standardizer_parts(
        homolog_embedding, standardizer_scale, standardizer_shift
    )
    mask_single_precision = presence_indicator.astype(jnp.float32)
    mask_half_precision = presence_indicator.astype(jnp.bfloat16)
    left = (
        jnp.einsum(
            "sic,cp->sip",
            standardized_bfloat,
            first_projection_matrix,
            preferred_element_type=jnp.float32,
        )
        * mask_single_precision[..., None]
    ).astype(jnp.bfloat16)
    right = (
        jnp.einsum(
            "sic,cp->sip",
            standardized_bfloat,
            second_projection_matrix,
            preferred_element_type=jnp.float32,
        )
        * mask_single_precision[..., None]
    ).astype(jnp.bfloat16)
    left_flat = left.reshape(shard_homolog_number, residue_line_number * width)
    right_flat = right.reshape(shard_homolog_number, residue_line_number * width)
    left_all, mask_left = (
        lax.all_gather(left_flat, "col", axis=0, tiled=True),
        lax.all_gather(mask_half_precision, "col", axis=0, tiled=True),
    )
    right_wide, mask_wide = (
        lax.all_gather(right_flat, "row", axis=1, tiled=True),
        lax.all_gather(mask_half_precision, "row", axis=1, tiled=True),
    )
    right_all, mask_right = (
        lax.all_to_all(right_wide, "col", split_axis=1, concat_axis=0, tiled=True),
        lax.all_to_all(mask_wide, "col", split_axis=1, concat_axis=0, tiled=True),
    )
    seq_total = left_all.shape[0]
    right_three = right_all.reshape(seq_total, tok_cols, width)
    counts = jnp.einsum("si,sj->ij", mask_left, mask_right, preferred_element_type=jnp.float32)
    scaled = coupling_change_derivative.astype(jnp.float32) / (counts + 0.001)[..., None]
    bias_part = jnp.sum(scaled, axis=(0, 1))
    scaled_bf = scaled.astype(jnp.bfloat16)
    block_rows = residue_line_number // TOKB
    right_acc = jnp.zeros((seq_total, tok_cols, width), jnp.float32)
    wout_acc = jnp.zeros(final_projection_matrix.shape, jnp.float32)
    left_pieces = []
    for block_index in range(TOKB):
        first = block_index * block_rows
        rows_bf = scaled_bf[first : first + block_rows]
        outer_grad = jnp.einsum(
            "ijz,fz->ijf", rows_bf, final_projection_matrix, preferred_element_type=jnp.float32
        ).astype(jnp.bfloat16)
        outer_grad = outer_grad.reshape(block_rows, tok_cols, width, width)
        left_block = left_all[:, first * width : (first + block_rows) * width].reshape(
            seq_total, block_rows, width
        )
        first_factor_derivative = jnp.einsum(
            "ijce,sje->sic", outer_grad, right_three, preferred_element_type=jnp.float32
        )
        right_acc = right_acc + jnp.einsum(
            "ijce,sic->sje", outer_grad, left_block, preferred_element_type=jnp.float32
        )
        outer = jnp.einsum(
            "sic,sje->ijce", left_block, right_three, preferred_element_type=jnp.float32
        ).astype(jnp.bfloat16)
        outer = outer.reshape(block_rows, tok_cols, width * width)
        wout_acc = wout_acc + jnp.einsum(
            "ijf,ijz->fz", outer, rows_bf, preferred_element_type=jnp.float32
        )
        first_factor_derivative = first_factor_derivative.reshape(seq_total, block_rows * width)
        left_pieces.append(first_factor_derivative)
    left_terms = jnp.concatenate(left_pieces, axis=1)
    left_own = lax.psum_scatter(left_terms, "col", scatter_dimension=0, tiled=True)
    right_spread = lax.all_to_all(
        right_acc.reshape(seq_total, tok_cols * width),
        "col",
        split_axis=0,
        concat_axis=1,
        tiled=True,
    )
    right_own = lax.psum_scatter(right_spread, "row", scatter_dimension=1, tiled=True)
    left_in = (
        left_own.reshape(shard_homolog_number, residue_line_number, width)
        * mask_single_precision[..., None]
    ).astype(jnp.bfloat16)
    right_in = (
        right_own.reshape(shard_homolog_number, residue_line_number, width)
        * mask_single_precision[..., None]
    ).astype(jnp.bfloat16)
    left_part = jnp.einsum(
        "sic,sip->cp", standardized_bfloat, left_in, preferred_element_type=jnp.float32
    )
    right_part = jnp.einsum(
        "sic,sip->cp", standardized_bfloat, right_in, preferred_element_type=jnp.float32
    )
    d_normal = jnp.einsum(
        "sip,cp->sic", left_in, first_projection_matrix, preferred_element_type=jnp.float32
    ) + jnp.einsum(
        "sip,cp->sic", right_in, second_projection_matrix, preferred_element_type=jnp.float32
    )
    gain_part = jnp.sum(d_normal * standardized_entries, axis=(0, 1))
    beta_part = jnp.sum(d_normal, axis=(0, 1))
    standardized_derivative = d_normal * standardizer_scale
    embedding_derivative = reciprocal_spread * (
        standardized_derivative
        - jnp.mean(standardized_derivative, axis=-1, keepdims=True)
        - standardized_entries
        * jnp.mean(standardized_derivative * standardized_entries, axis=-1, keepdims=True)
    )
    (
        final_matrix_derivative,
        first_matrix_derivative,
        second_matrix_derivative,
        scale_factor_derivative,
        shift_term_derivative,
        shift_derivative,
    ) = lax.psum((wout_acc, left_part, right_part, gain_part, beta_part, bias_part), ("row", "col"))
    return (
        embedding_derivative,
        final_matrix_derivative,
        first_matrix_derivative,
        second_matrix_derivative,
        scale_factor_derivative,
        shift_term_derivative,
        shift_derivative,
    )


BF = jnp.bfloat16
F32 = jnp.float32


def spread(rows, cols, rule):
    r = lax.broadcasted_iota(jnp.int32, (rows, cols), 0)
    c = lax.broadcasted_iota(jnp.int32, (rows, cols), 1)
    return rule(r, c)


def mm(a, b):
    return jnp.dot(a, b, preferred_element_type=F32)


def mm_nt(a, b):
    return lax.dot_general(a, b, (((1,), (1,)), ((), ())), preferred_element_type=F32)


def mm_tn(a, b):
    return lax.dot_general(a, b, (((0,), (0,)), ((), ())), preferred_element_type=F32)


def interleave(first, second):
    odd = lax.broadcasted_iota(jnp.int16, (32, 128), 1) & 32 != 0
    return (
        jnp.where(odd, pltpu.roll(second, 32, 1), first),
        jnp.where(odd, second, pltpu.roll(first, 96, 1)),
    )


def diagonal_pair(block):
    zero = jnp.zeros_like(block)
    return jnp.concatenate(
        [jnp.concatenate([block, zero], axis=1), jnp.concatenate([zero, block], axis=1)], axis=0
    )


ABSENT = 1024.0


def pack_kernel(msa_ref, mask_ref, pair_ref, out_ref):
    msa = msa_ref[...].astype(F32)
    pick = spread(8, 512, lambda r, c: jnp.where(c // 64 == r, 1.0, 0.0)).astype(BF)
    present = mm_tn(mask_ref[...].astype(F32).astype(BF), pick) > 0.5
    for g in range(4):
        rows = jnp.concatenate([msa[:, 2 * g, :], msa[:, 2 * g + 1, :]], axis=1)
        out_ref[32 * g : 32 * g + 32, :] = jnp.where(
            present[:, 128 * g : 128 * g + 128], rows, ABSENT
        ).astype(BF)
    out_ref[128:192, :] = pair_ref[...].astype(F32).reshape(64, 128).astype(BF)


def weights_kernel(*refs):
    sources, (norm_out, back_out, final_out, first_out) = refs[:5], refs[5:9]
    held, scr, sems = refs[9:14], refs[14], refs[15]
    copies = [pltpu.make_async_copy(sources[k], held[k], sems.at[k]) for k in range(5)]
    for copy in copies:
        copy.start()
    for copy in copies:
        copy.wait()
    gain_ref, offset_ref, first_ref, second_ref, final_ref = held
    norm_out[...] = jnp.concatenate(
        [
            jnp.concatenate([ref[...]] * 2, axis=1)
            for ref in (gain_ref, offset_ref, gain_ref, offset_ref) * 2
        ],
        axis=0,
    )
    for k, ref in enumerate((first_ref, second_ref)):
        narrow = ref[...].astype(F32)
        first_out[32 * k : 32 * k + 32, :] = narrow
        wide = jnp.concatenate([narrow] * 4, axis=1)
        wide = jnp.concatenate([wide] * 4, axis=0)
        own = spread(128, 256, lambda r, c: r // 32 == c // 64)
        back_out[128 * k : 128 * k + 128, :] = jnp.where(own, wide, 0.0).astype(BF)
    scr[...] = final_ref[...].astype(F32)
    for k in range(16):
        e = 4 * (k // 2) + k % 2
        final_out[32 * k : 32 * k + 32, :] = jnp.concatenate(
            [scr[pl.ds(e, 32, stride=32), :], scr[pl.ds(e + 2, 32, stride=32), :]], axis=1
        ).astype(BF)


def averager_of():
    return spread(128, 128, lambda r, c: jnp.where(r // 64 == c // 64, 1.0 / 64, 0.0)).astype(BF)


ORDER = (0, 2, 1, 3)


def stage_steps(
    n_col, a, last, place_ref, set_refs, norm_ref, back_ref, final_ref,
    rhs_out, left_out, leftt_out, rightt_out, grad_out, pair_out, found_out, *rest
):
    *own_out, turn_scr = rest
    blocks = [ref.at[k] for ref in set_refs for k in range(ref.shape[0])]

    gain = norm_ref[0:1, :]
    offset = norm_ref[1:2, :]
    averager = averager_of()
    x = jnp.concatenate(
        [blocks[b][32 * g : 32 * g + 32, :] for g in range(4) for b in range(n_col)], axis=0
    )
    mean = mm(x, averager)
    present = mean < ABSENT / 2
    here = jnp.where(present, 1.0, 0.0)
    lane = lax.broadcasted_iota(jnp.int32, (128, 128), 1)
    found = jnp.zeros((128, 128), F32)
    for g in range(4):
        found = jnp.where(lane % 32 // 2 == 4 * a + g, here[128 * g : 128 * g + 128], found)
    found_out[...] = found
    for b in range(n_col):
        at = pl.multiple_of(lax.bitwise_xor(place_ref[0], ORDER[b]) * 8, 8)
        pair_out[:, pl.ds(at, 8), :] = blocks[b][128:192, :].astype(F32).reshape(8, 8, 128)
    yield
    varied = x.astype(F32) - mean
    inverse = lax.rsqrt(mm((varied * varied).astype(BF), averager) + 1e-05)
    normed = varied * inverse
    if own_out:
        for g in range(4):
            own_out[0][32 * g : 32 * g + 32, :] = normed[128 * g : 128 * g + 32]
            own_out[1][32 * g : 32 * g + 32, :] = inverse[128 * g : 128 * g + 32]
    yield

    def grad_piece(n):
        pair = pair_out[4 * n : 4 * n + 4].reshape(128, 128).astype(BF)
        pairs = jnp.concatenate([diagonal_pair(pair[:64]), diagonal_pair(pair[64:])], axis=0)
        grad = mm_nt(final_ref[...], pairs).astype(BF)
        for p in range(2):
            for q in range(8):
                rows = 64 * (2 * n + p)
                block = grad[64 * q : 64 * q + 64, 128 * p : 128 * p + 128]
                even, odd = interleave(block[:32], block[32:])
                grad_out[rows : rows + 32, 128 * q : 128 * q + 128] = even
                grad_out[rows + 32 : rows + 64, 128 * q : 128 * q + 128] = odd

    if not last:
        grad_piece(0)
    yield

    normal = jnp.where(present, normed * gain + offset, 0.0).astype(BF)
    rhs_out[:, 0:128] = normal
    rhs_out[:, 128:256] = normed.astype(BF)
    masked = jnp.concatenate(
        [
            jnp.concatenate([normal[128 * g : 128 * g + 128] for g in (2 * h, 2 * h + 1)], axis=1)
            for h in range(2)
        ],
        axis=0,
    )
    lefts = mm_nt(masked, back_ref[:128, :]).astype(BF)
    sides = mm_nt(back_ref[...], masked)
    for h in range(2):
        at = slice(128 * h, 128 * h + 128)
        left_out[:, at] = lefts[at]
        both = sides[:, at]
        turn_scr[at, :] = both[128:]
        for k in range(2):
            leftt_out[64 * h + 32 * k : 64 * h + 32 * k + 32, :] = jnp.concatenate(
                [both[32 * k : 32 * k + 32], both[32 * k + 64 : 32 * k + 96]], axis=1
            ).astype(BF)
    yield
    if not last:
        grad_piece(1)
    yield
    for e in range(32):
        rightt_out[e] = turn_scr[pl.ds(e, 8, stride=32), :]
    if last:
        grad_piece(0)
        grad_piece(1)


def stage_kernel(*arguments):
    for _ in stage_steps(*arguments):
        pass


def own_kernel(n_col, place_ref, front_ref, rear_ref, norm_ref, back_ref, final_ref, *rest):
    stage_kernel(n_col, 0, False, place_ref, (front_ref, rear_ref), norm_ref, back_ref, final_ref, *rest)


def pair_kernel(n_col, place_ref, core_ref, front_ref, rear_ref, norm_ref, back_ref, final_ref, *rest):
    common = (norm_ref, back_ref, final_ref)
    both = (
        stage_steps(n_col, 1, False, place_ref, (core_ref,), *common, *rest[:7], rest[14]),
        stage_steps(n_col, 2, False, place_ref, (front_ref, rear_ref), *common, *rest[7:14], rest[15]),
    )
    for _ in zip_longest(*both):
        pass


def part_kernel(n_row, n_col, place_ref, front_ref, rear_ref, *refs):
    stages = [refs[7 * a : 7 * a + 7] for a in range(n_row - 1)]
    (
        normed_ref, inverse_ref, norm_ref, back_ref, final_ref, first_ref,
        emb_out, final_hbm_out, first_out, second_out, gain_out, offset_out, bias_out,
        right_scr, scaled_scr, grad_scr, outer_scr, wide_scr, all_scr,
        final_out, out_sem, turn_scr,
    ) = refs[7 * (n_row - 1) : -7]
    stages.append(refs[-7:])
    stage_kernel(
        n_col, n_row - 1, True, place_ref, (front_ref, rear_ref),
        norm_ref, back_ref, final_ref, *stages[-1], turn_scr,
    )
    gain = norm_ref[0:1, :]
    averager = averager_of()
    lane = lax.broadcasted_iota(jnp.int32, (128, 128), 1)

    found = sum(stage[6][...] for stage in stages)
    turned = pltpu.roll(found, 64, 1)
    mask = jnp.where((lane % 2 == 0) == (lane < 64), found, turned)
    mask_t = mask.T

    for e in range(32):
        right_scr[32 * e : 32 * e + 32, :] = jnp.concatenate(
            [stage[3][e] for stage in stages], axis=0
        ).astype(BF)

    mask_bf = mask.astype(BF)
    share = (1.0 / (mm_tn(mask_bf, mask_bf)[0:32] + 0.001)).astype(BF)
    for i in range(32):
        a, at = i // 8, 32 * (i % 8)
        for q in range(8):
            grad_scr[32 * i : 32 * i + 32, 128 * q : 128 * q + 128] = (
                stages[a][4][at : at + 32, 128 * q : 128 * q + 128] * share[i : i + 1]
            )
    left = jnp.concatenate([stage[1][...] for stage in stages], axis=1)
    right_grad = mm(left, grad_scr[...])
    left_grad = mm(grad_scr[...], right_scr[...])

    turn = spread(
        256, 256, lambda r, c: jnp.where((r // 8 == c % 32) & (r % 8 == c // 32), 1.0, 0.0)
    ).astype(BF)
    mask_two = jnp.concatenate([mask, mask], axis=1)
    right_in = []
    for h in range(2):
        pieces = [
            (right_grad[:, 256 * q : 256 * q + 256] * mask_two).astype(BF)
            for q in (2 * h, 2 * h + 1)
        ]
        turned = mm_nt(turn, jnp.concatenate(pieces, axis=0))
        right_in += [turned[:, :128], turned[:, 128:]]
    for t in range(32):
        at = slice(128 * (t // 2), 128 * (t // 2) + 128)
        row = 32 * (t % 2)
        all_scr[row : row + 32, at] = (
            left_grad[32 * t : 32 * t + 32] * mask_t[t : t + 1]
        ).astype(BF)
        all_scr[row + 64 : row + 96, at] = jnp.concatenate(
            [part[8 * t : 8 * t + 8] for part in right_in], axis=0
        ).astype(BF)

    bias = jnp.zeros((1, 128), F32)
    ones = jnp.ones((128, 128), BF)
    for p in range(8):
        both_on = jnp.concatenate(
            [mask_t[0:32] * mask_t[i : i + 1] for i in range(4 * p, 4 * p + 4)], axis=0
        ).astype(BF)
        counts = mm(both_on, ones)
        pair = stages[p // 2][5][4 * (p % 2) : 4 * (p % 2) + 4]
        scaled = pair.reshape(128, 128) / (counts + 0.001)
        bias = bias + jnp.sum(scaled, axis=0, keepdims=True)
        scaled_scr[128 * p : 128 * p + 128, :] = scaled.astype(BF)
    bias_out[...] = bias

    left_t = jnp.concatenate([stage[2][...] for stage in stages], axis=0)
    for n in range(8):
        rights = jnp.concatenate(
            [diagonal_pair(right_scr[64 * p : 64 * p + 64, :]) for p in (2 * n, 2 * n + 1)], axis=0
        )
        outer = mm_nt(left_t, rights).astype(BF)
        for p in range(2):
            for q in range(8):
                rows = 64 * (2 * n + p)
                block = outer[64 * q : 64 * q + 64, 128 * p : 128 * p + 128]
                even, odd = interleave(block[:32], block[32:])
                outer_scr[rows : rows + 32, 128 * q : 128 * q + 128] = even
                outer_scr[rows + 32 : rows + 64, 128 * q : 128 * q + 128] = odd
    wide_scr[...] = mm(outer_scr[...], scaled_scr[...])
    for c in range(32):
        final_out[32 * c : 32 * c + 32, :] = wide_scr[pl.ds(c, 32, stride=32), :]
    final_send = pltpu.make_async_copy(final_out, final_hbm_out, out_sem)
    final_send.start()

    total = mm(
        all_scr[...], jnp.concatenate([stage[0][...] for stage in stages], axis=0)
    )
    sums = all_scr[:, 0:128].astype(F32)
    for g in range(1, 16):
        sums = sums + all_scr[:, 128 * g : 128 * g + 128].astype(F32)

    def fold(block):
        return block[0:32, 0:64] + block[32:64, 64:128]

    first_out[...] = fold(total[0:64, 0:128])
    second_out[...] = fold(total[64:128, 0:128])
    sums = jnp.sum(sums, axis=1, keepdims=True)
    left_sum = sums[0:32] + sums[32:64]
    right_sum = sums[64:96] + sums[96:128]
    first, second = first_ref[0:32, :], first_ref[32:64, :]
    gain_out[...] = jnp.sum(
        first * fold(total[0:64, 128:256]) + second * fold(total[64:128, 128:256]),
        axis=0, keepdims=True,
    )
    offset_out[...] = jnp.sum(first * left_sum + second * right_sum, axis=0, keepdims=True)

    grads = jnp.concatenate(
        [
            jnp.concatenate(
                [
                    all_scr[row : row + 64, 128 * g : 128 * g + 128]
                    for row in (0, 64)
                    for g in (2 * h, 2 * h + 1)
                ],
                axis=0,
            )
            for h in range(2)
        ],
        axis=1,
    )
    d_normal = mm_tn(grads, back_ref[...])
    d_hat = jnp.concatenate(
        [
            d_normal[128 * h : 128 * h + 32, 128 * half : 128 * half + 128] * gain
            for h in range(2)
            for half in range(2)
        ],
        axis=0,
    )
    normed = normed_ref[...]
    means = mm(jnp.concatenate([d_hat, d_hat * normed], axis=0).astype(BF), averager)
    result = inverse_ref[...] * (d_hat - means[:128] - normed * means[128:])
    for g in range(4):
        emb_out[:, 2 * g, :] = result[32 * g : 32 * g + 32, 0:64]
        emb_out[:, 2 * g + 1, :] = result[32 * g : 32 * g + 32, 64:128]
    final_send.wait()


def vmem(count):
    return [pl.BlockSpec(memory_space=pltpu.VMEM)] * count


LIMIT = pltpu.CompilerParams(vmem_limit_bytes=32 * 1024 * 1024)


def gathered_body(
    n_row,
    n_col,
    homolog_embedding,
    presence_indicator,
    coupling_change_derivative,
    standardizer_scale,
    standardizer_shift,
    first_projection_matrix,
    second_projection_matrix,
    final_projection_matrix,
):
    shards, tokens, features = homolog_embedding.shape
    width = first_projection_matrix.shape[1]
    first_t, second_t = first_projection_matrix.T, second_projection_matrix.T
    shape = lambda *dims: jax.ShapeDtypeStruct(dims, F32)
    held = lambda *dims: pltpu.VMEM(dims, F32)
    held_bf = lambda *dims: pltpu.VMEM(dims, BF)
    hbm = pl.BlockSpec(memory_space=pltpu.HBM)
    place = lax.bitwise_xor(lax.axis_index("row"), lax.axis_index("col"))
    place = place.astype(jnp.int32).reshape(1)
    packed = pl.pallas_call(
        pack_kernel,
        out_shape=held_bf(192, 128),
        in_specs=vmem(3),
        out_specs=vmem(1)[0],
    )(homolog_embedding, presence_indicator.T, coupling_change_derivative)
    def over(axis, size, step, array):
        return lax.ppermute(array, axis, [(k, k ^ step) for k in range(size)])

    far = over("col", n_col, 2, packed)
    near = over("col", n_col, 1, packed)
    last = over("col", n_col, 3, packed)
    front = jnp.stack([packed, far])
    chip_front = over("row", n_row, 2, front)
    rear = jnp.stack([near, last])
    chip_rear = over("row", n_row, 2, rear)
    front, final_projection_matrix = lax.optimization_barrier((front, final_projection_matrix))
    weights = pl.pallas_call(
        weights_kernel,
        out_shape=(
            held(8, 128), held_bf(256, 256), held_bf(width * width // 2, 256), held(2 * width, features),
        ),
        in_specs=[hbm] * 5,
        out_specs=tuple(vmem(4)),
        scratch_shapes=[
            pltpu.VMEM((1, features), F32),
            pltpu.VMEM((1, features), F32),
            pltpu.VMEM((width, features), BF),
            pltpu.VMEM((width, features), BF),
            pltpu.VMEM((width * width, 128), BF),
            pltpu.VMEM((width * width, 128), F32),
            pltpu.SemaphoreType.DMA((5,)),
        ],
        compiler_params=LIMIT,
    )(
        *[
            pltpu.with_memory_space_constraint(x, pltpu.HBM)
            for x in (
                standardizer_scale.reshape(1, features),
                standardizer_shift.reshape(1, features),
                first_t,
                second_t,
                final_projection_matrix,
            )
        ]
    )
    norm, back, final_turned, first = weights
    own = jnp.concatenate([front, rear])
    own, chip_front, norm = lax.optimization_barrier((own, chip_front, norm))
    core = over("row", n_row, 1, own)
    stage_outs = [
        held_bf(512, 256), held_bf(128, 256), held_bf(128, 256), held(width, 8, 128),
        held_bf(256, 1024), held(8, 32, 128), held(128, 128),
    ]
    scalar = pl.BlockSpec(memory_space=pltpu.SMEM)

    def stages_of(kernel, sets, outs, flops):
        return pl.pallas_call(
            functools.partial(kernel, n_col),
            out_shape=tuple(outs),
            in_specs=[scalar] + vmem(len(sets) + 3),
            out_specs=tuple(vmem(len(outs))),
            scratch_shapes=[pltpu.VMEM((256, 128), F32)] * (len(outs) // 7),
            compiler_params=LIMIT,
            cost_estimate=pl.CostEstimate(
                flops=flops, bytes_accessed=flops // 256, transcendentals=0
            ),
        )(place, *sets, norm, back, final_turned)

    both_front = over("row", n_row, 1, chip_front)
    own_stage = stages_of(own_kernel, (front, rear), stage_outs + [held(128, 128)] * 2, 1_000_000_000)
    chip_rear, own_stage = lax.optimization_barrier((chip_rear, own_stage))
    both_rear = over("row", n_row, 1, chip_rear)
    pair_stages = stages_of(pair_kernel, (core, chip_front, chip_rear), stage_outs * 2, 1000000)
    stages = [own_stage[:7], pair_stages]
    outs = pl.pallas_call(
        functools.partial(part_kernel, n_row, n_col),
        out_shape=(
            shape(shards, tokens, features),
            shape(width * width, 128),
            shape(width, features),
            shape(width, features),
            shape(1, features),
            shape(1, features),
            shape(1, 128),
        ),
        in_specs=[scalar] + vmem(7 * (n_row - 1) + 8),
        out_specs=(*vmem(1), hbm, *vmem(5)),
        scratch_shapes=[
            pltpu.VMEM((1024, 128), BF),
            pltpu.VMEM((1024, 128), BF),
            pltpu.VMEM((1024, 1024), BF),
            pltpu.VMEM((1024, 1024), BF),
            pltpu.VMEM((1024, 128), F32),
            pltpu.VMEM((128, 2048), BF),
            pltpu.VMEM((1024, 128), F32),
            pltpu.SemaphoreType.DMA,
            pltpu.VMEM((256, 128), F32),
            *stage_outs,
        ],
        compiler_params=LIMIT,
    )(place, both_front, both_rear, *[x for s in stages for x in s], *own_stage[7:], norm, back, final_turned, first)
    emb, final, first, second, gain, offset, bias = outs
    return emb, final, first.T, second.T, gain.reshape(-1), offset.reshape(-1), bias.reshape(-1)


def body(n_row, n_col, *arguments):
    msa, _, pair = arguments[:3]
    width = arguments[5].shape[1]
    fits = (
        n_row == 4
        and n_col == 4
        and msa.shape == (32, 8, 64)
        and pair.shape == (8, 8, 128)
        and width == 32
    )
    if fits:
        return gathered_body(n_row, n_col, *arguments)
    return sharded_body(*arguments)


def solution(mesh):
    placed = (
        P(("grp", "col"), "row", None),
        P(("grp", "col"), "row"),
        P(("grp", "row"), "col", None),
        P(),
        P(),
        P(),
        P(),
        P(),
    )
    return jax.shard_map(
        functools.partial(body, mesh.shape["row"], mesh.shape["col"]),
        mesh=mesh,
        in_specs=placed,
        out_specs=(
            P(("grp", "col"), "row", None),
            P("grp", None),
            P("grp", None),
            P("grp", None),
            P("grp"),
            P("grp"),
            P("grp"),
        ),
        check_vma=False,
    )
```

```python
import functools
from itertools import zip_longest

import jax
import jax.numpy as jnp
from jax import lax
from jax.experimental import pallas as pl
from jax.experimental.pallas import tpu as pltpu
from jax.sharding import PartitionSpec as P

TOKB = 2


def standardizer_parts(homolog_embedding, standardizer_scale, standardizer_shift):
    incoming_entries = homolog_embedding.astype(jnp.float32)
    center = jnp.mean(incoming_entries, axis=-1, keepdims=True)
    varied = incoming_entries - center
    variance = jnp.mean(varied * varied, axis=-1, keepdims=True)
    reciprocal_spread = lax.rsqrt(variance + 1e-05)
    standardized_entries = varied * reciprocal_spread
    standardized_bfloat = (standardized_entries * standardizer_scale + standardizer_shift).astype(
        jnp.bfloat16
    )
    return (standardized_entries, reciprocal_spread, standardized_bfloat)


def sharded_body(
    homolog_embedding,
    presence_indicator,
    coupling_change_derivative,
    standardizer_scale,
    standardizer_shift,
    first_projection_matrix,
    second_projection_matrix,
    final_projection_matrix,
):
    shard_homolog_number, residue_line_number, feature_number = homolog_embedding.shape
    tok_cols = coupling_change_derivative.shape[1]
    width = first_projection_matrix.shape[1]
    standardized_entries, reciprocal_spread, standardized_bfloat = standardizer_parts(
        homolog_embedding, standardizer_scale, standardizer_shift
    )
    mask_single_precision = presence_indicator.astype(jnp.float32)
    mask_half_precision = presence_indicator.astype(jnp.bfloat16)
    left = (
        jnp.einsum(
            "sic,cp->sip",
            standardized_bfloat,
            first_projection_matrix,
            preferred_element_type=jnp.float32,
        )
        * mask_single_precision[..., None]
    ).astype(jnp.bfloat16)
    right = (
        jnp.einsum(
            "sic,cp->sip",
            standardized_bfloat,
            second_projection_matrix,
            preferred_element_type=jnp.float32,
        )
        * mask_single_precision[..., None]
    ).astype(jnp.bfloat16)
    left_flat = left.reshape(shard_homolog_number, residue_line_number * width)
    right_flat = right.reshape(shard_homolog_number, residue_line_number * width)
    left_all, mask_left = (
        lax.all_gather(left_flat, "col", axis=0, tiled=True),
        lax.all_gather(mask_half_precision, "col", axis=0, tiled=True),
    )
    right_wide, mask_wide = (
        lax.all_gather(right_flat, "row", axis=1, tiled=True),
        lax.all_gather(mask_half_precision, "row", axis=1, tiled=True),
    )
    right_all, mask_right = (
        lax.all_to_all(right_wide, "col", split_axis=1, concat_axis=0, tiled=True),
        lax.all_to_all(mask_wide, "col", split_axis=1, concat_axis=0, tiled=True),
    )
    seq_total = left_all.shape[0]
    right_three = right_all.reshape(seq_total, tok_cols, width)
    counts = jnp.einsum("si,sj->ij", mask_left, mask_right, preferred_element_type=jnp.float32)
    scaled = coupling_change_derivative.astype(jnp.float32) / (counts + 0.001)[..., None]
    bias_part = jnp.sum(scaled, axis=(0, 1))
    scaled_bf = scaled.astype(jnp.bfloat16)
    block_rows = residue_line_number // TOKB
    right_acc = jnp.zeros((seq_total, tok_cols, width), jnp.float32)
    wout_acc = jnp.zeros(final_projection_matrix.shape, jnp.float32)
    left_pieces = []
    for block_index in range(TOKB):
        first = block_index * block_rows
        rows_bf = scaled_bf[first : first + block_rows]
        outer_grad = jnp.einsum(
            "ijz,fz->ijf", rows_bf, final_projection_matrix, preferred_element_type=jnp.float32
        ).astype(jnp.bfloat16)
        outer_grad = outer_grad.reshape(block_rows, tok_cols, width, width)
        left_block = left_all[:, first * width : (first + block_rows) * width].reshape(
            seq_total, block_rows, width
        )
        first_factor_derivative = jnp.einsum(
            "ijce,sje->sic", outer_grad, right_three, preferred_element_type=jnp.float32
        )
        right_acc = right_acc + jnp.einsum(
            "ijce,sic->sje", outer_grad, left_block, preferred_element_type=jnp.float32
        )
        outer = jnp.einsum(
            "sic,sje->ijce", left_block, right_three, preferred_element_type=jnp.float32
        ).astype(jnp.bfloat16)
        outer = outer.reshape(block_rows, tok_cols, width * width)
        wout_acc = wout_acc + jnp.einsum(
            "ijf,ijz->fz", outer, rows_bf, preferred_element_type=jnp.float32
        )
        first_factor_derivative = first_factor_derivative.reshape(seq_total, block_rows * width)
        left_pieces.append(first_factor_derivative)
    left_terms = jnp.concatenate(left_pieces, axis=1)
    left_own = lax.psum_scatter(left_terms, "col", scatter_dimension=0, tiled=True)
    right_spread = lax.all_to_all(
        right_acc.reshape(seq_total, tok_cols * width),
        "col",
        split_axis=0,
        concat_axis=1,
        tiled=True,
    )
    right_own = lax.psum_scatter(right_spread, "row", scatter_dimension=1, tiled=True)
    left_in = (
        left_own.reshape(shard_homolog_number, residue_line_number, width)
        * mask_single_precision[..., None]
    ).astype(jnp.bfloat16)
    right_in = (
        right_own.reshape(shard_homolog_number, residue_line_number, width)
        * mask_single_precision[..., None]
    ).astype(jnp.bfloat16)
    left_part = jnp.einsum(
        "sic,sip->cp", standardized_bfloat, left_in, preferred_element_type=jnp.float32
    )
    right_part = jnp.einsum(
        "sic,sip->cp", standardized_bfloat, right_in, preferred_element_type=jnp.float32
    )
    d_normal = jnp.einsum(
        "sip,cp->sic", left_in, first_projection_matrix, preferred_element_type=jnp.float32
    ) + jnp.einsum(
        "sip,cp->sic", right_in, second_projection_matrix, preferred_element_type=jnp.float32
    )
    gain_part = jnp.sum(d_normal * standardized_entries, axis=(0, 1))
    beta_part = jnp.sum(d_normal, axis=(0, 1))
    standardized_derivative = d_normal * standardizer_scale
    embedding_derivative = reciprocal_spread * (
        standardized_derivative
        - jnp.mean(standardized_derivative, axis=-1, keepdims=True)
        - standardized_entries
        * jnp.mean(standardized_derivative * standardized_entries, axis=-1, keepdims=True)
    )
    (
        final_matrix_derivative,
        first_matrix_derivative,
        second_matrix_derivative,
        scale_factor_derivative,
        shift_term_derivative,
        shift_derivative,
    ) = lax.psum((wout_acc, left_part, right_part, gain_part, beta_part, bias_part), ("row", "col"))
    return (
        embedding_derivative,
        final_matrix_derivative,
        first_matrix_derivative,
        second_matrix_derivative,
        scale_factor_derivative,
        shift_term_derivative,
        shift_derivative,
    )


BF = jnp.bfloat16
F32 = jnp.float32


def spread(rows, cols, rule):
    r = lax.broadcasted_iota(jnp.int32, (rows, cols), 0)
    c = lax.broadcasted_iota(jnp.int32, (rows, cols), 1)
    return rule(r, c)


def mm(a, b):
    return jnp.dot(a, b, preferred_element_type=F32)


def mm_nt(a, b):
    return lax.dot_general(a, b, (((1,), (1,)), ((), ())), preferred_element_type=F32)


def mm_tn(a, b):
    return lax.dot_general(a, b, (((0,), (0,)), ((), ())), preferred_element_type=F32)


def interleave(first, second):
    odd = lax.broadcasted_iota(jnp.int16, (32, 128), 1) & 32 != 0
    return (
        jnp.where(odd, pltpu.roll(second, 32, 1), first),
        jnp.where(odd, second, pltpu.roll(first, 96, 1)),
    )


def diagonal_pair(block):
    zero = jnp.zeros_like(block)
    return jnp.concatenate(
        [jnp.concatenate([block, zero], axis=1), jnp.concatenate([zero, block], axis=1)], axis=0
    )


ABSENT = 1024.0


def pack_kernel(msa_ref, mask_ref, pair_ref, out_ref):
    msa = msa_ref[...].astype(F32)
    pick = spread(8, 512, lambda r, c: jnp.where(c // 64 == r, 1.0, 0.0)).astype(BF)
    present = mm_tn(mask_ref[...].astype(F32).astype(BF), pick) > 0.5
    for g in range(4):
        rows = jnp.concatenate([msa[:, 2 * g, :], msa[:, 2 * g + 1, :]], axis=1)
        out_ref[32 * g : 32 * g + 32, :] = jnp.where(
            present[:, 128 * g : 128 * g + 128], rows, ABSENT
        ).astype(BF)
    out_ref[128:192, :] = pair_ref[...].astype(F32).reshape(64, 128).astype(BF)


def weights_kernel(*refs):
    sources, (norm_out, back_out, final_out, first_out) = refs[:5], refs[5:9]
    held, scr, sems = refs[9:14], refs[14], refs[15]
    copies = [pltpu.make_async_copy(sources[k], held[k], sems.at[k]) for k in range(5)]
    for copy in copies:
        copy.start()
    for copy in copies:
        copy.wait()
    gain_ref, offset_ref, first_ref, second_ref, final_ref = held
    norm_out[...] = jnp.concatenate(
        [
            jnp.concatenate([ref[...]] * 2, axis=1)
            for ref in (gain_ref, offset_ref, gain_ref, offset_ref) * 2
        ],
        axis=0,
    )
    for k, ref in enumerate((first_ref, second_ref)):
        narrow = ref[...].astype(F32)
        first_out[32 * k : 32 * k + 32, :] = narrow
        wide = jnp.concatenate([narrow] * 4, axis=1)
        wide = jnp.concatenate([wide] * 4, axis=0)
        own = spread(128, 256, lambda r, c: r // 32 == c // 64)
        back_out[128 * k : 128 * k + 128, :] = jnp.where(own, wide, 0.0).astype(BF)
    scr[...] = final_ref[...].astype(F32)
    for k in range(16):
        e = 4 * (k // 2) + k % 2
        final_out[32 * k : 32 * k + 32, :] = jnp.concatenate(
            [scr[pl.ds(e, 32, stride=32), :], scr[pl.ds(e + 2, 32, stride=32), :]], axis=1
        ).astype(BF)


def averager_of():
    return spread(128, 128, lambda r, c: jnp.where(r // 64 == c // 64, 1.0 / 64, 0.0)).astype(BF)


ORDER = (0, 2, 1, 3)


def stage_steps(
    n_col, a, last, place_ref, set_refs, norm_ref, back_ref, final_ref,
    rhs_out, left_out, leftt_out, rightt_out, grad_out, pair_out, found_out, *rest
):
    *own_out, turn_scr = rest
    blocks = [ref.at[k] for ref in set_refs for k in range(ref.shape[0])]

    gain = norm_ref[0:1, :]
    offset = norm_ref[1:2, :]
    averager = averager_of()
    x = jnp.concatenate(
        [blocks[b][32 * g : 32 * g + 32, :] for g in range(4) for b in range(n_col)], axis=0
    )
    mean = mm(x, averager)
    present = mean < ABSENT / 2
    here = jnp.where(present, 1.0, 0.0)
    lane = lax.broadcasted_iota(jnp.int32, (128, 128), 1)
    found = jnp.zeros((128, 128), F32)
    for g in range(4):
        found = jnp.where(lane % 32 // 2 == 4 * a + g, here[128 * g : 128 * g + 128], found)
    found_out[...] = found
    for b in range(n_col):
        at = pl.multiple_of(lax.bitwise_xor(place_ref[0], ORDER[b]) * 8, 8)
        pair_out[:, pl.ds(at, 8), :] = blocks[b][128:192, :].astype(F32).reshape(8, 8, 128)
    yield
    varied = x.astype(F32) - mean
    inverse = lax.rsqrt(mm((varied * varied).astype(BF), averager) + 1e-05)
    normed = varied * inverse
    if own_out:
        for g in range(4):
            own_out[0][32 * g : 32 * g + 32, :] = normed[128 * g : 128 * g + 32]
            own_out[1][32 * g : 32 * g + 32, :] = inverse[128 * g : 128 * g + 32]
    yield

    def grad_piece(n):
        pair = pair_out[4 * n : 4 * n + 4].reshape(128, 128).astype(BF)
        pairs = jnp.concatenate([diagonal_pair(pair[:64]), diagonal_pair(pair[64:])], axis=0)
        grad = mm_nt(final_ref[...], pairs).astype(BF)
        for p in range(2):
            for q in range(8):
                rows = 64 * (2 * n + p)
                block = grad[64 * q : 64 * q + 64, 128 * p : 128 * p + 128]
                even, odd = interleave(block[:32], block[32:])
                grad_out[rows : rows + 32, 128 * q : 128 * q + 128] = even
                grad_out[rows + 32 : rows + 64, 128 * q : 128 * q + 128] = odd

    if not last:
        grad_piece(0)
    yield

    normal = jnp.where(present, normed * gain + offset, 0.0).astype(BF)
    rhs_out[:, 0:128] = normal
    rhs_out[:, 128:256] = normed.astype(BF)
    masked = jnp.concatenate(
        [
            jnp.concatenate([normal[128 * g : 128 * g + 128] for g in (2 * h, 2 * h + 1)], axis=1)
            for h in range(2)
        ],
        axis=0,
    )
    lefts = mm_nt(masked, back_ref[:128, :]).astype(BF)
    sides = mm_nt(back_ref[...], masked)
    for h in range(2):
        at = slice(128 * h, 128 * h + 128)
        left_out[:, at] = lefts[at]
        both = sides[:, at]
        turn_scr[at, :] = both[128:]
        for k in range(2):
            leftt_out[64 * h + 32 * k : 64 * h + 32 * k + 32, :] = jnp.concatenate(
                [both[32 * k : 32 * k + 32], both[32 * k + 64 : 32 * k + 96]], axis=1
            ).astype(BF)
    yield
    if not last:
        grad_piece(1)
    yield
    for e in range(32):
        rightt_out[e] = turn_scr[pl.ds(e, 8, stride=32), :]
    if last:
        grad_piece(0)
        grad_piece(1)


def stage_kernel(*arguments):
    for _ in stage_steps(*arguments):
        pass


def own_kernel(n_col, place_ref, front_ref, rear_ref, norm_ref, back_ref, final_ref, *rest):
    stage_kernel(n_col, 0, False, place_ref, (front_ref, rear_ref), norm_ref, back_ref, final_ref, *rest)


def pair_kernel(n_col, place_ref, core_ref, front_ref, rear_ref, norm_ref, back_ref, final_ref, *rest):
    common = (norm_ref, back_ref, final_ref)
    both = (
        stage_steps(n_col, 1, False, place_ref, (core_ref,), *common, *rest[:7], rest[14]),
        stage_steps(n_col, 2, False, place_ref, (front_ref, rear_ref), *common, *rest[7:14], rest[15]),
    )
    for _ in zip_longest(*both):
        pass


def part_kernel(n_row, n_col, place_ref, front_ref, rear_ref, *refs):
    stages = [refs[7 * a : 7 * a + 7] for a in range(n_row - 1)]
    (
        normed_ref, inverse_ref, norm_ref, back_ref, final_ref, first_ref,
        emb_out, final_hbm_out, first_out, second_out, gain_out, offset_out, bias_out,
        right_scr, scaled_scr, grad_scr, outer_scr, all_scr,
        final_out, out_sem, turn_scr,
    ) = refs[7 * (n_row - 1) : -7]
    stages.append(refs[-7:])
    stage_kernel(
        n_col, n_row - 1, True, place_ref, (front_ref, rear_ref),
        norm_ref, back_ref, final_ref, *stages[-1], turn_scr,
    )
    gain = norm_ref[0:1, :]
    averager = averager_of()
    lane = lax.broadcasted_iota(jnp.int32, (128, 128), 1)

    found = sum(stage[6][...] for stage in stages)
    turned = pltpu.roll(found, 64, 1)
    mask = jnp.where((lane % 2 == 0) == (lane < 64), found, turned)
    mask_t = mask.T

    for e in range(32):
        right_scr[32 * e : 32 * e + 32, :] = jnp.concatenate(
            [stage[3][e] for stage in stages], axis=0
        ).astype(BF)

    mask_bf = mask.astype(BF)
    share = (1.0 / (mm_tn(mask_bf, mask_bf)[0:32] + 0.001)).astype(BF)
    for i in range(32):
        a, at = i // 8, 32 * (i % 8)
        for q in range(8):
            grad_scr[32 * i : 32 * i + 32, 128 * q : 128 * q + 128] = (
                stages[a][4][at : at + 32, 128 * q : 128 * q + 128] * share[i : i + 1]
            )
    left = jnp.concatenate([stage[1][...] for stage in stages], axis=1)
    right_grad = mm(left, grad_scr[...])
    left_grad = mm(grad_scr[...], right_scr[...])

    turn = spread(
        256, 256, lambda r, c: jnp.where((r // 8 == c % 32) & (r % 8 == c // 32), 1.0, 0.0)
    ).astype(BF)
    mask_two = jnp.concatenate([mask, mask], axis=1)
    right_in = [
        mm_nt(turn, (right_grad[:, 256 * q : 256 * q + 256] * mask_two).astype(BF))
        for q in range(4)
    ]
    for t in range(32):
        at = slice(128 * (t // 2), 128 * (t // 2) + 128)
        row = 32 * (t % 2)
        all_scr[row : row + 32, at] = (
            left_grad[32 * t : 32 * t + 32] * mask_t[t : t + 1]
        ).astype(BF)
        all_scr[row + 64 : row + 96, at] = jnp.concatenate(
            [part[8 * t : 8 * t + 8] for part in right_in], axis=0
        ).astype(BF)

    bias = jnp.zeros((1, 128), F32)
    ones = jnp.ones((128, 128), BF)
    for p in range(8):
        both_on = jnp.concatenate(
            [mask_t[0:32] * mask_t[i : i + 1] for i in range(4 * p, 4 * p + 4)], axis=0
        ).astype(BF)
        counts = mm(both_on, ones)
        pair = stages[p // 2][5][4 * (p % 2) : 4 * (p % 2) + 4]
        scaled = pair.reshape(128, 128) / (counts + 0.001)
        bias = bias + jnp.sum(scaled, axis=0, keepdims=True)
        scaled_scr[128 * p : 128 * p + 128, :] = scaled.astype(BF)
    bias_out[...] = bias

    left_t = jnp.concatenate([stage[2][...] for stage in stages], axis=0)
    for n in range(8):
        rights = jnp.concatenate(
            [diagonal_pair(right_scr[64 * p : 64 * p + 64, :]) for p in (2 * n, 2 * n + 1)], axis=0
        )
        outer = mm_nt(left_t, rights).astype(BF)
        for p in range(2):
            for q in range(8):
                rows = 64 * (2 * n + p)
                block = outer[64 * q : 64 * q + 64, 128 * p : 128 * p + 128]
                even, odd = interleave(block[:32], block[32:])
                outer_scr[rows : rows + 32, 128 * q : 128 * q + 128] = even
                outer_scr[rows + 32 : rows + 64, 128 * q : 128 * q + 128] = odd
    final = mm(outer_scr[...], scaled_scr[...])
    for e in range(32):
        final_out[pl.ds(e, 32, stride=32), :] = final[32 * e : 32 * e + 32]
    final_send = pltpu.make_async_copy(final_out, final_hbm_out, out_sem)
    final_send.start()

    total = mm(
        all_scr[...], jnp.concatenate([stage[0][...] for stage in stages], axis=0)
    )
    sums = all_scr[:, 0:128].astype(F32)
    for g in range(1, 16):
        sums = sums + all_scr[:, 128 * g : 128 * g + 128].astype(F32)

    def fold(block):
        return block[0:32, 0:64] + block[32:64, 64:128]

    first_out[...] = fold(total[0:64, 0:128])
    second_out[...] = fold(total[64:128, 0:128])
    sums = jnp.sum(sums, axis=1, keepdims=True)
    left_sum = sums[0:32] + sums[32:64]
    right_sum = sums[64:96] + sums[96:128]
    first, second = first_ref[0:32, :], first_ref[32:64, :]
    gain_out[...] = jnp.sum(
        first * fold(total[0:64, 128:256]) + second * fold(total[64:128, 128:256]),
        axis=0, keepdims=True,
    )
    offset_out[...] = jnp.sum(first * left_sum + second * right_sum, axis=0, keepdims=True)

    grads = jnp.concatenate(
        [
            jnp.concatenate(
                [
                    all_scr[row : row + 64, 128 * g : 128 * g + 128]
                    for row in (0, 64)
                    for g in (2 * h, 2 * h + 1)
                ],
                axis=0,
            )
            for h in range(2)
        ],
        axis=1,
    )
    d_normal = mm_tn(grads, back_ref[...])
    d_hat = jnp.concatenate(
        [
            d_normal[128 * h : 128 * h + 32, 128 * half : 128 * half + 128] * gain
            for h in range(2)
            for half in range(2)
        ],
        axis=0,
    )
    normed = normed_ref[...]
    means = mm(jnp.concatenate([d_hat, d_hat * normed], axis=0).astype(BF), averager)
    result = inverse_ref[...] * (d_hat - means[:128] - normed * means[128:])
    for g in range(4):
        emb_out[:, 2 * g, :] = result[32 * g : 32 * g + 32, 0:64]
        emb_out[:, 2 * g + 1, :] = result[32 * g : 32 * g + 32, 64:128]
    final_send.wait()


def vmem(count):
    return [pl.BlockSpec(memory_space=pltpu.VMEM)] * count


LIMIT = pltpu.CompilerParams(vmem_limit_bytes=32 * 1024 * 1024)


def gathered_body(
    n_row,
    n_col,
    homolog_embedding,
    presence_indicator,
    coupling_change_derivative,
    standardizer_scale,
    standardizer_shift,
    first_projection_matrix,
    second_projection_matrix,
    final_projection_matrix,
):
    shards, tokens, features = homolog_embedding.shape
    width = first_projection_matrix.shape[1]
    first_t, second_t = first_projection_matrix.T, second_projection_matrix.T
    shape = lambda *dims: jax.ShapeDtypeStruct(dims, F32)
    held = lambda *dims: pltpu.VMEM(dims, F32)
    held_bf = lambda *dims: pltpu.VMEM(dims, BF)
    hbm = pl.BlockSpec(memory_space=pltpu.HBM)
    place = lax.bitwise_xor(lax.axis_index("row"), lax.axis_index("col"))
    place = place.astype(jnp.int32).reshape(1)
    packed = pl.pallas_call(
        pack_kernel,
        out_shape=held_bf(192, 128),
        in_specs=vmem(3),
        out_specs=vmem(1)[0],
    )(homolog_embedding, presence_indicator.T, coupling_change_derivative)
    def over(axis, size, step, array):
        return lax.ppermute(array, axis, [(k, k ^ step) for k in range(size)])

    far = over("col", n_col, 2, packed)
    near = over("col", n_col, 1, packed)
    last = over("col", n_col, 3, packed)
    front = jnp.stack([packed, far])
    chip_front = over("row", n_row, 2, front)
    rear = jnp.stack([near, last])
    chip_rear = over("row", n_row, 2, rear)
    front, final_projection_matrix = lax.optimization_barrier((front, final_projection_matrix))
    weights = pl.pallas_call(
        weights_kernel,
        out_shape=(
            held(8, 128), held_bf(256, 256), held_bf(width * width // 2, 256), held(2 * width, features),
        ),
        in_specs=[hbm] * 5,
        out_specs=tuple(vmem(4)),
        scratch_shapes=[
            pltpu.VMEM((1, features), F32),
            pltpu.VMEM((1, features), F32),
            pltpu.VMEM((width, features), BF),
            pltpu.VMEM((width, features), BF),
            pltpu.VMEM((width * width, 128), BF),
            pltpu.VMEM((width * width, 128), F32),
            pltpu.SemaphoreType.DMA((5,)),
        ],
        compiler_params=LIMIT,
    )(
        *[
            pltpu.with_memory_space_constraint(x, pltpu.HBM)
            for x in (
                standardizer_scale.reshape(1, features),
                standardizer_shift.reshape(1, features),
                first_t,
                second_t,
                final_projection_matrix,
            )
        ]
    )
    norm, back, final_turned, first = weights
    own = jnp.concatenate([front, rear])
    own, chip_front, norm = lax.optimization_barrier((own, chip_front, norm))
    core = over("row", n_row, 1, own)
    stage_outs = [
        held_bf(512, 256), held_bf(128, 256), held_bf(128, 256), held(width, 8, 128),
        held_bf(256, 1024), held(8, 32, 128), held(128, 128),
    ]
    scalar = pl.BlockSpec(memory_space=pltpu.SMEM)

    def stages_of(kernel, sets, outs, flops):
        return pl.pallas_call(
            functools.partial(kernel, n_col),
            out_shape=tuple(outs),
            in_specs=[scalar] + vmem(len(sets) + 3),
            out_specs=tuple(vmem(len(outs))),
            scratch_shapes=[pltpu.VMEM((256, 128), F32)] * (len(outs) // 7),
            compiler_params=LIMIT,
            cost_estimate=pl.CostEstimate(
                flops=flops, bytes_accessed=flops // 256, transcendentals=0
            ),
        )(place, *sets, norm, back, final_turned)

    both_front = over("row", n_row, 1, chip_front)
    own_stage = stages_of(own_kernel, (front, rear), stage_outs + [held(128, 128)] * 2, 1_000_000_000)
    chip_rear, own_stage = lax.optimization_barrier((chip_rear, own_stage))
    both_rear = over("row", n_row, 1, chip_rear)
    pair_stages = stages_of(pair_kernel, (core, chip_front, chip_rear), stage_outs * 2, 1000000)
    stages = [own_stage[:7], pair_stages]
    outs = pl.pallas_call(
        functools.partial(part_kernel, n_row, n_col),
        out_shape=(
            shape(shards, tokens, features),
            shape(width * width, 128),
            shape(width, features),
            shape(width, features),
            shape(1, features),
            shape(1, features),
            shape(1, 128),
        ),
        in_specs=[scalar] + vmem(7 * (n_row - 1) + 8),
        out_specs=(*vmem(1), hbm, *vmem(5)),
        scratch_shapes=[
            pltpu.VMEM((1024, 128), BF),
            pltpu.VMEM((1024, 128), BF),
            pltpu.VMEM((1024, 1024), BF),
            pltpu.VMEM((1024, 1024), BF),
            pltpu.VMEM((128, 2048), BF),
            pltpu.VMEM((1024, 128), F32),
            pltpu.SemaphoreType.DMA,
            pltpu.VMEM((256, 128), F32),
            *stage_outs,
        ],
        compiler_params=LIMIT,
    )(place, both_front, both_rear, *[x for s in stages for x in s], *own_stage[7:], norm, back, final_turned, first)
    emb, final, first, second, gain, offset, bias = outs
    return emb, final, first.T, second.T, gain.reshape(-1), offset.reshape(-1), bias.reshape(-1)


def body(n_row, n_col, *arguments):
    msa, _, pair = arguments[:3]
    width = arguments[5].shape[1]
    fits = (
        n_row == 4
        and n_col == 4
        and msa.shape == (32, 8, 64)
        and pair.shape == (8, 8, 128)
        and width == 32
    )
    if fits:
        return gathered_body(n_row, n_col, *arguments)
    return sharded_body(*arguments)


def solution(mesh):
    placed = (
        P(("grp", "col"), "row", None),
        P(("grp", "col"), "row"),
        P(("grp", "row"), "col", None),
        P(),
        P(),
        P(),
        P(),
        P(),
    )
    return jax.shard_map(
        functools.partial(body, mesh.shape["row"], mesh.shape["col"]),
        mesh=mesh,
        in_specs=placed,
        out_specs=(
            P(("grp", "col"), "row", None),
            P("grp", None),
            P("grp", None),
            P("grp", None),
            P("grp"),
            P("grp"),
            P("grp"),
        ),
        check_vma=False,
    )
```
